32 devices in a mesh: seq: 4 (over z), head: 2 (over core), batch: 4 (over y, x).
Axes of the slice: x: 2, y: 2, z: 4, core: 2. Of those that a mesh axis runs over, the one named last changes fastest.
Arguments:
- tokens: bfloat16 [4, 2048, 1024], P('batch', 'seq'), may hold values from -6 to 6
- seg_ids: int32 [4, 2048], P('batch'), may hold values from 0 to 66, as said below
- mixer_gain: float32 [1024], replicated, may hold values from 0.5 to 1.5
- mamba_gate: bfloat16 [1024, 1536], P(None, 'head'), may hold values from -0.1875 to 0.1875
- mamba_input: bfloat16 [1024, 1536], P(None, 'head'), may hold values from -0.1875 to 0.1875
- mamba_maps: bfloat16 [1024, 256], replicated, may hold values from -0.1875 to 0.1875
- mamba_step: bfloat16 [1024, 24], P(None, 'head'), may hold values from -0.1875 to 0.1875
- conv_inner: float32 [4, 1536], P(None, 'head'), may hold values from -3 to 3
- conv_maps: float32 [4, 256], replicated, may hold values from -3 to 3
- log_rate: float32 [24], P('head'), may hold values from -11 to -1
- step_bias: float32 [24], P('head'), may hold values from -3 to 1
- skip_gain: float32 [24], P('head'), may hold values from 0.5 to 1.5
- mamba_gain: float32 [1536], P('head'), may hold values from 0.5 to 1.5
- mamba_output: bfloat16 [1024, 1536], P(None, 'head'), may hold values from -0.15625 to 0.15625
- query_weight: bfloat16 [1024, 512], P(None, 'head'), may hold values from -0.4375 to 0.4375
- memory_weight: bfloat16 [1024, 256], P(None, 'head'), may hold values from -0.1875 to 0.1875
- attention_out: bfloat16 [1024, 512], P(None, 'head'), may hold values from -1.5 to 1.5
- feed_gain: float32 [1024], replicated, may hold values from 0.5 to 1.5
- gate_weight: bfloat16 [1024, 2048], P(None, 'head'), may hold values from -0.1875 to 0.1875
- lift_weight: bfloat16 [1024, 2048], P(None, 'head'), may hold values from -0.1875 to 0.1875
- down_weight: bfloat16 [1024, 2048], P(None, 'head'), may hold values from -0.125 to 0.125
- cotangent: bfloat16 [4, 2048, 1024], P('batch', 'seq'), may hold values from -6 to 6
Outputs:
- layer_out: bfloat16 [4, 2048, 1024], P('batch', 'seq')
- grad_tokens: float32 [4, 2048, 1024], P('batch', 'seq')
- grad_mixer_gain: float32 [1024], P('seq')
- grad_mamba_gate: float32 [1024, 1536], P('seq', 'head')
- grad_mamba_input: float32 [1024, 1536], P('seq', 'head')
- grad_mamba_maps: float32 [1024, 256], P('seq')
- grad_mamba_step: float32 [1024, 24], P('seq', 'head')
- grad_conv_inner: float32 [4, 1536], P(None, 'head')
- grad_conv_maps: float32 [4, 256], replicated
- grad_log_rate: float32 [24], P('head')
- grad_step_bias: float32 [24], P('head')
- grad_skip_gain: float32 [24], P('head')
- grad_mamba_gain: float32 [1536], P('head')
- grad_mamba_output: float32 [1024, 1536], P('seq', 'head')
- grad_query_weight: float32 [1024, 512], P('seq', 'head')
- grad_memory_weight: float32 [1024, 256], P('seq', 'head')
- grad_attention_out: float32 [1024, 512], P('seq', 'head')
- grad_feed_gain: float32 [1024], P('seq')
- grad_gate_weight: float32 [1024, 2048], P('seq', 'head')
- grad_lift_weight: float32 [1024, 2048], P('seq', 'head')
- grad_down_weight: float32 [1024, 2048], P('seq', 'head')
The draws below stay inside these ranges and needn't reach their ends.
Inputs may be any that keep to these rules, and one draw needn't show every extreme that they name: In each sequence seg_ids begin at 0, never fall and rise by at most one from a position to the next; one document begins within the first 512 positions and ends within the last 512; every sequence holds exactly 3 + 2 * max(1, 32) documents.
All inputs are finite; a program needn't handle non-finite values.
Results may differ from the reference program's by a relative error of at most 0.024.
Values may be sent and summed in bfloat16 or wider, within the bound.
A program may use at most 192 MiB of HBM per device.

```python
import jax
import jax.numpy as jnp
from jax import lax

D = 1024
MH = 24
HEAD_P = 64
STATE = 128
CONV = 4
QH = 8
KVH = 2
HD = 64
FF = 2048
TOK_DEV = 512
LENGTH = 2048
SEQS = 4


def draw_seg_ids(key, part):
    key = jax.random.fold_in(key, 7)
    open_key, close_key, score_key = jax.random.split(key, 3)
    extra_count = max(1, TOK_DEV // 16)
    opening = jax.random.randint(open_key, (SEQS, 1), TOK_DEV // 2, TOK_DEV)
    closing = jax.random.randint(close_key, (SEQS, 1), LENGTH - TOK_DEV + 1, LENGTH - TOK_DEV // 2 + 1)
    places = jnp.arange(LENGTH, dtype=jnp.int32)[None, :]
    scores = jax.random.randint(score_key, (SEQS, LENGTH), 0, LENGTH) * LENGTH + places
    head_region = (places >= 1) & (places < opening)
    tail_region = places > closing
    head_scores = jnp.where(head_region, scores, -1)
    tail_scores = jnp.where(tail_region, scores, -1)
    head_picks = lax.top_k(head_scores, extra_count)[1].astype(jnp.int32)
    tail_picks = lax.top_k(tail_scores, extra_count)[1].astype(jnp.int32)
    picks = jnp.concatenate([head_picks, tail_picks], axis=1)
    chosen = jnp.any(places[:, :, None] == picks[:, None, :], axis=2)
    starts = chosen | (places == opening) | (places == closing) | (places == 0)
    return jnp.cumsum(starts.astype(jnp.int32), axis=1) - 1


def levels(own_key, extent, cuts, low, top_value):
    loudness, own = 1.0, jax.random.fold_in(own_key, 6)
    for dim, shards_of in cuts:
        heights = jnp.exp(jax.random.uniform(jax.random.fold_in(own, dim), (shards_of,), jnp.float32, low / len(cuts), top_value / len(cuts)))
        loudness = loudness * jnp.repeat(heights, extent[dim] // shards_of).reshape([-1 if axis == dim else 1 for axis in range(len(extent))])
    return loudness


def noise(own_key, shape, scale, most, cuts=(), kind=jnp.bfloat16):
    level = levels(own_key, shape, cuts, -0.22, 0.18) if cuts else 1.0
    values = jax.random.normal(own_key, shape, jnp.float32) * scale * level
    return jnp.minimum(jnp.maximum(values, -most), most).astype(kind)


def setup_inputs(seed: int = 0) -> dict:
    splits = jax.random.split(jax.random.key(seed), 23)
    return {
        "tokens": noise(splits[0], (SEQS, LENGTH, D), 1.0, 6.0, ((0, 4), (1, 4))),
        "seg_ids": draw_seg_ids(jax.random.fold_in(splits[22], 71), 0),
        "mixer_gain": jnp.clip(1.0 + 0.1 * jax.random.normal(splits[2], (D,), jnp.float32), 0.5, 1.5),
        "mamba_gate": noise(splits[3], (D, MH * HEAD_P), D ** -0.5, 0.1875, ((1, 2),)),
        "mamba_input": noise(splits[4], (D, MH * HEAD_P), D ** -0.5, 0.1875, ((1, 2),)),
        "mamba_maps": noise(splits[5], (D, 2 * STATE), D ** -0.5, 0.1875),
        "mamba_step": noise(splits[6], (D, MH), D ** -0.5, 0.1875, ((1, 2),)),
        "conv_inner": noise(splits[7], (CONV, MH * HEAD_P), 0.5, 3.0, ((1, 2),), jnp.float32),
        "conv_maps": noise(splits[8], (CONV, 2 * STATE), 0.5, 3.0, (), jnp.float32),
        "log_rate": jnp.clip(-11.0 + 10.0 * jax.random.uniform(splits[9], (MH,), jnp.float32) ** levels(splits[9], (MH,), ((0, 2),), -0.2, 0.2), -11.0, -1.0),
        "step_bias": jnp.clip(-3.0 + 4.0 * jax.random.uniform(splits[10], (MH,), jnp.float32) ** levels(splits[10], (MH,), ((0, 2),), -0.2, 0.2), -3.0, 1.0),
        "skip_gain": jnp.clip(0.5 + 1.0 * jax.random.uniform(splits[11], (MH,), jnp.float32) ** levels(splits[11], (MH,), ((0, 2),), -0.2, 0.2), 0.5, 1.5),
        "mamba_gain": jnp.clip(1.0 + 0.1 * jax.random.normal(splits[12], (MH * HEAD_P,), jnp.float32), 0.5, 1.5),
        "mamba_output": noise(splits[13], (D, MH * HEAD_P), (MH * HEAD_P) ** -0.5, 0.15625, ((1, 2),)),
        "query_weight": noise(splits[14], (D, QH * HD), (D // 6) ** -0.5, 0.4375, ((1, 2),)),
        "memory_weight": noise(splits[15], (D, 2 * KVH * HD), D ** -0.5, 0.1875, ((1, 2),)),
        "attention_out": noise(splits[16], (D, QH * HD), (QH * HD // 32) ** -0.5, 1.5, ((1, 2),)),
        "feed_gain": jnp.clip(1.0 + 0.1 * jax.random.normal(splits[17], (D,), jnp.float32), 0.5, 1.5),
        "gate_weight": noise(splits[18], (D, FF), D ** -0.5, 0.1875, ((1, 2),)),
        "lift_weight": noise(splits[19], (D, FF), D ** -0.5, 0.1875, ((1, 2),)),
        "down_weight": noise(splits[20], (D, FF), FF ** -0.5, 0.125, ((1, 2),)),
        "cotangent": noise(splits[21], (SEQS, LENGTH, D), 1.0, 6.0, ((0, 4), (1, 4))),
    }


eps_norm = 1e-05
rope_base = 10000.0
neg_large = -1e+30
highest = lax.Precision.HIGHEST

@jax.custom_vjp
def low(v):
    return lax.optimization_barrier(v.astype(jnp.bfloat16)).astype(jnp.float32)

@jax.custom_vjp
def low_back(v):
    return v

def low_keep(v):
    return (low(v), None)

def low_pass(kept, grad):
    return (grad,)

def back_keep(v):
    return (v, None)

def back_low(kept, grad):
    return (low(grad),)
low.defvjp(low_keep, low_pass)
low_back.defvjp(back_keep, back_low)

def dense(former, latter):
    return jnp.dot(former, latter, precision=highest)

def dense_last(former, latter):
    return jnp.dot(former, latter.T, precision=highest)

def rms_scale(hidden, gain):
    inverse = lax.rsqrt(lax.optimization_barrier(jnp.mean(hidden * hidden, axis=-1, keepdims=True)) + eps_norm)
    return hidden * inverse * gain

def rotate(values, position, factor):
    half_dim = values.shape[-1] // 2
    inverse_freq = rope_base ** (-jnp.arange(half_dim, dtype=jnp.float32) / half_dim)
    angles = position.astype(jnp.float32)[:, None] * inverse_freq[None, :]
    cosine = jnp.cos(angles)[:, None, :]
    sine_part = factor * jnp.sin(angles)[:, None, :]
    former = values[..., :half_dim]
    latter = values[..., half_dim:]
    return jnp.concatenate([former * cosine - latter * sine_part, latter * cosine + former * sine_part], axis=-1)

def conv_mix(extended, kernel, window_seg):
    tap_count = kernel.shape[0]
    row_count = extended.shape[0] - tap_count + 1
    own_seg = window_seg[tap_count - 1:]
    summed = jnp.zeros((row_count, extended.shape[1]), extended.dtype)
    for tap_index in range(tap_count):
        same_doc = (window_seg[tap_index:tap_index + row_count] == own_seg).astype(extended.dtype)
        summed = summed + kernel[tap_index][None, :] * extended[tap_index:tap_index + row_count] * same_doc[:, None]
    return jax.nn.silu(summed)

def state_part(scan_input, input_map, step_size, log_rate, local_seg, prev_seg):
    cumulative = jnp.cumsum(-jnp.exp(log_rate)[None, :] * step_size, axis=0)
    final_log = cumulative[-1]
    in_tail = local_seg == local_seg[-1]
    spread = jnp.where(in_tail[:, None], final_log[None, :] - cumulative, 0.0)
    weights = jnp.exp(spread) * in_tail[:, None].astype(step_size.dtype) * step_size
    local_state = jnp.einsum('sh,sn,shp->hnp', weights, input_map, scan_input, precision=highest)
    unbroken = (local_seg[-1] == prev_seg).astype(step_size.dtype)
    return (local_state, jnp.exp(final_log) * unbroken)

def output_part(scan_input, input_map, output_map, step_size, log_rate, skip_gain, state_in, local_seg, prev_seg):
    cumulative = jnp.cumsum(-jnp.exp(log_rate)[None, :] * step_size, axis=0)
    row_index = jnp.arange(local_seg.shape[0])
    causal = (row_index[:, None] >= row_index[None, :]) & (local_seg[:, None] == local_seg[None, :])
    gaps = jnp.where(causal[:, :, None], cumulative[:, None, :] - cumulative[None, :, :], 0.0)
    decays = jnp.exp(gaps) * causal[:, :, None].astype(step_size.dtype)
    intersection = jnp.dot(output_map, input_map.T, precision=highest)
    mixing = intersection[:, :, None] * decays * step_size[None, :, :]
    inside = jnp.einsum('tsh,shp->thp', mixing, scan_input, precision=highest)
    carried = (local_seg == prev_seg).astype(step_size.dtype)[:, None] * jnp.exp(cumulative)
    across = jnp.einsum('tn,hnp->thp', output_map, state_in, precision=highest) * carried[:, :, None]
    return inside + across + skip_gain[None, :, None] * scan_input

def gate_norm(mamba_y, gate_z, mamba_gain):
    row_count = mamba_y.shape[0]
    gated = mamba_y.reshape(row_count, -1) * jax.nn.silu(gate_z)
    inverse = lax.rsqrt(lax.optimization_barrier(jnp.mean(gated * gated, axis=-1, keepdims=True)) + eps_norm)
    return gated * inverse * mamba_gain

def layer(params, hidden, segments):
    mixer_gain, mamba_gate, mamba_input, mamba_maps, mamba_step, conv_inner, conv_maps, log_rate, step_bias, skip_gain, mamba_gain, mamba_output, query_weight, memory_weight, attention_out, feed_gain, gate_weight, lift_weight, down_weight = params
    length = hidden.shape[0]
    tap_count = conv_inner.shape[0]
    normed = low(rms_scale(hidden, mixer_gain))
    gate_z = low_back(dense(normed, mamba_gate))
    inner_x = low_back(dense(normed, mamba_input))
    maps = low_back(dense(normed, mamba_maps))
    raw_step = low_back(dense(normed, mamba_step))
    query = low_back(dense(normed, query_weight))
    memory = low_back(dense(normed, memory_weight))
    before = jnp.concatenate([inner_x, maps], axis=1)
    extended = jnp.concatenate([jnp.zeros((tap_count - 1, before.shape[1]), before.dtype), before], axis=0)
    padded_seg = jnp.concatenate([jnp.full((tap_count - 1,), -1, jnp.int32), segments.astype(jnp.int32)])
    kernel = jnp.concatenate([conv_inner, conv_maps], axis=1)
    activated = conv_mix(extended, kernel, padded_seg)
    inner_width = MH * HEAD_P
    scan_input = activated[:, :inner_width].reshape(length, MH, HEAD_P)
    input_map = activated[:, inner_width:inner_width + STATE]
    output_map = activated[:, inner_width + STATE:]
    step_size = jax.nn.softplus(raw_step + step_bias)
    block_count = length // TOK_DEV
    starts = jnp.arange(block_count, dtype=jnp.int32) * TOK_DEV
    prev_list = jnp.where(starts > 0, segments[jnp.maximum(starts - 1, 0)], -1).astype(jnp.int32)

    def stretch_step(state_now, pieces):
        part_input, part_in_map, part_out_map, part_step, part_seg, part_prev = pieces
        mamba_part = output_part(part_input, part_in_map, part_out_map, part_step, log_rate, skip_gain, state_now, part_seg, part_prev)
        local_state, decays = state_part(part_input, part_in_map, part_step, log_rate, part_seg, part_prev)
        return (decays[:, None, None] * state_now + local_state, mamba_part)
    _, mamba_blocks = lax.scan(jax.checkpoint(stretch_step), jnp.zeros((MH, STATE, HEAD_P), jnp.float32), (scan_input.reshape(block_count, TOK_DEV, MH, HEAD_P), input_map.reshape(block_count, TOK_DEV, STATE), output_map.reshape(block_count, TOK_DEV, STATE), step_size.reshape(block_count, TOK_DEV, MH), segments.reshape(block_count, TOK_DEV), prev_list))
    mamba_y = mamba_blocks.reshape(length, MH, HEAD_P)
    gated = low(gate_norm(mamba_y, gate_z, mamba_gain))
    mamba_out = dense_last(gated, mamba_output)
    position = jnp.arange(length, dtype=jnp.int32)
    query_low = low(rotate(query.reshape(length, QH, HD), position, 1.0))
    memory_split = memory.reshape(length, KVH, 2, HD)
    key_low = low(rotate(memory_split[:, :, 0], position, 1.0))
    value_low = low(memory_split[:, :, 1])
    group_size = QH // KVH
    key_all = jnp.repeat(key_low, group_size, axis=1)
    value_all = jnp.repeat(value_low, group_size, axis=1)
    query_rows = min(512, length)
    query_blocks = length // query_rows

    def attend(pieces):
        query_part, query_pos = pieces
        scores = low_back(jnp.einsum('qhd,khd->hqk', query_part, key_all, precision=highest) * HD ** (-0.5))
        allowed = (position[None, :] <= query_pos[:, None]) & (segments[None, :] == segments[query_pos][:, None])
        masked = jnp.where(allowed[None], scores, neg_large)
        row_max = lax.optimization_barrier(jnp.max(masked, axis=-1, keepdims=True))
        weights = jnp.where(allowed[None], jnp.exp(masked - row_max), 0.0)
        row_sum = lax.optimization_barrier(jnp.sum(weights, axis=-1))
        numer = low_back(jnp.einsum('hqk,khd->qhd', low(weights), value_all, precision=highest))
        return numer / row_sum.T[:, :, None]
    attention = lax.map(jax.checkpoint(attend), (query_low.reshape(query_blocks, query_rows, QH, HD), position.reshape(query_blocks, query_rows)))
    attention = low(attention.reshape(length, QH * HD))
    mixture = low_back(mamba_out + dense_last(attention, attention_out))
    second = hidden + mixture
    normed2 = low(rms_scale(second, feed_gain))
    gate_value = low_back(dense(normed2, gate_weight))
    lift_value = low_back(dense(normed2, lift_weight))
    active = low(jax.nn.silu(gate_value) * lift_value)
    return second + dense_last(active, down_weight)

def reference(tokens, seg_ids, mixer_gain, mamba_gate, mamba_input, mamba_maps, mamba_step, conv_inner, conv_maps, log_rate, step_bias, skip_gain, mamba_gain, mamba_output, query_weight, memory_weight, attention_out, feed_gain, gate_weight, lift_weight, down_weight, cotangent):
    params = tuple((member.astype(jnp.float32) for member in (mixer_gain, mamba_gate, mamba_input, mamba_maps, mamba_step, conv_inner, conv_maps, log_rate, step_bias, skip_gain, mamba_gain, mamba_output, query_weight, memory_weight, attention_out, feed_gain, gate_weight, lift_weight, down_weight)))

    def one_sequence(summed, pieces):
        hidden, segments, grad_out = pieces

        def apply_layer(weights_now, hidden_now):
            return layer(weights_now, hidden_now, segments)
        result, pullback = jax.vjp(apply_layer, params, hidden)
        weight_grads, hidden_grad = pullback(grad_out)
        return (jax.tree.map(jnp.add, summed, weight_grads), (result.astype(jnp.bfloat16), hidden_grad))
    initial = jax.tree.map(jnp.zeros_like, params)
    summed, (results, grad_tokens) = lax.scan(one_sequence, initial, (tokens.astype(jnp.float32), seg_ids.astype(jnp.int32), cotangent.astype(jnp.float32)))
    return (results, grad_tokens, summed[0], summed[1], summed[2], summed[3], summed[4], summed[5], summed[6], summed[7], summed[8], summed[9], summed[10], summed[11], summed[12], summed[13], summed[14], summed[15], summed[16], summed[17], summed[18])
```

```python
import functools

import jax
import jax.numpy as jnp
from jax import lax
from jax.experimental import pallas as pl
from jax.experimental.pallas import tpu as pltpu
from jax.sharding import PartitionSpec as P

HD = 64


eps_norm = 1e-05
rope_base = 10000.0
neg_large = -1e30
highest = lax.Precision.HIGHEST


LANES = 128
MESH = pl.DeviceIdType.MESH


def exchange(source, target, send_sem, recv_sem, device):
    return pltpu.make_async_remote_copy(
        src_ref=source,
        dst_ref=target,
        send_sem=send_sem,
        recv_sem=recv_sem,
        device_id=device,
        device_id_type=MESH,
    )


def column_chunks(widths, most):
    chunks = []
    for group, width in enumerate(widths):
        count = -(-width // most)
        tiles = width // LANES
        start = 0
        for k in range(count):
            size = (tiles // count + (1 if k < tiles % count else 0)) * LANES
            chunks.append((group, start, size))
            start += size
    return chunks


def reduce_kernel(seq_count, batch_count, chunks, *refs):
    count = 1 + max(c[0] for c in chunks)
    groups, refs = refs[:count], refs[count:]
    small_in, refs = refs[0], refs[1:]
    outs, refs = refs[:count], refs[count:]
    small_out, refs = refs[0], refs[1:]
    first_buf, refs = refs[:count], refs[count:]
    second_buf, refs = refs[:count], refs[count:]
    third_buf, refs = refs[:count], refs[count:]
    small_buf, sem_one, sem_two, sem_seq, sem_back, sem_small = refs
    seq, head, batch = lax.axis_index("seq"), lax.axis_index("head"), lax.axis_index("batch")
    low_bit = lax.rem(batch, 2)
    high_bit = batch // 2
    low_peer = (seq, head, batch + 1 - 2 * low_bit)
    high_peer = (seq, head, batch + 2 - 4 * high_bit)
    world = seq_count * batch_count
    mine = seq * batch_count + batch

    def other(step):
        place = lax.rem(mine + step, world)
        return (place // batch_count, head, lax.rem(place, batch_count))

    barrier = pltpu.get_barrier_semaphore()

    def greet(step, carry):
        pl.semaphore_signal(barrier, inc=1, device_id=other(step), device_id_type=MESH)
        return carry

    lax.fori_loop(1, world, greet, 0)
    pl.semaphore_wait(barrier, world - 1)

    def small_copy(step):
        return exchange(
            small_in,
            small_buf.at[mine],
            sem_small.at[0, step],
            sem_small.at[1, step],
            other(step),
        )

    def first_copy(k):
        group, start, size = chunks[k]
        columns = pl.ds(start, size)
        source, target = groups[group], first_buf[group]
        if k % 2 == 0:
            part = source.at[:, :, 1 - low_bit, :, columns]
            peer = low_peer
        else:
            part = source.at[:, 1 - high_bit, :, :, columns]
            peer = high_peer
        return exchange(part, target.at[:, :, :, columns], sem_one.at[0, k], sem_one.at[1, k], peer)

    def second_copy(k):
        group, start, size = chunks[k]
        columns = pl.ds(start, size)
        if k % 2 == 0:
            away, peer = 1 - high_bit, high_peer
        else:
            away, peer = 1 - low_bit, low_peer
        return exchange(
            first_buf[group].at[:, away, :, columns],
            second_buf[group].at[:, :, columns],
            sem_two.at[0, k],
            sem_two.at[1, k],
            peer,
        )

    def seq_copy(k, step):
        group, start, size = chunks[k]
        columns = pl.ds(start, size)
        place = lax.rem(seq + step, seq_count)
        return exchange(
            second_buf[group].at[place, :, columns],
            third_buf[group].at[step - 1, :, columns],
            sem_seq.at[0, k, step - 1],
            sem_seq.at[1, k, step - 1],
            (place, head, batch),
        )

    def back_copy(k, turn):
        group, start, size = chunks[k]
        columns = pl.ds(start, size)
        out = outs[group]
        if (k + turn) % 2 == 0:
            peer = high_peer
        else:
            peer = low_peer
        if turn == 0:
            part = out.at[high_bit, low_bit, :, columns]
        elif k % 2 == 0:
            part = out.at[:, low_bit, :, columns]
        else:
            part = out.at[high_bit, :, :, columns]
        return exchange(part, part, sem_back.at[0, k, turn], sem_back.at[1, k, turn], peer)

    def each_seq(action):
        lax.fori_loop(1, seq_count, lambda step, carry: (action(step), carry)[1], 0)

    def add_first(k):
        group, start, size = chunks[k]
        columns = pl.ds(start, size)

        def one(place, carry):
            if k % 2 == 0:
                own = groups[group][place, :, low_bit, :, columns]
            else:
                own = groups[group][place, high_bit, :, :, columns]
            came = first_buf[group][place, :, :, columns]
            first_buf[group][place, :, :, columns] = (
                own.astype(jnp.float32) + came.astype(jnp.float32)
            ).astype(jnp.bfloat16)
            return carry

        lax.fori_loop(0, seq_count, one, 0)

    def add_second(k):
        group, start, size = chunks[k]
        columns = pl.ds(start, size)
        keep = high_bit if k % 2 == 0 else low_bit

        def one(place, carry):
            own = first_buf[group][place, keep, :, columns]
            came = second_buf[group][place, :, columns]
            second_buf[group][place, :, columns] = (
                own.astype(jnp.float32) + came.astype(jnp.float32)
            ).astype(jnp.bfloat16)
            return carry

        lax.fori_loop(0, seq_count, one, 0)

    def add_third(k):
        group, start, size = chunks[k]
        columns = pl.ds(start, size)

        def one(slot, total):
            return total + third_buf[group][slot, :, columns].astype(jnp.float32)

        total = second_buf[group][seq, :, columns].astype(jnp.float32)
        total = lax.fori_loop(0, seq_count - 1, one, total)
        outs[group][high_bit, low_bit, :, columns] = total.astype(jnp.bfloat16)

    total_chunks = len(chunks)
    ahead = 3
    for k in range(min(ahead, total_chunks)):
        first_copy(k).start()
    lax.fori_loop(1, world, lambda step, carry: (small_copy(step).start(), carry)[1], 0)
    for turn in range(total_chunks + 4):
        k = turn
        if k < total_chunks:
            first_copy(k).wait()
            if k + ahead < total_chunks:
                first_copy(k + ahead).start()
            add_first(k)
            second_copy(k).start()
        k = turn - 1
        if 0 <= k < total_chunks:
            second_copy(k).wait()
            add_second(k)
            each_seq(lambda step: seq_copy(k, step).start())
        k = turn - 2
        if 0 <= k < total_chunks:
            each_seq(lambda step: seq_copy(k, step).wait())
            add_third(k)
            back_copy(k, 0).start()
        k = turn - 3
        if 0 <= k < total_chunks:
            back_copy(k, 0).wait()
            back_copy(k, 1).start()
        k = turn - 4
        if 0 <= k < total_chunks:
            back_copy(k, 1).wait()
    lax.fori_loop(1, world, lambda step, carry: (small_copy(step).wait(), carry)[1], 0)
    small_buf[mine] = small_in[...]
    small_out[...] = lax.fori_loop(
        1, world, lambda place, total: total + small_buf[place], small_buf[0]
    )


def reduce_gradients(groups, small):
    seq_count, batch_count = lax.axis_size("seq"), lax.axis_size("batch")
    world = seq_count * batch_count
    rows = groups[0].shape[0] // world
    widths = [g.shape[1] for g in groups]
    chunks = column_chunks(widths, 512)
    blocks = [g.reshape(seq_count, 2, 2, rows, g.shape[1]) for g in groups]
    vmem = pl.BlockSpec(memory_space=pltpu.VMEM)
    count, parts = len(groups), len(chunks)
    result = pl.pallas_call(
        functools.partial(reduce_kernel, seq_count, batch_count, chunks),
        out_shape=[jax.ShapeDtypeStruct((2, 2, rows, w), jnp.bfloat16) for w in widths]
        + [jax.ShapeDtypeStruct(small.shape, jnp.float32)],
        in_specs=[vmem] * (count + 1),
        out_specs=[vmem] * (count + 1),
        scratch_shapes=[pltpu.VMEM((seq_count, 2, rows, w), jnp.bfloat16) for w in widths]
        + [pltpu.VMEM((seq_count, rows, w), jnp.bfloat16) for w in widths]
        + [pltpu.VMEM((seq_count - 1, rows, w), jnp.bfloat16) for w in widths]
        + [
            pltpu.VMEM((world,) + small.shape, jnp.float32),
            pltpu.SemaphoreType.DMA((2, parts)),
            pltpu.SemaphoreType.DMA((2, parts)),
            pltpu.SemaphoreType.DMA((2, parts, seq_count - 1)),
            pltpu.SemaphoreType.DMA((2, parts, 2)),
            pltpu.SemaphoreType.DMA((2, world)),
        ],
        compiler_params=pltpu.CompilerParams(
            collective_id=0, has_side_effects=True, vmem_limit_bytes=56 << 20
        ),
        name="reduce_gradients",
    )(*blocks, small)
    return [r.reshape(4 * rows, w) for r, w in zip(result[:-1], widths)], result[-1]


def shifted(value, axis, steps):
    count = lax.axis_size(axis)
    first, last = (max(0, -steps), min(count, count - steps))
    return lax.ppermute(value, axis, [(source, source + steps) for source in range(first, last)])


def entering(shard, axis, combine, identity):
    count, mine = (lax.axis_size(axis), lax.axis_index(axis))
    everything = jax.tree.map(
        lambda part, kind: lax.all_gather(part.astype(kind), axis),
        shard,
        (jnp.bfloat16, jnp.bfloat16),
    )
    start = jax.tree.map(
        lambda part, zero: jnp.broadcast_to(jnp.asarray(zero, part.dtype), part.shape),
        shard,
        identity,
    )

    def lap(k, before):
        reached = k < mine
        new = combine(
            before, jax.tree.map(lambda part, own: part[k].astype(own.dtype), everything, shard)
        )
        return jax.tree.map(lambda a, b: jnp.where(reached, a, b), new, before)

    return lax.fori_loop(0, count, lap, start)


def carried_in(shard, axis, join, neutral):
    count = lax.axis_size(axis)
    place = lax.axis_index(axis)
    ahead = count - 1 - place
    gathered = jax.tree.map(
        lambda a, kind: lax.all_gather(a.astype(kind), axis),
        shard,
        jax.tree.map(lambda a: jnp.bfloat16 if a.dtype == jnp.float32 else a.dtype, shard),
    )
    state = jax.tree.map(lambda a, e: jnp.zeros_like(a) + jnp.asarray(e, a.dtype), shard, neutral)

    def one(lap, state):
        source = count - 1 - lap
        return join(
            state,
            jax.tree.map(
                lambda a, own: lax.dynamic_index_in_dim(a, source, 0, False).astype(own.dtype),
                gathered,
                shard,
            ),
        )

    return lax.fori_loop(0, ahead, one, state)


def matmul(former, latter):
    return jnp.dot(former, latter, preferred_element_type=jnp.float32)


def matmul_last(former, latter):
    return lax.dot_general(
        former, latter, (((1,), (1,)), ((), ())), preferred_element_type=jnp.float32
    )


def matmul_first(former, latter):
    return lax.dot_general(
        former, latter, (((0,), (0,)), ((), ())), preferred_element_type=jnp.float32
    )


def rms_scale(hidden, gain):
    inverse = lax.rsqrt(jnp.mean(hidden * hidden, axis=-1, keepdims=True) + eps_norm)
    return hidden * inverse * gain


def rotate(values, position, factor):
    half_dim = values.shape[-1] // 2
    inverse_freq = rope_base ** (-jnp.arange(half_dim, dtype=jnp.float32) / half_dim)
    angles = position.astype(jnp.float32)[:, None] * inverse_freq[None, :]
    cosine = jnp.cos(angles)[:, None, :]
    sine_part = factor * jnp.sin(angles)[:, None, :]
    former = values[..., :half_dim]
    latter = values[..., half_dim:]
    return jnp.concatenate(
        [former * cosine - latter * sine_part, latter * cosine + former * sine_part], axis=-1
    )


def conv_mix(extended, kernel, window_seg):
    tap_count = kernel.shape[0]
    row_count = extended.shape[0] - tap_count + 1
    own_seg = window_seg[tap_count - 1 :]
    summed = jnp.zeros((row_count, extended.shape[1]), extended.dtype)
    for tap_index in range(tap_count):
        same_doc = (window_seg[tap_index : tap_index + row_count] == own_seg).astype(extended.dtype)
        summed = (
            summed
            + kernel[tap_index][None, :]
            * extended[tap_index : tap_index + row_count]
            * same_doc[:, None]
        )
    return jax.nn.silu(summed)


def state_part(scan_input, input_map, step_size, log_rate, local_seg, prev_seg):
    cumulative = jnp.cumsum(-jnp.exp(log_rate)[None, :] * step_size, axis=0)
    final_log = cumulative[-1]
    in_tail = local_seg == local_seg[-1]
    spread = jnp.where(in_tail[:, None], final_log[None, :] - cumulative, 0.0)
    weights = jnp.exp(spread) * in_tail[:, None].astype(step_size.dtype) * step_size
    local_state = jnp.einsum("sh,sn,shp->hnp", weights, input_map, scan_input, precision=highest)
    unbroken = (local_seg[-1] == prev_seg).astype(step_size.dtype)
    return (local_state, jnp.exp(final_log) * unbroken)


def output_part(
    scan_input, input_map, output_map, step_size, log_rate, skip_gain, state_in, local_seg, prev_seg
):
    cumulative = jnp.cumsum(-jnp.exp(log_rate)[None, :] * step_size, axis=0)
    row_index = jnp.arange(local_seg.shape[0])
    causal = (row_index[:, None] >= row_index[None, :]) & (local_seg[:, None] == local_seg[None, :])
    gaps = jnp.where(causal[:, :, None], cumulative[:, None, :] - cumulative[None, :, :], 0.0)
    decays = jnp.exp(gaps) * causal[:, :, None].astype(step_size.dtype)
    intersection = jnp.dot(output_map, input_map.T, precision=highest)
    mixing = intersection[:, :, None] * decays * step_size[None, :, :]
    inside = jnp.einsum("tsh,shp->thp", mixing, scan_input, precision=highest)
    carried = (local_seg == prev_seg).astype(step_size.dtype)[:, None] * jnp.exp(cumulative)
    across = (
        jnp.einsum("tn,hnp->thp", output_map, state_in, precision=highest) * carried[:, :, None]
    )
    return inside + across + skip_gain[None, :, None] * scan_input


def link_states(earlier, latter):
    return (earlier[0] * latter[0], latter[0][:, None, None] * earlier[1] + latter[1])


def head_total(partial_sum):
    return lax.psum(partial_sum.astype(jnp.bfloat16), "head").astype(jnp.float32)


def group_total(partial_sum):
    return lax.psum(partial_sum, "head")


def fold_rows(gradient, seq_count):
    return gradient.reshape((seq_count, gradient.shape[0] // seq_count) + gradient.shape[1:])


def score_block(queries, key_rows, key_start, position, local_seg, segments):
    span_rows = key_rows.shape[0]
    key_pos = key_start + jnp.arange(span_rows, dtype=jnp.int32)
    key_seg = lax.dynamic_slice_in_dim(segments, key_start, span_rows)
    allowed = (key_pos[None, :] <= position[:, None]) & (key_seg[None, :] == local_seg[:, None])
    scores = jnp.einsum(
        "kgrd,nkd->kgrn", queries, key_rows, preferred_element_type=jnp.float32
    ) * queries.shape[-1] ** (-0.5)
    return (jnp.where(allowed, scores, neg_large), allowed)


def body(
    tokens,
    seg_ids,
    mixer_gain,
    mamba_gate,
    mamba_input,
    mamba_maps,
    mamba_step,
    conv_inner,
    conv_maps,
    log_rate,
    step_bias,
    skip_gain,
    mamba_gain,
    mamba_output,
    query_weight,
    memory_weight,
    attention_out,
    feed_gain,
    gate_weight,
    lift_weight,
    down_weight,
    cotangent,
):
    row_count = tokens.shape[1]
    tap_count = conv_inner.shape[0]
    head_count = log_rate.shape[0]
    inner_width = conv_inner.shape[1]
    head_size = inner_width // head_count
    state_width = conv_maps.shape[1] // 2
    query_heads = query_weight.shape[1] // HD
    memory_heads = memory_weight.shape[1] // (2 * HD)
    group_size = query_heads // memory_heads
    all_width = inner_width * lax.axis_size("head")
    hidden = tokens[0].astype(jnp.float32)
    segments = seg_ids[0]
    offset = lax.axis_index("seq") * row_count
    last_row = offset + row_count - 1
    padded_seg = jnp.concatenate([jnp.full((tap_count - 1,), -1, jnp.int32), segments])
    window_seg = lax.dynamic_slice_in_dim(padded_seg, offset, row_count + tap_count - 1)
    local_seg = window_seg[tap_count - 1 :]
    prev_seg = window_seg[tap_count - 2]
    position = offset + jnp.arange(row_count, dtype=jnp.int32)
    normed, norm1_back = jax.vjp(rms_scale, hidden, mixer_gain)
    normed_low = normed.astype(jnp.bfloat16)
    gate_z = matmul(normed_low, mamba_gate)
    inner_x = matmul(normed_low, mamba_input)
    maps = matmul(normed_low, mamba_maps)
    raw_step = matmul(normed_low, mamba_step)
    query = matmul(normed_low, query_weight)
    memory = matmul(normed_low, memory_weight)
    before = jnp.concatenate([inner_x, maps], axis=1)
    edge_rows = shifted(before[row_count - tap_count + 1 :], "seq", 1)
    extended = jnp.concatenate([edge_rows, before], axis=0)
    kernel = jnp.concatenate([conv_inner, conv_maps], axis=1)

    def conv_apply(extended_rows, kernel_taps):
        return conv_mix(extended_rows, kernel_taps, window_seg)

    activated, conv_back = jax.vjp(conv_apply, extended, kernel)
    scan_input = activated[:, :inner_width].reshape(row_count, head_count, head_size)
    input_map = activated[:, inner_width : inner_width + state_width]
    output_map = activated[:, inner_width + state_width :]

    def step_apply(raw_rows, bias_now):
        return jax.nn.softplus(raw_rows + bias_now)

    step_size, step_back = jax.vjp(step_apply, raw_step, step_bias)

    def state_apply(input_now, in_map_now, step_now, rate_now):
        return state_part(input_now, in_map_now, step_now, rate_now, local_seg, prev_seg)

    (local_state, decays), state_back = jax.vjp(
        state_apply, scan_input, input_map, step_size, log_rate
    )
    identity = (jnp.ones_like(decays), jnp.zeros_like(local_state))
    prefix = entering((decays, local_state), "seq", link_states, identity)
    state_in = prefix[1]

    def output_apply(input_now, in_map_now, out_map_now, step_now, rate_now, skip_now, state_now):
        return output_part(
            input_now,
            in_map_now,
            out_map_now,
            step_now,
            rate_now,
            skip_now,
            state_now,
            local_seg,
            prev_seg,
        )

    mamba_y, output_back = jax.vjp(
        output_apply, scan_input, input_map, output_map, step_size, log_rate, skip_gain, state_in
    )
    gate_silu, silu_back = jax.vjp(jax.nn.silu, gate_z)
    flat_y = mamba_y.reshape(row_count, inner_width)
    g_six = flat_y * gate_silu
    square_total = group_total(jnp.sum(g_six * g_six, axis=1))
    inverse_six = lax.rsqrt(square_total / all_width + eps_norm)[:, None]
    gated = g_six * inverse_six * mamba_gain
    gated_low = gated.astype(jnp.bfloat16)
    mamba_out = matmul_last(gated_low, mamba_output)
    query_rot = rotate(query.reshape(row_count, query_heads, HD), position, 1.0)
    queries = (
        query_rot.astype(jnp.bfloat16)
        .reshape(row_count, memory_heads, group_size, HD)
        .transpose(1, 2, 0, 3)
    )
    memory_split = memory.reshape(row_count, memory_heads, 2, HD)
    key_low = rotate(memory_split[:, :, 0], position, 1.0).astype(jnp.bfloat16)
    value_low = memory_split[:, :, 1].astype(jnp.bfloat16)
    all_keys, all_values = (
        lax.all_gather(key_low, "seq", axis=0, tiled=True),
        lax.all_gather(value_low, "seq", axis=0, tiled=True),
    )
    total_rows = all_keys.shape[0]
    block_rows = min(512, total_rows)
    block_count = total_rows // block_rows
    key_blocks = all_keys.reshape((block_count, block_rows) + all_keys.shape[1:])
    value_blocks = all_values.reshape((block_count, block_rows) + all_values.shape[1:])
    block_starts = jnp.arange(block_count, dtype=jnp.int32) * block_rows

    def fold_step(running, pieces):
        key_rows, value_rows, key_start = pieces

        def live_fold(carried):
            running_max, running_sum, running_acc = carried
            scores, allowed = score_block(
                queries, key_rows, key_start, position, local_seg, segments
            )
            new_max = jnp.maximum(running_max, jnp.max(scores, axis=-1))
            weights = jnp.where(allowed, jnp.exp(scores - new_max[..., None]), 0.0)
            factor = jnp.exp(running_max - new_max)
            new_sum = running_sum * factor + jnp.sum(weights, axis=-1)
            new_acc = running_acc * factor[..., None] + jnp.einsum(
                "kgrn,nkd->kgrd",
                weights.astype(jnp.bfloat16),
                value_rows,
                preferred_element_type=jnp.float32,
            )
            return (new_max, new_sum, new_acc)

        def keep_fold(carried):
            return carried

        return (lax.cond(key_start <= last_row, live_fold, keep_fold, running), None)

    start_state = (
        jnp.full(queries.shape[:3], neg_large, jnp.float32),
        jnp.zeros(queries.shape[:3], jnp.float32),
        jnp.zeros(queries.shape, jnp.float32),
    )
    (final_max, final_sum, numer), _ = lax.scan(
        fold_step, start_state, (key_blocks, value_blocks, block_starts)
    )
    attention = numer / final_sum[..., None]
    attention_low = (
        attention.transpose(2, 0, 1, 3).reshape(row_count, query_heads * HD).astype(jnp.bfloat16)
    )
    attention_part = matmul_last(attention_low, attention_out)
    second = hidden + head_total(mamba_out + attention_part)
    normed2, norm2_back = jax.vjp(rms_scale, second, feed_gain)
    normed2_low = normed2.astype(jnp.bfloat16)
    gate_value = matmul(normed2_low, gate_weight)
    lift_value = matmul(normed2_low, lift_weight)

    def active_apply(gate_now, lift_now):
        return jax.nn.silu(gate_now) * lift_now

    active, active_back = jax.vjp(active_apply, gate_value, lift_value)
    active_low = active.astype(jnp.bfloat16)
    layer_out = (second + head_total(matmul_last(active_low, down_weight))).astype(jnp.bfloat16)
    grad_out = cotangent[0]
    d_active = matmul(grad_out, down_weight)
    g_down = matmul_first(grad_out, active_low)
    d_gate_f, d_lift_f = active_back(d_active)
    d_gate_low = d_gate_f.astype(jnp.bfloat16)
    d_lift_low = d_lift_f.astype(jnp.bfloat16)
    g_gate = matmul_first(normed2_low, d_gate_low)
    g_lift = matmul_first(normed2_low, d_lift_low)
    d_normed2 = head_total(
        matmul_last(d_gate_low, gate_weight) + matmul_last(d_lift_low, lift_weight)
    )
    d_second_norm, g_feed_gain = norm2_back(d_normed2)
    d_second = grad_out.astype(jnp.float32) + d_second_norm
    d_mix = d_second.astype(jnp.bfloat16)
    g_attn_out = matmul_first(d_mix, attention_low)
    g_mamba_out = matmul_first(d_mix, gated_low)
    d_attention = (
        matmul(d_mix, attention_out)
        .reshape(row_count, memory_heads, group_size, HD)
        .transpose(1, 2, 0, 3)
    )
    d_gated = matmul(d_mix, mamba_output)
    delta = jnp.sum(d_attention * attention, axis=-1)
    num_grad = (d_attention / final_sum[..., None]).astype(jnp.bfloat16)
    scale_now = HD ** (-0.5)

    def back_step(query_grad, pieces):
        key_rows, value_rows, key_start = pieces

        def live_back(grad_now):
            scores, allowed = score_block(
                queries, key_rows, key_start, position, local_seg, segments
            )
            weights = jnp.where(allowed, jnp.exp(scores - final_max[..., None]), 0.0)
            value_inner = jnp.einsum(
                "kgrd,nkd->kgrn", num_grad, value_rows, preferred_element_type=jnp.float32
            )
            score_grad = (weights * (value_inner - (delta / final_sum)[..., None])).astype(
                jnp.bfloat16
            )
            grad_next = (
                grad_now
                + jnp.einsum(
                    "kgrn,nkd->kgrd", score_grad, key_rows, preferred_element_type=jnp.float32
                )
                * scale_now
            )
            key_grad = (
                jnp.einsum(
                    "kgrn,kgrd->nkd", score_grad, queries, preferred_element_type=jnp.float32
                )
                * scale_now
            )
            value_grad = jnp.einsum(
                "kgrn,kgrd->nkd",
                weights.astype(jnp.bfloat16),
                num_grad,
                preferred_element_type=jnp.float32,
            )
            return (grad_next, jnp.stack([key_grad, value_grad], axis=2))

        def skip_back(grad_now):
            return (grad_now, jnp.zeros((key_rows.shape[0], memory_heads, 2, HD), jnp.float32))

        return lax.cond(key_start <= last_row, live_back, skip_back, query_grad)

    query_grad, pair_blocks = lax.scan(
        back_step, jnp.zeros(queries.shape, jnp.float32), (key_blocks, value_blocks, block_starts)
    )
    pair_grads = lax.psum_scatter(
        pair_blocks.reshape(total_rows, memory_heads * 2 * HD).astype(jnp.bfloat16),
        "seq",
        scatter_dimension=0,
        tiled=True,
    ).astype(jnp.float32)
    pair_local = pair_grads.reshape(row_count, memory_heads, 2, HD)
    key_back = rotate(pair_local[:, :, 0], position, -1.0)
    d_memory_low = (
        jnp.stack([key_back, pair_local[:, :, 1]], axis=2)
        .reshape(row_count, memory_heads * 2 * HD)
        .astype(jnp.bfloat16)
    )
    query_back = rotate(
        query_grad.transpose(2, 0, 1, 3).reshape(row_count, query_heads, HD), position, -1.0
    )
    d_query_low = query_back.reshape(row_count, query_heads * HD).astype(jnp.bfloat16)
    e_six = d_gated * mamba_gain
    cross_mean = group_total(jnp.sum(e_six * g_six, axis=1))[:, None] / all_width
    d_g_six = inverse_six * e_six - g_six * inverse_six * inverse_six * inverse_six * cross_mean
    d_mamba_y = (d_g_six * gate_silu).reshape(row_count, head_count, head_size)
    d_gate_z = silu_back(d_g_six * flat_y)[0]
    g_mamba_gain = jnp.sum(d_gated * g_six * inverse_six, axis=0)
    d_gate_z_low = d_gate_z.astype(jnp.bfloat16)
    d_input1, d_in_map1, d_out_map, d_step1, d_rate1, g_skip, d_state_in = output_back(d_mamba_y)
    later_grad = carried_in((decays, d_state_in), "seq", link_states, identity)[1]
    d_decays = jnp.sum(state_in * later_grad, axis=(1, 2))
    d_input2, d_in_map2, d_step2, d_rate2 = state_back((later_grad, d_decays))
    map_grads = lax.psum(
        jnp.concatenate([d_in_map1 + d_in_map2, d_out_map], axis=1).astype(jnp.bfloat16), "head"
    ).astype(jnp.float32)
    d_activated = jnp.concatenate(
        [(d_input1 + d_input2).reshape(row_count, inner_width), map_grads], axis=1
    )
    d_extended, g_kernel = conv_back(d_activated)
    back_edge = shifted(d_extended[: tap_count - 1], "seq", -1)
    d_before = d_extended[tap_count - 1 :] + jnp.concatenate(
        [jnp.zeros((row_count - tap_count + 1, d_extended.shape[1]), jnp.float32), back_edge],
        axis=0,
    )
    d_inner_low = d_before[:, :inner_width].astype(jnp.bfloat16)
    d_maps_low = d_before[:, inner_width:].astype(jnp.bfloat16)
    d_raw, g_step_bias = step_back(d_step1 + d_step2)
    d_raw_low = d_raw.astype(jnp.bfloat16)
    g_log_rate = d_rate1 + d_rate2
    d_normed = (
        matmul_last(d_gate_z_low, mamba_gate)
        + matmul_last(d_inner_low, mamba_input)
        + matmul_last(d_maps_low, mamba_maps) / lax.axis_size("head")
        + matmul_last(d_raw_low, mamba_step)
        + matmul_last(d_query_low, query_weight)
        + matmul_last(d_memory_low, memory_weight)
    )
    d_normed = head_total(d_normed)
    d_hidden_norm, g_mixer_gain = norm1_back(d_normed)
    grad_tokens = d_second + d_hidden_norm
    d_raw_wide = jnp.pad(d_raw_low, ((0, 0), (0, LANES - head_count)))
    mixer_side = jnp.concatenate(
        [d_gate_z_low, d_inner_low, d_maps_low, d_raw_wide, d_query_low, d_memory_low], axis=1
    )
    feed_side = jnp.concatenate([d_gate_low, d_lift_low], axis=1)
    mixed_side = jnp.concatenate([gated_low, attention_low], axis=1)
    groups = [
        matmul_first(normed_low, mixer_side).astype(jnp.bfloat16),
        matmul_first(normed2_low, feed_side).astype(jnp.bfloat16),
        matmul_first(d_mix, mixed_side).astype(jnp.bfloat16),
        matmul_first(grad_out, active_low).astype(jnp.bfloat16),
    ]
    wide = hidden.shape[1]
    scalars = jnp.concatenate([g_log_rate, g_step_bias, g_skip])
    small = jnp.concatenate(
        [
            g_kernel,
            jnp.stack(
                [
                    jnp.pad(g_mamba_gain, (0, wide - inner_width)),
                    g_mixer_gain,
                    g_feed_gain,
                    jnp.pad(scalars, (0, wide - scalars.shape[0])),
                ]
            ),
        ],
        axis=0,
    )
    (mixer_sum, feed_sum, mixed_sum, down_sum), small = reduce_gradients(groups, small)
    maps_width = conv_maps.shape[1]
    query_width = query_weight.shape[1]
    memory_width = memory_weight.shape[1]
    edges = [0]
    for width in (inner_width, inner_width, maps_width, LANES, query_width, memory_width):
        edges.append(edges[-1] + width)
    pieces = [mixer_sum[:, a:b].astype(jnp.float32) for a, b in zip(edges[:-1], edges[1:])]
    own_rows = wide // lax.axis_size("seq")
    own_at = lax.axis_index("seq") * own_rows
    ff_width = gate_weight.shape[1]
    return (
        layer_out[None],
        grad_tokens[None],
        lax.dynamic_slice_in_dim(small[5], own_at, own_rows),
        pieces[0],
        pieces[1],
        pieces[2],
        pieces[3][:, :head_count],
        small[:4, :inner_width],
        small[:4, inner_width:],
        small[7, :head_count],
        small[7, head_count : 2 * head_count],
        small[7, 2 * head_count : 3 * head_count],
        small[4, :inner_width],
        mixed_sum[:, :inner_width].astype(jnp.float32),
        pieces[4],
        pieces[5],
        mixed_sum[:, inner_width:].astype(jnp.float32),
        lax.dynamic_slice_in_dim(small[6], own_at, own_rows),
        feed_sum[:, :ff_width].astype(jnp.float32),
        feed_sum[:, ff_width:].astype(jnp.float32),
        down_sum.astype(jnp.float32),
    )


def solution(mesh):
    return jax.shard_map(
        body,
        mesh=mesh,
        in_specs=(
            P("batch", "seq", None),
            P("batch", None),
            P(),
            P(None, "head"),
            P(None, "head"),
            P(),
            P(None, "head"),
            P(None, "head"),
            P(),
            P("head"),
            P("head"),
            P("head"),
            P("head"),
            P(None, "head"),
            P(None, "head"),
            P(None, "head"),
            P(None, "head"),
            P(),
            P(None, "head"),
            P(None, "head"),
            P(None, "head"),
            P("batch", "seq", None),
        ),
        out_specs=(
            P("batch", "seq", None),
            P("batch", "seq", None),
            P("seq"),
            P("seq", "head"),
            P("seq", "head"),
            P("seq", None),
            P("seq", "head"),
            P(None, "head"),
            P(),
            P("head"),
            P("head"),
            P("head"),
            P("head"),
            P("seq", "head"),
            P("seq", "head"),
            P("seq", "head"),
            P("seq", "head"),
            P("seq"),
            P("seq", "head"),
            P("seq", "head"),
            P("seq", "head"),
        ),
        check_vma=False,
    )
```

```python
import functools

import jax
import jax.numpy as jnp
from jax import lax
from jax.experimental import pallas as pl
from jax.experimental.pallas import tpu as pltpu
from jax.sharding import PartitionSpec as P

HD = 64
eps_norm = 1e-05
rope_base = 10000.0
neg_large = -1e30
highest = lax.Precision.HIGHEST


LANES = 128
MESH = pl.DeviceIdType.MESH


def exchange(source, target, send_sem, recv_sem, device):
    return pltpu.make_async_remote_copy(
        src_ref=source,
        dst_ref=target,
        send_sem=send_sem,
        recv_sem=recv_sem,
        device_id=device,
        device_id_type=MESH,
    )


def column_chunks(widths, most):
    chunks = []
    for group, width in enumerate(widths):
        count = -(-width // most)
        tiles = width // LANES
        start = 0
        for k in range(count):
            size = (tiles // count + (1 if k < tiles % count else 0)) * LANES
            chunks.append((group, start, size))
            start += size
    return chunks


def reduce_kernel(seq_count, batch_count, chunks, *refs):
    count = 1 + max(c[0] for c in chunks)
    groups, refs = refs[:count], refs[count:]
    small_in, refs = refs[0], refs[1:]
    outs, refs = refs[:count], refs[count:]
    small_out, refs = refs[0], refs[1:]
    first_buf, refs = refs[:count], refs[count:]
    second_buf, refs = refs[:count], refs[count:]
    third_buf, refs = refs[:count], refs[count:]
    small_buf, sem_one, sem_two, sem_seq, sem_back, sem_small = refs
    seq, head, batch = lax.axis_index("seq"), lax.axis_index("head"), lax.axis_index("batch")
    low_bit = lax.rem(batch, 2)
    high_bit = batch // 2
    low_peer = (seq, head, batch + 1 - 2 * low_bit)
    high_peer = (seq, head, batch + 2 - 4 * high_bit)
    world = seq_count * batch_count
    mine = seq * batch_count + batch

    def other(step):
        place = lax.rem(mine + step, world)
        return (place // batch_count, head, lax.rem(place, batch_count))

    barrier = pltpu.get_barrier_semaphore()

    def greet(step, carry):
        pl.semaphore_signal(barrier, inc=1, device_id=other(step), device_id_type=MESH)
        return carry

    lax.fori_loop(1, world, greet, 0)
    pl.semaphore_wait(barrier, world - 1)

    def small_copy(step):
        return exchange(
            small_in,
            small_buf.at[mine],
            sem_small.at[0, step],
            sem_small.at[1, step],
            other(step),
        )

    def first_copy(k):
        group, start, size = chunks[k]
        columns = pl.ds(start, size)
        source, target = groups[group], first_buf[group]
        if k % 2 == 0:
            part = source.at[:, :, 1 - low_bit, :, columns]
            peer = low_peer
        else:
            part = source.at[:, 1 - high_bit, :, :, columns]
            peer = high_peer
        return exchange(part, target.at[:, :, :, columns], sem_one.at[0, k], sem_one.at[1, k], peer)

    def second_copy(k):
        group, start, size = chunks[k]
        columns = pl.ds(start, size)
        if k % 2 == 0:
            away, peer = 1 - high_bit, high_peer
        else:
            away, peer = 1 - low_bit, low_peer
        return exchange(
            first_buf[group].at[:, away, :, columns],
            second_buf[group].at[:, :, columns],
            sem_two.at[0, k],
            sem_two.at[1, k],
            peer,
        )

    def seq_copy(k, step):
        group, start, size = chunks[k]
        columns = pl.ds(start, size)
        place = lax.rem(seq + step, seq_count)
        return exchange(
            second_buf[group].at[place, :, columns],
            third_buf[group].at[step - 1, :, columns],
            sem_seq.at[0, k, step - 1],
            sem_seq.at[1, k, step - 1],
            (place, head, batch),
        )

    def back_copy(k, turn):
        group, start, size = chunks[k]
        columns = pl.ds(start, size)
        out = outs[group]
        if (k + turn) % 2 == 0:
            peer = high_peer
        else:
            peer = low_peer
        if turn == 0:
            part = out.at[high_bit, low_bit, :, columns]
        elif k % 2 == 0:
            part = out.at[:, low_bit, :, columns]
        else:
            part = out.at[high_bit, :, :, columns]
        return exchange(part, part, sem_back.at[0, k, turn], sem_back.at[1, k, turn], peer)

    def each_seq(action):
        lax.fori_loop(1, seq_count, lambda step, carry: (action(step), carry)[1], 0)

    def add_first(k):
        group, start, size = chunks[k]
        columns = pl.ds(start, size)

        def one(place, carry):
            if k % 2 == 0:
                own = groups[group][place, :, low_bit, :, columns]
            else:
                own = groups[group][place, high_bit, :, :, columns]
            came = first_buf[group][place, :, :, columns]
            first_buf[group][place, :, :, columns] = (
                own.astype(jnp.float32) + came.astype(jnp.float32)
            ).astype(jnp.bfloat16)
            return carry

        lax.fori_loop(0, seq_count, one, 0)

    def add_second(k):
        group, start, size = chunks[k]
        columns = pl.ds(start, size)
        keep = high_bit if k % 2 == 0 else low_bit

        def one(place, carry):
            own = first_buf[group][place, keep, :, columns]
            came = second_buf[group][place, :, columns]
            second_buf[group][place, :, columns] = (
                own.astype(jnp.float32) + came.astype(jnp.float32)
            ).astype(jnp.bfloat16)
            return carry

        lax.fori_loop(0, seq_count, one, 0)

    def add_third(k):
        group, start, size = chunks[k]
        columns = pl.ds(start, size)

        def one(slot, total):
            return total + third_buf[group][slot, :, columns].astype(jnp.float32)

        total = second_buf[group][seq, :, columns].astype(jnp.float32)
        total = lax.fori_loop(0, seq_count - 1, one, total)
        outs[group][high_bit, low_bit, :, columns] = total.astype(jnp.bfloat16)

    total_chunks = len(chunks)
    ahead = 3
    for k in range(min(ahead, total_chunks)):
        first_copy(k).start()
    lax.fori_loop(1, world, lambda step, carry: (small_copy(step).start(), carry)[1], 0)
    for turn in range(total_chunks + 4):
        k = turn
        if k < total_chunks:
            first_copy(k).wait()
            if k + ahead < total_chunks:
                first_copy(k + ahead).start()
            add_first(k)
            second_copy(k).start()
        k = turn - 1
        if 0 <= k < total_chunks:
            second_copy(k).wait()
            add_second(k)
            each_seq(lambda step: seq_copy(k, step).start())
        k = turn - 2
        if 0 <= k < total_chunks:
            each_seq(lambda step: seq_copy(k, step).wait())
            add_third(k)
            back_copy(k, 0).start()
        k = turn - 3
        if 0 <= k < total_chunks:
            back_copy(k, 0).wait()
            back_copy(k, 1).start()
        k = turn - 4
        if 0 <= k < total_chunks:
            back_copy(k, 1).wait()
    lax.fori_loop(1, world, lambda step, carry: (small_copy(step).wait(), carry)[1], 0)
    small_buf[mine] = small_in[...]
    small_out[...] = lax.fori_loop(
        1, world, lambda place, total: total + small_buf[place], small_buf[0]
    )


def reduce_gradients(groups, small):
    seq_count, batch_count = lax.axis_size("seq"), lax.axis_size("batch")
    world = seq_count * batch_count
    rows = groups[0].shape[0] // world
    widths = [g.shape[1] for g in groups]
    chunks = column_chunks(widths, 512)
    blocks = [g.reshape(seq_count, 2, 2, rows, g.shape[1]) for g in groups]
    vmem = pl.BlockSpec(memory_space=pltpu.VMEM)
    count, parts = len(groups), len(chunks)
    result = pl.pallas_call(
        functools.partial(reduce_kernel, seq_count, batch_count, chunks),
        out_shape=[jax.ShapeDtypeStruct((2, 2, rows, w), jnp.bfloat16) for w in widths]
        + [jax.ShapeDtypeStruct(small.shape, jnp.float32)],
        in_specs=[vmem] * (count + 1),
        out_specs=[vmem] * (count + 1),
        scratch_shapes=[pltpu.VMEM((seq_count, 2, rows, w), jnp.bfloat16) for w in widths]
        + [pltpu.VMEM((seq_count, rows, w), jnp.bfloat16) for w in widths]
        + [pltpu.VMEM((seq_count - 1, rows, w), jnp.bfloat16) for w in widths]
        + [
            pltpu.VMEM((world,) + small.shape, jnp.float32),
            pltpu.SemaphoreType.DMA((2, parts)),
            pltpu.SemaphoreType.DMA((2, parts)),
            pltpu.SemaphoreType.DMA((2, parts, seq_count - 1)),
            pltpu.SemaphoreType.DMA((2, parts, 2)),
            pltpu.SemaphoreType.DMA((2, world)),
        ],
        compiler_params=pltpu.CompilerParams(
            collective_id=0, has_side_effects=True, vmem_limit_bytes=56 << 20
        ),
        name="reduce_gradients",
    )(*blocks, small)
    return [r.reshape(4 * rows, w) for r, w in zip(result[:-1], widths)], result[-1]


def matmul(former, latter):
    return jnp.dot(former, latter, preferred_element_type=jnp.float32)


def matmul_last(former, latter):
    return lax.dot_general(
        former, latter, (((1,), (1,)), ((), ())), preferred_element_type=jnp.float32
    )


def matmul_first(former, latter):
    return lax.dot_general(
        former, latter, (((0,), (0,)), ((), ())), preferred_element_type=jnp.float32
    )


TILE = 128


def sigmoid(v):
    return 1.0 / (1.0 + jnp.exp(-v))


def peer_device():
    return (lax.axis_index("seq"), 1 - lax.axis_index("head"), lax.axis_index("batch"))


def greet_peer(barrier, peer):
    pl.semaphore_signal(barrier, inc=1, device_id=peer, device_id_type=MESH)
    pl.semaphore_wait(barrier, 1)


def tile_rows(i):
    return pl.ds(pl.multiple_of(i * TILE, TILE), TILE)


def each(count, action):
    lax.fori_loop(0, count, lambda i, carry: (action(i), carry)[1], 0)


def feed_kernel(
    y_ref,
    gate_z_ref,
    attention_ref,
    tokens_ref,
    cotangent_ref,
    mamba_gain_ref,
    feed_gain_ref,
    mamba_output_ref,
    attention_out_ref,
    gate_weight_hbm,
    lift_weight_hbm,
    down_weight_hbm,
    out_ref,
    d_second_ref,
    d_y_ref,
    d_gate_z_ref,
    d_attention_ref,
    g_feed_ref,
    g_mixed_ref,
    g_down_ref,
    g_feed_gain_ref,
    g_mamba_gain_ref,
    gate_weight,
    lift_weight,
    down_weight,
    gated,
    g_six,
    inverse_six,
    second,
    inverse_two,
    normed2,
    active,
    d_feed,
    d_mix,
    d_gated,
    square_send,
    square_recv,
    cross_send,
    cross_recv,
    mixed_send,
    mixed_recv,
    lift_send,
    lift_recv,
    norm_send,
    norm_recv,
    weight_sem,
    sem_square,
    sem_cross,
    sem_mixed,
    sem_lift,
    sem_norm,
):
    rows = y_ref.shape[0]
    tiles = rows // TILE
    inner = y_ref.shape[1]
    width = feed_gain_ref.shape[1]
    feed = down_weight.shape[1]
    all_inner = inner * lax.axis_size("head")
    peer = peer_device()
    loads = [
        pltpu.make_async_copy(source, target, weight_sem.at[k])
        for k, (source, target) in enumerate(
            (
                (gate_weight_hbm, gate_weight),
                (lift_weight_hbm, lift_weight),
                (down_weight_hbm, down_weight),
            )
        )
    ]
    for load in loads:
        load.start()
    greet_peer(pltpu.get_barrier_semaphore(), peer)

    def swap(send, recv, sems, i):
        rows_now = tile_rows(i)
        return exchange(send.at[rows_now], recv.at[rows_now], sems.at[0, i], sems.at[1, i], peer)

    def gate_tile(i):
        at = tile_rows(i)
        gate_now = gate_z_ref[at, :]
        value = y_ref[at, :] * gate_now * sigmoid(gate_now)
        g_six[at, :] = value
        square_send[at, :] = jnp.broadcast_to(
            jnp.sum(value * value, axis=1, keepdims=True), (TILE, LANES)
        )
        swap(square_send, square_recv, sem_square, i).start()

    each(tiles, gate_tile)

    def mixed_tile(i):
        at = tile_rows(i)
        swap(square_send, square_recv, sem_square, i).wait()
        total = square_send[at, :] + square_recv[at, :]
        inverse = lax.rsqrt(total[:, :1] / all_inner + eps_norm)
        inverse_six[at, :] = jnp.broadcast_to(inverse, (TILE, LANES))
        low = (g_six[at, :] * inverse * mamba_gain_ref[...]).astype(jnp.bfloat16)
        gated[at, :] = low
        part = matmul_last(low, mamba_output_ref[...]) + matmul_last(
            attention_ref[at, :], attention_out_ref[...]
        )
        mixed_send[at, :] = part.astype(jnp.bfloat16)
        swap(mixed_send, mixed_recv, sem_mixed, i).start()

    each(tiles, mixed_tile)
    for load in loads:
        load.wait()

    def feed_tile(i):
        at = tile_rows(i)
        swap(mixed_send, mixed_recv, sem_mixed, i).wait()
        total = mixed_send[at, :].astype(jnp.float32) + mixed_recv[at, :].astype(jnp.float32)
        hidden = tokens_ref[at, :].astype(jnp.float32) + total
        second[at, :] = hidden
        inverse = lax.rsqrt(jnp.mean(hidden * hidden, axis=1, keepdims=True) + eps_norm)
        inverse_two[at, :] = jnp.broadcast_to(inverse, (TILE, LANES))
        low = (hidden * inverse * feed_gain_ref[...]).astype(jnp.bfloat16)
        normed2[at, :] = low
        gate_now = matmul(low, gate_weight[...])
        lift_now = matmul(low, lift_weight[...])
        sig = sigmoid(gate_now)
        silu = gate_now * sig
        act = (silu * lift_now).astype(jnp.bfloat16)
        active[at, :] = act
        lift_send[at, :] = matmul_last(act, down_weight[...]).astype(jnp.bfloat16)
        swap(lift_send, lift_recv, sem_lift, i).start()
        d_act = matmul(cotangent_ref[at, :], down_weight[...])
        d_gate = (d_act * lift_now * (sig * (1.0 + gate_now * (1.0 - sig)))).astype(jnp.bfloat16)
        d_lift = (d_act * silu).astype(jnp.bfloat16)
        d_feed[at, :feed] = d_gate
        d_feed[at, feed:] = d_lift
        part = matmul_last(d_gate, gate_weight[...]) + matmul_last(d_lift, lift_weight[...])
        norm_send[at, :] = part.astype(jnp.bfloat16)
        swap(norm_send, norm_recv, sem_norm, i).start()

    each(tiles, feed_tile)
    g_feed_gain_ref[...] = jnp.zeros_like(g_feed_gain_ref)
    g_mamba_gain_ref[...] = jnp.zeros_like(g_mamba_gain_ref)

    def norm_tile(i):
        at = tile_rows(i)
        swap(norm_send, norm_recv, sem_norm, i).wait()
        d_norm = norm_send[at, :].astype(jnp.float32) + norm_recv[at, :].astype(jnp.float32)
        hidden = second[at, :]
        inverse = inverse_two[at, :][:, :1]
        e_two = d_norm * feed_gain_ref[...]
        g_feed_gain_ref[...] += jnp.sum(d_norm * hidden * inverse, axis=0, keepdims=True)
        cross = jnp.sum(e_two * hidden, axis=1, keepdims=True) / width
        d_hidden = (
            cotangent_ref[at, :].astype(jnp.float32)
            + inverse * e_two
            - hidden * (inverse * inverse * inverse * cross)
        )
        d_second_ref[at, :] = d_hidden
        low = d_hidden.astype(jnp.bfloat16)
        d_mix[at, :] = low
        d_attention_ref[at, :] = matmul(low, attention_out_ref[...])
        d_gated_now = matmul(low, mamba_output_ref[...])
        d_gated[at, :] = d_gated_now
        six = g_six[at, :]
        g_mamba_gain_ref[...] += jnp.sum(
            d_gated_now * six * inverse_six[at, :][:, :1], axis=0, keepdims=True
        )
        cross_send[at, :] = jnp.broadcast_to(
            jnp.sum(d_gated_now * mamba_gain_ref[...] * six, axis=1, keepdims=True), (TILE, LANES)
        )
        swap(cross_send, cross_recv, sem_cross, i).start()

    each(tiles, norm_tile)

    def gate_back(i):
        at = tile_rows(i)
        swap(cross_send, cross_recv, sem_cross, i).wait()
        cross = (cross_send[at, :] + cross_recv[at, :])[:, :1] / all_inner
        inverse = inverse_six[at, :][:, :1]
        d_six = inverse * (d_gated[at, :] * mamba_gain_ref[...]) - g_six[at, :] * (
            inverse * inverse * inverse * cross
        )
        gate_now = gate_z_ref[at, :]
        sig = sigmoid(gate_now)
        d_y_ref[at, :] = d_six * gate_now * sig
        d_gate_z_ref[at, :] = (
            d_six * y_ref[at, :] * (sig * (1.0 + gate_now * (1.0 - sig)))
        ).astype(jnp.bfloat16)

    each(tiles, gate_back)

    def out_tile(i):
        at = tile_rows(i)
        swap(lift_send, lift_recv, sem_lift, i).wait()
        total = lift_send[at, :].astype(jnp.float32) + lift_recv[at, :].astype(jnp.float32)
        out_ref[at, :] = (second[at, :] + total).astype(jnp.bfloat16)

    each(tiles, out_tile)

    def weight_block(k):
        block = pl.ds(pl.multiple_of(k * 256, 256), 256)
        g_down_ref[block, :] = matmul_first(cotangent_ref[:, block], active[...]).astype(
            jnp.bfloat16
        )
        g_feed_ref[block, :] = matmul_first(normed2[:, block], d_feed[...]).astype(jnp.bfloat16)
        d_mix_now = d_mix[:, block]
        g_mixed_ref[block, :inner] = matmul_first(d_mix_now, gated[...]).astype(jnp.bfloat16)
        g_mixed_ref[block, inner:] = matmul_first(d_mix_now, attention_ref[...]).astype(
            jnp.bfloat16
        )

    each(width // 256, weight_block)


def feed_layer(
    y,
    gate_z,
    attention_low,
    tokens,
    cotangent,
    mamba_gain,
    feed_gain,
    mamba_output,
    attention_out,
    gate_weight,
    lift_weight,
    down_weight,
):
    rows, inner = y.shape
    width = tokens.shape[1]
    feed = gate_weight.shape[1]
    att = attention_low.shape[1]
    tiles = rows // TILE
    vmem = pl.BlockSpec(memory_space=pltpu.VMEM)
    hbm = pl.BlockSpec(memory_space=pl.ANY)
    low, full = jnp.bfloat16, jnp.float32
    shape = jax.ShapeDtypeStruct
    return pl.pallas_call(
        feed_kernel,
        out_shape=[
            shape((rows, width), low),
            shape((rows, width), full),
            shape((rows, inner), full),
            shape((rows, inner), low),
            shape((rows, att), full),
            shape((width, 2 * feed), low),
            shape((width, inner + att), low),
            shape((width, feed), low),
            shape((1, width), full),
            shape((1, inner), full),
        ],
        in_specs=[vmem] * 9 + [hbm] * 3,
        out_specs=[vmem] * 10,
        scratch_shapes=[
            pltpu.VMEM((width, feed), low),
            pltpu.VMEM((width, feed), low),
            pltpu.VMEM((width, feed), low),
            pltpu.VMEM((rows, inner), low),
            pltpu.VMEM((rows, inner), full),
            pltpu.VMEM((rows, LANES), full),
            pltpu.VMEM((rows, width), full),
            pltpu.VMEM((rows, LANES), full),
            pltpu.VMEM((rows, width), low),
            pltpu.VMEM((rows, feed), low),
            pltpu.VMEM((rows, 2 * feed), low),
            pltpu.VMEM((rows, width), low),
            pltpu.VMEM((rows, inner), full),
            pltpu.VMEM((rows, LANES), full),
            pltpu.VMEM((rows, LANES), full),
            pltpu.VMEM((rows, LANES), full),
            pltpu.VMEM((rows, LANES), full),
        ]
        + [pltpu.VMEM((rows, width), low)] * 6
        + [pltpu.SemaphoreType.DMA((3,))]
        + [pltpu.SemaphoreType.DMA((2, tiles))] * 5,
        compiler_params=pltpu.CompilerParams(
            collective_id=1, has_side_effects=True, vmem_limit_bytes=60 << 20
        ),
        name="feed_layer",
    )(
        y,
        gate_z,
        attention_low,
        tokens,
        cotangent,
        mamba_gain[None],
        feed_gain[None],
        mamba_output,
        attention_out,
        gate_weight,
        lift_weight,
        down_weight,
    )


CHUNK = 128
HALO = 8
PIECE = 256


def turn_half(values):
    lane = lax.broadcasted_iota(jnp.int32, values.shape, 1)
    return jnp.where(
        lax.rem(lane, HD) < HD // 2,
        pltpu.roll(values, LANES - HD // 2, 1),
        pltpu.roll(values, HD // 2, 1),
    )


def two_parts(values):
    high = values.astype(jnp.bfloat16)
    return high, (values - high.astype(jnp.float32)).astype(jnp.bfloat16)


def spread_heads(values, spread):
    high, rest = two_parts(values)
    return matmul(high, spread) + matmul(rest, spread)


def sum_heads(values, spread):
    high, rest = two_parts(values)
    return matmul_last(high, spread) + matmul_last(rest, spread)


def spread_matrix(inner, size):
    row = lax.broadcasted_iota(jnp.int32, (LANES, inner), 0)
    lane = lax.broadcasted_iota(jnp.int32, (LANES, inner), 1)
    return jnp.where(lane // size == row, 1.0, 0.0).astype(jnp.bfloat16)


def ordered(count):
    row = lax.broadcasted_iota(jnp.int32, (count, count), 0)
    lane = lax.broadcasted_iota(jnp.int32, (count, count), 1)
    return row >= lane


def halves(values, size):
    lane = lax.broadcasted_iota(jnp.int32, values.shape, 1)
    return jnp.concatenate(
        [jnp.where(lane < size, values, 0.0), jnp.where(lane < size, 0.0, values)], axis=0
    ).astype(jnp.bfloat16)


def soft_plus(v):
    return jnp.maximum(v, 0.0) + jnp.log1p(jnp.exp(-jnp.abs(v)))


def chunk_flags(seg_ref, c):
    window = seg_ref[pl.ds(pl.multiple_of(c * CHUNK, CHUNK), CHUNK + HALO), :]
    own = window[HALO:]
    start = jnp.where(own == window[HALO - 1 : HALO], 1.0, 0.0)
    end = jnp.where(own == own[CHUNK - 1 :], 1.0, 0.0)
    return own, start, end


def greet_seq(barrier, with_peer):
    seq, head, batch = lax.axis_index("seq"), lax.axis_index("head"), lax.axis_index("batch")
    count = lax.axis_size("seq")

    def one(step, carry):
        pl.semaphore_signal(
            barrier,
            inc=1,
            device_id=(lax.rem(seq + step, count), head, batch),
            device_id_type=MESH,
        )
        return carry

    lax.fori_loop(1, count, one, 0)
    if with_peer:
        pl.semaphore_signal(barrier, inc=1, device_id=peer_device(), device_id_type=MESH)
    pl.semaphore_wait(barrier, count - 1 + with_peer)


def mixer_kernel(
    size,
    tokens_ref,
    gain_ref,
    seg_ref,
    table_ref,
    gate_weight,
    input_weight,
    maps_weight,
    step_weight,
    query_weight,
    memory_weight,
    taps_ref,
    bias_ref,
    rate_ref,
    skip_ref,
    gate_z_ref,
    pre_ref,
    conv_ref,
    raw_ref,
    cum_ref,
    y_ref,
    states_ref,
    query_ref,
    memory_ref,
    normed,
    spread_ref,
    act,
    scaled,
    added,
    decay,
    total,
    local,
    state,
    chain_out,
    chain_in,
    sem_memory,
    sem_halo,
    sem_chain,
):
    seq, head, batch = lax.axis_index("seq"), lax.axis_index("head"), lax.axis_index("batch")
    count = lax.axis_size("seq")
    rows = tokens_ref.shape[0]
    tiles = rows // CHUNK
    inner = y_ref.shape[1]
    width = pre_ref.shape[1]
    state_width = (width - inner) // 2
    following = (lax.rem(seq + 1, count), head, batch)
    greet_seq(pltpu.get_barrier_semaphore(), 0)

    def memory_copy(step, place, owner):
        return exchange(
            memory_ref.at[owner],
            memory_ref.at[owner],
            sem_memory.at[0, step],
            sem_memory.at[1, step],
            (place, head, batch),
        )

    halo_copy = exchange(
        pre_ref.at[pl.ds(rows, HALO)],
        pre_ref.at[pl.ds(0, HALO)],
        sem_halo.at[0],
        sem_halo.at[1],
        following,
    )

    def memory_tile(i):
        at = tile_rows(i)
        hidden = tokens_ref[at, :].astype(jnp.float32)
        inverse = lax.rsqrt(jnp.mean(hidden * hidden, axis=1, keepdims=True) + eps_norm)
        low = (hidden * inverse * gain_ref[...]).astype(jnp.bfloat16)
        normed[at, :] = low
        value = matmul(low, memory_weight[...])
        lane = lax.broadcasted_iota(jnp.int32, value.shape, 1)
        turned = value * table_ref[at, :LANES] + turn_half(value) * table_ref[at, LANES:]
        memory_ref[seq, at, :] = jnp.where(lane < HD, turned, value).astype(jnp.bfloat16)

    each(tiles, memory_tile)

    def memory_start(step, carry):
        @pl.when(seq + step < count)
        def _():
            memory_copy(step, lax.rem(seq + step, count), seq).start()

        return carry

    lax.fori_loop(1, count, memory_start, 0)

    def pre_tile(i):
        at = tile_rows(i)
        to = pl.ds(pl.multiple_of(i * TILE + HALO, HALO), TILE)
        low = normed[at, :]
        pre_ref[to, :inner] = matmul(low, input_weight[...])
        pre_ref[to, inner:] = matmul(low, maps_weight[...])

    each(tiles, lambda i: pre_tile(tiles - 1 - i))

    @pl.when(seq < count - 1)
    def _():
        halo_copy.start()

    spread_ref[...] = spread_matrix(inner, size)
    lower = jnp.where(ordered(CHUNK), 1.0, 0.0)

    def project_tile(i):
        at = tile_rows(i)
        low = normed[at, :]
        gate_z_ref[at, :] = matmul(low, gate_weight[...])
        raw = matmul(low, step_weight[...]) + bias_ref[...]
        raw_ref[at, :] = raw
        cum_ref[at, :] = jnp.dot(
            lower, rate_ref[...] * soft_plus(raw), precision=highest
        )
        value = matmul(low, query_weight[...])
        for k in range(value.shape[1] // LANES):
            part = value[:, k * LANES : (k + 1) * LANES]
            turned = part * table_ref[at, :LANES] + turn_half(part) * table_ref[at, LANES:]
            query_ref[at, k * LANES : (k + 1) * LANES] = turned.astype(jnp.bfloat16)

    each(tiles, project_tile)

    @pl.when(seq == 0)
    def _():
        pre_ref[:HALO, :] = jnp.zeros((HALO, width), jnp.float32)

    @pl.when(seq > 0)
    def _():
        halo_copy.wait_recv()

    def conv_tile(i):
        at = tile_rows(i)
        window_at = pl.ds(pl.multiple_of(i * TILE, TILE), TILE + HALO)
        seg = seg_ref[window_at, :]
        own = seg[HALO:]
        masks = [
            jnp.where(seg[HALO - 3 + k : HALO - 3 + k + TILE] == own, 1.0, 0.0) for k in range(3)
        ]
        for j in range(width // LANES):
            columns = slice(j * LANES, (j + 1) * LANES)
            window = pre_ref[window_at, columns]
            summed = taps_ref[3:4, columns] * window[HALO:]
            for k in range(3):
                summed = summed + taps_ref[k : k + 1, columns] * (
                    window[HALO - 3 + k : HALO - 3 + k + TILE] * masks[k]
                )
            conv_ref[at, columns] = summed
            act[at, columns] = summed * sigmoid(summed)

    each(tiles, conv_tile)
    local[...] = jnp.zeros_like(local)
    total[...] = jnp.ones_like(total)

    def input_map(at):
        return act[at, inner : inner + state_width].astype(jnp.bfloat16)

    def output_map(at):
        return act[at, inner + state_width :].astype(jnp.bfloat16)

    def local_chunk(c):
        at = tile_rows(c)
        _, start, end = chunk_flags(seg_ref, c)
        cum = cum_ref[at, :]
        last = cum[CHUNK - 1 :]
        spread = spread_ref[...]
        value = act[at, :inner] * spread_heads(soft_plus(raw_ref[at, :]), spread)
        scaled[at, :] = value.astype(jnp.bfloat16)
        weight = spread_heads(jnp.exp(last - cum) * end, spread)
        fresh = matmul_first(input_map(at), (value * weight).astype(jnp.bfloat16))
        keep = jnp.broadcast_to(jnp.exp(last) * start[CHUNK - 1 :], (HALO, LANES))
        keep = spread_heads(keep, spread)
        added[c] = fresh
        decay[c] = keep
        local[...] = local[...] * keep[:1] + fresh
        total[...] = total[...] * keep

    each(tiles, local_chunk)
    pieces = inner // PIECE

    def chain_copy(p):
        columns = pl.ds(p * PIECE, PIECE)
        return exchange(
            chain_out.at[:, columns],
            chain_in.at[:, columns],
            sem_chain.at[0, p],
            sem_chain.at[1, p],
            following,
        )

    @pl.when(seq == 0)
    def _():
        state[...] = jnp.zeros_like(state)
        chain_out[...] = local[...].astype(jnp.bfloat16)
        if count > 1:
            for p in range(pieces):
                chain_copy(p).start()

    def inside_chunk(c):
        at = tile_rows(c)
        own, _, _ = chunk_flags(seg_ref, c)
        cum = cum_ref[at, :]
        turned = cum.T
        meet = matmul_last(output_map(at), input_map(at))
        meet = jnp.where(ordered(CHUNK) & (own == own.T), meet, 0.0)
        for i in range(inner // LANES):
            columns = slice(i * LANES, (i + 1) * LANES)
            mixing = []
            for h in (2 * i, 2 * i + 1):
                gap = cum[:, h : h + 1] - turned[h : h + 1, :]
                mixing.append(meet * jnp.exp(jnp.minimum(gap, 0.0)))
            y_ref[at, columns] = matmul(
                jnp.concatenate(mixing, axis=1).astype(jnp.bfloat16),
                halves(scaled[at, columns].astype(jnp.float32), size),
            )

    each(tiles, inside_chunk)

    @pl.when(seq > 0)
    def _():
        for p in range(pieces):
            columns = pl.ds(p * PIECE, PIECE)
            chain_copy(p).wait_recv()
            came = chain_in[:, columns].astype(jnp.float32)
            state[:, columns] = came

            @pl.when(seq < count - 1)
            def _():
                chain_out[:, columns] = (
                    came * total[:1, columns] + local[:, columns]
                ).astype(jnp.bfloat16)
                chain_copy(p).start()

    def across_chunk(c):
        at = tile_rows(c)
        _, start, _ = chunk_flags(seg_ref, c)
        now = state[...]
        low = now.astype(jnp.bfloat16)
        states_ref[c] = low
        carried = spread_heads(jnp.exp(cum_ref[at, :]) * start, spread_ref[...])
        y_ref[at, :] += matmul(output_map(at), low) * carried + skip_ref[...] * act[at, :inner]
        state[...] = now * decay[c][:1] + added[c]

    each(tiles, across_chunk)
    states_ref[tiles] = state[...].astype(jnp.bfloat16)

    def memory_wait(step, carry):
        @pl.when(seq + step < count)
        def _():
            memory_copy(step, lax.rem(seq + step, count), seq).wait_send()
            memory_ref[lax.rem(seq + step, count)] = jnp.zeros(memory_ref.shape[1:], jnp.bfloat16)

        @pl.when(seq - step >= 0)
        def _():
            memory_copy(step, seq, lax.rem(seq - step + count, count)).wait_recv()

        return carry

    lax.fori_loop(1, count, memory_wait, 0)

    @pl.when(seq < count - 1)
    def _():
        halo_copy.wait_send()
        for p in range(pieces):
            chain_copy(p).wait_send()


def mixer_forward(
    tokens,
    mixer_gain,
    segments,
    table,
    mamba_gate,
    mamba_input,
    mamba_maps,
    step_weight,
    query_weight,
    memory_weight,
    taps,
    bias,
    rate,
    skip,
):
    rows, width = tokens.shape
    count = lax.axis_size("seq")
    inner = mamba_gate.shape[1]
    conv_width = taps.shape[1]
    state_width = (conv_width - inner) // 2
    query = query_weight.shape[1]
    chunks = rows // CHUNK
    pieces = inner // PIECE
    vmem = pl.BlockSpec(memory_space=pltpu.VMEM)
    low, full = jnp.bfloat16, jnp.float32
    shape = jax.ShapeDtypeStruct
    return pl.pallas_call(
        functools.partial(mixer_kernel, HD),
        out_shape=[
            shape((rows, inner), full),
            shape((rows + HALO, conv_width), full),
            shape((rows, conv_width), full),
            shape((rows, LANES), full),
            shape((rows, LANES), full),
            shape((rows, inner), full),
            shape((chunks + 1, state_width, inner), low),
            shape((rows, query), low),
            shape((count, rows, memory_weight.shape[1]), low),
        ],
        in_specs=[vmem] * 14,
        out_specs=[vmem] * 9,
        scratch_shapes=[
            pltpu.VMEM((rows, width), low),
            pltpu.VMEM((LANES, inner), low),
            pltpu.VMEM((rows, conv_width), full),
            pltpu.VMEM((rows, inner), low),
            pltpu.VMEM((chunks, state_width, inner), full),
            pltpu.VMEM((chunks, HALO, inner), full),
            pltpu.VMEM((HALO, inner), full),
            pltpu.VMEM((state_width, inner), full),
            pltpu.VMEM((state_width, inner), full),
            pltpu.VMEM((state_width, inner), low),
            pltpu.VMEM((state_width, inner), low),
            pltpu.SemaphoreType.DMA((2, count)),
            pltpu.SemaphoreType.DMA((2,)),
            pltpu.SemaphoreType.DMA((2, pieces)),
        ],
        compiler_params=pltpu.CompilerParams(
            collective_id=2, has_side_effects=True, vmem_limit_bytes=60 << 20
        ),
        name="mixer_forward",
    )(
        tokens,
        mixer_gain[None],
        segments,
        table,
        mamba_gate,
        mamba_input,
        mamba_maps,
        step_weight,
        query_weight,
        memory_weight,
        taps,
        bias,
        rate,
        skip,
    )


KEY_TILE = 256


def stacked_heads(values, first, factor):
    lane = lax.broadcasted_iota(jnp.int32, (values.shape[0], LANES), 1)
    keep = (lane < HD) if first else (lane >= HD)
    parts = []
    for h in range(values.shape[1] // HD):
        tile = values[:, (h // 2) * LANES : (h // 2 + 1) * LANES].astype(jnp.float32)
        if (h % 2 == 0) != first:
            tile = pltpu.roll(tile, HD, 1)
        parts.append(jnp.where(keep, tile * factor, 0.0))
    return jnp.concatenate(parts, axis=0).astype(jnp.bfloat16)


def unstacked_heads(values, rows, first):
    lane = lax.broadcasted_iota(jnp.int32, (rows, LANES), 1)
    tiles = []
    for pair in range(values.shape[0] // rows // 2):
        even = values[2 * pair * rows : (2 * pair + 1) * rows]
        odd = values[(2 * pair + 1) * rows : (2 * pair + 2) * rows]
        if first:
            odd = pltpu.roll(odd, HD, 1)
        else:
            even = pltpu.roll(even, HD, 1)
        tiles.append(jnp.where(lane < HD, even, odd))
    return tiles


def score_tile(first_ref, seg_ref, key_seg_ref, memory_ref, queries, i, k):
    heads = queries.shape[0] // TILE
    at = pl.ds(pl.multiple_of(k * KEY_TILE, KEY_TILE), KEY_TILE)
    keys = memory_ref[at, :]
    scores = matmul_last(queries, keys).reshape(heads, TILE, KEY_TILE)
    row = first_ref[0] + i * TILE + lax.broadcasted_iota(jnp.int32, (TILE, KEY_TILE), 0)
    place = k * KEY_TILE + lax.broadcasted_iota(jnp.int32, (TILE, KEY_TILE), 1)
    own = seg_ref[pl.ds(pl.multiple_of(i * TILE, TILE) + HALO, TILE), :]
    own = jnp.concatenate([own] * (KEY_TILE // LANES), axis=1)
    allowed = (place <= row) & (key_seg_ref[0:1, at] == own)
    return keys, at, scores, allowed[None]


def attention_kernel(
    first_ref, low_ref, high_ref, query_ref, memory_ref, seg_ref, key_seg_ref, out_ref, low_out_ref, log_ref
):
    rows = query_ref.shape[0]
    heads = query_ref.shape[1] // HD

    def block(i):
        at_rows = tile_rows(i)
        queries = stacked_heads(query_ref[at_rows, :], True, HD ** (-0.5))
        last = high_ref[i]

        def one(step, carry):
            most, total, acc = carry
            keys, _, scores, allowed = score_tile(
                first_ref, seg_ref, key_seg_ref, memory_ref, queries, i, last - step
            )
            scores = jnp.where(allowed, scores, neg_large).reshape(heads * TILE, KEY_TILE)
            new = jnp.maximum(most, jnp.max(scores, axis=1, keepdims=True))
            weights = jnp.exp(scores - new)
            factor = jnp.exp(most - new)
            total = total * factor + jnp.sum(weights, axis=1, keepdims=True)
            acc = acc * factor + matmul(weights.astype(jnp.bfloat16), keys)
            return new, total, acc

        most, total, acc = lax.fori_loop(
            0,
            last - low_ref[i] + 1,
            one,
            (
                jnp.full((heads * TILE, 1), neg_large, jnp.float32),
                jnp.zeros((heads * TILE, 1), jnp.float32),
                jnp.zeros((heads * TILE, LANES), jnp.float32),
            ),
        )
        for pair, tile in enumerate(unstacked_heads(acc / total, TILE, False)):
            out_ref[at_rows, pair * LANES : (pair + 1) * LANES] = tile
            low_out_ref[at_rows, pair * LANES : (pair + 1) * LANES] = tile.astype(jnp.bfloat16)
        log = most + jnp.log(total)
        lane = lax.broadcasted_iota(jnp.int32, (TILE, LANES), 1)
        logs = jnp.zeros((TILE, LANES), jnp.float32)
        for h in range(heads):
            logs = jnp.where(lane == h, log[h * TILE : (h + 1) * TILE], logs)
        log_ref[at_rows, :] = logs

    each(rows // TILE, block)


def attention_back_kernel(
    first_ref,
    low_ref,
    high_ref,
    query_ref,
    memory_ref,
    seg_ref,
    key_seg_ref,
    out_ref,
    log_ref,
    d_out_ref,
    table_ref,
    d_query_ref,
    d_memory_ref,
    grads,
):
    rows = query_ref.shape[0]
    heads = query_ref.shape[1] // HD
    grads[...] = jnp.zeros_like(grads)

    def block(i):
        at_rows = tile_rows(i)
        queries = stacked_heads(query_ref[at_rows, :], True, HD ** (-0.5))
        d_out = d_out_ref[at_rows, :]
        outer = stacked_heads(d_out, False, 1.0)
        product = d_out * out_ref[at_rows, :]
        lane = lax.broadcasted_iota(jnp.int32, (TILE, LANES), 1)
        deltas, logs = [], []
        for h in range(heads):
            tile = product[:, (h // 2) * LANES : (h // 2 + 1) * LANES]
            mine = (lane < HD) if h % 2 == 0 else (lane >= HD)
            deltas.append(jnp.sum(jnp.where(mine, tile, 0.0), axis=1, keepdims=True))
            logs.append(log_ref[at_rows, h : h + 1])
        delta = jnp.concatenate(deltas, axis=0)
        log = jnp.concatenate(logs, axis=0)
        last = high_ref[i]

        def one(step, total):
            keys, at, scores, allowed = score_tile(
                first_ref, seg_ref, key_seg_ref, memory_ref, queries, i, last - step
            )
            weights = jnp.exp(scores - log.reshape(heads, TILE, 1))
            weights = jnp.where(allowed, weights, 0.0).reshape(heads * TILE, KEY_TILE)
            inner = matmul_last(outer, keys)
            low = (weights * (inner - delta)).astype(jnp.bfloat16)
            grads[at, :] += matmul_first(low, queries) + matmul_first(
                weights.astype(jnp.bfloat16), outer
            )
            return total + matmul(low, keys)

        total = lax.fori_loop(
            0, last - low_ref[i] + 1, one, jnp.zeros((heads * TILE, LANES), jnp.float32)
        )
        for pair, tile in enumerate(unstacked_heads(total * HD ** (-0.5), TILE, True)):
            turned = tile * table_ref[at_rows, :LANES] - turn_half(tile) * table_ref[at_rows, LANES:]
            d_query_ref[at_rows, pair * LANES : (pair + 1) * LANES] = turned.astype(jnp.bfloat16)

    each(rows // TILE, block)
    d_memory_ref[...] = grads[...].astype(jnp.bfloat16)


def attention_specs(count):
    return [pl.BlockSpec(memory_space=pltpu.SMEM)] * 3 + [
        pl.BlockSpec(memory_space=pltpu.VMEM)
    ] * count


def attention_forward(spans, query, memory, segments, key_segments):
    rows, width = query.shape
    full = jnp.float32
    return pl.pallas_call(
        attention_kernel,
        out_shape=[
            jax.ShapeDtypeStruct((rows, width), full),
            jax.ShapeDtypeStruct((rows, width), jnp.bfloat16),
            jax.ShapeDtypeStruct((rows, LANES), full),
        ],
        in_specs=attention_specs(4),
        out_specs=[pl.BlockSpec(memory_space=pltpu.VMEM)] * 3,
        compiler_params=pltpu.CompilerParams(vmem_limit_bytes=56 << 20),
        name="attention_forward",
    )(*spans, query, memory, segments, key_segments)


def attention_back(spans, query, memory, segments, key_segments, out, logs, d_out, table):
    rows, width = query.shape
    return pl.pallas_call(
        attention_back_kernel,
        out_shape=[
            jax.ShapeDtypeStruct((rows, width), jnp.bfloat16),
            jax.ShapeDtypeStruct(memory.shape, jnp.bfloat16),
        ],
        in_specs=attention_specs(8),
        out_specs=[pl.BlockSpec(memory_space=pltpu.VMEM)] * 2,
        scratch_shapes=[pltpu.VMEM(memory.shape, jnp.float32)],
        compiler_params=pltpu.CompilerParams(vmem_limit_bytes=56 << 20),
        name="attention_back",
    )(*spans, query, memory, segments, key_segments, out, logs, d_out, table)


def mixer_back_kernel(
    size,
    tokens_ref,
    gain_ref,
    seg_ref,
    table_ref,
    gate_weight,
    input_weight,
    maps_weight,
    step_weight,
    query_weight,
    memory_weight,
    taps_ref,
    rate_ref,
    skip_ref,
    pre_ref,
    conv_ref,
    raw_ref,
    cum_ref,
    y_ref,
    states_ref,
    d_second_ref,
    d_y_ref,
    d_gate_z_ref,
    d_query_ref,
    d_memory_ref,
    d_tokens_ref,
    g_side_ref,
    g_taps_ref,
    g_gain_ref,
    g_heads_ref,
    normed,
    spread_ref,
    act,
    d_act,
    d_conv,
    d_scaled,
    d_maps,
    row_term,
    added,
    local,
    total,
    state,
    skip_sum,
    side,
    chain_out,
    chain_in,
    maps_send,
    maps_recv,
    memory_recv,
    norm_send,
    norm_recv,
    sem_memory,
    sem_halo,
    sem_chain,
    sem_maps,
    sem_norm,
):
    seq, head, batch = lax.axis_index("seq"), lax.axis_index("head"), lax.axis_index("batch")
    count = lax.axis_size("seq")
    rows = tokens_ref.shape[0]
    tiles = rows // CHUNK
    inner = y_ref.shape[1]
    width = pre_ref.shape[1]
    state_width = (width - inner) // 2
    model = tokens_ref.shape[1]
    peer = peer_device()
    previous = (lax.rem(seq - 1 + count, count), head, batch)
    greet_seq(pltpu.get_barrier_semaphore(), 1)
    spread_ref[...] = spread_matrix(inner, size)
    pieces = inner // PIECE

    def chain_copy(p):
        columns = pl.ds(p * PIECE, PIECE)
        return exchange(
            chain_out.at[:, columns],
            chain_in.at[:, columns],
            sem_chain.at[0, p],
            sem_chain.at[1, p],
            previous,
        )

    def memory_copy(step):
        place = lax.rem(seq - step + count, count)
        return exchange(
            d_memory_ref.at[place],
            memory_recv.at[step - 1],
            sem_memory.at[0, step],
            sem_memory.at[1, step],
            (place, head, batch),
        )

    halo_copy = exchange(
        d_conv.at[pl.ds(0, HALO)],
        d_conv.at[pl.ds(rows, HALO)],
        sem_halo.at[0],
        sem_halo.at[1],
        previous,
    )
    maps_copy = exchange(maps_send, maps_recv, sem_maps.at[0], sem_maps.at[1], peer)

    def norm_copy(i):
        at = tile_rows(i)
        return exchange(
            norm_send.at[at], norm_recv.at[at], sem_norm.at[0, i], sem_norm.at[1, i], peer
        )

    def input_map(at):
        return act[at, inner : inner + state_width].astype(jnp.bfloat16)

    def output_map(at):
        return act[at, inner + state_width :].astype(jnp.bfloat16)

    def keep_of(c, start):
        last = cum_ref[tile_rows(c), :][CHUNK - 1 :]
        keep = jnp.broadcast_to(jnp.exp(last) * start[CHUNK - 1 :], (HALO, LANES))
        return spread_heads(keep, spread_ref[...])

    def carried_of(c, start):
        return spread_heads(jnp.exp(cum_ref[tile_rows(c), :]) * start, spread_ref[...])

    def activate(i):
        at = tile_rows(i)
        value = conv_ref[at, :]
        act[at, :] = value * sigmoid(value)

    each(tiles, activate)
    local[...] = jnp.zeros_like(local)
    total[...] = jnp.ones_like(total)

    def local_chunk(step):
        c = tiles - 1 - step
        at = tile_rows(c)
        _, start, _ = chunk_flags(seg_ref, c)
        keep = keep_of(c, start)
        value = (d_y_ref[at, :] * carried_of(c, start)).astype(jnp.bfloat16)
        fresh = matmul_first(output_map(at), value)
        added[c] = fresh
        local[...] = local[...] * keep[:1] + fresh
        total[...] = total[...] * keep

    each(tiles, local_chunk)

    @pl.when(seq == count - 1)
    def _():
        state[...] = jnp.zeros_like(state)
        chain_out[...] = local[...].astype(jnp.bfloat16)
        if count > 1:
            for p in range(pieces):
                chain_copy(p).start()

    skip_sum[...] = jnp.zeros_like(skip_sum)

    def inside_chunk(c):
        at = tile_rows(c)
        own, start, _ = chunk_flags(seg_ref, c)
        cum = cum_ref[at, :]
        turned = cum.T
        spread = spread_ref[...]
        low_in, low_out = input_map(at), output_map(at)
        allowed = ordered(CHUNK).astype(jnp.float32).T * jnp.where(own == own.T, 1.0, 0.0)
        meet = matmul_last(low_in, low_out) * allowed
        value = act[at, :inner]
        scaled = value * spread_heads(soft_plus(raw_ref[at, :]), spread)
        d_y = d_y_ref[at, :]
        d_meet = jnp.zeros((CHUNK, CHUNK), jnp.float32)
        for i in range(inner // LANES):
            columns = slice(i * LANES, (i + 1) * LANES)
            d_tile = d_y[:, columns]
            d_mixing = matmul_last(halves(scaled[:, columns], size), d_tile.astype(jnp.bfloat16))
            mixing = []
            for k, h in enumerate((2 * i, 2 * i + 1)):
                gap = turned[h : h + 1, :] - cum[:, h : h + 1]
                fade = jnp.exp(jnp.minimum(gap, 0.0))
                mixing.append(meet * fade)
                d_meet = d_meet + d_mixing[k * CHUNK : (k + 1) * CHUNK] * fade
            d_scaled[at, columns] = matmul(
                jnp.concatenate(mixing, axis=1).astype(jnp.bfloat16), halves(d_tile, size)
            )
        d_meet = (d_meet * allowed).astype(jnp.bfloat16)
        d_maps[at, :state_width] = matmul(d_meet, low_out)
        carried = (d_y * carried_of(c, start)).astype(jnp.bfloat16)
        d_maps[at, state_width:] = matmul_first(d_meet, low_in) + matmul_last(
            carried, states_ref[c]
        )
        product = d_y * value
        skip_sum[...] += jnp.sum(product, axis=0, keepdims=True)
        low = d_y.astype(jnp.bfloat16).astype(jnp.float32)
        row_term[at, :] = sum_heads(low * (y_ref[at, :] - skip_ref[...] * value), spread)

    each(tiles, inside_chunk)

    @pl.when(seq < count - 1)
    def _():
        for p in range(pieces):
            columns = pl.ds(p * PIECE, PIECE)
            chain_copy(p).wait_recv()
            came = chain_in[:, columns].astype(jnp.float32)
            state[:, columns] = came

            @pl.when(seq > 0)
            def _():
                chain_out[:, columns] = (
                    came * total[:1, columns] + local[:, columns]
                ).astype(jnp.bfloat16)
                chain_copy(p).start()

    def memory_start(step, carry):
        @pl.when(seq - step >= 0)
        def _():
            memory_copy(step).start()

        return carry

    lax.fori_loop(1, count, memory_start, 0)
    g_heads_ref[...] = jnp.zeros_like(g_heads_ref)
    upper = jnp.where(ordered(CHUNK), 1.0, 0.0).T

    def across_chunk(step):
        c = tiles - 1 - step
        at = tile_rows(c)
        _, start, end = chunk_flags(seg_ref, c)
        spread = spread_ref[...]
        cum = cum_ref[at, :]
        last = cum[CHUNK - 1 :]
        now = state[...]
        low = now.astype(jnp.bfloat16)
        raw = raw_ref[at, :]
        steps = soft_plus(raw)
        steps_wide = spread_heads(steps, spread)
        value = act[at, :inner]
        scaled = value * steps_wide
        weight = spread_heads(jnp.exp(last - cum) * end, spread)
        d_value = d_scaled[at, :] + matmul(input_map(at), low) * weight
        d_maps[at, :state_width] += matmul_last((scaled * weight).astype(jnp.bfloat16), low)
        final = jnp.sum(
            states_ref[c + 1].astype(jnp.float32) * low.astype(jnp.float32), axis=0, keepdims=True
        )
        final = sum_heads(jnp.broadcast_to(final, (HALO, inner)), spread)[:1]
        low_scaled = scaled.astype(jnp.bfloat16).astype(jnp.float32)
        d_cum = row_term[at, :] - sum_heads(low_scaled * d_value, spread)
        d_rate = jnp.dot(upper, d_cum, precision=highest) + final
        rate = rate_ref[...]
        d_steps = sum_heads(value * d_value, spread) + rate * d_rate
        d_raw = d_steps * sigmoid(raw)
        g_heads_ref[0:1, :] += rate * jnp.sum(steps * d_rate, axis=0, keepdims=True)
        g_heads_ref[1:2, :] += jnp.sum(d_raw, axis=0, keepdims=True)
        side[at, 2 * inner + 2 * state_width : 2 * inner + 2 * state_width + LANES] = d_raw.astype(
            jnp.bfloat16
        )
        d_act[at, :inner] = steps_wide * d_value + skip_ref[...] * d_y_ref[at, :]
        state[...] = now * keep_of(c, start)[:1] + added[c]

    each(tiles, across_chunk)
    g_heads_ref[2:3, :] = sum_heads(jnp.broadcast_to(skip_sum[:1], (HALO, inner)), spread_ref[...])[
        :1
    ]
    maps_send[...] = d_maps[...].astype(jnp.bfloat16)
    maps_copy.start()

    def copy_tile(i):
        at = tile_rows(i)
        side[at, :inner] = d_gate_z_ref[at, :]
        hidden = tokens_ref[at, :].astype(jnp.float32)
        inverse = lax.rsqrt(jnp.mean(hidden * hidden, axis=1, keepdims=True) + eps_norm)
        normed[at, :] = (hidden * inverse * gain_ref[...]).astype(jnp.bfloat16)

    each(tiles, copy_tile)
    maps_copy.wait()

    def conv_back_tile(i):
        at = tile_rows(i)
        d_act[at, inner:] = maps_send[at, :].astype(jnp.float32) + maps_recv[at, :].astype(
            jnp.float32
        )
        value = conv_ref[at, :]
        sig = sigmoid(value)
        d_conv[at, :] = d_act[at, :] * (sig * (1.0 + value * (1.0 - sig)))

    each(tiles, conv_back_tile)

    @pl.when(seq > 0)
    def _():
        halo_copy.start()

    @pl.when(seq == count - 1)
    def _():
        d_conv[pl.ds(rows, HALO), :] = jnp.zeros((HALO, width), jnp.float32)

    @pl.when(seq < count - 1)
    def _():
        halo_copy.wait_recv()

    g_taps_ref[...] = jnp.zeros_like(g_taps_ref)

    def taps_tile(i):
        at = tile_rows(i)
        window_at = pl.ds(pl.multiple_of(i * TILE, TILE), TILE + HALO)
        seg = seg_ref[pl.ds(pl.multiple_of(i * TILE, TILE), TILE + 2 * HALO), :]
        own = seg[HALO : HALO + TILE]
        before = [
            jnp.where(seg[HALO - 3 + k : HALO - 3 + k + TILE] == own, 1.0, 0.0) for k in range(3)
        ]
        after = [
            jnp.where(seg[HALO + 3 - k : HALO + 3 - k + TILE] == own, 1.0, 0.0) for k in range(3)
        ]
        for j in range(width // LANES):
            columns = slice(j * LANES, (j + 1) * LANES)
            window = pre_ref[window_at, columns]
            grads = d_conv[window_at, columns]
            own_grad = grads[:TILE]
            summed = taps_ref[3:4, columns] * own_grad
            g_taps_ref[3:4, columns] += jnp.sum(own_grad * window[HALO:], axis=0, keepdims=True)
            for k in range(3):
                summed = summed + taps_ref[k : k + 1, columns] * (
                    grads[3 - k : 3 - k + TILE] * after[k]
                )
                g_taps_ref[k : k + 1, columns] += jnp.sum(
                    own_grad * (window[HALO - 3 + k : HALO - 3 + k + TILE] * before[k]),
                    axis=0,
                    keepdims=True,
                )
            side[at, inner + j * LANES : inner + (j + 1) * LANES] = summed.astype(jnp.bfloat16)

    each(tiles, taps_tile)
    query_at = 2 * inner + 2 * state_width + LANES
    query_width = d_query_ref.shape[1]
    memory_at = query_at + query_width

    def memory_wait(step, carry):
        @pl.when(seq - step >= 0)
        def _():
            memory_copy(step).wait_send()

        @pl.when(seq + step < count)
        def _():
            memory_copy(step).wait_recv()

        return carry

    lax.fori_loop(1, count, memory_wait, 0)

    def memory_tile(i):
        at = tile_rows(i)

        def one(step, carry):
            came = memory_recv[step - 1, at, :].astype(jnp.float32)
            return carry + jnp.where(seq + step < count, came, 0.0)

        grad = lax.fori_loop(1, count, one, d_memory_ref[seq, at, :].astype(jnp.float32))
        lane = lax.broadcasted_iota(jnp.int32, grad.shape, 1)
        turned = grad * table_ref[at, :LANES] - turn_half(grad) * table_ref[at, LANES:]
        side[at, memory_at : memory_at + LANES] = jnp.where(lane < HD, turned, grad).astype(
            jnp.bfloat16
        )
        side[at, query_at:memory_at] = d_query_ref[at, :]

    each(tiles, memory_tile)

    def norm_tile(i):
        at = tile_rows(i)
        maps_at = 2 * inner
        step_at = maps_at + 2 * state_width
        part = (
            matmul_last(side[at, :inner], gate_weight[...])
            + matmul_last(side[at, inner:maps_at], input_weight[...])
            + matmul_last(side[at, maps_at:step_at], maps_weight[...]) / lax.axis_size("head")
            + matmul_last(side[at, step_at:query_at], step_weight[...])
            + matmul_last(side[at, query_at:memory_at], query_weight[...])
            + matmul_last(side[at, memory_at:], memory_weight[...])
        )
        norm_send[at, :] = part.astype(jnp.bfloat16)
        norm_copy(i).start()

    each(tiles, norm_tile)

    def weight_block(k):
        block = pl.ds(pl.multiple_of(k * 256, 256), 256)
        g_side_ref[block, :] = matmul_first(normed[:, block], side[...]).astype(jnp.bfloat16)

    each(model // 256, weight_block)
    g_gain_ref[...] = jnp.zeros_like(g_gain_ref)

    def last_tile(i):
        at = tile_rows(i)
        norm_copy(i).wait()
        d_norm = norm_send[at, :].astype(jnp.float32) + norm_recv[at, :].astype(jnp.float32)
        hidden = tokens_ref[at, :].astype(jnp.float32)
        inverse = lax.rsqrt(jnp.mean(hidden * hidden, axis=1, keepdims=True) + eps_norm)
        e_one = d_norm * gain_ref[...]
        cross = jnp.sum(e_one * hidden, axis=1, keepdims=True) / model
        d_tokens_ref[at, :] = (
            d_second_ref[at, :] + inverse * e_one - hidden * (inverse * inverse * inverse * cross)
        )
        g_gain_ref[...] += jnp.sum(d_norm * hidden * inverse, axis=0, keepdims=True)

    each(tiles, last_tile)

    @pl.when(seq > 0)
    def _():
        halo_copy.wait_send()
        for p in range(pieces):
            chain_copy(p).wait_send()


def mixer_back(
    tokens,
    mixer_gain,
    segments,
    table,
    mamba_gate,
    mamba_input,
    mamba_maps,
    step_weight,
    query_weight,
    memory_weight,
    taps,
    rate,
    skip,
    *saved,
):
    rows, model = tokens.shape
    count = lax.axis_size("seq")
    inner = mamba_gate.shape[1]
    width = taps.shape[1]
    state_width = (width - inner) // 2
    chunks = rows // CHUNK
    pieces = inner // PIECE
    side = 2 * inner + 2 * state_width + LANES + query_weight.shape[1] + memory_weight.shape[1]
    vmem = pl.BlockSpec(memory_space=pltpu.VMEM)
    low, full = jnp.bfloat16, jnp.float32
    shape = jax.ShapeDtypeStruct
    return pl.pallas_call(
        functools.partial(mixer_back_kernel, HD),
        out_shape=[
            shape((rows, model), full),
            shape((model, side), low),
            shape((HALO, width), full),
            shape((1, model), full),
            shape((HALO, LANES), full),
        ],
        in_specs=[vmem] * (13 + len(saved)),
        out_specs=[vmem] * 5,
        scratch_shapes=[
            pltpu.VMEM((rows, model), low),
            pltpu.VMEM((LANES, inner), low),
            pltpu.VMEM((rows, width), full),
            pltpu.VMEM((rows, width), full),
            pltpu.VMEM((rows + HALO, width), full),
            pltpu.VMEM((rows, inner), full),
            pltpu.VMEM((rows, 2 * state_width), full),
            pltpu.VMEM((rows, LANES), full),
            pltpu.VMEM((chunks, state_width, inner), full),
            pltpu.VMEM((state_width, inner), full),
            pltpu.VMEM((HALO, inner), full),
            pltpu.VMEM((state_width, inner), full),
            pltpu.VMEM((1, inner), full),
            pltpu.VMEM((rows, side), low),
            pltpu.VMEM((state_width, inner), low),
            pltpu.VMEM((state_width, inner), low),
            pltpu.VMEM((rows, 2 * state_width), low),
            pltpu.VMEM((rows, 2 * state_width), low),
            pltpu.VMEM((max(count - 1, 1), rows, memory_weight.shape[1]), low),
            pltpu.VMEM((rows, model), low),
            pltpu.VMEM((rows, model), low),
            pltpu.SemaphoreType.DMA((2, count)),
            pltpu.SemaphoreType.DMA((2,)),
            pltpu.SemaphoreType.DMA((2, pieces)),
            pltpu.SemaphoreType.DMA((2,)),
            pltpu.SemaphoreType.DMA((2, chunks)),
        ],
        compiler_params=pltpu.CompilerParams(
            collective_id=3, has_side_effects=True, vmem_limit_bytes=60 << 20
        ),
        name="mixer_back",
    )(
        tokens,
        mixer_gain[None],
        segments,
        table,
        mamba_gate,
        mamba_input,
        mamba_maps,
        step_weight,
        query_weight,
        memory_weight,
        taps,
        rate,
        skip,
        *saved,
    )


def rotation_table(position):
    half = HD // 2
    lane = jnp.arange(LANES)
    inverse_freq = rope_base ** (-(lane % half).astype(jnp.float32) / half)
    angles = position.astype(jnp.float32)[:, None] * inverse_freq[None, :]
    sign = jnp.where(lane % HD < half, -1.0, 1.0)
    return jnp.concatenate([jnp.cos(angles), sign[None, :] * jnp.sin(angles)], axis=1)


def body(
    tokens,
    seg_ids,
    mixer_gain,
    mamba_gate,
    mamba_input,
    mamba_maps,
    mamba_step,
    conv_inner,
    conv_maps,
    log_rate,
    step_bias,
    skip_gain,
    mamba_gain,
    mamba_output,
    query_weight,
    memory_weight,
    attention_out,
    feed_gain,
    gate_weight,
    lift_weight,
    down_weight,
    cotangent,
):
    tokens, cotangent = tokens[0], cotangent[0]
    rows, wide = tokens.shape
    tap_count, inner = conv_inner.shape
    head_count = log_rate.shape[0]
    segments = seg_ids[0]
    offset = lax.axis_index("seq") * rows
    padded = jnp.concatenate(
        [jnp.full((HALO,), -1, jnp.int32), segments, jnp.full((HALO,), -2, jnp.int32)]
    )
    window = lax.dynamic_slice_in_dim(padded, offset, rows + 2 * HALO)
    window_wide = jnp.broadcast_to(
        window.astype(jnp.float32)[:, None], (rows + 2 * HALO, LANES)
    )
    key_segments = segments.astype(jnp.float32)[None]
    table = rotation_table(offset + jnp.arange(rows, dtype=jnp.int32))
    starts = offset + jnp.arange(rows // TILE, dtype=jnp.int32) * TILE
    reach = segments[KEY_TILE - 1 :: KEY_TILE]
    low = jnp.sum(
        (reach[None, :] < window[HALO : HALO + rows : TILE][:, None]).astype(jnp.int32), axis=1
    )
    spans = (offset[None], low, (starts + TILE - 1) // KEY_TILE)

    def lanes_of(values):
        return jnp.pad(values, (0, LANES - head_count))[None]

    step_weight = jnp.pad(mamba_step, ((0, 0), (0, LANES - head_count)))
    taps = jnp.pad(
        jnp.concatenate([conv_inner, conv_maps], axis=1), ((0, HALO - tap_count), (0, 0))
    )
    bias, rate = lanes_of(step_bias), lanes_of(-jnp.exp(log_rate))
    skip = jnp.repeat(skip_gain, inner // head_count)[None]
    gate_z, pre, conv, raw, cum, y, states, query, memory = mixer_forward(
        tokens,
        mixer_gain,
        window_wide,
        table,
        mamba_gate,
        mamba_input,
        mamba_maps,
        step_weight,
        query_weight,
        memory_weight,
        taps,
        bias,
        rate,
        skip,
    )
    all_memory = memory.reshape(memory.shape[0] * rows, memory.shape[2])
    attention, attention_low, logs = attention_forward(
        spans, query, all_memory, window_wide, key_segments
    )
    (
        layer_out,
        d_second,
        d_y,
        d_gate_z,
        d_attention,
        g_feed,
        g_mixed,
        g_down,
        g_feed_gain,
        g_mamba_gain,
    ) = feed_layer(
        y,
        gate_z,
        attention_low,
        tokens,
        cotangent,
        mamba_gain,
        feed_gain,
        mamba_output,
        attention_out,
        gate_weight,
        lift_weight,
        down_weight,
    )
    d_query, d_memory = attention_back(
        spans, query, all_memory, window_wide, key_segments, attention, logs, d_attention, table
    )
    grad_tokens, g_side, g_taps, g_mixer_gain, g_heads = mixer_back(
        tokens,
        mixer_gain,
        window_wide,
        table,
        mamba_gate,
        mamba_input,
        mamba_maps,
        step_weight,
        query_weight,
        memory_weight,
        taps,
        rate,
        skip,
        pre,
        conv,
        raw,
        cum,
        y,
        states,
        d_second,
        d_y,
        d_gate_z,
        d_query,
        d_memory.reshape(memory.shape),
    )
    small = jnp.concatenate(
        [
            g_taps[:tap_count],
            jnp.pad(g_mamba_gain, ((0, 0), (0, wide - inner))),
            g_mixer_gain,
            g_feed_gain,
            jnp.pad(g_heads[:3].reshape(1, 3 * LANES), ((0, 0), (0, wide - 3 * LANES))),
        ],
        axis=0,
    )
    (mixer_sum, feed_sum, mixed_sum, down_sum), small = reduce_gradients(
        [g_side, g_feed, g_mixed, g_down], small
    )
    edges = [0]
    for width in (
        inner,
        inner,
        conv_maps.shape[1],
        LANES,
        query_weight.shape[1],
        memory_weight.shape[1],
    ):
        edges.append(edges[-1] + width)
    pieces = [mixer_sum[:, a:b].astype(jnp.float32) for a, b in zip(edges[:-1], edges[1:])]
    own_rows = wide // lax.axis_size("seq")
    own_at = lax.axis_index("seq") * own_rows
    feed = gate_weight.shape[1]
    return (
        layer_out[None],
        grad_tokens[None],
        lax.dynamic_slice_in_dim(small[5], own_at, own_rows),
        pieces[0],
        pieces[1],
        pieces[2],
        pieces[3][:, :head_count],
        small[:tap_count, :inner],
        small[:tap_count, inner:],
        small[7, :head_count],
        small[7, LANES : LANES + head_count],
        small[7, 2 * LANES : 2 * LANES + head_count],
        small[4, :inner],
        mixed_sum[:, :inner].astype(jnp.float32),
        pieces[4],
        pieces[5],
        mixed_sum[:, inner:].astype(jnp.float32),
        lax.dynamic_slice_in_dim(small[6], own_at, own_rows),
        feed_sum[:, :feed].astype(jnp.float32),
        feed_sum[:, feed:].astype(jnp.float32),
        down_sum.astype(jnp.float32),
    )


def solution(mesh):
    return jax.shard_map(
        body,
        mesh=mesh,
        in_specs=(
            P("batch", "seq", None),
            P("batch", None),
            P(),
            P(None, "head"),
            P(None, "head"),
            P(),
            P(None, "head"),
            P(None, "head"),
            P(),
            P("head"),
            P("head"),
            P("head"),
            P("head"),
            P(None, "head"),
            P(None, "head"),
            P(None, "head"),
            P(None, "head"),
            P(),
            P(None, "head"),
            P(None, "head"),
            P(None, "head"),
            P("batch", "seq", None),
        ),
        out_specs=(
            P("batch", "seq", None),
            P("batch", "seq", None),
            P("seq"),
            P("seq", "head"),
            P("seq", "head"),
            P("seq", None),
            P("seq", "head"),
            P(None, "head"),
            P(),
            P("head"),
            P("head"),
            P("head"),
            P("head"),
            P("seq", "head"),
            P("seq", "head"),
            P("seq", "head"),
            P("seq", "head"),
            P("seq"),
            P("seq", "head"),
            P("seq", "head"),
            P("seq", "head"),
        ),
        check_vma=False,
    )
```

```python
import functools

import jax
import jax.numpy as jnp
from jax import lax
from jax.experimental import pallas as pl
from jax.experimental.pallas import tpu as pltpu
from jax.sharding import PartitionSpec as P

HD = 64
eps_norm = 1e-05
rope_base = 10000.0
neg_large = -1e30
highest = lax.Precision.HIGHEST


LANES = 128
MOST = 512
AHEAD = 4
MESH = pl.DeviceIdType.MESH


def exchange(source, target, send_sem, recv_sem, device):
    return pltpu.make_async_remote_copy(
        src_ref=source,
        dst_ref=target,
        send_sem=send_sem,
        recv_sem=recv_sem,
        device_id=device,
        device_id_type=MESH,
    )


def each(count, action):
    span(0, count, action)


def span(first, last, action):
    lax.fori_loop(first, last, lambda i, carry: (action(i), carry)[1], 0)


def column_chunks(widths):
    chunks = []
    for group, width in enumerate(widths):
        count = -(-width // MOST)
        tiles = width // LANES
        start = 0
        for k in range(count):
            size = (tiles // count + (1 if k < tiles % count else 0)) * LANES
            chunks.append((group, start, size))
            start += size
    return chunks


def seq_blocks(grad):
    count = lax.axis_size("seq")
    return grad.reshape(count, 2, 2, grad.shape[0] // count // 4, grad.shape[1])


def peer_device():
    return (lax.axis_index("seq"), 1 - lax.axis_index("head"), lax.axis_index("batch"))


def other_device(step):
    seq, batch = lax.axis_index("seq"), lax.axis_index("batch")
    batches = lax.axis_size("batch")
    place = lax.rem(seq * batches + batch + step, lax.axis_size("seq") * batches)
    return (place // batches, lax.axis_index("head"), lax.rem(place, batches))


def greet_all(barrier, with_peer):
    world = lax.axis_size("seq") * lax.axis_size("batch")
    span(
        1,
        world,
        lambda step: pl.semaphore_signal(
            barrier, inc=1, device_id=other_device(step), device_id_type=MESH
        ),
    )
    if with_peer:
        pl.semaphore_signal(barrier, inc=1, device_id=peer_device(), device_id_type=MESH)
    pl.semaphore_wait(barrier, world - 1 + (1 if with_peer else 0))


class SmallSum:
    def __init__(self, source, slots, sems):
        self.source, self.slots, self.sems = source, slots, sems
        self.world = slots.shape[0]
        self.mine = lax.axis_index("seq") * lax.axis_size("batch") + lax.axis_index("batch")

    def copy(self, step):
        return exchange(
            self.source,
            self.slots.at[self.mine],
            self.sems.at[0, step],
            self.sems.at[1, step],
            other_device(step),
        )

    def start(self):
        span(1, self.world, lambda step: self.copy(step).start())

    def finish(self):
        span(1, self.world, lambda step: self.copy(step).wait())
        self.slots[self.mine] = self.source[...]
        return lax.fori_loop(
            1, self.world, lambda k, total: total + self.slots[k], self.slots[0]
        )


def small_scratch(shape):
    world = lax.axis_size("seq") * lax.axis_size("batch")
    return [
        pltpu.VMEM(shape, jnp.float32),
        pltpu.VMEM((world,) + shape, jnp.float32),
        pltpu.SemaphoreType.DMA((2, world)),
    ]


class Reduction:
    def __init__(self, chunks, sources, outs, scratch):
        self.chunks, self.sources, self.outs = chunks, sources, outs
        groups = len(sources)
        scratch = list(scratch)
        self.first, self.second, self.third = (
            scratch[:groups],
            scratch[groups : 2 * groups],
            scratch[2 * groups : 3 * groups],
        )
        self.own, self.sem_own, self.sem_one, self.sem_two, self.sem_seq, self.sem_back = scratch[
            3 * groups :
        ]
        self.count = lax.axis_size("seq")
        self.seq, self.head = lax.axis_index("seq"), lax.axis_index("head")
        self.batch = lax.axis_index("batch")
        self.low, self.high = lax.rem(self.batch, 2), self.batch // 2
        self.low_peer = (self.seq, self.head, self.batch + 1 - 2 * self.low)
        self.high_peer = (self.seq, self.head, self.batch + 2 - 4 * self.high)
        self.turn = self.sent = self.held = self.limit = 0

    def place(self, k):
        group, start, size = self.chunks[k]
        return group, pl.ds(start, size)

    def first_copy(self, k):
        group, columns = self.place(k)
        if k % 2 == 0:
            part, peer = (
                self.sources[group].at[:, :, 1 - self.low, :, columns],
                self.low_peer,
            )
        else:
            part, peer = (
                self.sources[group].at[:, 1 - self.high, :, :, columns],
                self.high_peer,
            )
        return exchange(
            part,
            self.first[group].at[:, :, :, columns],
            self.sem_one.at[0, k],
            self.sem_one.at[1, k],
            peer,
        )

    def own_copy(self, k):
        group, columns = self.place(k)
        size = self.chunks[k][2]
        if k % 2 == 0:
            part = self.sources[group].at[:, :, self.low, :, columns]
        else:
            part = self.sources[group].at[:, self.high, :, :, columns]
        return pltpu.make_async_copy(
            part, self.own.at[k % 2, :, :, :, pl.ds(0, size)], self.sem_own.at[k]
        )

    def second_copy(self, k):
        group, columns = self.place(k)
        if k % 2 == 0:
            away, peer = 1 - self.high, self.high_peer
        else:
            away, peer = 1 - self.low, self.low_peer
        return exchange(
            self.first[group].at[:, away, :, columns],
            self.second[group].at[:, :, columns],
            self.sem_two.at[0, k],
            self.sem_two.at[1, k],
            peer,
        )

    def seq_copy(self, k, step):
        group, columns = self.place(k)
        place = lax.rem(self.seq + step, self.count)
        return exchange(
            self.second[group].at[place, :, columns],
            self.third[group].at[step - 1, :, columns],
            self.sem_seq.at[0, k, step - 1],
            self.sem_seq.at[1, k, step - 1],
            (place, self.head, self.batch),
        )

    def back_copy(self, k, turn):
        group, columns = self.place(k)
        out = self.outs[group]
        peer = self.high_peer if (k + turn) % 2 == 0 else self.low_peer
        if turn == 0:
            part = out.at[self.high, self.low, :, columns]
        elif k % 2 == 0:
            part = out.at[:, self.low, :, columns]
        else:
            part = out.at[self.high, :, :, columns]
        return exchange(part, part, self.sem_back.at[0, k, turn], self.sem_back.at[1, k, turn], peer)

    def add_first(self, k):
        group, columns = self.place(k)
        size = self.chunks[k][2]

        def one(place):
            own = self.own[k % 2, place, :, :, :size].astype(jnp.float32)
            came = self.first[group][place, :, :, columns].astype(jnp.float32)
            self.first[group][place, :, :, columns] = (own + came).astype(jnp.bfloat16)

        each(self.count, one)

    def add_second(self, k):
        group, columns = self.place(k)
        keep = self.high if k % 2 == 0 else self.low

        def one(place):
            own = self.first[group][place, keep, :, columns].astype(jnp.float32)
            came = self.second[group][place, :, columns].astype(jnp.float32)
            self.second[group][place, :, columns] = (own + came).astype(jnp.bfloat16)

        each(self.count, one)

    def add_third(self, k):
        group, columns = self.place(k)
        total = lax.fori_loop(
            0,
            self.count - 1,
            lambda slot, total: total + self.third[group][slot, :, columns].astype(jnp.float32),
            self.second[group][self.seq, :, columns].astype(jnp.float32),
        )
        self.outs[group][self.high, self.low, :, columns] = total.astype(jnp.bfloat16)

    def refill(self):
        while self.sent < min(self.limit, self.turn + AHEAD):
            self.first_copy(self.sent).start()
            self.sent += 1
        while self.held < min(self.limit, self.turn + 2):
            self.own_copy(self.held).start()
            self.held += 1

    def allow(self, limit):
        self.limit = limit
        self.refill()

    def advance(self):
        total = len(self.chunks)
        k = self.turn
        if k < total:
            self.first_copy(k).wait()
            self.own_copy(k).wait()
            self.add_first(k)
            self.second_copy(k).start()
        self.turn += 1
        self.refill()
        k = self.turn - 2
        if 0 <= k < total:
            self.second_copy(k).wait()
            self.add_second(k)
            span(1, self.count, lambda step: self.seq_copy(k, step).start())
        k = self.turn - 3
        if 0 <= k < total:
            span(1, self.count, lambda step: self.seq_copy(k, step).wait())
            self.add_third(k)
            self.back_copy(k, 0).start()
        k = self.turn - 4
        if 0 <= k < total:
            self.back_copy(k, 0).wait()
            self.back_copy(k, 1).start()
        k = self.turn - 5
        if 0 <= k < total:
            self.back_copy(k, 1).wait()

    def finish(self):
        while self.turn < len(self.chunks) + 4:
            self.advance()


def reduction_scratch(chunks, widths, rows):
    count = lax.axis_size("seq")
    parts = len(chunks)
    most = max(size for _, _, size in chunks)
    low = jnp.bfloat16
    return (
        [pltpu.VMEM((count, 2, rows, w), low) for w in widths]
        + [pltpu.VMEM((count, rows, w), low) for w in widths]
        + [pltpu.VMEM((max(count - 1, 1), rows, w), low) for w in widths]
        + [
            pltpu.VMEM((2, count, 2, rows, most), low),
            pltpu.SemaphoreType.DMA((parts,)),
            pltpu.SemaphoreType.DMA((2, parts)),
            pltpu.SemaphoreType.DMA((2, parts)),
            pltpu.SemaphoreType.DMA((2, parts, max(count - 1, 1))),
            pltpu.SemaphoreType.DMA((2, parts, 2)),
        ]
    )


def reduce_kernel(chunks, *refs):
    count = 1 + max(c[0] for c in chunks)
    sources, refs = refs[:count], refs[count:]
    small_given, refs = refs[0], refs[1:]
    outs, refs = refs[:count], refs[count:]
    small_out, small_in, small_buf, sem_small, *refs = refs
    greet_all(pltpu.get_barrier_semaphore(), False)
    reduction = Reduction(chunks, sources, outs, refs)
    reduction.allow(len(chunks))
    small_in[...] = small_given[...]
    small_sum = SmallSum(small_in, small_buf, sem_small)
    small_sum.start()
    reduction.finish()
    small_out[...] = small_sum.finish()


def reduce_gradients(grads, small):
    widths = [g.shape[1] for g in grads]
    chunks = column_chunks(widths)
    blocks = [seq_blocks(g) for g in grads]
    rows = blocks[0].shape[3]
    vmem = pl.BlockSpec(memory_space=pltpu.VMEM)
    return pl.pallas_call(
        functools.partial(reduce_kernel, chunks),
        out_shape=[jax.ShapeDtypeStruct((2, 2, rows, w), jnp.bfloat16) for w in widths]
        + [jax.ShapeDtypeStruct(small.shape, jnp.float32)],
        in_specs=[pl.BlockSpec(memory_space=pl.ANY)] * len(grads) + [vmem],
        out_specs=[vmem] * (len(grads) + 1),
        scratch_shapes=small_scratch(small.shape) + reduction_scratch(chunks, widths, rows),
        compiler_params=pltpu.CompilerParams(
            collective_id=0, has_side_effects=True, vmem_limit_bytes=56 << 20
        ),
        name="reduce_gradients",
    )(*blocks, small)


def matmul(former, latter):
    return jnp.dot(former, latter, preferred_element_type=jnp.float32)


def matmul_last(former, latter):
    return lax.dot_general(
        former, latter, (((1,), (1,)), ((), ())), preferred_element_type=jnp.float32
    )


def matmul_first(former, latter):
    return lax.dot_general(
        former, latter, (((0,), (0,)), ((), ())), preferred_element_type=jnp.float32
    )


TILE = 128


def sigmoid(v):
    return 1.0 / (1.0 + jnp.exp(-v))


def greet_peer(barrier, peer):
    pl.semaphore_signal(barrier, inc=1, device_id=peer, device_id_type=MESH)
    pl.semaphore_wait(barrier, 1)


def tile_rows(i):
    return pl.ds(pl.multiple_of(i * TILE, TILE), TILE)


FEED_TILE = 256


def feed_rows(i):
    return pl.ds(pl.multiple_of(i * FEED_TILE, FEED_TILE), FEED_TILE)


def feed_kernel(
    y_ref,
    gate_z_ref,
    attention_ref,
    tokens_ref,
    cotangent_ref,
    mixer_gain_ref,
    mamba_gain_ref,
    feed_gain_ref,
    mamba_output_ref,
    attention_out_ref,
    gate_weight_hbm,
    lift_weight_hbm,
    down_weight_hbm,
    out_ref,
    d_second_ref,
    d_y_ref,
    d_gate_z_ref,
    d_attention_ref,
    g_feed_ref,
    g_mixed_ref,
    g_down_ref,
    g_gate_ref,
    g_feed_gain_ref,
    g_mamba_gain_ref,
    gate_weight,
    lift_weight,
    down_weight,
    normed,
    gated,
    g_six,
    inverse_six,
    second,
    inverse_two,
    normed2,
    active,
    d_feed,
    d_mix,
    d_gated,
    square_send,
    square_recv,
    cross_send,
    cross_recv,
    mixed_send,
    mixed_recv,
    lift_send,
    lift_recv,
    norm_send,
    norm_recv,
    weight_sem,
    sem_square,
    sem_cross,
    sem_mixed,
    sem_lift,
    sem_norm,
):
    rows = y_ref.shape[0]
    tiles = rows // FEED_TILE
    inner = y_ref.shape[1]
    width = feed_gain_ref.shape[1]
    feed = down_weight.shape[1]
    all_inner = inner * lax.axis_size("head")
    peer = peer_device()
    loads = [
        pltpu.make_async_copy(source, target, weight_sem.at[k])
        for k, (source, target) in enumerate(
            (
                (gate_weight_hbm, gate_weight),
                (lift_weight_hbm, lift_weight),
                (down_weight_hbm, down_weight),
            )
        )
    ]
    for load in loads:
        load.start()
    greet_peer(pltpu.get_barrier_semaphore(), peer)

    def swap(send, recv, sems, i):
        rows_now = feed_rows(i)
        return exchange(send.at[rows_now], recv.at[rows_now], sems.at[0, i], sems.at[1, i], peer)

    def gate_tile(i):
        at = feed_rows(i)
        hidden = tokens_ref[at, :].astype(jnp.float32)
        inverse = lax.rsqrt(jnp.mean(hidden * hidden, axis=1, keepdims=True) + eps_norm)
        normed[at, :] = (hidden * inverse * mixer_gain_ref[...]).astype(jnp.bfloat16)
        gate_now = gate_z_ref[at, :]
        value = y_ref[at, :] * gate_now * sigmoid(gate_now)
        g_six[at, :] = value
        square_send[at, :] = jnp.broadcast_to(
            jnp.sum(value * value, axis=1, keepdims=True), (FEED_TILE, LANES)
        )
        swap(square_send, square_recv, sem_square, i).start()

    each(tiles, gate_tile)

    def mixed_tile(i):
        at = feed_rows(i)
        swap(square_send, square_recv, sem_square, i).wait()
        total = square_send[at, :] + square_recv[at, :]
        inverse = lax.rsqrt(total[:, :1] / all_inner + eps_norm)
        inverse_six[at, :] = jnp.broadcast_to(inverse, (FEED_TILE, LANES))
        low = (g_six[at, :] * inverse * mamba_gain_ref[...]).astype(jnp.bfloat16)
        gated[at, :] = low
        part = matmul_last(low, mamba_output_ref[...]) + matmul_last(
            attention_ref[at, :], attention_out_ref[...]
        )
        mixed_send[at, :] = part.astype(jnp.bfloat16)
        swap(mixed_send, mixed_recv, sem_mixed, i).start()

    each(tiles, mixed_tile)
    for load in loads:
        load.wait()

    def feed_tile(i):
        at = feed_rows(i)
        swap(mixed_send, mixed_recv, sem_mixed, i).wait()
        total = mixed_send[at, :].astype(jnp.float32) + mixed_recv[at, :].astype(jnp.float32)
        hidden = tokens_ref[at, :].astype(jnp.float32) + total
        second[at, :] = hidden
        inverse = lax.rsqrt(jnp.mean(hidden * hidden, axis=1, keepdims=True) + eps_norm)
        inverse_two[at, :] = jnp.broadcast_to(inverse, (FEED_TILE, LANES))
        low = (hidden * inverse * feed_gain_ref[...]).astype(jnp.bfloat16)
        normed2[at, :] = low
        gate_now = matmul(low, gate_weight[...])
        lift_now = matmul(low, lift_weight[...])
        sig = sigmoid(gate_now)
        silu = gate_now * sig
        act = (silu * lift_now).astype(jnp.bfloat16)
        active[at, :] = act
        lift_send[at, :] = matmul_last(act, down_weight[...]).astype(jnp.bfloat16)
        swap(lift_send, lift_recv, sem_lift, i).start()
        d_act = matmul(cotangent_ref[at, :], down_weight[...])
        d_gate = (d_act * lift_now * (sig * (1.0 + gate_now * (1.0 - sig)))).astype(jnp.bfloat16)
        d_lift = (d_act * silu).astype(jnp.bfloat16)
        d_feed[at, :feed] = d_gate
        d_feed[at, feed:] = d_lift
        part = matmul_last(d_gate, gate_weight[...]) + matmul_last(d_lift, lift_weight[...])
        norm_send[at, :] = part.astype(jnp.bfloat16)
        swap(norm_send, norm_recv, sem_norm, i).start()

    each(tiles, feed_tile)
    g_feed_gain_ref[...] = jnp.zeros_like(g_feed_gain_ref)
    g_mamba_gain_ref[...] = jnp.zeros_like(g_mamba_gain_ref)

    def norm_tile(i):
        at = feed_rows(i)
        swap(norm_send, norm_recv, sem_norm, i).wait()
        d_norm = norm_send[at, :].astype(jnp.float32) + norm_recv[at, :].astype(jnp.float32)
        hidden = second[at, :]
        inverse = inverse_two[at, :][:, :1]
        e_two = d_norm * feed_gain_ref[...]
        g_feed_gain_ref[...] += jnp.sum(d_norm * hidden * inverse, axis=0, keepdims=True)
        cross = jnp.sum(e_two * hidden, axis=1, keepdims=True) / width
        d_hidden = (
            cotangent_ref[at, :].astype(jnp.float32)
            + inverse * e_two
            - hidden * (inverse * inverse * inverse * cross)
        )
        d_second_ref[at, :] = d_hidden
        low = d_hidden.astype(jnp.bfloat16)
        d_mix[at, :] = low
        d_attention_ref[at, :] = matmul(low, attention_out_ref[...])
        d_gated_now = matmul(low, mamba_output_ref[...])
        d_gated[at, :] = d_gated_now
        six = g_six[at, :]
        g_mamba_gain_ref[...] += jnp.sum(
            d_gated_now * six * inverse_six[at, :][:, :1], axis=0, keepdims=True
        )
        cross_send[at, :] = jnp.broadcast_to(
            jnp.sum(d_gated_now * mamba_gain_ref[...] * six, axis=1, keepdims=True), (FEED_TILE, LANES)
        )
        swap(cross_send, cross_recv, sem_cross, i).start()

    each(tiles, norm_tile)

    def gate_back(i):
        at = feed_rows(i)
        swap(cross_send, cross_recv, sem_cross, i).wait()
        cross = (cross_send[at, :] + cross_recv[at, :])[:, :1] / all_inner
        inverse = inverse_six[at, :][:, :1]
        d_six = inverse * (d_gated[at, :] * mamba_gain_ref[...]) - g_six[at, :] * (
            inverse * inverse * inverse * cross
        )
        gate_now = gate_z_ref[at, :]
        sig = sigmoid(gate_now)
        d_y_ref[at, :] = d_six * gate_now * sig
        d_gate_z_ref[at, :] = (
            d_six * y_ref[at, :] * (sig * (1.0 + gate_now * (1.0 - sig)))
        ).astype(jnp.bfloat16)

    each(tiles, gate_back)

    def out_tile(i):
        at = feed_rows(i)
        swap(lift_send, lift_recv, sem_lift, i).wait()
        total = lift_send[at, :].astype(jnp.float32) + lift_recv[at, :].astype(jnp.float32)
        out_ref[at, :] = (second[at, :] + total).astype(jnp.bfloat16)

    each(tiles, out_tile)

    def weight_block(k):
        block = pl.ds(pl.multiple_of(k * 256, 256), 256)
        g_down_ref[block, :] = matmul_first(cotangent_ref[:, block], active[...]).astype(
            jnp.bfloat16
        )
        g_feed_ref[block, :] = matmul_first(normed2[:, block], d_feed[...]).astype(jnp.bfloat16)
        g_gate_ref[block, :] = matmul_first(normed[:, block], d_gate_z_ref[...]).astype(
            jnp.bfloat16
        )
        d_mix_now = d_mix[:, block]
        g_mixed_ref[block, :inner] = matmul_first(d_mix_now, gated[...]).astype(jnp.bfloat16)
        g_mixed_ref[block, inner:] = matmul_first(d_mix_now, attention_ref[...]).astype(
            jnp.bfloat16
        )

    each(width // 256, weight_block)


def feed_layer(
    y,
    gate_z,
    attention_low,
    tokens,
    cotangent,
    mixer_gain,
    mamba_gain,
    feed_gain,
    mamba_output,
    attention_out,
    gate_weight,
    lift_weight,
    down_weight,
):
    rows, inner = y.shape
    width = tokens.shape[1]
    feed = gate_weight.shape[1]
    att = attention_low.shape[1]
    tiles = rows // FEED_TILE
    vmem = pl.BlockSpec(memory_space=pltpu.VMEM)
    hbm = pl.BlockSpec(memory_space=pl.ANY)
    low, full = jnp.bfloat16, jnp.float32
    shape = jax.ShapeDtypeStruct
    return pl.pallas_call(
        feed_kernel,
        out_shape=[
            shape((rows, width), low),
            shape((rows, width), full),
            shape((rows, inner), full),
            shape((rows, inner), low),
            shape((rows, att), full),
            shape((width, 2 * feed), low),
            shape((width, inner + att), low),
            shape((width, feed), low),
            shape((width, inner), low),
            shape((1, width), full),
            shape((1, inner), full),
        ],
        in_specs=[vmem] * 10 + [hbm] * 3,
        out_specs=[vmem] * 11,
        scratch_shapes=[
            pltpu.VMEM((width, feed), low),
            pltpu.VMEM((width, feed), low),
            pltpu.VMEM((width, feed), low),
            pltpu.VMEM((rows, width), low),
            pltpu.VMEM((rows, inner), low),
            pltpu.VMEM((rows, inner), full),
            pltpu.VMEM((rows, LANES), full),
            pltpu.VMEM((rows, width), full),
            pltpu.VMEM((rows, LANES), full),
            pltpu.VMEM((rows, width), low),
            pltpu.VMEM((rows, feed), low),
            pltpu.VMEM((rows, 2 * feed), low),
            pltpu.VMEM((rows, width), low),
            pltpu.VMEM((rows, inner), full),
            pltpu.VMEM((rows, LANES), full),
            pltpu.VMEM((rows, LANES), full),
            pltpu.VMEM((rows, LANES), full),
            pltpu.VMEM((rows, LANES), full),
        ]
        + [pltpu.VMEM((rows, width), low)] * 6
        + [pltpu.SemaphoreType.DMA((3,))]
        + [pltpu.SemaphoreType.DMA((2, tiles))] * 5,
        compiler_params=pltpu.CompilerParams(
            collective_id=1, has_side_effects=True, vmem_limit_bytes=60 << 20
        ),
        name="feed_layer",
    )(
        y,
        gate_z,
        attention_low,
        tokens,
        cotangent,
        mixer_gain[None],
        mamba_gain[None],
        feed_gain[None],
        mamba_output,
        attention_out,
        gate_weight,
        lift_weight,
        down_weight,
    )


CHUNK = 128
HALO = 8
PIECE = 256


def turn_half(values):
    lane = lax.broadcasted_iota(jnp.int32, values.shape, 1)
    return jnp.where(
        lax.rem(lane, HD) < HD // 2,
        pltpu.roll(values, LANES - HD // 2, 1),
        pltpu.roll(values, HD // 2, 1),
    )


def two_parts(values):
    high = values.astype(jnp.bfloat16)
    return high, (values - high.astype(jnp.float32)).astype(jnp.bfloat16)


def spread_heads(values, spread):
    high, rest = two_parts(values)
    return matmul(high, spread) + matmul(rest, spread)


def sum_heads(values, spread):
    high, rest = two_parts(values)
    return matmul_last(high, spread) + matmul_last(rest, spread)


def spread_matrix(inner, size):
    row = lax.broadcasted_iota(jnp.int32, (LANES, inner), 0)
    lane = lax.broadcasted_iota(jnp.int32, (LANES, inner), 1)
    return jnp.where(lane // size == row, 1.0, 0.0).astype(jnp.bfloat16)


def ordered(count):
    row = lax.broadcasted_iota(jnp.int32, (count, count), 0)
    lane = lax.broadcasted_iota(jnp.int32, (count, count), 1)
    return row >= lane


def halves(values, size):
    lane = lax.broadcasted_iota(jnp.int32, values.shape, 1)
    return jnp.concatenate(
        [jnp.where(lane < size, values, 0.0), jnp.where(lane < size, 0.0, values)], axis=0
    ).astype(jnp.bfloat16)


def soft_plus(v):
    return jnp.maximum(v, 0.0) + jnp.log1p(jnp.exp(-jnp.abs(v)))


def chunk_flags(seg_ref, c):
    window = seg_ref[pl.ds(pl.multiple_of(c * CHUNK, CHUNK), CHUNK + HALO), :]
    own = window[HALO:]
    start = jnp.where(own == window[HALO - 1 : HALO], 1.0, 0.0)
    end = jnp.where(own == own[CHUNK - 1 :], 1.0, 0.0)
    return own, start, end


def greet_seq(barrier, with_peer):
    seq, head, batch = lax.axis_index("seq"), lax.axis_index("head"), lax.axis_index("batch")
    count = lax.axis_size("seq")

    def one(step, carry):
        pl.semaphore_signal(
            barrier,
            inc=1,
            device_id=(lax.rem(seq + step, count), head, batch),
            device_id_type=MESH,
        )
        return carry

    lax.fori_loop(1, count, one, 0)
    if with_peer:
        pl.semaphore_signal(barrier, inc=1, device_id=peer_device(), device_id_type=MESH)
    pl.semaphore_wait(barrier, count - 1 + with_peer)


def mixer_kernel(
    tokens_ref,
    gain_ref,
    seg_ref,
    table_ref,
    gate_weight,
    input_weight,
    maps_weight,
    step_weight,
    query_weight,
    memory_weight,
    taps_ref,
    bias_ref,
    rate_ref,
    skip_ref,
    gate_z_ref,
    pre_ref,
    conv_ref,
    raw_ref,
    cum_ref,
    y_ref,
    states_ref,
    query_ref,
    memory_ref,
    normed,
    spread_ref,
    act,
    scaled,
    added,
    decay,
    total,
    local,
    state,
    chain_out,
    chain_in,
    sem_memory,
    sem_halo,
    sem_chain,
):
    seq, head, batch = lax.axis_index("seq"), lax.axis_index("head"), lax.axis_index("batch")
    count = lax.axis_size("seq")
    rows = tokens_ref.shape[0]
    tiles = rows // CHUNK
    inner = y_ref.shape[1]
    width = pre_ref.shape[1]
    state_width = (width - inner) // 2
    following = (lax.rem(seq + 1, count), head, batch)
    greet_seq(pltpu.get_barrier_semaphore(), 0)

    def memory_copy(step, place, owner):
        return exchange(
            memory_ref.at[owner],
            memory_ref.at[owner],
            sem_memory.at[0, step],
            sem_memory.at[1, step],
            (place, head, batch),
        )

    halo_copy = exchange(
        pre_ref.at[pl.ds(rows, HALO)],
        pre_ref.at[pl.ds(0, HALO)],
        sem_halo.at[0],
        sem_halo.at[1],
        following,
    )

    def memory_tile(i):
        at = tile_rows(i)
        hidden = tokens_ref[at, :].astype(jnp.float32)
        inverse = lax.rsqrt(jnp.mean(hidden * hidden, axis=1, keepdims=True) + eps_norm)
        low = (hidden * inverse * gain_ref[...]).astype(jnp.bfloat16)
        normed[at, :] = low
        value = matmul(low, memory_weight[...])
        lane = lax.broadcasted_iota(jnp.int32, value.shape, 1)
        turned = value * table_ref[at, :LANES] + turn_half(value) * table_ref[at, LANES:]
        memory_ref[seq, at, :] = jnp.where(lane < HD, turned, value).astype(jnp.bfloat16)

    each(tiles, memory_tile)

    def memory_start(step, carry):
        @pl.when(seq + step < count)
        def _():
            memory_copy(step, lax.rem(seq + step, count), seq).start()

        return carry

    lax.fori_loop(1, count, memory_start, 0)

    def pre_tile(i):
        at = tile_rows(i)
        to = pl.ds(pl.multiple_of(i * TILE + HALO, HALO), TILE)
        low = normed[at, :]
        pre_ref[to, :inner] = matmul(low, input_weight[...])
        pre_ref[to, inner:] = matmul(low, maps_weight[...])

    each(tiles, lambda i: pre_tile(tiles - 1 - i))

    @pl.when(seq < count - 1)
    def _():
        halo_copy.start()

    spread_ref[...] = spread_matrix(inner, HD)
    lower = jnp.where(ordered(CHUNK), 1.0, 0.0)

    def project_tile(i):
        at = tile_rows(i)
        low = normed[at, :]
        gate_z_ref[at, :] = matmul(low, gate_weight[...])
        raw = matmul(low, step_weight[...]) + bias_ref[...]
        raw_ref[at, :] = raw
        cum_ref[at, :] = jnp.dot(
            lower, rate_ref[...] * soft_plus(raw), precision=highest
        )
        value = matmul(low, query_weight[...])
        for k in range(value.shape[1] // LANES):
            part = value[:, k * LANES : (k + 1) * LANES]
            turned = part * table_ref[at, :LANES] + turn_half(part) * table_ref[at, LANES:]
            query_ref[at, k * LANES : (k + 1) * LANES] = turned.astype(jnp.bfloat16)

    each(tiles, project_tile)

    @pl.when(seq == 0)
    def _():
        pre_ref[:HALO, :] = jnp.zeros((HALO, width), jnp.float32)

    @pl.when(seq > 0)
    def _():
        halo_copy.wait_recv()

    def conv_tile(i):
        at = tile_rows(i)
        window_at = pl.ds(pl.multiple_of(i * TILE, TILE), TILE + HALO)
        seg = seg_ref[window_at, :]
        own = seg[HALO:]
        masks = [
            jnp.where(seg[HALO - 3 + k : HALO - 3 + k + TILE] == own, 1.0, 0.0) for k in range(3)
        ]
        for j in range(width // LANES):
            columns = slice(j * LANES, (j + 1) * LANES)
            window = pre_ref[window_at, columns]
            summed = taps_ref[3:4, columns] * window[HALO:]
            for k in range(3):
                summed = summed + taps_ref[k : k + 1, columns] * (
                    window[HALO - 3 + k : HALO - 3 + k + TILE] * masks[k]
                )
            conv_ref[at, columns] = summed
            act[at, columns] = summed * sigmoid(summed)

    each(tiles, conv_tile)
    local[...] = jnp.zeros_like(local)
    total[...] = jnp.ones_like(total)

    def input_map(at):
        return act[at, inner : inner + state_width].astype(jnp.bfloat16)

    def output_map(at):
        return act[at, inner + state_width :].astype(jnp.bfloat16)

    def local_chunk(c):
        at = tile_rows(c)
        _, start, end = chunk_flags(seg_ref, c)
        cum = cum_ref[at, :]
        last = cum[CHUNK - 1 :]
        spread = spread_ref[...]
        value = act[at, :inner] * spread_heads(soft_plus(raw_ref[at, :]), spread)
        scaled[at, :] = value.astype(jnp.bfloat16)
        weight = spread_heads(jnp.exp(last - cum) * end, spread)
        fresh = matmul_first(input_map(at), (value * weight).astype(jnp.bfloat16))
        keep = jnp.broadcast_to(jnp.exp(last) * start[CHUNK - 1 :], (HALO, LANES))
        keep = spread_heads(keep, spread)
        added[c] = fresh
        decay[c] = keep
        local[...] = local[...] * keep[:1] + fresh
        total[...] = total[...] * keep

    each(tiles, local_chunk)
    pieces = inner // PIECE

    def chain_copy(p):
        columns = pl.ds(p * PIECE, PIECE)
        return exchange(
            chain_out.at[:, columns],
            chain_in.at[:, columns],
            sem_chain.at[0, p],
            sem_chain.at[1, p],
            following,
        )

    @pl.when(seq == 0)
    def _():
        state[...] = jnp.zeros_like(state)
        chain_out[...] = local[...].astype(jnp.bfloat16)
        if count > 1:
            for p in range(pieces):
                chain_copy(p).start()

    def inside_chunk(c):
        at = tile_rows(c)
        own, _, _ = chunk_flags(seg_ref, c)
        cum = cum_ref[at, :]
        turned = cum.T
        meet = matmul_last(output_map(at), input_map(at))
        meet = jnp.where(ordered(CHUNK) & (own == own.T), meet, 0.0)
        for i in range(inner // LANES):
            columns = slice(i * LANES, (i + 1) * LANES)
            mixing = []
            for h in (2 * i, 2 * i + 1):
                gap = cum[:, h : h + 1] - turned[h : h + 1, :]
                mixing.append(meet * jnp.exp(jnp.minimum(gap, 0.0)))
            y_ref[at, columns] = matmul(
                jnp.concatenate(mixing, axis=1).astype(jnp.bfloat16),
                halves(scaled[at, columns].astype(jnp.float32), HD),
            )

    each(tiles, inside_chunk)

    @pl.when(seq > 0)
    def _():
        for p in range(pieces):
            columns = pl.ds(p * PIECE, PIECE)
            chain_copy(p).wait_recv()
            came = chain_in[:, columns].astype(jnp.float32)
            state[:, columns] = came

            @pl.when(seq < count - 1)
            def _():
                chain_out[:, columns] = (
                    came * total[:1, columns] + local[:, columns]
                ).astype(jnp.bfloat16)
                chain_copy(p).start()

    def across_chunk(c):
        at = tile_rows(c)
        _, start, _ = chunk_flags(seg_ref, c)
        now = state[...]
        low = now.astype(jnp.bfloat16)
        states_ref[c] = low
        carried = spread_heads(jnp.exp(cum_ref[at, :]) * start, spread_ref[...])
        y_ref[at, :] += matmul(output_map(at), low) * carried + skip_ref[...] * act[at, :inner]
        state[...] = now * decay[c][:1] + added[c]

    each(tiles, across_chunk)
    states_ref[tiles] = state[...].astype(jnp.bfloat16)

    def memory_wait(step, carry):
        @pl.when(seq + step < count)
        def _():
            memory_copy(step, lax.rem(seq + step, count), seq).wait_send()
            memory_ref[lax.rem(seq + step, count)] = jnp.zeros(memory_ref.shape[1:], jnp.bfloat16)

        @pl.when(seq - step >= 0)
        def _():
            memory_copy(step, seq, lax.rem(seq - step + count, count)).wait_recv()

        return carry

    lax.fori_loop(1, count, memory_wait, 0)

    @pl.when(seq < count - 1)
    def _():
        halo_copy.wait_send()
        for p in range(pieces):
            chain_copy(p).wait_send()


def mixer_forward(
    tokens,
    mixer_gain,
    segments,
    table,
    mamba_gate,
    mamba_input,
    mamba_maps,
    step_weight,
    query_weight,
    memory_weight,
    taps,
    bias,
    rate,
    skip,
):
    rows, width = tokens.shape
    count = lax.axis_size("seq")
    inner = mamba_gate.shape[1]
    conv_width = taps.shape[1]
    state_width = (conv_width - inner) // 2
    query = query_weight.shape[1]
    chunks = rows // CHUNK
    pieces = inner // PIECE
    vmem = pl.BlockSpec(memory_space=pltpu.VMEM)
    low, full = jnp.bfloat16, jnp.float32
    shape = jax.ShapeDtypeStruct
    return pl.pallas_call(
        mixer_kernel,
        out_shape=[
            shape((rows, inner), full),
            shape((rows + HALO, conv_width), full),
            shape((rows, conv_width), full),
            shape((rows, LANES), full),
            shape((rows, LANES), full),
            shape((rows, inner), full),
            shape((chunks + 1, state_width, inner), low),
            shape((rows, query), low),
            shape((count, rows, memory_weight.shape[1]), low),
        ],
        in_specs=[vmem] * 14,
        out_specs=[vmem] * 9,
        scratch_shapes=[
            pltpu.VMEM((rows, width), low),
            pltpu.VMEM((LANES, inner), low),
            pltpu.VMEM((rows, conv_width), full),
            pltpu.VMEM((rows, inner), low),
            pltpu.VMEM((chunks, state_width, inner), full),
            pltpu.VMEM((chunks, HALO, inner), full),
            pltpu.VMEM((HALO, inner), full),
            pltpu.VMEM((state_width, inner), full),
            pltpu.VMEM((state_width, inner), full),
            pltpu.VMEM((state_width, inner), low),
            pltpu.VMEM((state_width, inner), low),
            pltpu.SemaphoreType.DMA((2, count)),
            pltpu.SemaphoreType.DMA((2,)),
            pltpu.SemaphoreType.DMA((2, pieces)),
        ],
        compiler_params=pltpu.CompilerParams(
            collective_id=2, has_side_effects=True, vmem_limit_bytes=60 << 20
        ),
        name="mixer_forward",
    )(
        tokens,
        mixer_gain,
        segments,
        table,
        mamba_gate,
        mamba_input,
        mamba_maps,
        step_weight,
        query_weight,
        memory_weight,
        taps,
        bias,
        rate,
        skip,
    )


KEY_TILE = 256


def stacked_heads(values, first, factor):
    lane = lax.broadcasted_iota(jnp.int32, (values.shape[0], LANES), 1)
    keep = (lane < HD) if first else (lane >= HD)
    parts = []
    for h in range(values.shape[1] // HD):
        tile = values[:, (h // 2) * LANES : (h // 2 + 1) * LANES].astype(jnp.float32)
        if (h % 2 == 0) != first:
            tile = pltpu.roll(tile, HD, 1)
        parts.append(jnp.where(keep, tile * factor, 0.0))
    return jnp.concatenate(parts, axis=0)


def unstacked_heads(turned, first):
    heads = turned.shape[1] // TILE
    blocks = [turned[:, h * TILE : (h + 1) * TILE].T for h in range(heads)]
    lane = lax.broadcasted_iota(jnp.int32, (TILE, LANES), 1)
    tiles = []
    for even, odd in zip(blocks[::2], blocks[1::2]):
        if first:
            odd = pltpu.roll(odd, HD, 1)
        else:
            even = pltpu.roll(even, HD, 1)
        tiles.append(jnp.where(lane < HD, even, odd))
    return tiles


def key_tile(seg_turned, key_seg_ref, first, i, k, heads):
    at = pl.ds(pl.multiple_of(k * KEY_TILE, KEY_TILE), KEY_TILE)
    place = k * KEY_TILE + lax.broadcasted_iota(jnp.int32, (KEY_TILE, TILE), 0)
    row = first + i * TILE + lax.broadcasted_iota(jnp.int32, (KEY_TILE, TILE), 1)
    allowed = jnp.where((place <= row) & (key_seg_ref[at, :] == seg_turned), 1.0, 0.0)
    return at, jnp.concatenate([allowed] * heads, axis=1) > 0.5


def query_segments(seg_ref, i):
    own = seg_ref[pl.ds(pl.multiple_of(i * TILE, TILE) + HALO, TILE), :].T
    return jnp.concatenate([own] * (KEY_TILE // TILE), axis=0)


def attend_block(first, low, high, i, queries_in, memory_of, seg_ref, key_seg_ref):
    heads = queries_in.shape[1] // HD
    turned = stacked_heads(queries_in, True, HD ** (-0.5)).T.astype(jnp.bfloat16)
    segs = query_segments(seg_ref, i)
    wide = heads * TILE

    def one(step, carry):
        most, total, acc = carry
        k = high - step
        at, allowed = key_tile(segs, key_seg_ref, first, i, k, heads)
        keys = memory_of(at)
        scores = jnp.where(allowed, matmul(keys, turned), neg_large)
        new = jnp.maximum(most, jnp.max(scores, axis=0, keepdims=True))
        weights = jnp.exp(scores - new)
        factor = jnp.exp(most - new)
        total = total * factor + jnp.sum(weights, axis=0, keepdims=True)
        acc = acc * factor + matmul_first(keys, weights.astype(jnp.bfloat16))
        return new, total, acc

    most, total, acc = lax.fori_loop(
        0,
        high - low + 1,
        one,
        (
            jnp.full((1, wide), neg_large, jnp.float32),
            jnp.zeros((1, wide), jnp.float32),
            jnp.zeros((LANES, wide), jnp.float32),
        ),
    )
    return acc / total, most + jnp.log(total)


def attend_back_block(
    first, low, high, i, queries_in, d_out, out, log, memory_of, seg_ref, key_seg_ref, grads
):
    heads = queries_in.shape[1] // HD
    queries = stacked_heads(queries_in, True, HD ** (-0.5))
    outer = stacked_heads(d_out, False, 1.0)
    queries_turned, outer_turned = queries.T.astype(jnp.bfloat16), outer.T.astype(jnp.bfloat16)
    queries, outer = queries.astype(jnp.bfloat16), outer.astype(jnp.bfloat16)
    segs = query_segments(seg_ref, i)
    row = lax.broadcasted_iota(jnp.int32, (HALO, heads * HD), 0)
    lane = lax.broadcasted_iota(jnp.int32, (HALO, heads * HD), 1)
    pick = jnp.where(lane // HD == row, 1.0, 0.0).astype(jnp.bfloat16)
    high_part, low_part = two_parts(d_out * out)
    deltas = matmul_last(pick, high_part) + matmul_last(pick, low_part)
    delta = jnp.concatenate([deltas[h : h + 1] for h in range(heads)], axis=1)

    def one(step, total):
        at, allowed = key_tile(segs, key_seg_ref, first, i, high - step, heads)
        keys = memory_of(at)
        weights = jnp.exp(matmul(keys, queries_turned) - log)
        weights = jnp.where(allowed, weights, 0.0)
        slope = (weights * (matmul(keys, outer_turned) - delta)).astype(jnp.bfloat16)
        grads[at, :] += matmul(slope, queries) + matmul(weights.astype(jnp.bfloat16), outer)
        return total + matmul_first(keys, slope)

    total = lax.fori_loop(
        0, high - low + 1, one, jnp.zeros((LANES, heads * TILE), jnp.float32)
    )
    return total * HD ** (-0.5)


def attention_kernel(
    first_ref,
    low_ref,
    high_ref,
    query_ref,
    memory_ref,
    seg_ref,
    key_seg_ref,
    out_ref,
    low_out_ref,
    log_ref,
):
    def block(i):
        at_rows = tile_rows(i)
        turned, log = attend_block(
            first_ref[0],
            low_ref[i],
            high_ref[i],
            i,
            query_ref[at_rows, :],
            lambda at: memory_ref[at, :],
            seg_ref,
            key_seg_ref,
        )
        for pair, tile in enumerate(unstacked_heads(turned, False)):
            columns = slice(pair * LANES, (pair + 1) * LANES)
            out_ref[at_rows, columns] = tile
            low_out_ref[at_rows, columns] = tile.astype(jnp.bfloat16)
        log_ref[i] = jnp.broadcast_to(log, log_ref.shape[1:])

    each(query_ref.shape[0] // TILE, block)


def attention_forward(spans, query, memory, segments, key_segments):
    rows, width = query.shape
    full = jnp.float32
    vmem = pl.BlockSpec(memory_space=pltpu.VMEM)
    return pl.pallas_call(
        attention_kernel,
        out_shape=[
            jax.ShapeDtypeStruct((rows, width), full),
            jax.ShapeDtypeStruct((rows, width), jnp.bfloat16),
            jax.ShapeDtypeStruct((rows // TILE, HALO, width // HD * TILE), full),
        ],
        in_specs=[pl.BlockSpec(memory_space=pltpu.SMEM)] * 3 + [vmem] * 4,
        out_specs=[vmem] * 3,
        compiler_params=pltpu.CompilerParams(vmem_limit_bytes=56 << 20),
        name="attention_forward",
    )(*spans, query, memory, segments, key_segments)


def attention_back_kernel(
    first_ref,
    low_ref,
    high_ref,
    query_ref,
    memory_ref,
    seg_ref,
    key_seg_ref,
    out_ref,
    log_ref,
    d_out_ref,
    table_ref,
    d_query_ref,
    d_memory_ref,
    grads,
):
    grads[...] = jnp.zeros_like(grads)

    def block(i):
        at = tile_rows(i)
        d_turned = attend_back_block(
            first_ref[0],
            low_ref[i],
            high_ref[i],
            i,
            query_ref[at, :],
            d_out_ref[at, :],
            out_ref[at, :],
            log_ref[i][:1],
            lambda key_at: memory_ref[key_at, :],
            seg_ref,
            key_seg_ref,
            grads,
        )
        for pair, tile in enumerate(unstacked_heads(d_turned, True)):
            turned = tile * table_ref[at, :LANES] - turn_half(tile) * table_ref[at, LANES:]
            d_query_ref[at, pair * LANES : (pair + 1) * LANES] = turned.astype(jnp.bfloat16)

    each(query_ref.shape[0] // TILE, block)
    d_memory_ref[...] = grads[...].astype(jnp.bfloat16)


def attention_back(spans, query, memory, segments, key_segments, out, logs, d_out, table):
    vmem = pl.BlockSpec(memory_space=pltpu.VMEM)
    return pl.pallas_call(
        attention_back_kernel,
        out_shape=[
            jax.ShapeDtypeStruct(query.shape, jnp.bfloat16),
            jax.ShapeDtypeStruct(memory.shape, jnp.bfloat16),
        ],
        in_specs=[pl.BlockSpec(memory_space=pltpu.SMEM)] * 3 + [vmem] * 8,
        out_specs=[vmem] * 2,
        scratch_shapes=[pltpu.VMEM(memory.shape, jnp.float32)],
        compiler_params=pltpu.CompilerParams(vmem_limit_bytes=56 << 20),
        name="attention_back",
    )(*spans, query, memory, segments, key_segments, out, logs, d_out, table)


def mixer_back_kernel(merged, chunks, *refs):
    refs = list(refs)

    def take(names):
        nonlocal refs
        now, refs = refs[: len(names)], refs[len(names) :]
        return now

    (
        tokens_ref,
        gain_ref,
        seg_ref,
        table_ref,
        gate_weight,
        input_weight,
        maps_weight,
        step_weight,
        query_weight,
        memory_weight,
        taps_ref,
        rate_ref,
        skip_ref,
        pre_ref,
        conv_ref,
        raw_ref,
        cum_ref,
        y_ref,
        states_ref,
        d_second_ref,
        d_y_ref,
        d_gate_z_ref,
    ) = take(range(22))
    if merged:
        (
            query_ref,
            memory_ref,
            key_seg_ref,
            attention_ref,
            logs_ref,
            d_attention_ref,
            feed_gain_ref,
            mamba_gain_ref,
        ) = take(range(8))
        early = take(range(4))
        d_tokens_ref, *outs, small_out = take(range(7))
    else:
        d_query_ref, d_memory_ref = take(range(2))
        d_tokens_ref, g_side_ref, g_taps_ref, g_gain_ref, g_heads_ref = take(range(5))
    (
        normed,
        spread_ref,
        act,
        d_conv,
        d_scaled,
        d_maps,
        row_term,
        added,
        local,
        total,
        state,
        skip_sum,
        side,
        chain_out,
        chain_in,
        maps_send,
        maps_recv,
        memory_recv,
        norm_send,
        norm_recv,
        sem_memory,
        sem_halo,
        sem_chain,
        sem_maps,
        sem_norm,
    ) = take(range(25))
    if merged:
        g_side_ref, grads, d_memory_ref, small_in, small_buf, sem_small = take(range(6))
        g_taps_ref = g_gain_ref = g_heads_ref = small_in
    seq, head, batch = lax.axis_index("seq"), lax.axis_index("head"), lax.axis_index("batch")
    count = lax.axis_size("seq")
    rows = tokens_ref.shape[0]
    tiles = rows // CHUNK
    inner = y_ref.shape[1]
    width = pre_ref.shape[1]
    state_width = (width - inner) // 2
    model = tokens_ref.shape[1]
    peer = peer_device()
    previous = (lax.rem(seq - 1 + count, count), head, batch)
    pieces = inner // PIECE
    step_at = width
    query_at = step_at + LANES
    memory_at = query_at + query_weight.shape[1]
    if merged:
        greet_all(pltpu.get_barrier_semaphore(), True)
        reduction = Reduction(chunks, list(early) + [g_side_ref], outs, refs)
        reduction.allow(sum(1 for c in chunks if c[0] < len(early)))
        advance = reduction.advance
    else:
        greet_seq(pltpu.get_barrier_semaphore(), 1)

        def advance():
            return None

    spread_ref[...] = spread_matrix(inner, HD)

    def chain_copy(p):
        columns = pl.ds(p * PIECE, PIECE)
        return exchange(
            chain_out.at[:, columns],
            chain_in.at[:, columns],
            sem_chain.at[0, p],
            sem_chain.at[1, p],
            previous,
        )

    def memory_copy(step):
        place = lax.rem(seq - step + count, count)
        return exchange(
            d_memory_ref.at[place],
            memory_recv.at[step - 1],
            sem_memory.at[0, step],
            sem_memory.at[1, step],
            (place, head, batch),
        )

    halo_copy = exchange(
        d_conv.at[pl.ds(0, HALO)],
        d_conv.at[pl.ds(rows, HALO)],
        sem_halo.at[0],
        sem_halo.at[1],
        previous,
    )
    maps_copy = exchange(maps_send, maps_recv, sem_maps.at[0], sem_maps.at[1], peer)

    def norm_copy(i):
        at = tile_rows(i)
        return exchange(
            norm_send.at[at], norm_recv.at[at], sem_norm.at[0, i], sem_norm.at[1, i], peer
        )

    def input_map(at):
        return act[at, inner : inner + state_width].astype(jnp.bfloat16)

    def output_map(at):
        return act[at, inner + state_width :].astype(jnp.bfloat16)

    def keep_of(c, start):
        last = cum_ref[tile_rows(c), :][CHUNK - 1 :]
        keep = jnp.broadcast_to(jnp.exp(last) * start[CHUNK - 1 :], (HALO, LANES))
        return spread_heads(keep, spread_ref[...])

    def carried_of(c, start):
        return spread_heads(jnp.exp(cum_ref[tile_rows(c), :]) * start, spread_ref[...])

    def activate(i):
        at = tile_rows(i)
        value = conv_ref[at, :]
        act[at, :] = value * sigmoid(value)

    each(tiles, activate)
    local[...] = jnp.zeros_like(local)
    total[...] = jnp.ones_like(total)

    def local_chunk(step):
        c = tiles - 1 - step
        at = tile_rows(c)
        _, start, _ = chunk_flags(seg_ref, c)
        keep = keep_of(c, start)
        value = (d_y_ref[at, :] * carried_of(c, start)).astype(jnp.bfloat16)
        fresh = matmul_first(output_map(at), value)
        added[c] = fresh
        local[...] = local[...] * keep[:1] + fresh
        total[...] = total[...] * keep

    each(tiles, local_chunk)

    @pl.when(seq == count - 1)
    def _():
        state[...] = jnp.zeros_like(state)
        chain_out[...] = local[...].astype(jnp.bfloat16)
        if count > 1:
            for p in range(pieces):
                chain_copy(p).start()

    if merged:
        first = seq * rows
        grads[...] = jnp.zeros_like(grads)

        def attention_block(i):
            at = tile_rows(i)
            d_turned = attend_back_block(
                first,
                0,
                (first + i * TILE + TILE - 1) // KEY_TILE,
                i,
                query_ref[at, :],
                d_attention_ref[at, :],
                attention_ref[at, :],
                logs_ref[i][:1],
                lambda key_at: memory_ref[key_at, :],
                seg_ref,
                key_seg_ref,
                grads,
            )
            for pair, tile in enumerate(unstacked_heads(d_turned, True)):
                turned = tile * table_ref[at, :LANES] - turn_half(tile) * table_ref[at, LANES:]
                columns = pl.ds(query_at + pair * LANES, LANES)
                side[at, columns] = turned.astype(jnp.bfloat16)

        half = tiles // 2
        span(0, half, attention_block)
        advance()
        span(half, tiles, attention_block)
        advance()

        def low_block(place):
            at = pl.ds(pl.multiple_of(place * rows, rows), rows)
            d_memory_ref[place] = grads[at, :].astype(jnp.bfloat16)

        each(count, low_block)

    def chain_wait(p):
        columns = pl.ds(p * PIECE, PIECE)
        chain_copy(p).wait_recv()
        came = chain_in[:, columns].astype(jnp.float32)
        state[:, columns] = came
        return came

    @pl.when((seq > 0) & (seq < count - 1))
    def _():
        for p in range(pieces):
            columns = pl.ds(p * PIECE, PIECE)
            came = chain_wait(p)
            chain_out[:, columns] = (came * total[:1, columns] + local[:, columns]).astype(
                jnp.bfloat16
            )
            chain_copy(p).start()

    def memory_start(step, carry):
        @pl.when(seq - step >= 0)
        def _():
            memory_copy(step).start()

        return carry

    lax.fori_loop(1, count, memory_start, 0)
    skip_sum[...] = jnp.zeros_like(skip_sum)

    def inside_chunk(c):
        at = tile_rows(c)
        own, start, _ = chunk_flags(seg_ref, c)
        cum = cum_ref[at, :]
        turned = cum.T
        spread = spread_ref[...]
        low_in, low_out = input_map(at), output_map(at)
        allowed = ordered(CHUNK).astype(jnp.float32).T * jnp.where(own == own.T, 1.0, 0.0)
        meet = matmul_last(low_in, low_out) * allowed
        value = act[at, :inner]
        scaled = value * spread_heads(soft_plus(raw_ref[at, :]), spread)
        d_y = d_y_ref[at, :]
        d_meet = jnp.zeros((CHUNK, CHUNK), jnp.float32)
        for i in range(inner // LANES):
            columns = slice(i * LANES, (i + 1) * LANES)
            d_tile = d_y[:, columns]
            d_mixing = matmul_last(halves(scaled[:, columns], HD), d_tile.astype(jnp.bfloat16))
            mixing = []
            for k, h in enumerate((2 * i, 2 * i + 1)):
                gap = turned[h : h + 1, :] - cum[:, h : h + 1]
                fade = jnp.exp(jnp.minimum(gap, 0.0))
                mixing.append(meet * fade)
                d_meet = d_meet + d_mixing[k * CHUNK : (k + 1) * CHUNK] * fade
            d_scaled[at, columns] = matmul(
                jnp.concatenate(mixing, axis=1).astype(jnp.bfloat16), halves(d_tile, HD)
            )
        d_meet = (d_meet * allowed).astype(jnp.bfloat16)
        d_maps[at, :state_width] = matmul(d_meet, low_out)
        carried = (d_y * carried_of(c, start)).astype(jnp.bfloat16)
        d_maps[at, state_width:] = matmul_first(d_meet, low_in) + matmul_last(
            carried, states_ref[c]
        )
        product = d_y * value
        skip_sum[...] += jnp.sum(product, axis=0, keepdims=True)
        low = d_y.astype(jnp.bfloat16).astype(jnp.float32)
        row_term[at, :] = sum_heads(low * (y_ref[at, :] - skip_ref[...] * value), spread)

    span(0, tiles // 2, inside_chunk)
    advance()
    span(tiles // 2, tiles, inside_chunk)
    advance()

    @pl.when((seq == 0) & (seq < count - 1))
    def _():
        for p in range(pieces):
            chain_wait(p)

    if merged:
        small_in[...] = jnp.zeros_like(small_in)
        small_in[4:5, :inner] = mamba_gain_ref[...]
        small_in[6:7, :] = feed_gain_ref[...]
    else:
        g_heads_ref[...] = jnp.zeros_like(g_heads_ref)

    gain_row = 5 if merged else 0

    def add_heads(k, values):
        row, lane = (7, k * LANES) if merged else (k, 0)
        g_heads_ref[row : row + 1, lane : lane + LANES] += values

    upper = jnp.where(ordered(CHUNK), 1.0, 0.0).T

    def across_chunk(step):
        c = tiles - 1 - step
        at = tile_rows(c)
        _, start, end = chunk_flags(seg_ref, c)
        spread = spread_ref[...]
        cum = cum_ref[at, :]
        last = cum[CHUNK - 1 :]
        now = state[...]
        low = now.astype(jnp.bfloat16)
        raw = raw_ref[at, :]
        steps = soft_plus(raw)
        steps_wide = spread_heads(steps, spread)
        value = act[at, :inner]
        scaled = value * steps_wide
        weight = spread_heads(jnp.exp(last - cum) * end, spread)
        d_value = d_scaled[at, :] + matmul(input_map(at), low) * weight
        d_maps[at, :state_width] += matmul_last((scaled * weight).astype(jnp.bfloat16), low)
        final = jnp.sum(
            states_ref[c + 1].astype(jnp.float32) * low.astype(jnp.float32), axis=0, keepdims=True
        )
        final = sum_heads(jnp.broadcast_to(final, (HALO, inner)), spread)[:1]
        low_scaled = scaled.astype(jnp.bfloat16).astype(jnp.float32)
        d_cum = row_term[at, :] - sum_heads(low_scaled * d_value, spread)
        d_rate = jnp.dot(upper, d_cum, precision=highest) + final
        rate = rate_ref[...]
        d_steps = sum_heads(value * d_value, spread) + rate * d_rate
        d_raw = d_steps * sigmoid(raw)
        add_heads(0, rate * jnp.sum(steps * d_rate, axis=0, keepdims=True))
        add_heads(1, jnp.sum(d_raw, axis=0, keepdims=True))
        side[at, step_at:query_at] = d_raw.astype(jnp.bfloat16)
        d_conv[at, :inner] = steps_wide * d_value + skip_ref[...] * d_y_ref[at, :]
        state[...] = now * keep_of(c, start)[:1] + added[c]

    span(0, tiles // 2, across_chunk)
    advance()
    span(tiles // 2, tiles, across_chunk)
    advance()
    add_heads(2, sum_heads(jnp.broadcast_to(skip_sum[:1], (HALO, inner)), spread_ref[...])[:1])
    maps_send[...] = d_maps[...].astype(jnp.bfloat16)
    maps_copy.start()

    def copy_tile(i):
        at = tile_rows(i)
        hidden = tokens_ref[at, :].astype(jnp.float32)
        inverse = lax.rsqrt(jnp.mean(hidden * hidden, axis=1, keepdims=True) + eps_norm)
        normed[at, :] = (hidden * inverse * gain_ref[...]).astype(jnp.bfloat16)

    each(tiles, copy_tile)
    maps_copy.wait()

    def conv_back_tile(i):
        at = tile_rows(i)
        d_conv[at, inner:] = maps_send[at, :].astype(jnp.float32) + maps_recv[at, :].astype(
            jnp.float32
        )
        value = conv_ref[at, :]
        sig = sigmoid(value)
        d_conv[at, :] = d_conv[at, :] * (sig * (1.0 + value * (1.0 - sig)))

    each(tiles, conv_back_tile)

    @pl.when(seq > 0)
    def _():
        halo_copy.start()

    @pl.when(seq == count - 1)
    def _():
        d_conv[pl.ds(rows, HALO), :] = jnp.zeros((HALO, width), jnp.float32)

    @pl.when(seq < count - 1)
    def _():
        halo_copy.wait_recv()

    if not merged:
        g_taps_ref[...] = jnp.zeros_like(g_taps_ref)

    def taps_tile(i):
        at = tile_rows(i)
        window_at = pl.ds(pl.multiple_of(i * TILE, TILE), TILE + HALO)
        seg = seg_ref[pl.ds(pl.multiple_of(i * TILE, TILE), TILE + 2 * HALO), :]
        own = seg[HALO : HALO + TILE]
        before = [
            jnp.where(seg[HALO - 3 + k : HALO - 3 + k + TILE] == own, 1.0, 0.0) for k in range(3)
        ]
        after = [
            jnp.where(seg[HALO + 3 - k : HALO + 3 - k + TILE] == own, 1.0, 0.0) for k in range(3)
        ]
        for j in range(width // LANES):
            columns = slice(j * LANES, (j + 1) * LANES)
            window = pre_ref[window_at, columns]
            grads = d_conv[window_at, columns]
            own_grad = grads[:TILE]
            summed = taps_ref[3:4, columns] * own_grad
            g_taps_ref[3:4, columns] += jnp.sum(own_grad * window[HALO:], axis=0, keepdims=True)
            for k in range(3):
                summed = summed + taps_ref[k : k + 1, columns] * (
                    grads[3 - k : 3 - k + TILE] * after[k]
                )
                g_taps_ref[k : k + 1, columns] += jnp.sum(
                    own_grad * (window[HALO - 3 + k : HALO - 3 + k + TILE] * before[k]),
                    axis=0,
                    keepdims=True,
                )
            side[at, j * LANES : (j + 1) * LANES] = summed.astype(jnp.bfloat16)

    each(tiles, taps_tile)
    advance()

    def memory_wait(step, carry):
        @pl.when(seq - step >= 0)
        def _():
            memory_copy(step).wait_send()

        @pl.when(seq + step < count)
        def _():
            memory_copy(step).wait_recv()

        return carry

    lax.fori_loop(1, count, memory_wait, 0)

    def memory_tile(i):
        at = tile_rows(i)

        def one(step, carry):
            came = memory_recv[step - 1, at, :].astype(jnp.float32)
            return carry + jnp.where(seq + step < count, came, 0.0)

        grad = lax.fori_loop(1, count, one, d_memory_ref[seq, at, :].astype(jnp.float32))
        lane = lax.broadcasted_iota(jnp.int32, grad.shape, 1)
        turned = grad * table_ref[at, :LANES] - turn_half(grad) * table_ref[at, LANES:]
        side[at, memory_at : memory_at + LANES] = jnp.where(lane < HD, turned, grad).astype(
            jnp.bfloat16
        )
        if not merged:
            side[at, query_at:memory_at] = d_query_ref[at, :]

    each(tiles, memory_tile)

    def weight_block(k):
        block = pl.ds(pl.multiple_of(k * 256, 256), 256)
        grad = matmul_first(normed[:, block], side[...])
        if merged:
            _, high, low, own, columns = g_side_ref.shape
            parts = 256 // (high * low * own)
            g_side_ref[pl.ds(k * parts, parts)] = grad.reshape(
                parts, high, low, own, columns
            ).astype(jnp.bfloat16)
        else:
            g_side_ref[block, :] = grad.astype(jnp.bfloat16)

    each(model // 256, weight_block)
    if merged:
        reduction.allow(len(chunks))
    advance()

    def norm_tile(i):
        at = tile_rows(i)
        part = (
            matmul_last(d_gate_z_ref[at, :], gate_weight[...])
            + matmul_last(side[at, :inner], input_weight[...])
            + matmul_last(side[at, inner:step_at], maps_weight[...]) / lax.axis_size("head")
            + matmul_last(side[at, step_at:query_at], step_weight[...])
            + matmul_last(side[at, query_at:memory_at], query_weight[...])
            + matmul_last(side[at, memory_at:], memory_weight[...])
        )
        norm_send[at, :] = part.astype(jnp.bfloat16)
        norm_copy(i).start()

    each(tiles, norm_tile)

    advance()
    if not merged:
        g_gain_ref[...] = jnp.zeros_like(g_gain_ref)

    def last_tile(i):
        at = tile_rows(i)
        norm_copy(i).wait()
        d_norm = norm_send[at, :].astype(jnp.float32) + norm_recv[at, :].astype(jnp.float32)
        hidden = tokens_ref[at, :].astype(jnp.float32)
        inverse = lax.rsqrt(jnp.mean(hidden * hidden, axis=1, keepdims=True) + eps_norm)
        e_one = d_norm * gain_ref[...]
        cross = jnp.sum(e_one * hidden, axis=1, keepdims=True) / model
        d_tokens_ref[at, :] = (
            d_second_ref[at, :] + inverse * e_one - hidden * (inverse * inverse * inverse * cross)
        )
        g_gain_ref[gain_row : gain_row + 1, :] += jnp.sum(
            d_norm * hidden * inverse, axis=0, keepdims=True
        )

    each(tiles, last_tile)
    if merged:
        small_sum = SmallSum(small_in, small_buf, sem_small)
        small_sum.start()
        reduction.finish()
        small_out[...] = small_sum.finish()

    @pl.when(seq > 0)
    def _():
        halo_copy.wait_send()
        for p in range(pieces):
            chain_copy(p).wait_send()


def mixer_back(common, saved, attention=None, grads=None):
    tokens = common[0]
    rows, model = tokens.shape
    gate_weight, query_weight, memory_weight, taps = common[4], common[8], common[9], common[10]
    merged = grads is not None
    count = lax.axis_size("seq")
    inner = gate_weight.shape[1]
    width = taps.shape[1]
    state_width = (width - inner) // 2
    tiles = rows // CHUNK
    pieces = inner // PIECE
    memory_width = memory_weight.shape[1]
    side = width + LANES + query_weight.shape[1] + memory_width
    vmem = pl.BlockSpec(memory_space=pltpu.VMEM)
    hbm = pl.BlockSpec(memory_space=pl.ANY)
    low, full = jnp.bfloat16, jnp.float32
    shape = jax.ShapeDtypeStruct
    operands = [*common, *saved]
    in_specs = [vmem] * (len(operands) + len(attention))
    operands += attention
    chunks = None
    scratch = [
        pltpu.VMEM((rows, model), low),
        pltpu.VMEM((LANES, inner), low),
        pltpu.VMEM((rows, width), full),
        pltpu.VMEM((rows + HALO, width), full),
        pltpu.VMEM((rows, inner), full),
        pltpu.VMEM((rows, 2 * state_width), full),
        pltpu.VMEM((rows, LANES), full),
        pltpu.VMEM((tiles, state_width, inner), full),
        pltpu.VMEM((state_width, inner), full),
        pltpu.VMEM((HALO, inner), full),
        pltpu.VMEM((state_width, inner), full),
        pltpu.VMEM((1, inner), full),
        pltpu.VMEM((rows, side), low),
        pltpu.VMEM((state_width, inner), low),
        pltpu.VMEM((state_width, inner), low),
        pltpu.VMEM((rows, 2 * state_width), low),
        pltpu.VMEM((rows, 2 * state_width), low),
        pltpu.VMEM((max(count - 1, 1), rows, memory_width), low),
        pltpu.VMEM((rows, model), low),
        pltpu.VMEM((rows, model), low),
        pltpu.SemaphoreType.DMA((2, count)),
        pltpu.SemaphoreType.DMA((2,)),
        pltpu.SemaphoreType.DMA((2, pieces)),
        pltpu.SemaphoreType.DMA((2,)),
        pltpu.SemaphoreType.DMA((2, tiles)),
    ]
    if merged:
        blocks = [seq_blocks(g) for g in grads]
        widths = [g.shape[1] for g in grads] + [side]
        chunks = column_chunks(widths)
        operands += blocks
        in_specs += [hbm] * len(blocks)
        own = blocks[0].shape[3]
        small = (HALO, model)
        out_shape = (
            [shape((rows, model), full)]
            + [shape((2, 2, own, w), low) for w in widths]
            + [shape(small, full)]
        )
        scratch += [
            pltpu.VMEM(blocks[0].shape[:4] + (side,), low),
            pltpu.VMEM((count * rows, memory_width), full),
            pltpu.VMEM((count, rows, memory_width), low),
        ]
        scratch += small_scratch(small) + reduction_scratch(chunks, widths, own)
    else:
        out_shape = [
            shape((rows, model), full),
            shape((model, side), low),
            shape((HALO, width), full),
            shape((1, model), full),
            shape((HALO, LANES), full),
        ]
    return pl.pallas_call(
        functools.partial(mixer_back_kernel, merged, chunks),
        out_shape=out_shape,
        in_specs=in_specs,
        out_specs=[vmem] * len(out_shape),
        scratch_shapes=scratch,
        compiler_params=pltpu.CompilerParams(
            collective_id=3, has_side_effects=True, vmem_limit_bytes=62 << 20
        ),
        name="mixer_back",
    )(*operands)


def finish_kernel(sizes, down, feed, mixed, gate, side, small, *outs):
    inner, maps, heads, query, own = sizes
    full = jnp.float32
    seq = lax.axis_index("seq")
    wide = small.shape[1]
    columns = [0, inner, inner + maps, inner + maps + heads]
    query_at = inner + maps + LANES
    (
        o_gate_z,
        o_inner,
        o_maps,
        o_step,
        o_output,
        o_query,
        o_memory,
        o_attention,
        o_gate,
        o_lift,
        o_down,
        o_conv_inner,
        o_conv_maps,
        o_mixer_gain,
        o_rate,
        o_bias,
        o_skip,
        o_mamba_gain,
        o_feed_gain,
    ) = outs
    o_gate_z[...] = gate[...].astype(full)
    o_inner[...] = side[:, : columns[1]].astype(full)
    o_maps[...] = side[:, columns[1] : columns[2]].astype(full)
    o_step[...] = side[:, columns[2] : columns[2] + LANES].astype(full)[:, :heads]
    o_query[...] = side[:, query_at : query_at + query].astype(full)
    o_memory[...] = side[:, query_at + query :].astype(full)
    o_output[...] = mixed[:, :inner].astype(full)
    o_attention[...] = mixed[:, inner:].astype(full)
    o_gate[...] = feed[:, : o_gate.shape[1]].astype(full)
    o_lift[...] = feed[:, o_gate.shape[1] :].astype(full)
    o_down[...] = down[...].astype(full)
    value = small[...]
    o_conv_inner[...] = value[:4, :inner]
    o_conv_maps[...] = value[:4, inner:]
    turned = pltpu.roll(value, lax.rem(wide - seq * own, wide), 1)
    o_mixer_gain[...] = turned[5:6, :own]
    o_feed_gain[...] = turned[6:7, :own]
    for k, out in enumerate((o_rate, o_bias, o_skip)):
        out[...] = value[7:8, k * LANES : (k + 1) * LANES][:, :heads]
    o_mamba_gain[...] = value[4:5, :inner]


def finish_outputs(sums, small, sizes):
    inner, maps, heads, query, own = sizes
    rows = own
    sums = [s.reshape(rows, s.shape[-1]) for s in sums]
    down, feed, mixed, gate, side = sums
    half = feed.shape[1] // 2
    memory = side.shape[1] - inner - maps - LANES - query
    shapes = [
        (rows, inner),
        (rows, inner),
        (rows, maps),
        (rows, heads),
        (rows, inner),
        (rows, query),
        (rows, memory),
        (rows, mixed.shape[1] - inner),
        (rows, half),
        (rows, half),
        (rows, half),
        (4, inner),
        (4, maps),
        (1, own),
        (1, heads),
        (1, heads),
        (1, heads),
        (1, inner),
        (1, own),
    ]
    vmem = pl.BlockSpec(memory_space=pltpu.VMEM)
    return pl.pallas_call(
        functools.partial(finish_kernel, sizes),
        out_shape=[jax.ShapeDtypeStruct(s, jnp.float32) for s in shapes],
        in_specs=[vmem] * 6,
        out_specs=[vmem] * len(shapes),
        compiler_params=pltpu.CompilerParams(vmem_limit_bytes=32 << 20),
        name="finish_outputs",
    )(*sums, small)


def rotation_table(position):
    half = HD // 2
    lane = jnp.arange(LANES)
    inverse_freq = rope_base ** (-(lane % half).astype(jnp.float32) / half)
    angles = position.astype(jnp.float32)[:, None] * inverse_freq[None, :]
    sign = jnp.where(lane % HD < half, -1.0, 1.0)
    return jnp.concatenate([jnp.cos(angles), sign[None, :] * jnp.sin(angles)], axis=1)


def body(
    tokens,
    seg_ids,
    mixer_gain,
    mamba_gate,
    mamba_input,
    mamba_maps,
    mamba_step,
    conv_inner,
    conv_maps,
    log_rate,
    step_bias,
    skip_gain,
    mamba_gain,
    mamba_output,
    query_weight,
    memory_weight,
    attention_out,
    feed_gain,
    gate_weight,
    lift_weight,
    down_weight,
    cotangent,
):
    tokens, cotangent = tokens[0], cotangent[0]
    rows, wide = tokens.shape
    tap_count, inner = conv_inner.shape
    head_count = log_rate.shape[0]
    segments = seg_ids[0]
    offset = lax.axis_index("seq") * rows
    padded = jnp.concatenate(
        [jnp.full((HALO,), -1, jnp.int32), segments, jnp.full((HALO,), -2, jnp.int32)]
    )
    window = lax.dynamic_slice_in_dim(padded, offset, rows + 2 * HALO)
    window_wide = jnp.broadcast_to(
        window.astype(jnp.float32)[:, None], (rows + 2 * HALO, LANES)
    )
    key_segments = jnp.broadcast_to(
        segments.astype(jnp.float32)[:, None], (segments.shape[0], LANES)
    )
    table = rotation_table(offset + jnp.arange(rows, dtype=jnp.int32))
    starts = offset + jnp.arange(rows // TILE, dtype=jnp.int32) * TILE
    reach = segments[KEY_TILE - 1 :: KEY_TILE]
    low = jnp.sum(
        (reach[None, :] < window[HALO : HALO + rows : TILE][:, None]).astype(jnp.int32), axis=1
    )
    spans = (offset[None], low, (starts + TILE - 1) // KEY_TILE)

    def lanes_of(values):
        return jnp.pad(values, (0, LANES - head_count))[None]

    step_weight = jnp.pad(mamba_step, ((0, 0), (0, LANES - head_count)))
    taps = jnp.pad(
        jnp.concatenate([conv_inner, conv_maps], axis=1), ((0, HALO - tap_count), (0, 0))
    )
    bias, rate = lanes_of(step_bias), lanes_of(-jnp.exp(log_rate))
    skip = jnp.repeat(skip_gain, inner // head_count)[None]
    common = [
        tokens,
        mixer_gain[None],
        window_wide,
        table,
        mamba_gate,
        mamba_input,
        mamba_maps,
        step_weight,
        query_weight,
        memory_weight,
        taps,
    ]
    gate_z, pre, conv, raw, cum, y, states, query, memory = mixer_forward(
        *common, bias, rate, skip
    )
    all_memory = memory.reshape(memory.shape[0] * rows, memory.shape[2])
    attention, attention_low, logs = attention_forward(
        spans, query, all_memory, window_wide, key_segments
    )
    (
        layer_out,
        d_second,
        d_y,
        d_gate_z,
        d_attention,
        g_feed,
        g_mixed,
        g_down,
        g_gate,
        g_feed_gain,
        g_mamba_gain,
    ) = feed_layer(
        y,
        gate_z,
        attention_low,
        tokens,
        cotangent,
        mixer_gain,
        mamba_gain,
        feed_gain,
        mamba_output,
        attention_out,
        gate_weight,
        lift_weight,
        down_weight,
    )
    common += [rate, skip]
    saved = [pre, conv, raw, cum, y, states, d_second, d_y, d_gate_z]
    early = [g_down, g_feed, g_mixed, g_gate]
    if lax.axis_size("seq") <= 4:
        grad_tokens, *sums, small = mixer_back(
            common,
            saved,
            [
                query,
                all_memory,
                key_segments,
                attention,
                logs,
                d_attention,
                g_feed_gain,
                g_mamba_gain,
            ],
            early,
        )
    else:
        d_query, d_memory = attention_back(
            spans, query, all_memory, window_wide, key_segments, attention, logs, d_attention, table
        )
        grad_tokens, g_side, g_taps, g_mixer_gain, g_heads = mixer_back(
            common, saved, [d_query, d_memory.reshape(memory.shape)]
        )
        *sums, small = reduce_gradients(
            early + [g_side],
            jnp.concatenate(
                [
                    g_taps[:tap_count],
                    jnp.pad(g_mamba_gain, ((0, 0), (0, wide - inner))),
                    g_mixer_gain,
                    g_feed_gain,
                    jnp.pad(g_heads[:3].reshape(1, 3 * LANES), ((0, 0), (0, wide - 3 * LANES))),
                ],
                axis=0,
            ),
        )
    sizes = (
        inner,
        conv_maps.shape[1],
        head_count,
        query_weight.shape[1],
        wide // lax.axis_size("seq"),
    )
    (
        o_gate_z,
        o_inner,
        o_maps,
        o_step,
        o_output,
        o_query,
        o_memory,
        o_attention,
        o_gate,
        o_lift,
        o_down,
        o_conv_inner,
        o_conv_maps,
        o_mixer_gain,
        o_rate,
        o_bias,
        o_skip,
        o_mamba_gain,
        o_feed_gain,
    ) = finish_outputs(sums, small, sizes)
    return (
        layer_out[None],
        grad_tokens[None],
        o_mixer_gain[0],
        o_gate_z,
        o_inner,
        o_maps,
        o_step,
        o_conv_inner,
        o_conv_maps,
        o_rate[0],
        o_bias[0],
        o_skip[0],
        o_mamba_gain[0],
        o_output,
        o_query,
        o_memory,
        o_attention,
        o_feed_gain[0],
        o_gate,
        o_lift,
        o_down,
    )


def solution(mesh):
    return jax.shard_map(
        body,
        mesh=mesh,
        in_specs=(
            P("batch", "seq", None),
            P("batch", None),
            P(),
            P(None, "head"),
            P(None, "head"),
            P(),
            P(None, "head"),
            P(None, "head"),
            P(),
            P("head"),
            P("head"),
            P("head"),
            P("head"),
            P(None, "head"),
            P(None, "head"),
            P(None, "head"),
            P(None, "head"),
            P(),
            P(None, "head"),
            P(None, "head"),
            P(None, "head"),
            P("batch", "seq", None),
        ),
        out_specs=(
            P("batch", "seq", None),
            P("batch", "seq", None),
            P("seq"),
            P("seq", "head"),
            P("seq", "head"),
            P("seq", None),
            P("seq", "head"),
            P(None, "head"),
            P(),
            P("head"),
            P("head"),
            P("head"),
            P("head"),
            P("seq", "head"),
            P("seq", "head"),
            P("seq", "head"),
            P("seq", "head"),
            P("seq"),
            P("seq", "head"),
            P("seq", "head"),
            P("seq", "head"),
        ),
        check_vma=False,
    )
```

```python
import functools

import jax
import jax.numpy as jnp
from jax import lax
from jax.experimental import pallas as pl
from jax.experimental.pallas import tpu as pltpu
from jax.sharding import PartitionSpec as P

HD = 64
eps_norm = 1e-05
rope_base = 10000.0
neg_large = -1e30
highest = lax.Precision.HIGHEST


LANES = 128
MOST = 512
TAIL = (512, 384, 256, 128, 128, 128)
AHEAD = 7
EARLIER = 3
LAG = 3
PATTERN = (0, 1, 2, 0, 1, 3, 0, 1, 0, 1, 2, 0, 1, 3, 0, 1)
MESH = pl.DeviceIdType.MESH


def exchange(source, target, send_sem, recv_sem, device):
    return pltpu.make_async_remote_copy(
        src_ref=source,
        dst_ref=target,
        send_sem=send_sem,
        recv_sem=recv_sem,
        device_id=device,
        device_id_type=MESH,
    )


def each(count, action):
    span(0, count, action)


def span(first, last, action):
    lax.fori_loop(first, last, lambda i, carry: (action(i), carry)[1], 0)


def column_chunks(widths):
    chunks = []
    for group, width in enumerate(widths):
        count = -(-width // MOST)
        tiles = width // LANES
        sizes = [(tiles // count + (1 if k < tiles % count else 0)) * LANES for k in range(count)]
        if group == len(widths) - 1 and width == sum(TAIL):
            sizes = TAIL
        start = 0
        for size in sizes:
            chunks.append((group, start, size))
            start += size
    return chunks


def seq_bits():
    return (lax.axis_size("seq") - 1).bit_length()


def place_bits(place, bits):
    return tuple(lax.rem(place // 2 ** (bits - 1 - b), 2) for b in range(bits))


def seq_blocks(grad):
    bits = seq_bits() + 2
    return grad.reshape((2,) * bits + (grad.shape[0] >> bits, grad.shape[1]))


def peer_device():
    return (lax.axis_index("seq"), 1 - lax.axis_index("head"), lax.axis_index("batch"))


def other_device(step):
    seq, batch = lax.axis_index("seq"), lax.axis_index("batch")
    batches = lax.axis_size("batch")
    place = lax.rem(seq * batches + batch + step, lax.axis_size("seq") * batches)
    return (place // batches, lax.axis_index("head"), lax.rem(place, batches))


def greet_all(barrier, with_peer):
    world = lax.axis_size("seq") * lax.axis_size("batch")
    span(
        1,
        world,
        lambda step: pl.semaphore_signal(
            barrier, inc=1, device_id=other_device(step), device_id_type=MESH
        ),
    )
    if with_peer:
        pl.semaphore_signal(barrier, inc=1, device_id=peer_device(), device_id_type=MESH)
    pl.semaphore_wait(barrier, world - 1 + (1 if with_peer else 0))


class SmallSum:
    def __init__(self, source, slots, sems):
        self.source, self.slots, self.sems = source, slots, sems
        self.world = slots.shape[0]
        self.mine = lax.axis_index("seq") * lax.axis_size("batch") + lax.axis_index("batch")

    def copy(self, step):
        return exchange(
            self.source,
            self.slots.at[self.mine],
            self.sems.at[0, step],
            self.sems.at[1, step],
            other_device(step),
        )

    def start(self):
        span(1, self.world, lambda step: self.copy(step).start())

    def finish(self):
        span(1, self.world, lambda step: self.copy(step).wait())
        self.slots[self.mine] = self.source[...]
        return lax.fori_loop(
            1, self.world, lambda k, total: total + self.slots[k], self.slots[0]
        )


def small_scratch(shape):
    world = lax.axis_size("seq") * lax.axis_size("batch")
    return [
        pltpu.VMEM(shape, jnp.float32),
        pltpu.VMEM((world,) + shape, jnp.float32),
        pltpu.SemaphoreType.DMA((2, world)),
    ]


class Reduction:
    def __init__(self, chunks, sources, outs, scratch, given=()):
        self.chunks, self.sources, self.outs, self.given = chunks, sources, outs, given
        groups = len(sources)
        self.bits = seq_bits() + 2
        scratch = list(scratch)
        self.parts = [scratch[k * groups : (k + 1) * groups] for k in range(self.bits)]
        self.own, self.sem_own, self.sem_halve, self.sem_back = scratch[self.bits * groups :]
        self.setup()

    def setup(self):
        self.seq, self.head = lax.axis_index("seq"), lax.axis_index("head")
        self.batch = lax.axis_index("batch")
        place = self.seq * 4 + self.batch
        self.mine = [lax.rem(place // 2 ** (self.bits - 1 - k), 2) for k in range(self.bits)]
        self.done = [0] * (self.bits + 2)
        self.sent = self.held = self.limit = 0

    def peer(self, bit):
        step = (1 - 2 * self.mine[bit]) * 2 ** (self.bits - 1 - bit)
        if bit < self.bits - 2:
            return (self.seq + step // 4, self.head, self.batch)
        return (self.seq, self.head, self.batch + step)

    def order(self, k):
        low, high, last = self.bits - 1, self.bits - 2, self.bits - 3
        rest = [b for b in range(self.bits - 3, -1, -1)]
        if last < 0:
            return [low, high] if k % 2 == 0 else [high, low]
        kind = PATTERN[k % len(PATTERN)]
        if kind == 0:
            return [low, high] + rest
        if kind == 1:
            return [high, low] + rest
        if kind == 2:
            return [last, low, high] + rest[1:]
        return [last, high, low] + rest[1:]

    def place(self, k):
        group, start, size = self.chunks[k]
        return group, pl.ds(start, size)

    def cut(self, k, step, kept):
        order = self.order(k)
        left = [b for b in range(self.bits) if b not in order[:step]]
        bit = order[step]
        value = self.mine[bit] if kept else 1 - self.mine[bit]
        return tuple(value if b == bit else slice(None) for b in left)

    def halve_copy(self, k, step):
        group, columns = self.place(k)
        source = self.sources[group] if step == 0 else self.parts[step - 1][group]
        target = self.parts[step][group]
        away = self.cut(k, step, False)
        return exchange(
            source.at[away + (slice(None), columns)],
            target.at[(slice(None),) * (len(away) - 1) + (slice(None), columns)],
            self.sem_halve.at[0, k, step],
            self.sem_halve.at[1, k, step],
            self.peer(self.order(k)[step]),
        )

    def first_copy(self, k):
        group, columns = self.place(k)
        if group >= len(self.given) or k >= EARLIER:
            return self.halve_copy(k, 0)
        where = (slice(None),) * self.bits + (columns,)
        return pltpu.make_async_copy(
            self.given[group].at[where], self.parts[0][group].at[where], self.sem_halve.at[0, k, 0]
        )

    def own_copy(self, k):
        group, columns = self.place(k)
        size = self.chunks[k][2]
        kept = self.cut(k, 0, True)
        return pltpu.make_async_copy(
            self.sources[group].at[kept + (slice(None), columns)],
            self.own.at[(k % 2,) + (slice(None),) * self.bits + (pl.ds(0, size),)],
            self.sem_own.at[k],
        )

    def add(self, k, step):
        group, columns = self.place(k)
        size = self.chunks[k][2]
        target = self.parts[step][group]
        left = self.bits - 1 - step

        def one(index):
            every = index + (slice(None), columns)
            if step == 0:
                own = self.own[(k % 2,) + index + (slice(None), slice(0, size))]
            else:
                kept = self.cut(k, step, True)
                spot = [v for v in kept]
                rest = iter(index)
                spot = tuple(v if not isinstance(v, slice) else next(rest) for v in spot)
                own = self.parts[step - 1][group][spot + (slice(None), columns)]
            value = own + target[every]
            if step == self.bits - 1:
                self.outs[group][self.mine[-2], self.mine[-1], :, columns] = value
            else:
                target[every] = value

        span(
            0,
            2**left,
            lambda n: one(place_bits(n, left)),
        )

    def back_copy(self, k, turn):
        group, columns = self.place(k)
        out = self.outs[group]
        high, low = self.mine[-2], self.mine[-1]
        first_low = self.order(k).index(self.bits - 1) < self.order(k).index(self.bits - 2)
        bit = self.bits - 2 if first_low == (turn == 0) else self.bits - 1
        if turn == 0:
            part = out.at[high, low, :, columns]
        elif first_low:
            part = out.at[:, low, :, columns]
        else:
            part = out.at[high, :, :, columns]
        return exchange(
            part, part, self.sem_back.at[0, k, turn], self.sem_back.at[1, k, turn], self.peer(bit)
        )

    def refill(self):
        while self.sent < min(self.limit, self.done[0] + AHEAD):
            self.first_copy(self.sent).start()
            self.sent += 1
        while self.held < min(self.limit, self.done[0] + 2):
            self.own_copy(self.held).start()
            self.held += 1

    def allow(self, limit):
        self.limit = limit
        self.refill()

    def advance(self):
        stages = self.bits + 2
        for step in range(stages - 1, -1, -1):
            k = self.done[step]
            before = self.done[step - 1] if step else self.limit
            if k >= before or (step and before - k < LAG and before < self.limit):
                continue
            if step < self.bits:
                if step == 0:
                    self.first_copy(k).wait()
                    self.own_copy(k).wait()
                else:
                    self.halve_copy(k, step).wait()
                self.add(k, step)
                if step + 1 < self.bits:
                    self.halve_copy(k, step + 1).start()
                else:
                    self.back_copy(k, 0).start()
            elif step == self.bits:
                self.back_copy(k, 0).wait()
                self.back_copy(k, 1).start()
            else:
                self.back_copy(k, 1).wait()
            self.done[step] += 1
            if step == 0:
                self.refill()

    def finish(self):
        while self.done[-1] < len(self.chunks):
            self.advance()


class FirstHalving(Reduction):
    def __init__(self, chunks, sources, targets, sems):
        self.chunks, self.sources = chunks, sources
        self.bits = seq_bits() + 2
        self.parts, self.sem_halve = [targets], sems
        self.setup()


def reduction_scratch(chunks, widths, rows):
    bits = seq_bits() + 2
    parts = len(chunks)
    most = max(size for _, _, size in chunks)
    low = jnp.bfloat16
    return [
        pltpu.VMEM((2,) * (bits - 1 - step) + (rows, w), low)
        for step in range(bits)
        for w in widths
    ] + [
        pltpu.VMEM((2,) * bits + (rows, most), low),
        pltpu.SemaphoreType.DMA((parts,)),
        pltpu.SemaphoreType.DMA((2, parts, bits)),
        pltpu.SemaphoreType.DMA((2, parts, 2)),
    ]


def reduce_kernel(chunks, *refs):
    count = 1 + max(c[0] for c in chunks)
    sources, refs = refs[:count], refs[count:]
    small_given, refs = refs[0], refs[1:]
    outs, refs = refs[:count], refs[count:]
    small_out, small_in, small_buf, sem_small, *refs = refs
    greet_all(pltpu.get_barrier_semaphore(), False)
    reduction = Reduction(chunks, sources, outs, refs)
    reduction.allow(len(chunks))
    small_in[...] = small_given[...]
    small_sum = SmallSum(small_in, small_buf, sem_small)
    small_sum.start()
    reduction.finish()
    small_out[...] = small_sum.finish()


def reduce_gradients(grads, small):
    widths = [g.shape[1] for g in grads]
    chunks = column_chunks(widths)
    blocks = [seq_blocks(g) for g in grads]
    rows = blocks[0].shape[-2]
    vmem = pl.BlockSpec(memory_space=pltpu.VMEM)
    return pl.pallas_call(
        functools.partial(reduce_kernel, chunks),
        out_shape=[jax.ShapeDtypeStruct((2, 2, rows, w), jnp.bfloat16) for w in widths]
        + [jax.ShapeDtypeStruct(small.shape, jnp.float32)],
        in_specs=[pl.BlockSpec(memory_space=pl.ANY)] * len(grads) + [vmem],
        out_specs=[vmem] * (len(grads) + 1),
        scratch_shapes=small_scratch(small.shape) + reduction_scratch(chunks, widths, rows),
        compiler_params=pltpu.CompilerParams(
            collective_id=0, has_side_effects=True, vmem_limit_bytes=56 << 20
        ),
        name="reduce_gradients",
    )(*blocks, small)


def matmul(former, latter):
    return jnp.dot(former, latter, preferred_element_type=jnp.float32)


def matmul_last(former, latter):
    return lax.dot_general(
        former, latter, (((1,), (1,)), ((), ())), preferred_element_type=jnp.float32
    )


def matmul_first(former, latter):
    return lax.dot_general(
        former, latter, (((0,), (0,)), ((), ())), preferred_element_type=jnp.float32
    )


TILE = 128


def sigmoid(v):
    return 1.0 / (1.0 + jnp.exp(-v))


def greet(barrier, devices):
    for device in devices:
        pl.semaphore_signal(barrier, inc=1, device_id=device, device_id_type=MESH)
    pl.semaphore_wait(barrier, len(devices))


def tile_rows(i):
    return pl.ds(pl.multiple_of(i * TILE, TILE), TILE)


FEED_TILE = 256


def feed_rows(i):
    return pl.ds(pl.multiple_of(i * FEED_TILE, FEED_TILE), FEED_TILE)


def feed_kernel(merged, *refs):
    (
        y_ref,
        gate_z_ref,
        attention_ref,
        tokens_ref,
        cotangent_ref,
        mixer_gain_ref,
        mamba_gain_ref,
        feed_gain_ref,
        mamba_output_ref,
        attention_out_ref,
        gate_weight_hbm,
        lift_weight_hbm,
        down_weight_hbm,
        out_ref,
        d_second_ref,
        d_y_ref,
        d_gate_z_ref,
        d_attention_ref,
        g_feed_ref,
        g_mixed_ref,
        g_down_ref,
        g_gate_ref,
        g_feed_gain_ref,
        g_mamba_gain_ref,
    ) = refs[: 24]
    refs = refs[24:]
    if merged:
        came_refs, refs = refs[:2], refs[2:]
    (
        gate_weight,
        lift_weight,
        down_weight,
        normed,
        gated,
        g_six,
        inverse_six,
        second,
        inverse_two,
        normed2,
        active,
        d_feed,
        d_mix,
        d_gated,
        square_send,
        square_recv,
        cross_send,
        cross_recv,
        mixed_send,
        mixed_recv,
        lift_send,
        lift_recv,
        norm_send,
        norm_recv,
        weight_sem,
        sem_square,
        sem_cross,
        sem_mixed,
        sem_lift,
        sem_norm,
        *sem_first,
    ) = refs
    rows = y_ref.shape[0]
    tiles = rows // FEED_TILE
    inner = y_ref.shape[1]
    width = feed_gain_ref.shape[1]
    feed = down_weight.shape[1]
    all_inner = inner * lax.axis_size("head")
    peer = peer_device()
    loads = [
        pltpu.make_async_copy(source, target, weight_sem.at[k])
        for k, (source, target) in enumerate(
            (
                (gate_weight_hbm, gate_weight),
                (lift_weight_hbm, lift_weight),
                (down_weight_hbm, down_weight),
            )
        )
    ]
    for load in loads:
        load.start()
    devices = [peer]
    if merged:
        first = FirstHalving(
            column_chunks((g_down_ref.shape[-1], g_feed_ref.shape[-1]))[:EARLIER],
            [g_down_ref, g_feed_ref],
            came_refs,
            sem_first[0],
        )
        devices += [first.peer(bit) for bit in range(first.bits - 3, first.bits)]
    greet(pltpu.get_barrier_semaphore(), devices)

    def swap(send, recv, sems, i):
        rows_now = feed_rows(i)
        return exchange(send.at[rows_now], recv.at[rows_now], sems.at[0, i], sems.at[1, i], peer)

    def gate_tile(i):
        at = feed_rows(i)
        hidden = tokens_ref[at, :].astype(jnp.float32)
        inverse = lax.rsqrt(jnp.mean(hidden * hidden, axis=1, keepdims=True) + eps_norm)
        normed[at, :] = (hidden * inverse * mixer_gain_ref[...]).astype(jnp.bfloat16)
        gate_now = gate_z_ref[at, :]
        value = y_ref[at, :] * gate_now * sigmoid(gate_now)
        g_six[at, :] = value
        square_send[at, :] = jnp.broadcast_to(
            jnp.sum(value * value, axis=1, keepdims=True), (FEED_TILE, LANES)
        )
        swap(square_send, square_recv, sem_square, i).start()

    each(tiles, gate_tile)

    def mixed_tile(i):
        at = feed_rows(i)
        swap(square_send, square_recv, sem_square, i).wait()
        total = square_send[at, :] + square_recv[at, :]
        inverse = lax.rsqrt(total[:, :1] / all_inner + eps_norm)
        inverse_six[at, :] = jnp.broadcast_to(inverse, (FEED_TILE, LANES))
        low = (g_six[at, :] * inverse * mamba_gain_ref[...]).astype(jnp.bfloat16)
        gated[at, :] = low
        part = matmul_last(low, mamba_output_ref[...]) + matmul_last(
            attention_ref[at, :], attention_out_ref[...]
        )
        mixed_send[at, :] = part.astype(jnp.bfloat16)
        swap(mixed_send, mixed_recv, sem_mixed, i).start()

    each(tiles, mixed_tile)
    for load in loads:
        load.wait()

    def feed_tile(i):
        at = feed_rows(i)
        swap(mixed_send, mixed_recv, sem_mixed, i).wait()
        total = mixed_send[at, :].astype(jnp.float32) + mixed_recv[at, :].astype(jnp.float32)
        hidden = tokens_ref[at, :].astype(jnp.float32) + total
        second[at, :] = hidden
        inverse = lax.rsqrt(jnp.mean(hidden * hidden, axis=1, keepdims=True) + eps_norm)
        inverse_two[at, :] = jnp.broadcast_to(inverse, (FEED_TILE, LANES))
        low = (hidden * inverse * feed_gain_ref[...]).astype(jnp.bfloat16)
        normed2[at, :] = low
        gate_now = matmul(low, gate_weight[...])
        lift_now = matmul(low, lift_weight[...])
        sig = sigmoid(gate_now)
        silu = gate_now * sig
        act = (silu * lift_now).astype(jnp.bfloat16)
        active[at, :] = act
        lift_send[at, :] = matmul_last(act, down_weight[...]).astype(jnp.bfloat16)
        swap(lift_send, lift_recv, sem_lift, i).start()
        d_act = matmul(cotangent_ref[at, :], down_weight[...])
        d_gate = (d_act * lift_now * (sig * (1.0 + gate_now * (1.0 - sig)))).astype(jnp.bfloat16)
        d_lift = (d_act * silu).astype(jnp.bfloat16)
        d_feed[at, :feed] = d_gate
        d_feed[at, feed:] = d_lift
        part = matmul_last(d_gate, gate_weight[...]) + matmul_last(d_lift, lift_weight[...])
        norm_send[at, :] = part.astype(jnp.bfloat16)
        swap(norm_send, norm_recv, sem_norm, i).start()

    each(tiles, feed_tile)
    blocks = lax.axis_size("seq") if merged else width // 256

    def store(target, k, grad):
        if merged:
            index = place_bits(k, seq_bits())
            target[index] = grad.reshape(target.shape[len(index) :]).astype(jnp.bfloat16)
        else:
            target[pl.ds(pl.multiple_of(k * 256, 256), 256), :] = grad.astype(jnp.bfloat16)

    def block_columns(k):
        size = width // blocks
        return pl.ds(pl.multiple_of(k * size, LANES), size)

    def feed_weights(k):
        block = block_columns(k)
        store(g_down_ref, k, matmul_first(cotangent_ref[:, block], active[...]))
        store(g_feed_ref, k, matmul_first(normed2[:, block], d_feed[...]))

    each(blocks, feed_weights)
    if merged:
        for k in range(EARLIER):
            first.halve_copy(k, 0).start()
    g_feed_gain_ref[...] = jnp.zeros_like(g_feed_gain_ref)
    g_mamba_gain_ref[...] = jnp.zeros_like(g_mamba_gain_ref)

    def norm_tile(i):
        at = feed_rows(i)
        swap(norm_send, norm_recv, sem_norm, i).wait()
        d_norm = norm_send[at, :].astype(jnp.float32) + norm_recv[at, :].astype(jnp.float32)
        hidden = second[at, :]
        inverse = inverse_two[at, :][:, :1]
        e_two = d_norm * feed_gain_ref[...]
        g_feed_gain_ref[...] += jnp.sum(d_norm * hidden * inverse, axis=0, keepdims=True)
        cross = jnp.sum(e_two * hidden, axis=1, keepdims=True) / width
        d_hidden = (
            cotangent_ref[at, :].astype(jnp.float32)
            + inverse * e_two
            - hidden * (inverse * inverse * inverse * cross)
        )
        d_second_ref[at, :] = d_hidden
        low = d_hidden.astype(jnp.bfloat16)
        d_mix[at, :] = low
        d_attention_ref[at, :] = matmul(low, attention_out_ref[...])
        d_gated_now = matmul(low, mamba_output_ref[...])
        d_gated[at, :] = d_gated_now
        six = g_six[at, :]
        g_mamba_gain_ref[...] += jnp.sum(
            d_gated_now * six * inverse_six[at, :][:, :1], axis=0, keepdims=True
        )
        cross_send[at, :] = jnp.broadcast_to(
            jnp.sum(d_gated_now * mamba_gain_ref[...] * six, axis=1, keepdims=True), (FEED_TILE, LANES)
        )
        swap(cross_send, cross_recv, sem_cross, i).start()

    each(tiles, norm_tile)

    def gate_back(i):
        at = feed_rows(i)
        swap(cross_send, cross_recv, sem_cross, i).wait()
        cross = (cross_send[at, :] + cross_recv[at, :])[:, :1] / all_inner
        inverse = inverse_six[at, :][:, :1]
        d_six = inverse * (d_gated[at, :] * mamba_gain_ref[...]) - g_six[at, :] * (
            inverse * inverse * inverse * cross
        )
        gate_now = gate_z_ref[at, :]
        sig = sigmoid(gate_now)
        d_y_ref[at, :] = d_six * gate_now * sig
        d_gate_z_ref[at, :] = (
            d_six * y_ref[at, :] * (sig * (1.0 + gate_now * (1.0 - sig)))
        ).astype(jnp.bfloat16)

    each(tiles, gate_back)

    def out_tile(i):
        at = feed_rows(i)
        swap(lift_send, lift_recv, sem_lift, i).wait()
        total = lift_send[at, :].astype(jnp.float32) + lift_recv[at, :].astype(jnp.float32)
        out_ref[at, :] = (second[at, :] + total).astype(jnp.bfloat16)

    each(tiles, out_tile)

    def mixed_weights(k):
        block = block_columns(k)
        store(g_gate_ref, k, matmul_first(normed[:, block], d_gate_z_ref[...]))
        d_mix_now = d_mix[:, block]
        grad = jnp.concatenate(
            [matmul_first(d_mix_now, gated[...]), matmul_first(d_mix_now, attention_ref[...])],
            axis=1,
        )
        store(g_mixed_ref, k, grad)

    each(blocks, mixed_weights)
    if merged:
        for k in range(EARLIER):
            first.halve_copy(k, 0).wait()


def feed_layer(
    y,
    gate_z,
    attention_low,
    tokens,
    cotangent,
    mixer_gain,
    mamba_gain,
    feed_gain,
    mamba_output,
    attention_out,
    gate_weight,
    lift_weight,
    down_weight,
):
    rows, inner = y.shape
    width = tokens.shape[1]
    feed = gate_weight.shape[1]
    att = attention_low.shape[1]
    tiles = rows // FEED_TILE
    vmem = pl.BlockSpec(memory_space=pltpu.VMEM)
    hbm = pl.BlockSpec(memory_space=pl.ANY)
    low, full = jnp.bfloat16, jnp.float32
    shape = jax.ShapeDtypeStruct
    merged = lax.axis_size("seq") == 4

    def grad_shape(columns):
        if merged:
            return shape((2,) * (seq_bits() + 2) + (width // 16, columns), low)
        return shape((width, columns), low)

    out_shape = [
            shape((rows, width), low),
            shape((rows, width), full),
            shape((rows, inner), full),
            shape((rows, inner), low),
            shape((rows, att), full),
            grad_shape(2 * feed),
            grad_shape(inner + att),
            grad_shape(feed),
            grad_shape(inner),
            shape((1, width), full),
            shape((1, inner), full),
        ]
    scratch = []
    if merged:
        out_shape += [shape((2,) * 3 + (width // 16, n), low) for n in (feed, MOST)]
        scratch = [pltpu.SemaphoreType.DMA((2, EARLIER, 1))]
    return pl.pallas_call(
        functools.partial(feed_kernel, merged),
        out_shape=out_shape,
        in_specs=[vmem] * 10 + [hbm] * 3,
        out_specs=[vmem] * len(out_shape),
        scratch_shapes=[
            pltpu.VMEM((width, feed), low),
            pltpu.VMEM((width, feed), low),
            pltpu.VMEM((width, feed), low),
            pltpu.VMEM((rows, width), low),
            pltpu.VMEM((rows, inner), low),
            pltpu.VMEM((rows, inner), full),
            pltpu.VMEM((rows, LANES), full),
            pltpu.VMEM((rows, width), full),
            pltpu.VMEM((rows, LANES), full),
            pltpu.VMEM((rows, width), low),
            pltpu.VMEM((rows, feed), low),
            pltpu.VMEM((rows, 2 * feed), low),
            pltpu.VMEM((rows, width), low),
            pltpu.VMEM((rows, inner), full),
            pltpu.VMEM((rows, LANES), full),
            pltpu.VMEM((rows, LANES), full),
            pltpu.VMEM((rows, LANES), full),
            pltpu.VMEM((rows, LANES), full),
        ]
        + [pltpu.VMEM((rows, width), low)] * 6
        + [pltpu.SemaphoreType.DMA((3,))]
        + [pltpu.SemaphoreType.DMA((2, tiles))] * 5
        + scratch,
        compiler_params=pltpu.CompilerParams(
            collective_id=1, has_side_effects=True, vmem_limit_bytes=60 << 20
        ),
        name="feed_layer",
    )(
        y,
        gate_z,
        attention_low,
        tokens,
        cotangent,
        mixer_gain[None],
        mamba_gain[None],
        feed_gain[None],
        mamba_output,
        attention_out,
        gate_weight,
        lift_weight,
        down_weight,
    )


CHUNK = 128
HALO = 8
PIECE = 256


def turn_half(values):
    lane = lax.broadcasted_iota(jnp.int32, values.shape, 1)
    return jnp.where(
        lax.rem(lane, HD) < HD // 2,
        pltpu.roll(values, LANES - HD // 2, 1),
        pltpu.roll(values, HD // 2, 1),
    )


def two_parts(values):
    high = values.astype(jnp.bfloat16)
    return high, (values - high.astype(jnp.float32)).astype(jnp.bfloat16)


def spread_heads(values, spread):
    high, rest = two_parts(values)
    return matmul(high, spread) + matmul(rest, spread)


def sum_heads(values, spread):
    high, rest = two_parts(values)
    return matmul_last(high, spread) + matmul_last(rest, spread)


def spread_matrix(inner, size):
    row = lax.broadcasted_iota(jnp.int32, (LANES, inner), 0)
    lane = lax.broadcasted_iota(jnp.int32, (LANES, inner), 1)
    return jnp.where(lane // size == row, 1.0, 0.0).astype(jnp.bfloat16)


def ordered(count):
    row = lax.broadcasted_iota(jnp.int32, (count, count), 0)
    lane = lax.broadcasted_iota(jnp.int32, (count, count), 1)
    return row >= lane


def halves(values, size):
    lane = lax.broadcasted_iota(jnp.int32, values.shape, 1)
    return jnp.concatenate(
        [jnp.where(lane < size, values, 0.0), jnp.where(lane < size, 0.0, values)], axis=0
    ).astype(jnp.bfloat16)


def soft_plus(v):
    return jnp.maximum(v, 0.0) + jnp.log1p(jnp.exp(-jnp.abs(v)))


def chunk_flags(seg_ref, c):
    window = seg_ref[pl.ds(pl.multiple_of(c * CHUNK, CHUNK), CHUNK + HALO), :]
    own = window[HALO:]
    start = jnp.where(own == window[HALO - 1 : HALO], 1.0, 0.0)
    end = jnp.where(own == own[CHUNK - 1 :], 1.0, 0.0)
    return own, start, end


def greet_seq(barrier, with_peer):
    seq, head, batch = lax.axis_index("seq"), lax.axis_index("head"), lax.axis_index("batch")
    count = lax.axis_size("seq")

    def one(step, carry):
        pl.semaphore_signal(
            barrier,
            inc=1,
            device_id=(lax.rem(seq + step, count), head, batch),
            device_id_type=MESH,
        )
        return carry

    lax.fori_loop(1, count, one, 0)
    if with_peer:
        pl.semaphore_signal(barrier, inc=1, device_id=peer_device(), device_id_type=MESH)
    pl.semaphore_wait(barrier, count - 1 + with_peer)


def mixer_kernel(
    tokens_ref,
    gain_ref,
    seg_ref,
    table_ref,
    gate_weight,
    input_weight,
    maps_weight,
    step_weight,
    query_weight,
    memory_weight,
    taps_ref,
    bias_ref,
    rate_ref,
    skip_ref,
    gate_z_ref,
    pre_ref,
    conv_ref,
    raw_ref,
    cum_ref,
    y_ref,
    states_ref,
    query_ref,
    memory_ref,
    normed,
    spread_ref,
    act,
    scaled,
    added,
    decay,
    total,
    local,
    state,
    chain_out,
    chain_in,
    sem_memory,
    sem_halo,
    sem_chain,
):
    seq, head, batch = lax.axis_index("seq"), lax.axis_index("head"), lax.axis_index("batch")
    count = lax.axis_size("seq")
    rows = tokens_ref.shape[0]
    tiles = rows // CHUNK
    inner = y_ref.shape[1]
    width = pre_ref.shape[1]
    state_width = (width - inner) // 2
    following = (lax.rem(seq + 1, count), head, batch)
    greet_seq(pltpu.get_barrier_semaphore(), 0)

    def memory_copy(step, place, owner):
        return exchange(
            memory_ref.at[owner],
            memory_ref.at[owner],
            sem_memory.at[0, step],
            sem_memory.at[1, step],
            (place, head, batch),
        )

    halo_copy = exchange(
        pre_ref.at[pl.ds(rows, HALO)],
        pre_ref.at[pl.ds(0, HALO)],
        sem_halo.at[0],
        sem_halo.at[1],
        following,
    )

    def memory_tile(i):
        at = feed_rows(i)
        hidden = tokens_ref[at, :].astype(jnp.float32)
        inverse = lax.rsqrt(jnp.mean(hidden * hidden, axis=1, keepdims=True) + eps_norm)
        low = (hidden * inverse * gain_ref[...]).astype(jnp.bfloat16)
        normed[at, :] = low
        value = matmul(low, memory_weight[...])
        lane = lax.broadcasted_iota(jnp.int32, value.shape, 1)
        turned = value * table_ref[at, :LANES] + turn_half(value) * table_ref[at, LANES:]
        memory_ref[seq, at, :] = jnp.where(lane < HD, turned, value).astype(jnp.bfloat16)

    wide_tiles = rows // FEED_TILE
    each(wide_tiles, memory_tile)

    def memory_start(step, carry):
        @pl.when(seq + step < count)
        def _():
            memory_copy(step, lax.rem(seq + step, count), seq).start()

        return carry

    lax.fori_loop(1, count, memory_start, 0)

    def pre_tile(i):
        at = feed_rows(i)
        to = pl.ds(pl.multiple_of(i * FEED_TILE + HALO, HALO), FEED_TILE)
        low = normed[at, :]
        pre_ref[to, :inner] = matmul(low, input_weight[...])
        pre_ref[to, inner:] = matmul(low, maps_weight[...])

    each(wide_tiles, lambda i: pre_tile(wide_tiles - 1 - i))

    @pl.when(seq < count - 1)
    def _():
        halo_copy.start()

    spread_ref[...] = spread_matrix(inner, HD)
    lower = jnp.where(ordered(CHUNK), 1.0, 0.0)

    def step_tile(i):
        at = tile_rows(i)
        raw = matmul(normed[at, :], step_weight[...]) + bias_ref[...]
        raw_ref[at, :] = raw
        cum_ref[at, :] = jnp.dot(lower, rate_ref[...] * soft_plus(raw), precision=highest)

    each(tiles, step_tile)

    @pl.when(seq == 0)
    def _():
        pre_ref[:HALO, :] = jnp.zeros((HALO, width), jnp.float32)

    @pl.when(seq > 0)
    def _():
        halo_copy.wait_recv()

    def conv_tile(i):
        at = tile_rows(i)
        window_at = pl.ds(pl.multiple_of(i * TILE, TILE), TILE + HALO)
        seg = seg_ref[window_at, :]
        own = seg[HALO:]
        masks = [
            jnp.where(seg[HALO - 3 + k : HALO - 3 + k + TILE] == own, 1.0, 0.0) for k in range(3)
        ]
        for j in range(width // LANES):
            columns = slice(j * LANES, (j + 1) * LANES)
            window = pre_ref[window_at, columns]
            summed = taps_ref[3:4, columns] * window[HALO:]
            for k in range(3):
                summed = summed + taps_ref[k : k + 1, columns] * (
                    window[HALO - 3 + k : HALO - 3 + k + TILE] * masks[k]
                )
            conv_ref[at, columns] = summed
            act[at, columns] = summed * sigmoid(summed)

    each(tiles, conv_tile)
    local[...] = jnp.zeros_like(local)
    total[...] = jnp.ones_like(total)

    def input_map(at):
        return act[at, inner : inner + state_width].astype(jnp.bfloat16)

    def output_map(at):
        return act[at, inner + state_width :].astype(jnp.bfloat16)

    def local_chunk(c):
        at = tile_rows(c)
        _, start, end = chunk_flags(seg_ref, c)
        cum = cum_ref[at, :]
        last = cum[CHUNK - 1 :]
        spread = spread_ref[...]
        value = act[at, :inner] * spread_heads(soft_plus(raw_ref[at, :]), spread)
        scaled[at, :] = value.astype(jnp.bfloat16)
        weight = spread_heads(jnp.exp(last - cum) * end, spread)
        fresh = matmul_first(input_map(at), (value * weight).astype(jnp.bfloat16))
        keep = jnp.broadcast_to(jnp.exp(last) * start[CHUNK - 1 :], (HALO, LANES))
        keep = spread_heads(keep, spread)
        added[c] = fresh
        decay[c] = keep
        local[...] = local[...] * keep[:1] + fresh
        total[...] = total[...] * keep

    each(tiles, local_chunk)
    pieces = inner // PIECE

    def chain_copy(p):
        columns = pl.ds(p * PIECE, PIECE)
        return exchange(
            chain_out.at[:, columns],
            chain_in.at[:, columns],
            sem_chain.at[0, p],
            sem_chain.at[1, p],
            following,
        )

    @pl.when(seq == 0)
    def _():
        state[...] = jnp.zeros_like(state)
        chain_out[...] = local[...].astype(jnp.bfloat16)
        if count > 1:
            for p in range(pieces):
                chain_copy(p).start()

    def inside_chunk(c):
        at = tile_rows(c)
        own, _, _ = chunk_flags(seg_ref, c)
        cum = cum_ref[at, :]
        turned = cum.T
        meet = matmul_last(output_map(at), input_map(at))
        meet = jnp.where(ordered(CHUNK) & (own == own.T), meet, 0.0)
        for i in range(inner // LANES):
            columns = slice(i * LANES, (i + 1) * LANES)
            mixing = []
            for h in (2 * i, 2 * i + 1):
                gap = cum[:, h : h + 1] - turned[h : h + 1, :]
                mixing.append(meet * jnp.exp(jnp.minimum(gap, 0.0)))
            y_ref[at, columns] = matmul(
                jnp.concatenate(mixing, axis=1).astype(jnp.bfloat16),
                halves(scaled[at, columns].astype(jnp.float32), HD),
            )

    each(tiles, inside_chunk)

    def project_tile(i):
        at = feed_rows(i)
        low = normed[at, :]
        gate_z_ref[at, :] = matmul(low, gate_weight[...])
        value = matmul(low, query_weight[...])
        for k in range(value.shape[1] // LANES):
            part = value[:, k * LANES : (k + 1) * LANES]
            turned = part * table_ref[at, :LANES] + turn_half(part) * table_ref[at, LANES:]
            query_ref[at, k * LANES : (k + 1) * LANES] = turned.astype(jnp.bfloat16)

    @pl.when(seq >= 2)
    def _():
        each(wide_tiles, project_tile)

    @pl.when(seq > 0)
    def _():
        for p in range(pieces):
            columns = pl.ds(p * PIECE, PIECE)
            chain_copy(p).wait_recv()
            came = chain_in[:, columns].astype(jnp.float32)
            state[:, columns] = came

            @pl.when(seq < count - 1)
            def _():
                chain_out[:, columns] = (
                    came * total[:1, columns] + local[:, columns]
                ).astype(jnp.bfloat16)
                chain_copy(p).start()

    @pl.when(seq < 2)
    def _():
        each(wide_tiles, project_tile)

    def across_chunk(c):
        at = tile_rows(c)
        _, start, _ = chunk_flags(seg_ref, c)
        now = state[...]
        low = now.astype(jnp.bfloat16)
        states_ref[c] = low
        carried = spread_heads(jnp.exp(cum_ref[at, :]) * start, spread_ref[...])
        y_ref[at, :] += matmul(output_map(at), low) * carried + skip_ref[...] * act[at, :inner]
        state[...] = now * decay[c][:1] + added[c]

    each(tiles, across_chunk)
    states_ref[tiles] = state[...].astype(jnp.bfloat16)

    def memory_wait(step, carry):
        @pl.when(seq + step < count)
        def _():
            memory_copy(step, lax.rem(seq + step, count), seq).wait_send()
            memory_ref[lax.rem(seq + step, count)] = jnp.zeros(memory_ref.shape[1:], jnp.bfloat16)

        @pl.when(seq - step >= 0)
        def _():
            memory_copy(step, seq, lax.rem(seq - step + count, count)).wait_recv()

        return carry

    lax.fori_loop(1, count, memory_wait, 0)

    @pl.when(seq < count - 1)
    def _():
        halo_copy.wait_send()
        for p in range(pieces):
            chain_copy(p).wait_send()


def mixer_forward(
    tokens,
    mixer_gain,
    segments,
    table,
    mamba_gate,
    mamba_input,
    mamba_maps,
    step_weight,
    query_weight,
    memory_weight,
    taps,
    bias,
    rate,
    skip,
):
    rows, width = tokens.shape
    count = lax.axis_size("seq")
    inner = mamba_gate.shape[1]
    conv_width = taps.shape[1]
    state_width = (conv_width - inner) // 2
    query = query_weight.shape[1]
    chunks = rows // CHUNK
    pieces = inner // PIECE
    vmem = pl.BlockSpec(memory_space=pltpu.VMEM)
    low, full = jnp.bfloat16, jnp.float32
    shape = jax.ShapeDtypeStruct
    return pl.pallas_call(
        mixer_kernel,
        out_shape=[
            shape((rows, inner), full),
            shape((rows + HALO, conv_width), full),
            shape((rows, conv_width), full),
            shape((rows, LANES), full),
            shape((rows, LANES), full),
            shape((rows, inner), full),
            shape((chunks + 1, state_width, inner), low),
            shape((rows, query), low),
            shape((count, rows, memory_weight.shape[1]), low),
        ],
        in_specs=[vmem] * 14,
        out_specs=[vmem] * 9,
        scratch_shapes=[
            pltpu.VMEM((rows, width), low),
            pltpu.VMEM((LANES, inner), low),
            pltpu.VMEM((rows, conv_width), full),
            pltpu.VMEM((rows, inner), low),
            pltpu.VMEM((chunks, state_width, inner), full),
            pltpu.VMEM((chunks, HALO, inner), full),
            pltpu.VMEM((HALO, inner), full),
            pltpu.VMEM((state_width, inner), full),
            pltpu.VMEM((state_width, inner), full),
            pltpu.VMEM((state_width, inner), low),
            pltpu.VMEM((state_width, inner), low),
            pltpu.SemaphoreType.DMA((2, count)),
            pltpu.SemaphoreType.DMA((2,)),
            pltpu.SemaphoreType.DMA((2, pieces)),
        ],
        compiler_params=pltpu.CompilerParams(
            collective_id=2, has_side_effects=True, vmem_limit_bytes=60 << 20
        ),
        name="mixer_forward",
    )(
        tokens,
        mixer_gain,
        segments,
        table,
        mamba_gate,
        mamba_input,
        mamba_maps,
        step_weight,
        query_weight,
        memory_weight,
        taps,
        bias,
        rate,
        skip,
    )


KEY_TILE = 512


def stacked_heads(values, first, factor):
    lane = lax.broadcasted_iota(jnp.int32, (values.shape[0], LANES), 1)
    keep = (lane < HD) if first else (lane >= HD)
    parts = []
    for h in range(values.shape[1] // HD):
        tile = values[:, (h // 2) * LANES : (h // 2 + 1) * LANES].astype(jnp.float32)
        if (h % 2 == 0) != first:
            tile = pltpu.roll(tile, HD, 1)
        parts.append(jnp.where(keep, tile * factor, 0.0))
    return jnp.concatenate(parts, axis=0)


def unstacked_heads(turned, first):
    heads = turned.shape[1] // TILE
    blocks = [turned[:, h * TILE : (h + 1) * TILE].T for h in range(heads)]
    lane = lax.broadcasted_iota(jnp.int32, (TILE, LANES), 1)
    tiles = []
    for even, odd in zip(blocks[::2], blocks[1::2]):
        if first:
            odd = pltpu.roll(odd, HD, 1)
        else:
            even = pltpu.roll(even, HD, 1)
        tiles.append(jnp.where(lane < HD, even, odd))
    return tiles


def key_tile(seg_turned, key_seg_ref, first, i, k):
    at = pl.ds(pl.multiple_of(k * KEY_TILE, KEY_TILE), KEY_TILE)
    place = k * KEY_TILE + lax.broadcasted_iota(jnp.int32, (KEY_TILE, TILE), 0)
    row = first + i * TILE + lax.broadcasted_iota(jnp.int32, (KEY_TILE, TILE), 1)
    return at, (place <= row) & (key_seg_ref[at, :] == seg_turned)


def query_segments(seg_ref, i):
    own = seg_ref[pl.ds(pl.multiple_of(i * TILE, TILE) + HALO, TILE), :].T
    return jnp.concatenate([own] * (KEY_TILE // TILE), axis=0)


def attend_block(first, low, high, i, queries_in, memory_of, seg_ref, key_seg_ref):
    heads = queries_in.shape[1] // HD
    turned = stacked_heads(queries_in, True, HD ** (-0.5)).T.astype(jnp.bfloat16)
    segs = query_segments(seg_ref, i)
    parts = [turned[:, h * TILE : (h + 1) * TILE] for h in range(heads)]

    def one(step, carry):
        at, allowed = key_tile(segs, key_seg_ref, first, i, high - step)
        keys = memory_of(at)
        after = []
        for part, (most, total, acc) in zip(parts, carry):
            scores = jnp.where(allowed, matmul(keys, part), neg_large)
            new = jnp.maximum(most, jnp.max(scores, axis=0, keepdims=True))
            weights = jnp.exp(scores - new)
            factor = jnp.exp(most - new)
            total = total * factor + jnp.sum(weights, axis=0, keepdims=True)
            acc = acc * factor + matmul_first(keys, weights.astype(jnp.bfloat16))
            after.append((new, total, acc))
        return tuple(after)

    zero = (
        jnp.full((1, TILE), neg_large, jnp.float32),
        jnp.zeros((1, TILE), jnp.float32),
        jnp.zeros((LANES, TILE), jnp.float32),
    )
    result = lax.fori_loop(0, high - low + 1, one, (zero,) * heads)
    return (
        jnp.concatenate([acc / total for _, total, acc in result], axis=1),
        jnp.concatenate([most + jnp.log(total) for most, total, _ in result], axis=1),
    )


def attend_back_block(
    first, low, high, i, queries_in, d_out, out, log, memory_of, seg_ref, key_seg_ref, grads
):
    heads = queries_in.shape[1] // HD
    queries = stacked_heads(queries_in, True, HD ** (-0.5))
    outer = stacked_heads(d_out, False, 1.0)
    queries_turned, outer_turned = queries.T.astype(jnp.bfloat16), outer.T.astype(jnp.bfloat16)
    queries, outer = queries.astype(jnp.bfloat16), outer.astype(jnp.bfloat16)
    segs = query_segments(seg_ref, i)
    row = lax.broadcasted_iota(jnp.int32, (HALO, heads * HD), 0)
    lane = lax.broadcasted_iota(jnp.int32, (HALO, heads * HD), 1)
    pick = jnp.where(lane // HD == row, 1.0, 0.0).astype(jnp.bfloat16)
    high_part, low_part = two_parts(d_out * out)
    deltas = matmul_last(pick, high_part) + matmul_last(pick, low_part)
    spans = [slice(h * TILE, (h + 1) * TILE) for h in range(heads)]

    def one(step, totals):
        at, allowed = key_tile(segs, key_seg_ref, first, i, high - step)
        keys = memory_of(at)
        slopes, lows, after = [], [], []
        for h, (part, total) in enumerate(zip(spans, totals)):
            weights = jnp.exp(matmul(keys, queries_turned[:, part]) - log[:, part])
            weights = jnp.where(allowed, weights, 0.0)
            slope = weights * (matmul(keys, outer_turned[:, part]) - deltas[h : h + 1])
            slopes.append(slope.astype(jnp.bfloat16))
            lows.append(weights.astype(jnp.bfloat16))
            after.append(total + matmul_first(keys, slopes[-1]))
        grads[at, :] += matmul(jnp.concatenate(slopes, axis=1), queries) + matmul(
            jnp.concatenate(lows, axis=1), outer
        )
        return tuple(after)

    totals = lax.fori_loop(
        0, high - low + 1, one, (jnp.zeros((LANES, TILE), jnp.float32),) * heads
    )
    return jnp.concatenate(totals, axis=1) * HD ** (-0.5)


def attention_kernel(
    first_ref,
    low_ref,
    high_ref,
    query_ref,
    memory_ref,
    seg_ref,
    key_seg_ref,
    out_ref,
    low_out_ref,
    log_ref,
):
    def block(i):
        at_rows = tile_rows(i)
        turned, log = attend_block(
            first_ref[0],
            low_ref[i],
            high_ref[i],
            i,
            query_ref[at_rows, :],
            lambda at: memory_ref[at, :],
            seg_ref,
            key_seg_ref,
        )
        for pair, tile in enumerate(unstacked_heads(turned, False)):
            columns = slice(pair * LANES, (pair + 1) * LANES)
            out_ref[at_rows, columns] = tile
            low_out_ref[at_rows, columns] = tile.astype(jnp.bfloat16)
        log_ref[i] = jnp.broadcast_to(log, log_ref.shape[1:])

    each(query_ref.shape[0] // TILE, block)


def attention_forward(spans, query, memory, segments, key_segments):
    rows, width = query.shape
    full = jnp.float32
    vmem = pl.BlockSpec(memory_space=pltpu.VMEM)
    return pl.pallas_call(
        attention_kernel,
        out_shape=[
            jax.ShapeDtypeStruct((rows, width), full),
            jax.ShapeDtypeStruct((rows, width), jnp.bfloat16),
            jax.ShapeDtypeStruct((rows // TILE, HALO, width // HD * TILE), full),
        ],
        in_specs=[pl.BlockSpec(memory_space=pltpu.SMEM)] * 3 + [vmem] * 4,
        out_specs=[vmem] * 3,
        compiler_params=pltpu.CompilerParams(vmem_limit_bytes=56 << 20),
        name="attention_forward",
    )(*spans, query, memory, segments, key_segments)


def attention_back_kernel(
    first_ref,
    low_ref,
    high_ref,
    query_ref,
    memory_ref,
    seg_ref,
    key_seg_ref,
    out_ref,
    log_ref,
    d_out_ref,
    table_ref,
    d_query_ref,
    d_memory_ref,
    grads,
):
    grads[...] = jnp.zeros_like(grads)

    def block(i):
        at = tile_rows(i)
        d_turned = attend_back_block(
            first_ref[0],
            low_ref[i],
            high_ref[i],
            i,
            query_ref[at, :],
            d_out_ref[at, :],
            out_ref[at, :],
            log_ref[i][:1],
            lambda key_at: memory_ref[key_at, :],
            seg_ref,
            key_seg_ref,
            grads,
        )
        for pair, tile in enumerate(unstacked_heads(d_turned, True)):
            turned = tile * table_ref[at, :LANES] - turn_half(tile) * table_ref[at, LANES:]
            d_query_ref[at, pair * LANES : (pair + 1) * LANES] = turned.astype(jnp.bfloat16)

    each(query_ref.shape[0] // TILE, block)
    d_memory_ref[...] = grads[...].astype(jnp.bfloat16)


def attention_back(spans, query, memory, segments, key_segments, out, logs, d_out, table):
    vmem = pl.BlockSpec(memory_space=pltpu.VMEM)
    return pl.pallas_call(
        attention_back_kernel,
        out_shape=[
            jax.ShapeDtypeStruct(query.shape, jnp.bfloat16),
            jax.ShapeDtypeStruct(memory.shape, jnp.bfloat16),
        ],
        in_specs=[pl.BlockSpec(memory_space=pltpu.SMEM)] * 3 + [vmem] * 8,
        out_specs=[vmem] * 2,
        scratch_shapes=[pltpu.VMEM(memory.shape, jnp.float32)],
        compiler_params=pltpu.CompilerParams(vmem_limit_bytes=56 << 20),
        name="attention_back",
    )(*spans, query, memory, segments, key_segments, out, logs, d_out, table)


MERGED_INPUTS = 30


def mixer_back_kernel(merged, chunks, *refs):
    refs = list(refs)

    def take(count):
        nonlocal refs
        now, refs = refs[:count], refs[count:]
        return now

    if merged:
        given = take(MERGED_INPUTS)
        early, came = take(4), take(2)
        d_tokens_ref, *outs, small_out = take(7)
        copies = take(MERGED_INPUTS)
        (sem_load,) = take(1)
        loads = [
            pltpu.make_async_copy(source, target, sem_load.at[k])
            for k, (source, target) in enumerate(zip(given, copies))
        ]
        for load in loads:
            load.start()
        refs = copies + refs
    (
        tokens_ref,
        gain_ref,
        seg_ref,
        table_ref,
        gate_weight,
        input_weight,
        maps_weight,
        step_weight,
        query_weight,
        memory_weight,
        taps_ref,
        rate_ref,
        skip_ref,
        pre_ref,
        conv_ref,
        raw_ref,
        cum_ref,
        y_ref,
        states_ref,
        d_second_ref,
        d_y_ref,
        d_gate_z_ref,
    ) = take(22)
    if merged:
        (
            query_ref,
            memory_ref,
            key_seg_ref,
            attention_ref,
            logs_ref,
            d_attention_ref,
            feed_gain_ref,
            mamba_gain_ref,
        ) = take(8)
    else:
        d_query_ref, d_memory_ref = take(2)
        d_tokens_ref, g_side_ref, g_taps_ref, g_gain_ref, g_heads_ref = take(5)
    (
        normed,
        spread_ref,
        act,
        d_conv,
        d_scaled,
        d_maps,
        row_term,
        added,
        local,
        total,
        state,
        skip_sum,
        side,
        chain_out,
        chain_in,
        maps_send,
        maps_recv,
        memory_recv,
        norm_send,
        norm_recv,
        sem_memory,
        sem_halo,
        sem_chain,
        sem_maps,
        sem_norm,
    ) = take(25)
    if merged:
        g_side_ref, grads, d_memory_ref, small_in, small_buf, sem_small = take(6)
        g_taps_ref = g_gain_ref = g_heads_ref = small_in
    seq, head, batch = lax.axis_index("seq"), lax.axis_index("head"), lax.axis_index("batch")
    count = lax.axis_size("seq")
    rows = tokens_ref.shape[0]
    tiles = rows // CHUNK
    inner = y_ref.shape[1]
    width = pre_ref.shape[1]
    state_width = (width - inner) // 2
    model = tokens_ref.shape[1]
    peer = peer_device()
    previous = (lax.rem(seq - 1 + count, count), head, batch)
    pieces = inner // PIECE
    step_at = width
    query_at = step_at + LANES
    memory_at = query_at + query_weight.shape[1]
    if merged:
        greet_all(pltpu.get_barrier_semaphore(), True)
        reduction = Reduction(chunks, list(early) + [g_side_ref], outs, refs, came)
        reduction.allow(sum(1 for c in chunks if c[0] < len(early)))
        advance = reduction.advance
        for load in loads:
            load.wait()
    else:
        greet_seq(pltpu.get_barrier_semaphore(), 1)

        def advance():
            return None

    spread_ref[...] = spread_matrix(inner, HD)

    def chain_copy(p):
        columns = pl.ds(p * PIECE, PIECE)
        return exchange(
            chain_out.at[:, columns],
            chain_in.at[:, columns],
            sem_chain.at[0, p],
            sem_chain.at[1, p],
            previous,
        )

    def memory_copy(step):
        place = lax.rem(seq - step + count, count)
        return exchange(
            d_memory_ref.at[place],
            memory_recv.at[step - 1],
            sem_memory.at[0, step],
            sem_memory.at[1, step],
            (place, head, batch),
        )

    halo_copy = exchange(
        d_conv.at[pl.ds(0, HALO)],
        d_conv.at[pl.ds(rows, HALO)],
        sem_halo.at[0],
        sem_halo.at[1],
        previous,
    )
    maps_copy = exchange(maps_send, maps_recv, sem_maps.at[0], sem_maps.at[1], peer)

    def norm_copy(i):
        at = tile_rows(i)
        return exchange(
            norm_send.at[at], norm_recv.at[at], sem_norm.at[0, i], sem_norm.at[1, i], peer
        )

    def input_map(at):
        return act[at, inner : inner + state_width].astype(jnp.bfloat16)

    def output_map(at):
        return act[at, inner + state_width :].astype(jnp.bfloat16)

    def keep_of(c, start):
        last = cum_ref[tile_rows(c), :][CHUNK - 1 :]
        keep = jnp.broadcast_to(jnp.exp(last) * start[CHUNK - 1 :], (HALO, LANES))
        return spread_heads(keep, spread_ref[...])

    def carried_of(c, start):
        return spread_heads(jnp.exp(cum_ref[tile_rows(c), :]) * start, spread_ref[...])

    def activate(i):
        at = tile_rows(i)
        value = conv_ref[at, :]
        act[at, :] = value * sigmoid(value)

    each(tiles, activate)
    local[...] = jnp.zeros_like(local)
    total[...] = jnp.ones_like(total)

    def local_chunk(step):
        c = tiles - 1 - step
        at = tile_rows(c)
        _, start, _ = chunk_flags(seg_ref, c)
        keep = keep_of(c, start)
        value = (d_y_ref[at, :] * carried_of(c, start)).astype(jnp.bfloat16)
        fresh = matmul_first(output_map(at), value)
        added[c] = fresh
        local[...] = local[...] * keep[:1] + fresh
        total[...] = total[...] * keep

    each(tiles, local_chunk)

    @pl.when(seq == count - 1)
    def _():
        state[...] = jnp.zeros_like(state)
        chain_out[...] = local[...].astype(jnp.bfloat16)
        if count > 1:
            for p in range(pieces):
                chain_copy(p).start()

    if merged:
        first = seq * rows
        grads[...] = jnp.zeros_like(grads)

        def attention_block(i):
            at = tile_rows(i)
            d_turned = attend_back_block(
                first,
                0,
                (first + i * TILE + TILE - 1) // KEY_TILE,
                i,
                query_ref[at, :],
                d_attention_ref[at, :],
                attention_ref[at, :],
                logs_ref[i][:1],
                lambda key_at: memory_ref[key_at, :],
                seg_ref,
                key_seg_ref,
                grads,
            )
            for pair, tile in enumerate(unstacked_heads(d_turned, True)):
                turned = tile * table_ref[at, :LANES] - turn_half(tile) * table_ref[at, LANES:]
                columns = pl.ds(query_at + pair * LANES, LANES)
                side[at, columns] = turned.astype(jnp.bfloat16)

        span(0, 1, attention_block)
        advance()

    def chain_wait(p):
        columns = pl.ds(p * PIECE, PIECE)
        chain_copy(p).wait_recv()
        came = chain_in[:, columns].astype(jnp.float32)
        state[:, columns] = came
        return came

    @pl.when((seq > 0) & (seq < count - 1))
    def _():
        for p in range(pieces):
            columns = pl.ds(p * PIECE, PIECE)
            came = chain_wait(p)
            chain_out[:, columns] = (came * total[:1, columns] + local[:, columns]).astype(
                jnp.bfloat16
            )
            chain_copy(p).start()

    if merged:
        for i in range(1, tiles):
            span(i, i + 1, attention_block)
            advance()

        def low_block(place):
            at = pl.ds(pl.multiple_of(place * rows, rows), rows)
            d_memory_ref[place] = grads[at, :].astype(jnp.bfloat16)

        each(count, low_block)

    def memory_start(step, carry):
        @pl.when(seq - step >= 0)
        def _():
            memory_copy(step).start()

        return carry

    lax.fori_loop(1, count, memory_start, 0)
    skip_sum[...] = jnp.zeros_like(skip_sum)

    def inside_chunk(c):
        at = tile_rows(c)
        own, start, _ = chunk_flags(seg_ref, c)
        cum = cum_ref[at, :]
        turned = cum.T
        spread = spread_ref[...]
        low_in, low_out = input_map(at), output_map(at)
        allowed = ordered(CHUNK).astype(jnp.float32).T * jnp.where(own == own.T, 1.0, 0.0)
        meet = matmul_last(low_in, low_out) * allowed
        value = act[at, :inner]
        scaled = value * spread_heads(soft_plus(raw_ref[at, :]), spread)
        d_y = d_y_ref[at, :]
        d_meet = jnp.zeros((CHUNK, CHUNK), jnp.float32)
        for i in range(inner // LANES):
            columns = slice(i * LANES, (i + 1) * LANES)
            d_tile = d_y[:, columns]
            d_mixing = matmul_last(halves(scaled[:, columns], HD), d_tile.astype(jnp.bfloat16))
            mixing = []
            for k, h in enumerate((2 * i, 2 * i + 1)):
                gap = turned[h : h + 1, :] - cum[:, h : h + 1]
                fade = jnp.exp(jnp.minimum(gap, 0.0))
                mixing.append(meet * fade)
                d_meet = d_meet + d_mixing[k * CHUNK : (k + 1) * CHUNK] * fade
            d_scaled[at, columns] = matmul(
                jnp.concatenate(mixing, axis=1).astype(jnp.bfloat16), halves(d_tile, HD)
            )
        d_meet = (d_meet * allowed).astype(jnp.bfloat16)
        d_maps[at, :state_width] = matmul(d_meet, low_out)
        carried = (d_y * carried_of(c, start)).astype(jnp.bfloat16)
        d_maps[at, state_width:] = matmul_first(d_meet, low_in) + matmul_last(
            carried, states_ref[c]
        )
        product = d_y * value
        skip_sum[...] += jnp.sum(product, axis=0, keepdims=True)
        low = d_y.astype(jnp.bfloat16).astype(jnp.float32)
        row_term[at, :] = sum_heads(low * (y_ref[at, :] - skip_ref[...] * value), spread)

    span(0, tiles // 2, inside_chunk)
    advance()
    span(tiles // 2, tiles, inside_chunk)
    advance()

    @pl.when((seq == 0) & (seq < count - 1))
    def _():
        for p in range(pieces):
            chain_wait(p)

    if merged:
        small_in[...] = jnp.zeros_like(small_in)
        small_in[4:5, :inner] = mamba_gain_ref[...]
        small_in[6:7, :] = feed_gain_ref[...]
    else:
        g_heads_ref[...] = jnp.zeros_like(g_heads_ref)

    gain_row = 5 if merged else 0

    def add_heads(k, values):
        row, lane = (7, k * LANES) if merged else (k, 0)
        g_heads_ref[row : row + 1, lane : lane + LANES] += values

    upper = jnp.where(ordered(CHUNK), 1.0, 0.0).T

    def across_chunk(step):
        c = tiles - 1 - step
        at = tile_rows(c)
        _, start, end = chunk_flags(seg_ref, c)
        spread = spread_ref[...]
        cum = cum_ref[at, :]
        last = cum[CHUNK - 1 :]
        now = state[...]
        low = now.astype(jnp.bfloat16)
        raw = raw_ref[at, :]
        steps = soft_plus(raw)
        steps_wide = spread_heads(steps, spread)
        value = act[at, :inner]
        scaled = value * steps_wide
        weight = spread_heads(jnp.exp(last - cum) * end, spread)
        d_value = d_scaled[at, :] + matmul(input_map(at), low) * weight
        d_maps[at, :state_width] += matmul_last((scaled * weight).astype(jnp.bfloat16), low)
        final = jnp.sum(
            states_ref[c + 1].astype(jnp.float32) * low.astype(jnp.float32), axis=0, keepdims=True
        )
        final = sum_heads(jnp.broadcast_to(final, (HALO, inner)), spread)[:1]
        low_scaled = scaled.astype(jnp.bfloat16).astype(jnp.float32)
        d_cum = row_term[at, :] - sum_heads(low_scaled * d_value, spread)
        d_rate = jnp.dot(upper, d_cum, precision=highest) + final
        rate = rate_ref[...]
        d_steps = sum_heads(value * d_value, spread) + rate * d_rate
        d_raw = d_steps * sigmoid(raw)
        add_heads(0, rate * jnp.sum(steps * d_rate, axis=0, keepdims=True))
        add_heads(1, jnp.sum(d_raw, axis=0, keepdims=True))
        side[at, step_at:query_at] = d_raw.astype(jnp.bfloat16)
        d_conv[at, :inner] = steps_wide * d_value + skip_ref[...] * d_y_ref[at, :]
        state[...] = now * keep_of(c, start)[:1] + added[c]

    span(0, tiles // 2, across_chunk)
    advance()
    span(tiles // 2, tiles, across_chunk)
    advance()
    add_heads(2, sum_heads(jnp.broadcast_to(skip_sum[:1], (HALO, inner)), spread_ref[...])[:1])
    maps_send[...] = d_maps[...].astype(jnp.bfloat16)
    maps_copy.start()

    def copy_tile(i):
        at = tile_rows(i)
        hidden = tokens_ref[at, :].astype(jnp.float32)
        inverse = lax.rsqrt(jnp.mean(hidden * hidden, axis=1, keepdims=True) + eps_norm)
        normed[at, :] = (hidden * inverse * gain_ref[...]).astype(jnp.bfloat16)

    each(tiles, copy_tile)
    maps_copy.wait()

    def conv_back_tile(i):
        at = tile_rows(i)
        d_conv[at, inner:] = maps_send[at, :].astype(jnp.float32) + maps_recv[at, :].astype(
            jnp.float32
        )
        value = conv_ref[at, :]
        sig = sigmoid(value)
        d_conv[at, :] = d_conv[at, :] * (sig * (1.0 + value * (1.0 - sig)))

    each(tiles, conv_back_tile)

    @pl.when(seq > 0)
    def _():
        halo_copy.start()

    @pl.when(seq == count - 1)
    def _():
        d_conv[pl.ds(rows, HALO), :] = jnp.zeros((HALO, width), jnp.float32)

    @pl.when(seq < count - 1)
    def _():
        halo_copy.wait_recv()

    if not merged:
        g_taps_ref[...] = jnp.zeros_like(g_taps_ref)

    def taps_tile(i):
        at = tile_rows(i)
        window_at = pl.ds(pl.multiple_of(i * TILE, TILE), TILE + HALO)
        seg = seg_ref[pl.ds(pl.multiple_of(i * TILE, TILE), TILE + 2 * HALO), :]
        own = seg[HALO : HALO + TILE]
        before = [
            jnp.where(seg[HALO - 3 + k : HALO - 3 + k + TILE] == own, 1.0, 0.0) for k in range(3)
        ]
        after = [
            jnp.where(seg[HALO + 3 - k : HALO + 3 - k + TILE] == own, 1.0, 0.0) for k in range(3)
        ]
        for j in range(width // LANES):
            columns = slice(j * LANES, (j + 1) * LANES)
            window = pre_ref[window_at, columns]
            grads = d_conv[window_at, columns]
            own_grad = grads[:TILE]
            summed = taps_ref[3:4, columns] * own_grad
            g_taps_ref[3:4, columns] += jnp.sum(own_grad * window[HALO:], axis=0, keepdims=True)
            for k in range(3):
                summed = summed + taps_ref[k : k + 1, columns] * (
                    grads[3 - k : 3 - k + TILE] * after[k]
                )
                g_taps_ref[k : k + 1, columns] += jnp.sum(
                    own_grad * (window[HALO - 3 + k : HALO - 3 + k + TILE] * before[k]),
                    axis=0,
                    keepdims=True,
                )
            side[at, j * LANES : (j + 1) * LANES] = summed.astype(jnp.bfloat16)

    each(tiles, taps_tile)
    advance()

    def memory_wait(step, carry):
        @pl.when(seq - step >= 0)
        def _():
            memory_copy(step).wait_send()

        @pl.when(seq + step < count)
        def _():
            memory_copy(step).wait_recv()

        return carry

    lax.fori_loop(1, count, memory_wait, 0)

    def memory_tile(i):
        at = tile_rows(i)

        def one(step, carry):
            came = memory_recv[step - 1, at, :].astype(jnp.float32)
            return carry + jnp.where(seq + step < count, came, 0.0)

        grad = lax.fori_loop(1, count, one, d_memory_ref[seq, at, :].astype(jnp.float32))
        lane = lax.broadcasted_iota(jnp.int32, grad.shape, 1)
        turned = grad * table_ref[at, :LANES] - turn_half(grad) * table_ref[at, LANES:]
        side[at, memory_at : memory_at + LANES] = jnp.where(lane < HD, turned, grad).astype(
            jnp.bfloat16
        )
        if not merged:
            side[at, query_at:memory_at] = d_query_ref[at, :]

    each(tiles, memory_tile)

    def weight_block(k):
        size = model // count
        block = pl.ds(pl.multiple_of(k * size, LANES), size)
        grad = matmul_first(normed[:, block], side[...])
        if merged:
            bits = seq_bits()
            g_side_ref[place_bits(k, bits)] = grad.reshape(g_side_ref.shape[bits:]).astype(
                jnp.bfloat16
            )
        else:
            g_side_ref[block, :] = grad.astype(jnp.bfloat16)

    each(count, weight_block)
    if merged:
        reduction.allow(len(chunks))
    advance()

    def norm_tile(i):
        at = tile_rows(i)
        part = (
            matmul_last(d_gate_z_ref[at, :], gate_weight[...])
            + matmul_last(side[at, :inner], input_weight[...])
            + matmul_last(side[at, inner:step_at], maps_weight[...]) / lax.axis_size("head")
            + matmul_last(side[at, step_at:query_at], step_weight[...])
            + matmul_last(side[at, query_at:memory_at], query_weight[...])
            + matmul_last(side[at, memory_at:], memory_weight[...])
        )
        norm_send[at, :] = part.astype(jnp.bfloat16)
        norm_copy(i).start()

    each(tiles, norm_tile)

    advance()
    if not merged:
        g_gain_ref[...] = jnp.zeros_like(g_gain_ref)

    def last_tile(i):
        at = tile_rows(i)
        norm_copy(i).wait()
        d_norm = norm_send[at, :].astype(jnp.float32) + norm_recv[at, :].astype(jnp.float32)
        hidden = tokens_ref[at, :].astype(jnp.float32)
        inverse = lax.rsqrt(jnp.mean(hidden * hidden, axis=1, keepdims=True) + eps_norm)
        e_one = d_norm * gain_ref[...]
        cross = jnp.sum(e_one * hidden, axis=1, keepdims=True) / model
        d_tokens_ref[at, :] = (
            d_second_ref[at, :] + inverse * e_one - hidden * (inverse * inverse * inverse * cross)
        )
        g_gain_ref[gain_row : gain_row + 1, :] += jnp.sum(
            d_norm * hidden * inverse, axis=0, keepdims=True
        )

    each(tiles, last_tile)
    if merged:
        small_sum = SmallSum(small_in, small_buf, sem_small)
        small_sum.start()
        reduction.finish()
        small_out[...] = small_sum.finish()

    @pl.when(seq > 0)
    def _():
        halo_copy.wait_send()
        for p in range(pieces):
            chain_copy(p).wait_send()


def mixer_back(common, saved, attention, grads=None, came=()):
    tokens = common[0]
    rows, model = tokens.shape
    gate_weight, query_weight, memory_weight, taps = common[4], common[8], common[9], common[10]
    merged = grads is not None
    count = lax.axis_size("seq")
    inner = gate_weight.shape[1]
    width = taps.shape[1]
    state_width = (width - inner) // 2
    tiles = rows // CHUNK
    pieces = inner // PIECE
    memory_width = memory_weight.shape[1]
    side = width + LANES + query_weight.shape[1] + memory_width
    vmem = pl.BlockSpec(memory_space=pltpu.VMEM)
    hbm = pl.BlockSpec(memory_space=pl.ANY)
    low, full = jnp.bfloat16, jnp.float32
    shape = jax.ShapeDtypeStruct
    operands = [*common, *saved]
    in_specs = [vmem] * (len(operands) + len(attention))
    operands += attention
    chunks = None
    scratch = [
        pltpu.VMEM((rows, model), low),
        pltpu.VMEM((LANES, inner), low),
        pltpu.VMEM((rows, width), full),
        pltpu.VMEM((rows + HALO, width), full),
        pltpu.VMEM((rows, inner), full),
        pltpu.VMEM((rows, 2 * state_width), full),
        pltpu.VMEM((rows, LANES), full),
        pltpu.VMEM((tiles, state_width, inner), full),
        pltpu.VMEM((state_width, inner), full),
        pltpu.VMEM((HALO, inner), full),
        pltpu.VMEM((state_width, inner), full),
        pltpu.VMEM((1, inner), full),
        pltpu.VMEM((rows, side), low),
        pltpu.VMEM((state_width, inner), low),
        pltpu.VMEM((state_width, inner), low),
        pltpu.VMEM((rows, 2 * state_width), low),
        pltpu.VMEM((rows, 2 * state_width), low),
        pltpu.VMEM((max(count - 1, 1), rows, memory_width), low),
        pltpu.VMEM((rows, model), low),
        pltpu.VMEM((rows, model), low),
        pltpu.SemaphoreType.DMA((2, count)),
        pltpu.SemaphoreType.DMA((2,)),
        pltpu.SemaphoreType.DMA((2, pieces)),
        pltpu.SemaphoreType.DMA((2,)),
        pltpu.SemaphoreType.DMA((2, tiles)),
    ]
    if merged:
        blocks = list(grads)
        widths = [g.shape[-1] for g in grads] + [side]
        chunks = column_chunks(widths)
        loaded = [pltpu.VMEM(x.shape, x.dtype) for x in operands]
        scratch = loaded + [pltpu.SemaphoreType.DMA((len(loaded),))] + scratch
        operands += blocks + list(came)
        in_specs = [hbm] * len(operands)
        own = blocks[0].shape[-2]
        small = (HALO, model)
        out_shape = (
            [shape((rows, model), full)]
            + [shape((2, 2, own, w), low) for w in widths]
            + [shape(small, full)]
        )
        scratch += [
            pltpu.VMEM(blocks[0].shape[:-1] + (side,), low),
            pltpu.VMEM((count * rows, memory_width), full),
            pltpu.VMEM((count, rows, memory_width), low),
        ]
        scratch += small_scratch(small) + reduction_scratch(chunks, widths, own)
    else:
        out_shape = [
            shape((rows, model), full),
            shape((model, side), low),
            shape((HALO, width), full),
            shape((1, model), full),
            shape((HALO, LANES), full),
        ]
    return pl.pallas_call(
        functools.partial(mixer_back_kernel, merged, chunks),
        out_shape=out_shape,
        in_specs=in_specs,
        out_specs=[vmem] * len(out_shape),
        scratch_shapes=scratch,
        compiler_params=pltpu.CompilerParams(
            collective_id=3, has_side_effects=True, vmem_limit_bytes=62 << 20
        ),
        name="mixer_back",
    )(*operands)


def finish_kernel(sizes, down, feed, mixed, gate, side, small, *outs):
    inner, maps, heads, query, own = sizes
    full = jnp.float32
    seq = lax.axis_index("seq")
    wide = small.shape[1]
    columns = [0, inner, inner + maps, inner + maps + heads]
    query_at = inner + maps + LANES
    (
        o_gate_z,
        o_inner,
        o_maps,
        o_step,
        o_output,
        o_query,
        o_memory,
        o_attention,
        o_gate,
        o_lift,
        o_down,
        o_conv_inner,
        o_conv_maps,
        o_mixer_gain,
        o_rate,
        o_bias,
        o_skip,
        o_mamba_gain,
        o_feed_gain,
    ) = outs
    o_gate_z[...] = gate[...].astype(full)
    o_inner[...] = side[:, : columns[1]].astype(full)
    o_maps[...] = side[:, columns[1] : columns[2]].astype(full)
    o_step[...] = side[:, columns[2] : columns[2] + LANES].astype(full)[:, :heads]
    o_query[...] = side[:, query_at : query_at + query].astype(full)
    o_memory[...] = side[:, query_at + query :].astype(full)
    o_output[...] = mixed[:, :inner].astype(full)
    o_attention[...] = mixed[:, inner:].astype(full)
    o_gate[...] = feed[:, : o_gate.shape[1]].astype(full)
    o_lift[...] = feed[:, o_gate.shape[1] :].astype(full)
    o_down[...] = down[...].astype(full)
    value = small[...]
    o_conv_inner[...] = value[:4, :inner]
    o_conv_maps[...] = value[:4, inner:]
    turned = pltpu.roll(value, lax.rem(wide - seq * own, wide), 1)
    o_mixer_gain[...] = turned[5:6, :own]
    o_feed_gain[...] = turned[6:7, :own]
    for k, out in enumerate((o_rate, o_bias, o_skip)):
        out[...] = value[7:8, k * LANES : (k + 1) * LANES][:, :heads]
    o_mamba_gain[...] = value[4:5, :inner]


def finish_outputs(sums, small, sizes):
    inner, maps, heads, query, own = sizes
    rows = own
    sums = [s.reshape(rows, s.shape[-1]) for s in sums]
    down, feed, mixed, gate, side = sums
    half = feed.shape[1] // 2
    memory = side.shape[1] - inner - maps - LANES - query
    shapes = [
        (rows, inner),
        (rows, inner),
        (rows, maps),
        (rows, heads),
        (rows, inner),
        (rows, query),
        (rows, memory),
        (rows, mixed.shape[1] - inner),
        (rows, half),
        (rows, half),
        (rows, half),
        (4, inner),
        (4, maps),
        (1, own),
        (1, heads),
        (1, heads),
        (1, heads),
        (1, inner),
        (1, own),
    ]
    vmem = pl.BlockSpec(memory_space=pltpu.VMEM)
    return pl.pallas_call(
        functools.partial(finish_kernel, sizes),
        out_shape=[jax.ShapeDtypeStruct(s, jnp.float32) for s in shapes],
        in_specs=[vmem] * 6,
        out_specs=[vmem] * len(shapes),
        compiler_params=pltpu.CompilerParams(vmem_limit_bytes=60 << 20),
        name="finish_outputs",
    )(*sums, small)


def rotation_table(position):
    half = HD // 2
    lane = jnp.arange(LANES)
    inverse_freq = rope_base ** (-(lane % half).astype(jnp.float32) / half)
    angles = position.astype(jnp.float32)[:, None] * inverse_freq[None, :]
    sign = jnp.where(lane % HD < half, -1.0, 1.0)
    return jnp.concatenate([jnp.cos(angles), sign[None, :] * jnp.sin(angles)], axis=1)


def body(
    tokens,
    seg_ids,
    mixer_gain,
    mamba_gate,
    mamba_input,
    mamba_maps,
    mamba_step,
    conv_inner,
    conv_maps,
    log_rate,
    step_bias,
    skip_gain,
    mamba_gain,
    mamba_output,
    query_weight,
    memory_weight,
    attention_out,
    feed_gain,
    gate_weight,
    lift_weight,
    down_weight,
    cotangent,
):
    tokens, cotangent = tokens[0], cotangent[0]
    rows, wide = tokens.shape
    tap_count, inner = conv_inner.shape
    head_count = log_rate.shape[0]
    segments = seg_ids[0]
    offset = lax.axis_index("seq") * rows
    padded = jnp.concatenate(
        [jnp.full((HALO,), -1, jnp.int32), segments, jnp.full((HALO,), -2, jnp.int32)]
    )
    window = lax.dynamic_slice_in_dim(padded, offset, rows + 2 * HALO)
    window_wide = jnp.broadcast_to(
        window.astype(jnp.float32)[:, None], (rows + 2 * HALO, LANES)
    )
    key_segments = jnp.broadcast_to(
        segments.astype(jnp.float32)[:, None], (segments.shape[0], LANES)
    )
    table = rotation_table(offset + jnp.arange(rows, dtype=jnp.int32))
    starts = offset + jnp.arange(rows // TILE, dtype=jnp.int32) * TILE
    reach = segments[KEY_TILE - 1 :: KEY_TILE]
    low = jnp.sum(
        (reach[None, :] < window[HALO : HALO + rows : TILE][:, None]).astype(jnp.int32), axis=1
    )
    spans = (offset[None], low, (starts + TILE - 1) // KEY_TILE)

    def lanes_of(values):
        return jnp.pad(values, (0, LANES - head_count))[None]

    step_weight = jnp.pad(mamba_step, ((0, 0), (0, LANES - head_count)))
    taps = jnp.pad(
        jnp.concatenate([conv_inner, conv_maps], axis=1), ((0, HALO - tap_count), (0, 0))
    )
    bias, rate = lanes_of(step_bias), lanes_of(-jnp.exp(log_rate))
    skip = jnp.repeat(skip_gain, inner // head_count)[None]
    common = [
        tokens,
        mixer_gain[None],
        window_wide,
        table,
        mamba_gate,
        mamba_input,
        mamba_maps,
        step_weight,
        query_weight,
        memory_weight,
        taps,
    ]
    gate_z, pre, conv, raw, cum, y, states, query, memory = mixer_forward(
        *common, bias, rate, skip
    )
    all_memory = memory.reshape(memory.shape[0] * rows, memory.shape[2])
    attention, attention_low, logs = attention_forward(
        spans, query, all_memory, window_wide, key_segments
    )
    (
        layer_out,
        d_second,
        d_y,
        d_gate_z,
        d_attention,
        g_feed,
        g_mixed,
        g_down,
        g_gate,
        g_feed_gain,
        g_mamba_gain,
        *came,
    ) = feed_layer(
        y,
        gate_z,
        attention_low,
        tokens,
        cotangent,
        mixer_gain,
        mamba_gain,
        feed_gain,
        mamba_output,
        attention_out,
        gate_weight,
        lift_weight,
        down_weight,
    )
    common += [rate, skip]
    saved = [pre, conv, raw, cum, y, states, d_second, d_y, d_gate_z]
    early = [g_down, g_feed, g_mixed, g_gate]
    if lax.axis_size("seq") == 4:
        grad_tokens, *sums, small = mixer_back(
            common,
            saved,
            [
                query,
                all_memory,
                key_segments,
                attention,
                logs,
                d_attention,
                g_feed_gain,
                g_mamba_gain,
            ],
            early,
            came,
        )
    else:
        d_query, d_memory = attention_back(
            spans, query, all_memory, window_wide, key_segments, attention, logs, d_attention, table
        )
        grad_tokens, g_side, g_taps, g_mixer_gain, g_heads = mixer_back(
            common, saved, [d_query, d_memory.reshape(memory.shape)]
        )
        *sums, small = reduce_gradients(
            early + [g_side],
            jnp.concatenate(
                [
                    g_taps[:tap_count],
                    jnp.pad(g_mamba_gain, ((0, 0), (0, wide - inner))),
                    g_mixer_gain,
                    g_feed_gain,
                    jnp.pad(g_heads[:3].reshape(1, 3 * LANES), ((0, 0), (0, wide - 3 * LANES))),
                ],
                axis=0,
            ),
        )
    sizes = (
        inner,
        conv_maps.shape[1],
        head_count,
        query_weight.shape[1],
        wide // lax.axis_size("seq"),
    )
    (
        o_gate_z,
        o_inner,
        o_maps,
        o_step,
        o_output,
        o_query,
        o_memory,
        o_attention,
        o_gate,
        o_lift,
        o_down,
        o_conv_inner,
        o_conv_maps,
        o_mixer_gain,
        o_rate,
        o_bias,
        o_skip,
        o_mamba_gain,
        o_feed_gain,
    ) = finish_outputs(sums, small, sizes)
    return (
        layer_out[None],
        grad_tokens[None],
        o_mixer_gain[0],
        o_gate_z,
        o_inner,
        o_maps,
        o_step,
        o_conv_inner,
        o_conv_maps,
        o_rate[0],
        o_bias[0],
        o_skip[0],
        o_mamba_gain[0],
        o_output,
        o_query,
        o_memory,
        o_attention,
        o_feed_gain[0],
        o_gate,
        o_lift,
        o_down,
    )


def solution(mesh):
    return jax.shard_map(
        body,
        mesh=mesh,
        in_specs=(
            P("batch", "seq", None),
            P("batch", None),
            P(),
            P(None, "head"),
            P(None, "head"),
            P(),
            P(None, "head"),
            P(None, "head"),
            P(),
            P("head"),
            P("head"),
            P("head"),
            P("head"),
            P(None, "head"),
            P(None, "head"),
            P(None, "head"),
            P(None, "head"),
            P(),
            P(None, "head"),
            P(None, "head"),
            P(None, "head"),
            P("batch", "seq", None),
        ),
        out_specs=(
            P("batch", "seq", None),
            P("batch", "seq", None),
            P("seq"),
            P("seq", "head"),
            P("seq", "head"),
            P("seq", None),
            P("seq", "head"),
            P(None, "head"),
            P(),
            P("head"),
            P("head"),
            P("head"),
            P("head"),
            P("seq", "head"),
            P("seq", "head"),
            P("seq", "head"),
            P("seq", "head"),
            P("seq"),
            P("seq", "head"),
            P("seq", "head"),
            P("seq", "head"),
        ),
        check_vma=False,
    )
```

```python
import functools

import jax
import jax.numpy as jnp
from jax import lax
from jax.experimental import pallas as pl
from jax.experimental.pallas import tpu as pltpu
from jax.sharding import PartitionSpec as P

HD = 64
eps_norm = 1e-05
rope_base = 10000.0
neg_large = -1e30
highest = lax.Precision.HIGHEST


LANES = 128
MOST = 512
TAIL = (512, 384, 256, 128, 128, 128)
AHEAD = 7
EARLIER = 3
LAG = 3
PATTERN = (0, 1, 2, 0, 1, 3, 0, 1, 0, 1, 2, 0, 1, 3, 0, 1)
MESH = pl.DeviceIdType.MESH


def exchange(source, target, send_sem, recv_sem, device):
    return pltpu.make_async_remote_copy(
        src_ref=source,
        dst_ref=target,
        send_sem=send_sem,
        recv_sem=recv_sem,
        device_id=device,
        device_id_type=MESH,
    )


def each(count, action):
    span(0, count, action)


def span(first, last, action):
    lax.fori_loop(first, last, lambda i, carry: (action(i), carry)[1], 0)


def column_chunks(widths):
    chunks = []
    for group, width in enumerate(widths):
        count = -(-width // MOST)
        tiles = width // LANES
        sizes = [(tiles // count + (1 if k < tiles % count else 0)) * LANES for k in range(count)]
        if group == len(widths) - 1 and width == sum(TAIL):
            sizes = TAIL
        start = 0
        for size in sizes:
            chunks.append((group, start, size))
            start += size
    return chunks


def seq_bits():
    return (lax.axis_size("seq") - 1).bit_length()


def place_bits(place, bits):
    return tuple(lax.rem(place // 2 ** (bits - 1 - b), 2) for b in range(bits))


def seq_blocks(grad):
    bits = seq_bits() + 2
    return grad.reshape((2,) * bits + (grad.shape[0] >> bits, grad.shape[1]))


def peer_device():
    return (lax.axis_index("seq"), 1 - lax.axis_index("head"), lax.axis_index("batch"))


def other_device(step):
    seq, batch = lax.axis_index("seq"), lax.axis_index("batch")
    batches = lax.axis_size("batch")
    place = lax.rem(seq * batches + batch + step, lax.axis_size("seq") * batches)
    return (place // batches, lax.axis_index("head"), lax.rem(place, batches))


def greet_all(barrier, with_peer):
    world = lax.axis_size("seq") * lax.axis_size("batch")
    span(
        1,
        world,
        lambda step: pl.semaphore_signal(
            barrier, inc=1, device_id=other_device(step), device_id_type=MESH
        ),
    )
    if with_peer:
        pl.semaphore_signal(barrier, inc=1, device_id=peer_device(), device_id_type=MESH)
    pl.semaphore_wait(barrier, world - 1 + (1 if with_peer else 0))


class SmallSum:
    def __init__(self, source, slots, sems):
        self.source, self.slots, self.sems = source, slots, sems
        self.world = slots.shape[0]
        self.mine = lax.axis_index("seq") * lax.axis_size("batch") + lax.axis_index("batch")

    def copy(self, step):
        return exchange(
            self.source,
            self.slots.at[self.mine],
            self.sems.at[0, step],
            self.sems.at[1, step],
            other_device(step),
        )

    def start(self):
        span(1, self.world, lambda step: self.copy(step).start())

    def finish(self):
        span(1, self.world, lambda step: self.copy(step).wait())
        self.slots[self.mine] = self.source[...]
        return lax.fori_loop(
            1, self.world, lambda k, total: total + self.slots[k], self.slots[0]
        )


def small_scratch(shape):
    world = lax.axis_size("seq") * lax.axis_size("batch")
    return [
        pltpu.VMEM(shape, jnp.float32),
        pltpu.VMEM((world,) + shape, jnp.float32),
        pltpu.SemaphoreType.DMA((2, world)),
    ]


class Reduction:
    def __init__(self, chunks, sources, outs, scratch, given=()):
        self.chunks, self.sources, self.outs, self.given = chunks, sources, outs, given
        groups = len(sources)
        self.bits = seq_bits() + 2
        scratch = list(scratch)
        self.parts = [scratch[k * groups : (k + 1) * groups] for k in range(self.bits)]
        self.own, self.sem_own, self.sem_halve, self.sem_back = scratch[self.bits * groups :]
        self.setup()

    def setup(self):
        self.seq, self.head = lax.axis_index("seq"), lax.axis_index("head")
        self.batch = lax.axis_index("batch")
        place = self.seq * 4 + self.batch
        self.mine = [lax.rem(place // 2 ** (self.bits - 1 - k), 2) for k in range(self.bits)]
        self.done = [0] * (self.bits + 2)
        self.sent = self.held = self.limit = 0

    def peer(self, bit):
        step = (1 - 2 * self.mine[bit]) * 2 ** (self.bits - 1 - bit)
        if bit < self.bits - 2:
            return (self.seq + step // 4, self.head, self.batch)
        return (self.seq, self.head, self.batch + step)

    def order(self, k):
        low, high, last = self.bits - 1, self.bits - 2, self.bits - 3
        rest = [b for b in range(self.bits - 3, -1, -1)]
        if last < 0:
            return [low, high] if k % 2 == 0 else [high, low]
        kind = PATTERN[k % len(PATTERN)]
        if kind == 0:
            return [low, high] + rest
        if kind == 1:
            return [high, low] + rest
        if kind == 2:
            return [last, low, high] + rest[1:]
        return [last, high, low] + rest[1:]

    def place(self, k):
        group, start, size = self.chunks[k]
        return group, pl.ds(start, size)

    def cut(self, k, step, kept):
        order = self.order(k)
        left = [b for b in range(self.bits) if b not in order[:step]]
        bit = order[step]
        value = self.mine[bit] if kept else 1 - self.mine[bit]
        return tuple(value if b == bit else slice(None) for b in left)

    def halve_copy(self, k, step):
        group, columns = self.place(k)
        source = self.sources[group] if step == 0 else self.parts[step - 1][group]
        target = self.parts[step][group]
        away = self.cut(k, step, False)
        return exchange(
            source.at[away + (slice(None), columns)],
            target.at[(slice(None),) * (len(away) - 1) + (slice(None), columns)],
            self.sem_halve.at[0, k, step],
            self.sem_halve.at[1, k, step],
            self.peer(self.order(k)[step]),
        )

    def first_copy(self, k):
        group, columns = self.place(k)
        if group >= len(self.given) or k >= EARLIER:
            return self.halve_copy(k, 0)
        where = (slice(None),) * self.bits + (columns,)
        return pltpu.make_async_copy(
            self.given[group].at[where], self.parts[0][group].at[where], self.sem_halve.at[0, k, 0]
        )

    def own_copy(self, k):
        group, columns = self.place(k)
        size = self.chunks[k][2]
        kept = self.cut(k, 0, True)
        return pltpu.make_async_copy(
            self.sources[group].at[kept + (slice(None), columns)],
            self.own.at[(k % 2,) + (slice(None),) * self.bits + (pl.ds(0, size),)],
            self.sem_own.at[k],
        )

    def add(self, k, step):
        group, columns = self.place(k)
        size = self.chunks[k][2]
        target = self.parts[step][group]
        left = self.bits - 1 - step

        def one(index):
            every = index + (slice(None), columns)
            if step == 0:
                own = self.own[(k % 2,) + index + (slice(None), slice(0, size))]
            else:
                kept = self.cut(k, step, True)
                spot = [v for v in kept]
                rest = iter(index)
                spot = tuple(v if not isinstance(v, slice) else next(rest) for v in spot)
                own = self.parts[step - 1][group][spot + (slice(None), columns)]
            value = own + target[every]
            if step == self.bits - 1:
                self.outs[group][self.mine[-2], self.mine[-1], :, columns] = value
            else:
                target[every] = value

        span(
            0,
            2**left,
            lambda n: one(place_bits(n, left)),
        )

    def back_copy(self, k, turn):
        group, columns = self.place(k)
        out = self.outs[group]
        high, low = self.mine[-2], self.mine[-1]
        first_low = self.order(k).index(self.bits - 1) < self.order(k).index(self.bits - 2)
        bit = self.bits - 2 if first_low == (turn == 0) else self.bits - 1
        if turn == 0:
            part = out.at[high, low, :, columns]
        elif first_low:
            part = out.at[:, low, :, columns]
        else:
            part = out.at[high, :, :, columns]
        return exchange(
            part, part, self.sem_back.at[0, k, turn], self.sem_back.at[1, k, turn], self.peer(bit)
        )

    def refill(self):
        while self.sent < min(self.limit, self.done[0] + AHEAD):
            self.first_copy(self.sent).start()
            self.sent += 1
        while self.held < min(self.limit, self.done[0] + 2):
            self.own_copy(self.held).start()
            self.held += 1

    def allow(self, limit):
        self.limit = limit
        self.refill()

    def advance(self):
        stages = self.bits + 2
        for step in range(stages - 1, -1, -1):
            k = self.done[step]
            before = self.done[step - 1] if step else self.limit
            if k >= before or (step and before - k < LAG and before < self.limit):
                continue
            if step < self.bits:
                if step == 0:
                    self.first_copy(k).wait()
                    self.own_copy(k).wait()
                else:
                    self.halve_copy(k, step).wait()
                self.add(k, step)
                if step + 1 < self.bits:
                    self.halve_copy(k, step + 1).start()
                else:
                    self.back_copy(k, 0).start()
            elif step == self.bits:
                self.back_copy(k, 0).wait()
                self.back_copy(k, 1).start()
            else:
                self.back_copy(k, 1).wait()
            self.done[step] += 1
            if step == 0:
                self.refill()

    def finish(self):
        while self.done[-1] < len(self.chunks):
            self.advance()


class FirstHalving(Reduction):
    def __init__(self, chunks, sources, targets, sems):
        self.chunks, self.sources = chunks, sources
        self.bits = seq_bits() + 2
        self.parts, self.sem_halve = [targets], sems
        self.setup()


def reduction_scratch(chunks, widths, rows):
    bits = seq_bits() + 2
    parts = len(chunks)
    most = max(size for _, _, size in chunks)
    low = jnp.bfloat16
    return [
        pltpu.VMEM((2,) * (bits - 1 - step) + (rows, w), low)
        for step in range(bits)
        for w in widths
    ] + [
        pltpu.VMEM((2,) * bits + (rows, most), low),
        pltpu.SemaphoreType.DMA((parts,)),
        pltpu.SemaphoreType.DMA((2, parts, bits)),
        pltpu.SemaphoreType.DMA((2, parts, 2)),
    ]


def reduce_kernel(chunks, *refs):
    count = 1 + max(c[0] for c in chunks)
    sources, refs = refs[:count], refs[count:]
    small_given, refs = refs[0], refs[1:]
    outs, refs = refs[:count], refs[count:]
    small_out, small_in, small_buf, sem_small, *refs = refs
    greet_all(pltpu.get_barrier_semaphore(), False)
    reduction = Reduction(chunks, sources, outs, refs)
    reduction.allow(len(chunks))
    small_in[...] = small_given[...]
    small_sum = SmallSum(small_in, small_buf, sem_small)
    small_sum.start()
    reduction.finish()
    small_out[...] = small_sum.finish()


def reduce_gradients(grads, small):
    widths = [g.shape[1] for g in grads]
    chunks = column_chunks(widths)
    blocks = [seq_blocks(g) for g in grads]
    rows = blocks[0].shape[-2]
    vmem = pl.BlockSpec(memory_space=pltpu.VMEM)
    return pl.pallas_call(
        functools.partial(reduce_kernel, chunks),
        out_shape=[jax.ShapeDtypeStruct((2, 2, rows, w), jnp.bfloat16) for w in widths]
        + [jax.ShapeDtypeStruct(small.shape, jnp.float32)],
        in_specs=[pl.BlockSpec(memory_space=pl.ANY)] * len(grads) + [vmem],
        out_specs=[vmem] * (len(grads) + 1),
        scratch_shapes=small_scratch(small.shape) + reduction_scratch(chunks, widths, rows),
        compiler_params=pltpu.CompilerParams(
            collective_id=0, has_side_effects=True, vmem_limit_bytes=56 << 20
        ),
        name="reduce_gradients",
    )(*blocks, small)


def matmul(former, latter):
    return jnp.dot(former, latter, preferred_element_type=jnp.float32)


def matmul_last(former, latter):
    return lax.dot_general(
        former, latter, (((1,), (1,)), ((), ())), preferred_element_type=jnp.float32
    )


def matmul_first(former, latter):
    return lax.dot_general(
        former, latter, (((0,), (0,)), ((), ())), preferred_element_type=jnp.float32
    )


TILE = 128


def sigmoid(v):
    return 1.0 / (1.0 + jnp.exp(-v))


def greet(barrier, devices):
    for device in devices:
        pl.semaphore_signal(barrier, inc=1, device_id=device, device_id_type=MESH)
    pl.semaphore_wait(barrier, len(devices))


def tile_rows(i):
    return pl.ds(pl.multiple_of(i * TILE, TILE), TILE)


FEED_TILE = 256


def feed_rows(i):
    return pl.ds(pl.multiple_of(i * FEED_TILE, FEED_TILE), FEED_TILE)


def feed_kernel(merged, *refs):
    (
        y_ref,
        gate_z_ref,
        attention_ref,
        tokens_ref,
        cotangent_ref,
        mixer_gain_ref,
        mamba_gain_ref,
        feed_gain_ref,
        mamba_output_ref,
        attention_out_ref,
        gate_weight_hbm,
        lift_weight_hbm,
        down_weight_hbm,
        out_ref,
        d_second_ref,
        d_y_ref,
        d_gate_z_ref,
        d_attention_ref,
        g_feed_ref,
        g_mixed_ref,
        g_down_ref,
        g_gate_ref,
        g_feed_gain_ref,
        g_mamba_gain_ref,
    ) = refs[: 24]
    refs = refs[24:]
    if merged:
        came_refs, refs = refs[:2], refs[2:]
    (
        gate_weight,
        lift_weight,
        down_weight,
        normed,
        gated,
        g_six,
        inverse_six,
        second,
        inverse_two,
        normed2,
        active,
        d_feed,
        d_mix,
        d_gated,
        square_send,
        square_recv,
        cross_send,
        cross_recv,
        mixed_send,
        mixed_recv,
        lift_send,
        lift_recv,
        norm_send,
        norm_recv,
        weight_sem,
        sem_square,
        sem_cross,
        sem_mixed,
        sem_lift,
        sem_norm,
        *sem_first,
    ) = refs
    rows = y_ref.shape[0]
    tiles = rows // FEED_TILE
    mamba_gain = jnp.concatenate(
        [mamba_gain_ref[k : k + 1, :] for k in range(mamba_gain_ref.shape[0])], axis=1
    )
    inner = y_ref.shape[1]
    width = feed_gain_ref.shape[1]
    feed = down_weight.shape[1]
    all_inner = inner * lax.axis_size("head")
    peer = peer_device()
    loads = [
        pltpu.make_async_copy(source, target, weight_sem.at[k])
        for k, (source, target) in enumerate(
            (
                (gate_weight_hbm, gate_weight),
                (lift_weight_hbm, lift_weight),
                (down_weight_hbm, down_weight),
            )
        )
    ]
    for load in loads:
        load.start()
    devices = [peer]
    if merged:
        first = FirstHalving(
            column_chunks((g_down_ref.shape[-1], g_feed_ref.shape[-1]))[:EARLIER],
            [g_down_ref, g_feed_ref],
            came_refs,
            sem_first[0],
        )
        devices += [first.peer(bit) for bit in range(first.bits - 3, first.bits)]
    greet(pltpu.get_barrier_semaphore(), devices)

    def swap(send, recv, sems, i):
        rows_now = feed_rows(i)
        return exchange(send.at[rows_now], recv.at[rows_now], sems.at[0, i], sems.at[1, i], peer)

    def gate_tile(i):
        at = feed_rows(i)
        hidden = tokens_ref[at, :].astype(jnp.float32)
        inverse = lax.rsqrt(jnp.mean(hidden * hidden, axis=1, keepdims=True) + eps_norm)
        normed[at, :] = (hidden * inverse * mixer_gain_ref[...]).astype(jnp.bfloat16)
        gate_now = gate_z_ref[at, :]
        value = y_ref[at, :] * gate_now * sigmoid(gate_now)
        g_six[at, :] = value
        square_send[at, :] = jnp.broadcast_to(
            jnp.sum(value * value, axis=1, keepdims=True), (FEED_TILE, LANES)
        )
        swap(square_send, square_recv, sem_square, i).start()

    each(tiles, gate_tile)

    def mixed_tile(i):
        at = feed_rows(i)
        swap(square_send, square_recv, sem_square, i).wait()
        total = square_send[at, :] + square_recv[at, :]
        inverse = lax.rsqrt(total[:, :1] / all_inner + eps_norm)
        inverse_six[at, :] = jnp.broadcast_to(inverse, (FEED_TILE, LANES))
        low = (g_six[at, :] * inverse * mamba_gain).astype(jnp.bfloat16)
        gated[at, :] = low
        part = matmul_last(low, mamba_output_ref[...]) + matmul_last(
            attention_ref[at, :], attention_out_ref[...]
        )
        mixed_send[at, :] = part.astype(jnp.bfloat16)
        swap(mixed_send, mixed_recv, sem_mixed, i).start()

    each(tiles, mixed_tile)
    for load in loads:
        load.wait()

    def feed_tile(i):
        at = feed_rows(i)
        swap(mixed_send, mixed_recv, sem_mixed, i).wait()
        total = mixed_send[at, :].astype(jnp.float32) + mixed_recv[at, :].astype(jnp.float32)
        hidden = tokens_ref[at, :].astype(jnp.float32) + total
        second[at, :] = hidden
        inverse = lax.rsqrt(jnp.mean(hidden * hidden, axis=1, keepdims=True) + eps_norm)
        inverse_two[at, :] = jnp.broadcast_to(inverse, (FEED_TILE, LANES))
        low = (hidden * inverse * feed_gain_ref[...]).astype(jnp.bfloat16)
        normed2[at, :] = low
        gate_now = matmul(low, gate_weight[...])
        lift_now = matmul(low, lift_weight[...])
        sig = sigmoid(gate_now)
        silu = gate_now * sig
        act = (silu * lift_now).astype(jnp.bfloat16)
        active[at, :] = act
        lift_send[at, :] = matmul_last(act, down_weight[...]).astype(jnp.bfloat16)
        swap(lift_send, lift_recv, sem_lift, i).start()
        d_act = matmul(cotangent_ref[at, :], down_weight[...])
        d_gate = (d_act * lift_now * (sig * (1.0 + gate_now * (1.0 - sig)))).astype(jnp.bfloat16)
        d_lift = (d_act * silu).astype(jnp.bfloat16)
        d_feed[at, :feed] = d_gate
        d_feed[at, feed:] = d_lift
        part = matmul_last(d_gate, gate_weight[...]) + matmul_last(d_lift, lift_weight[...])
        norm_send[at, :] = part.astype(jnp.bfloat16)
        swap(norm_send, norm_recv, sem_norm, i).start()

    each(tiles, feed_tile)
    blocks = lax.axis_size("seq") if merged else width // 256

    def store(target, k, grad):
        if merged:
            index = place_bits(k, seq_bits())
            target[index] = grad.reshape(target.shape[len(index) :]).astype(jnp.bfloat16)
        else:
            target[pl.ds(pl.multiple_of(k * 256, 256), 256), :] = grad.astype(jnp.bfloat16)

    def block_columns(k):
        size = width // blocks
        return pl.ds(pl.multiple_of(k * size, LANES), size)

    def feed_weights(k):
        block = block_columns(k)
        store(g_down_ref, k, matmul_first(cotangent_ref[:, block], active[...]))
        store(g_feed_ref, k, matmul_first(normed2[:, block], d_feed[...]))

    each(blocks, feed_weights)
    if merged:
        for k in range(EARLIER):
            first.halve_copy(k, 0).start()
    g_feed_gain_ref[...] = jnp.zeros_like(g_feed_gain_ref)
    g_mamba_gain_ref[...] = jnp.zeros_like(g_mamba_gain_ref)

    def norm_tile(i):
        at = feed_rows(i)
        swap(norm_send, norm_recv, sem_norm, i).wait()
        d_norm = norm_send[at, :].astype(jnp.float32) + norm_recv[at, :].astype(jnp.float32)
        hidden = second[at, :]
        inverse = inverse_two[at, :][:, :1]
        e_two = d_norm * feed_gain_ref[...]
        g_feed_gain_ref[...] += jnp.sum(d_norm * hidden * inverse, axis=0, keepdims=True)
        cross = jnp.sum(e_two * hidden, axis=1, keepdims=True) / width
        d_hidden = (
            cotangent_ref[at, :].astype(jnp.float32)
            + inverse * e_two
            - hidden * (inverse * inverse * inverse * cross)
        )
        d_second_ref[at, :] = d_hidden
        low = d_hidden.astype(jnp.bfloat16)
        d_mix[at, :] = low
        d_attention_ref[at, :] = matmul(low, attention_out_ref[...])
        d_gated_now = matmul(low, mamba_output_ref[...])
        d_gated[at, :] = d_gated_now
        six = g_six[at, :]
        g_mamba_gain_ref[...] += jnp.sum(
            d_gated_now * six * inverse_six[at, :][:, :1], axis=0, keepdims=True
        )
        cross_send[at, :] = jnp.broadcast_to(
            jnp.sum(d_gated_now * mamba_gain * six, axis=1, keepdims=True), (FEED_TILE, LANES)
        )
        swap(cross_send, cross_recv, sem_cross, i).start()

    each(tiles, norm_tile)

    def gate_back(i):
        at = feed_rows(i)
        swap(cross_send, cross_recv, sem_cross, i).wait()
        cross = (cross_send[at, :] + cross_recv[at, :])[:, :1] / all_inner
        inverse = inverse_six[at, :][:, :1]
        d_six = inverse * (d_gated[at, :] * mamba_gain) - g_six[at, :] * (
            inverse * inverse * inverse * cross
        )
        gate_now = gate_z_ref[at, :]
        sig = sigmoid(gate_now)
        d_y_ref[at, :] = d_six * gate_now * sig
        d_gate_z_ref[at, :] = (
            d_six * y_ref[at, :] * (sig * (1.0 + gate_now * (1.0 - sig)))
        ).astype(jnp.bfloat16)

    each(tiles, gate_back)

    def out_tile(i):
        at = feed_rows(i)
        swap(lift_send, lift_recv, sem_lift, i).wait()
        total = lift_send[at, :].astype(jnp.float32) + lift_recv[at, :].astype(jnp.float32)
        out_ref[at, :] = (second[at, :] + total).astype(jnp.bfloat16)

    each(tiles, out_tile)

    def mixed_weights(k):
        block = block_columns(k)
        store(g_gate_ref, k, matmul_first(normed[:, block], d_gate_z_ref[...]))
        d_mix_now = d_mix[:, block]
        grad = jnp.concatenate(
            [matmul_first(d_mix_now, gated[...]), matmul_first(d_mix_now, attention_ref[...])],
            axis=1,
        )
        store(g_mixed_ref, k, grad)

    each(blocks, mixed_weights)
    if merged:
        for k in range(EARLIER):
            first.halve_copy(k, 0).wait()


def feed_layer(
    y,
    gate_z,
    attention_low,
    tokens,
    cotangent,
    mixer_gain,
    mamba_gain,
    feed_gain,
    mamba_output,
    attention_out,
    gate_weight,
    lift_weight,
    down_weight,
):
    rows, inner = y.shape
    width = tokens.shape[1]
    feed = gate_weight.shape[1]
    att = attention_low.shape[1]
    tiles = rows // FEED_TILE
    vmem = pl.BlockSpec(memory_space=pltpu.VMEM)
    hbm = pl.BlockSpec(memory_space=pl.ANY)
    low, full = jnp.bfloat16, jnp.float32
    shape = jax.ShapeDtypeStruct
    merged = lax.axis_size("seq") == 4

    def grad_shape(columns):
        if merged:
            return shape((2,) * (seq_bits() + 2) + (width // 16, columns), low)
        return shape((width, columns), low)

    out_shape = [
            shape((rows, width), low),
            shape((rows, width), full),
            shape((rows, inner), full),
            shape((rows, inner), low),
            shape((rows, att), full),
            grad_shape(2 * feed),
            grad_shape(inner + att),
            grad_shape(feed),
            grad_shape(inner),
            shape((1, width), full),
            shape((1, inner), full),
        ]
    scratch = []
    if merged:
        out_shape += [shape((2,) * 3 + (width // 16, n), low) for n in (feed, MOST)]
        scratch = [pltpu.SemaphoreType.DMA((2, EARLIER, 1))]
    return pl.pallas_call(
        functools.partial(feed_kernel, merged),
        out_shape=out_shape,
        in_specs=[vmem] * 10 + [hbm] * 3,
        out_specs=[vmem] * len(out_shape),
        scratch_shapes=[
            pltpu.VMEM((width, feed), low),
            pltpu.VMEM((width, feed), low),
            pltpu.VMEM((width, feed), low),
            pltpu.VMEM((rows, width), low),
            pltpu.VMEM((rows, inner), low),
            pltpu.VMEM((rows, inner), full),
            pltpu.VMEM((rows, LANES), full),
            pltpu.VMEM((rows, width), full),
            pltpu.VMEM((rows, LANES), full),
            pltpu.VMEM((rows, width), low),
            pltpu.VMEM((rows, feed), low),
            pltpu.VMEM((rows, 2 * feed), low),
            pltpu.VMEM((rows, width), low),
            pltpu.VMEM((rows, inner), full),
            pltpu.VMEM((rows, LANES), full),
            pltpu.VMEM((rows, LANES), full),
            pltpu.VMEM((rows, LANES), full),
            pltpu.VMEM((rows, LANES), full),
        ]
        + [pltpu.VMEM((rows, width), low)] * 6
        + [pltpu.SemaphoreType.DMA((3,))]
        + [pltpu.SemaphoreType.DMA((2, tiles))] * 5
        + scratch,
        compiler_params=pltpu.CompilerParams(
            collective_id=1, has_side_effects=True, vmem_limit_bytes=60 << 20
        ),
        name="feed_layer",
    )(
        y,
        gate_z,
        attention_low,
        tokens,
        cotangent,
        mixer_gain[None],
        mamba_gain.reshape(inner // LANES, LANES),
        feed_gain[None],
        mamba_output,
        attention_out,
        gate_weight,
        lift_weight,
        down_weight,
    )


CHUNK = 128
HALO = 8
PIECE = 256


def turn_half(values):
    lane = lax.broadcasted_iota(jnp.int32, values.shape, 1)
    return jnp.where(
        lax.rem(lane, HD) < HD // 2,
        pltpu.roll(values, LANES - HD // 2, 1),
        pltpu.roll(values, HD // 2, 1),
    )


def two_parts(values):
    high = values.astype(jnp.bfloat16)
    return high, (values - high.astype(jnp.float32)).astype(jnp.bfloat16)


def spread_heads(values, spread):
    high, rest = two_parts(values)
    return matmul(high, spread) + matmul(rest, spread)


def sum_heads(values, spread):
    high, rest = two_parts(values)
    return matmul_last(high, spread) + matmul_last(rest, spread)


def spread_matrix(inner, size):
    row = lax.broadcasted_iota(jnp.int32, (LANES, inner), 0)
    lane = lax.broadcasted_iota(jnp.int32, (LANES, inner), 1)
    return jnp.where(lane // size == row, 1.0, 0.0).astype(jnp.bfloat16)


def ordered(count):
    row = lax.broadcasted_iota(jnp.int32, (count, count), 0)
    lane = lax.broadcasted_iota(jnp.int32, (count, count), 1)
    return row >= lane


def halves(values, size):
    lane = lax.broadcasted_iota(jnp.int32, values.shape, 1)
    return jnp.concatenate(
        [jnp.where(lane < size, values, 0.0), jnp.where(lane < size, 0.0, values)], axis=0
    ).astype(jnp.bfloat16)


def soft_plus(v):
    return jnp.maximum(v, 0.0) + jnp.log1p(jnp.exp(-jnp.abs(v)))


def chunk_flags(seg_ref, c):
    window = seg_ref[pl.ds(pl.multiple_of(c * CHUNK, CHUNK), CHUNK + HALO), :]
    own = window[HALO:]
    start = jnp.where(own == window[HALO - 1 : HALO], 1.0, 0.0)
    end = jnp.where(own == own[CHUNK - 1 :], 1.0, 0.0)
    return own, start, end


def greet_seq(barrier, with_peer):
    seq, head, batch = lax.axis_index("seq"), lax.axis_index("head"), lax.axis_index("batch")
    count = lax.axis_size("seq")

    def one(step, carry):
        pl.semaphore_signal(
            barrier,
            inc=1,
            device_id=(lax.rem(seq + step, count), head, batch),
            device_id_type=MESH,
        )
        return carry

    lax.fori_loop(1, count, one, 0)
    if with_peer:
        pl.semaphore_signal(barrier, inc=1, device_id=peer_device(), device_id_type=MESH)
    pl.semaphore_wait(barrier, count - 1 + with_peer)


def mixer_kernel(
    tokens_ref,
    gain_ref,
    seg_row_ref,
    table_ref,
    gate_weight,
    input_weight,
    maps_weight,
    step_given,
    query_weight,
    memory_weight,
    conv_inner_ref,
    conv_maps_ref,
    step_bias_ref,
    log_rate_ref,
    skip_gain_ref,
    gate_z_ref,
    pre_ref,
    conv_ref,
    raw_ref,
    cum_ref,
    y_ref,
    states_ref,
    query_ref,
    memory_ref,
    attention_ref,
    attention_low_ref,
    logs_ref,
    seg_ref,
    key_seg_ref,
    step_weight,
    taps_ref,
    rate_ref,
    skip_ref,
    step_wide,
    bias_ref,
    normed,
    spread_ref,
    act,
    scaled,
    added,
    decay,
    total,
    local,
    state,
    chain_out,
    chain_in,
    sem_memory,
    sem_halo,
    sem_chain,
):
    seq, head, batch = lax.axis_index("seq"), lax.axis_index("head"), lax.axis_index("batch")
    count = lax.axis_size("seq")
    rows = tokens_ref.shape[0]
    tiles = rows // CHUNK
    inner = y_ref.shape[1]
    width = pre_ref.shape[1]
    state_width = (width - inner) // 2
    following = (lax.rem(seq + 1, count), head, batch)
    greet_seq(pltpu.get_barrier_semaphore(), 0)
    first = seq * rows

    def memory_copy(hop, owner):
        return exchange(
            memory_ref.at[owner],
            memory_ref.at[owner],
            sem_memory.at[0, hop],
            sem_memory.at[1, hop],
            following,
        )

    def memory_send(hop):
        @pl.when((seq - hop + 1 >= 0) & (seq < count - 1))
        def _():
            memory_copy(hop, lax.rem(seq - hop + 1 + count, count)).start()

    def memory_receive(hop):
        @pl.when(seq - hop >= 0)
        def _():
            memory_copy(hop, lax.rem(seq - hop + count, count)).wait_recv()

    def memory_hop(hop):
        memory_receive(hop - 1)
        memory_send(hop)

    halo_copy = exchange(
        pre_ref.at[pl.ds(rows, HALO)],
        pre_ref.at[pl.ds(0, HALO)],
        sem_halo.at[0],
        sem_halo.at[1],
        following,
    )

    def memory_tile(i):
        at = feed_rows(i)
        hidden = tokens_ref[at, :].astype(jnp.float32)
        inverse = lax.rsqrt(jnp.mean(hidden * hidden, axis=1, keepdims=True) + eps_norm)
        low = (hidden * inverse * gain_ref[...]).astype(jnp.bfloat16)
        normed[at, :] = low
        value = matmul(low, memory_weight[...])
        lane = lax.broadcasted_iota(jnp.int32, value.shape, 1)
        turned = value * table_ref[at, :LANES] + turn_half(value) * table_ref[at, LANES:]
        memory_ref[seq, at, :] = jnp.where(lane < HD, turned, value).astype(jnp.bfloat16)

    wide_tiles = rows // FEED_TILE
    each(wide_tiles, memory_tile)

    memory_send(1)

    def pre_tile(i):
        at = feed_rows(i)
        to = pl.ds(pl.multiple_of(i * FEED_TILE + HALO, HALO), FEED_TILE)
        low = normed[at, :]
        pre_ref[to, :inner] = matmul(low, input_weight[...])
        pre_ref[to, inner:] = matmul(low, maps_weight[...])

    each(wide_tiles, lambda i: pre_tile(wide_tiles - 1 - i))

    @pl.when(seq < count - 1)
    def _():
        halo_copy.start()

    if count > 2:
        memory_hop(2)

    def key_block(k):
        at = pl.ds(pl.multiple_of(k * LANES, LANES), LANES)
        row = seg_row_ref[:, at].astype(jnp.float32)
        key_seg_ref[at, :] = jnp.broadcast_to(row, (LANES, LANES)).T

    each(seg_row_ref.shape[1] // LANES, key_block)
    seg_ref[HALO : HALO + rows, :] = key_seg_ref[pl.ds(pl.multiple_of(first, TILE), rows), :]
    seg_ref[:HALO, :] = jnp.full((HALO, LANES), -1.0, jnp.float32)
    seg_ref[HALO + rows :, :] = jnp.full((HALO, LANES), -2.0, jnp.float32)

    @pl.when(seq > 0)
    def _():
        seg_ref[:HALO, :] = key_seg_ref[pl.ds(pl.multiple_of(first - HALO, HALO), HALO), :]

    @pl.when(seq < count - 1)
    def _():
        seg_ref[HALO + rows :, :] = key_seg_ref[pl.ds(pl.multiple_of(first + rows, TILE), HALO), :]

    heads = step_given.shape[0]
    lane = lax.broadcasted_iota(jnp.int32, (1, LANES), 1)
    wide_lane = lax.broadcasted_iota(jnp.int32, (1, inner), 1)
    bias_row = log_row = jnp.zeros((1, LANES), jnp.float32)
    skip_row = jnp.zeros((1, inner), jnp.float32)
    for h in range(heads):
        bias_row = jnp.where(lane == h, step_bias_ref[h], bias_row)
        log_row = jnp.where(lane == h, log_rate_ref[h], log_row)
        skip_row = jnp.where(wide_lane // HD == h, skip_gain_ref[h], skip_row)
    bias_ref[...] = bias_row
    rate_ref[...] = jnp.where(lane < heads, -jnp.exp(log_row), 0.0)
    skip_ref[...] = skip_row
    step_wide[...] = jnp.zeros_like(step_wide)
    step_wide[:heads, :] = step_given[...].astype(jnp.float32)
    step_weight[...] = step_wide[...].astype(jnp.bfloat16)
    taps_ref[...] = jnp.zeros_like(taps_ref)
    taps_ref[: conv_inner_ref.shape[0], :inner] = conv_inner_ref[...]
    taps_ref[: conv_inner_ref.shape[0], inner:] = conv_maps_ref[...]
    spread_ref[...] = spread_matrix(inner, HD)
    lower = jnp.where(ordered(CHUNK), 1.0, 0.0)

    def step_tile(i):
        at = tile_rows(i)
        raw = matmul_last(normed[at, :], step_weight[...]) + bias_ref[...]
        raw_ref[at, :] = raw
        cum_ref[at, :] = jnp.dot(lower, rate_ref[...] * soft_plus(raw), precision=highest)

    each(tiles, step_tile)

    @pl.when(seq == 0)
    def _():
        pre_ref[:HALO, :] = jnp.zeros((HALO, width), jnp.float32)

    @pl.when(seq > 0)
    def _():
        halo_copy.wait_recv()

    def conv_tile(i):
        at = tile_rows(i)
        window_at = pl.ds(pl.multiple_of(i * TILE, TILE), TILE + HALO)
        seg = seg_ref[window_at, :]
        own = seg[HALO:]
        masks = [
            jnp.where(seg[HALO - 3 + k : HALO - 3 + k + TILE] == own, 1.0, 0.0) for k in range(3)
        ]
        for j in range(width // LANES):
            columns = slice(j * LANES, (j + 1) * LANES)
            window = pre_ref[window_at, columns]
            summed = taps_ref[3:4, columns] * window[HALO:]
            for k in range(3):
                summed = summed + taps_ref[k : k + 1, columns] * (
                    window[HALO - 3 + k : HALO - 3 + k + TILE] * masks[k]
                )
            conv_ref[at, columns] = summed
            act[at, columns] = summed * sigmoid(summed)

    each(tiles, conv_tile)
    local[...] = jnp.zeros_like(local)
    total[...] = jnp.ones_like(total)

    def input_map(at):
        return act[at, inner : inner + state_width].astype(jnp.bfloat16)

    def output_map(at):
        return act[at, inner + state_width :].astype(jnp.bfloat16)

    def local_chunk(c):
        at = tile_rows(c)
        _, start, end = chunk_flags(seg_ref, c)
        cum = cum_ref[at, :]
        last = cum[CHUNK - 1 :]
        spread = spread_ref[...]
        value = act[at, :inner] * spread_heads(soft_plus(raw_ref[at, :]), spread)
        scaled[at, :] = value.astype(jnp.bfloat16)
        weight = spread_heads(jnp.exp(last - cum) * end, spread)
        fresh = matmul_first(input_map(at), (value * weight).astype(jnp.bfloat16))
        keep = jnp.broadcast_to(jnp.exp(last) * start[CHUNK - 1 :], (HALO, LANES))
        keep = spread_heads(keep, spread)
        added[c] = fresh
        decay[c] = keep
        local[...] = local[...] * keep[:1] + fresh
        total[...] = total[...] * keep

    each(tiles, local_chunk)
    pieces = inner // PIECE

    def chain_copy(p):
        columns = pl.ds(p * PIECE, PIECE)
        return exchange(
            chain_out.at[:, columns],
            chain_in.at[:, columns],
            sem_chain.at[0, p],
            sem_chain.at[1, p],
            following,
        )

    @pl.when(seq == 0)
    def _():
        state[...] = jnp.zeros_like(state)
        chain_out[...] = local[...].astype(jnp.bfloat16)
        if count > 1:
            for p in range(pieces):
                chain_copy(p).start()

    if count > 3:
        memory_hop(3)

    def inside_chunk(c):
        at = tile_rows(c)
        own, _, _ = chunk_flags(seg_ref, c)
        cum = cum_ref[at, :]
        turned = cum.T
        meet = matmul_last(output_map(at), input_map(at))
        meet = jnp.where(ordered(CHUNK) & (own == own.T), meet, 0.0)
        for i in range(inner // LANES):
            columns = slice(i * LANES, (i + 1) * LANES)
            mixing = []
            for h in (2 * i, 2 * i + 1):
                gap = cum[:, h : h + 1] - turned[h : h + 1, :]
                mixing.append(meet * jnp.exp(jnp.minimum(gap, 0.0)))
            y_ref[at, columns] = matmul(
                jnp.concatenate(mixing, axis=1).astype(jnp.bfloat16),
                halves(scaled[at, columns].astype(jnp.float32), HD),
            )

    each(tiles, inside_chunk)

    def project_tile(i):
        at = feed_rows(i)
        low = normed[at, :]
        gate_z_ref[at, :] = matmul(low, gate_weight[...])
        value = matmul(low, query_weight[...])
        for k in range(value.shape[1] // LANES):
            part = value[:, k * LANES : (k + 1) * LANES]
            turned = part * table_ref[at, :LANES] + turn_half(part) * table_ref[at, LANES:]
            query_ref[at, k * LANES : (k + 1) * LANES] = turned.astype(jnp.bfloat16)

    def chain_wait(p):
        columns = pl.ds(p * PIECE, PIECE)
        chain_copy(p).wait_recv()
        came = chain_in[:, columns].astype(jnp.float32)
        state[:, columns] = came
        return came

    @pl.when(seq >= 2)
    def _():
        each(wide_tiles, project_tile)

    @pl.when((seq > 0) & (seq < count - 1))
    def _():
        for p in range(pieces):
            columns = pl.ds(p * PIECE, PIECE)
            chain_out[:, columns] = (
                chain_wait(p) * total[:1, columns] + local[:, columns]
            ).astype(jnp.bfloat16)
            chain_copy(p).start()

    @pl.when(seq < 2)
    def _():
        each(wide_tiles, project_tile)

    span(4, count, memory_hop)
    if count > 1:
        memory_receive(count - 1)

    def memory_rest(hop):
        @pl.when((seq - hop + 1 >= 0) & (seq < count - 1))
        def _():
            memory_copy(hop, lax.rem(seq - hop + 1 + count, count)).wait_send()

        @pl.when(seq + hop < count)
        def _():
            memory_ref[lax.rem(seq + hop, count)] = jnp.zeros(memory_ref.shape[1:], jnp.bfloat16)

    span(1, count, memory_rest)
    def attention_block(i):
        at = tile_rows(i)
        turned, log = attend_block(
            first,
            0,
            (first + i * TILE + TILE - 1) // KEY_TILE,
            i,
            query_ref[at, :],
            lambda k: memory_ref[k],
            seg_ref,
            key_seg_ref,
        )
        for pair, tile in enumerate(unstacked_heads(turned, False)):
            columns = slice(pair * LANES, (pair + 1) * LANES)
            attention_ref[at, columns] = tile
            attention_low_ref[at, columns] = tile.astype(jnp.bfloat16)
        logs_ref[i] = jnp.broadcast_to(log, logs_ref.shape[1:])

    each(tiles, attention_block)

    @pl.when((seq > 0) & (seq == count - 1))
    def _():
        for p in range(pieces):
            chain_wait(p)

    def across_chunk(c):
        at = tile_rows(c)
        _, start, _ = chunk_flags(seg_ref, c)
        now = state[...]
        low = now.astype(jnp.bfloat16)
        states_ref[c] = low
        carried = spread_heads(jnp.exp(cum_ref[at, :]) * start, spread_ref[...])
        y_ref[at, :] += matmul(output_map(at), low) * carried + skip_ref[...] * act[at, :inner]
        state[...] = now * decay[c][:1] + added[c]

    each(tiles, across_chunk)
    states_ref[tiles] = state[...].astype(jnp.bfloat16)

    @pl.when(seq < count - 1)
    def _():
        halo_copy.wait_send()
        for p in range(pieces):
            chain_copy(p).wait_send()


def mixer_forward(*operands):
    tokens, seg_row, table = operands[0], operands[2], operands[3]
    mamba_gate, step_given, query_weight, memory_weight = (
        operands[4],
        operands[7],
        operands[8],
        operands[9],
    )
    rows, width = tokens.shape
    total = seg_row.shape[1]
    count = lax.axis_size("seq")
    inner = mamba_gate.shape[1]
    conv_width = inner + operands[6].shape[1]
    state_width = (conv_width - inner) // 2
    query = query_weight.shape[1]
    chunks = rows // CHUNK
    pieces = inner // PIECE
    smem = pl.BlockSpec(memory_space=pltpu.SMEM)
    vmem = pl.BlockSpec(memory_space=pltpu.VMEM)
    low, full = jnp.bfloat16, jnp.float32
    shape = jax.ShapeDtypeStruct
    return pl.pallas_call(
        mixer_kernel,
        out_shape=[
            shape((rows, inner), full),
            shape((rows + HALO, conv_width), full),
            shape((rows, conv_width), full),
            shape((rows, LANES), full),
            shape((rows, LANES), full),
            shape((rows, inner), full),
            shape((chunks + 1, state_width, inner), low),
            shape((rows, query), low),
            shape((count, rows, memory_weight.shape[1]), low),
            shape((rows, query), full),
            shape((rows, query), low),
            shape((chunks, HALO, query // HD * TILE), full),
            shape((rows + 2 * HALO, LANES), full),
            shape((total, LANES), full),
            shape((LANES, width), low),
            shape((HALO, conv_width), full),
            shape((1, LANES), full),
            shape((1, inner), full),
        ],
        in_specs=[vmem] * 12 + [smem] * 3,
        out_specs=[vmem] * 18,
        scratch_shapes=[
            pltpu.VMEM((LANES, width), full),
            pltpu.VMEM((1, LANES), full),
            pltpu.VMEM((rows, width), low),
            pltpu.VMEM((LANES, inner), low),
            pltpu.VMEM((rows, conv_width), full),
            pltpu.VMEM((rows, inner), low),
            pltpu.VMEM((chunks, state_width, inner), full),
            pltpu.VMEM((chunks, HALO, inner), full),
            pltpu.VMEM((HALO, inner), full),
            pltpu.VMEM((state_width, inner), full),
            pltpu.VMEM((state_width, inner), full),
            pltpu.VMEM((state_width, inner), low),
            pltpu.VMEM((state_width, inner), low),
            pltpu.SemaphoreType.DMA((2, count)),
            pltpu.SemaphoreType.DMA((2,)),
            pltpu.SemaphoreType.DMA((2, pieces)),
        ],
        compiler_params=pltpu.CompilerParams(
            collective_id=2, has_side_effects=True, vmem_limit_bytes=60 << 20
        ),
        name="mixer_forward",
    )(*operands)


KEY_TILE = 512


def stacked_heads(values, first, factor):
    lane = lax.broadcasted_iota(jnp.int32, (values.shape[0], LANES), 1)
    keep = (lane < HD) if first else (lane >= HD)
    parts = []
    for h in range(values.shape[1] // HD):
        tile = values[:, (h // 2) * LANES : (h // 2 + 1) * LANES].astype(jnp.float32)
        if (h % 2 == 0) != first:
            tile = pltpu.roll(tile, HD, 1)
        parts.append(jnp.where(keep, tile * factor, 0.0))
    return jnp.concatenate(parts, axis=0)


def unstacked_heads(turned, first):
    heads = turned.shape[1] // TILE
    blocks = [turned[:, h * TILE : (h + 1) * TILE].T for h in range(heads)]
    lane = lax.broadcasted_iota(jnp.int32, (TILE, LANES), 1)
    tiles = []
    for even, odd in zip(blocks[::2], blocks[1::2]):
        if first:
            odd = pltpu.roll(odd, HD, 1)
        else:
            even = pltpu.roll(even, HD, 1)
        tiles.append(jnp.where(lane < HD, even, odd))
    return tiles


def key_tile(seg_turned, key_seg_ref, first, i, k):
    at = pl.ds(pl.multiple_of(k * KEY_TILE, KEY_TILE), KEY_TILE)
    place = k * KEY_TILE + lax.broadcasted_iota(jnp.int32, (KEY_TILE, TILE), 0)
    row = first + i * TILE + lax.broadcasted_iota(jnp.int32, (KEY_TILE, TILE), 1)
    return at, (place <= row) & (key_seg_ref[at, :] == seg_turned)


def query_segments(seg_ref, i):
    own = seg_ref[pl.ds(pl.multiple_of(i * TILE, TILE) + HALO, TILE), :].T
    return jnp.concatenate([own] * (KEY_TILE // TILE), axis=0)


def attend_block(first, low, high, i, queries_in, memory_of, seg_ref, key_seg_ref):
    heads = queries_in.shape[1] // HD
    turned = stacked_heads(queries_in, True, HD ** (-0.5)).T.astype(jnp.bfloat16)
    segs = query_segments(seg_ref, i)
    parts = [turned[:, h * TILE : (h + 1) * TILE] for h in range(heads)]

    def one(step, carry):
        at, allowed = key_tile(segs, key_seg_ref, first, i, high - step)
        keys = memory_of(high - step)
        after = []
        for part, (most, total, acc) in zip(parts, carry):
            scores = jnp.where(allowed, matmul(keys, part), neg_large)
            new = jnp.maximum(most, jnp.max(scores, axis=0, keepdims=True))
            weights = jnp.exp(scores - new)
            factor = jnp.exp(most - new)
            total = total * factor + jnp.sum(weights, axis=0, keepdims=True)
            acc = acc * factor + matmul_first(keys, weights.astype(jnp.bfloat16))
            after.append((new, total, acc))
        return tuple(after)

    zero = (
        jnp.full((1, TILE), neg_large, jnp.float32),
        jnp.zeros((1, TILE), jnp.float32),
        jnp.zeros((LANES, TILE), jnp.float32),
    )
    result = lax.fori_loop(0, high - low + 1, one, (zero,) * heads)
    return (
        jnp.concatenate([acc / total for _, total, acc in result], axis=1),
        jnp.concatenate([most + jnp.log(total) for most, total, _ in result], axis=1),
    )


def attend_back_block(
    first, low, high, i, queries_in, d_out, out, log, memory_of, seg_ref, key_seg_ref, grads
):
    heads = queries_in.shape[1] // HD
    queries = stacked_heads(queries_in, True, HD ** (-0.5))
    outer = stacked_heads(d_out, False, 1.0)
    queries_turned, outer_turned = queries.T.astype(jnp.bfloat16), outer.T.astype(jnp.bfloat16)
    queries, outer = queries.astype(jnp.bfloat16), outer.astype(jnp.bfloat16)
    segs = query_segments(seg_ref, i)
    row = lax.broadcasted_iota(jnp.int32, (HALO, heads * HD), 0)
    lane = lax.broadcasted_iota(jnp.int32, (HALO, heads * HD), 1)
    pick = jnp.where(lane // HD == row, 1.0, 0.0).astype(jnp.bfloat16)
    high_part, low_part = two_parts(d_out * out)
    deltas = matmul_last(pick, high_part) + matmul_last(pick, low_part)
    spans = [slice(h * TILE, (h + 1) * TILE) for h in range(heads)]

    def one(step, totals):
        at, allowed = key_tile(segs, key_seg_ref, first, i, high - step)
        keys = memory_of(high - step)
        slopes, lows, after = [], [], []
        for h, (part, total) in enumerate(zip(spans, totals)):
            weights = jnp.exp(matmul(keys, queries_turned[:, part]) - log[:, part])
            weights = jnp.where(allowed, weights, 0.0)
            slope = weights * (matmul(keys, outer_turned[:, part]) - deltas[h : h + 1])
            slopes.append(slope.astype(jnp.bfloat16))
            lows.append(weights.astype(jnp.bfloat16))
            after.append(total + matmul_first(keys, slopes[-1]))
        grads[at, :] += matmul(jnp.concatenate(slopes, axis=1), queries) + matmul(
            jnp.concatenate(lows, axis=1), outer
        )
        return tuple(after)

    totals = lax.fori_loop(
        0, high - low + 1, one, (jnp.zeros((LANES, TILE), jnp.float32),) * heads
    )
    return jnp.concatenate(totals, axis=1) * HD ** (-0.5)


def attention_back_kernel(
    first_ref,
    low_ref,
    high_ref,
    query_ref,
    memory_ref,
    seg_ref,
    key_seg_ref,
    out_ref,
    log_ref,
    d_out_ref,
    table_ref,
    d_query_ref,
    d_memory_ref,
    grads,
):
    grads[...] = jnp.zeros_like(grads)

    def block(i):
        at = tile_rows(i)
        d_turned = attend_back_block(
            first_ref[0],
            low_ref[i],
            high_ref[i],
            i,
            query_ref[at, :],
            d_out_ref[at, :],
            out_ref[at, :],
            log_ref[i][:1],
            lambda k: memory_ref[pl.ds(pl.multiple_of(k * KEY_TILE, KEY_TILE), KEY_TILE), :],
            seg_ref,
            key_seg_ref,
            grads,
        )
        for pair, tile in enumerate(unstacked_heads(d_turned, True)):
            turned = tile * table_ref[at, :LANES] - turn_half(tile) * table_ref[at, LANES:]
            d_query_ref[at, pair * LANES : (pair + 1) * LANES] = turned.astype(jnp.bfloat16)

    each(query_ref.shape[0] // TILE, block)
    d_memory_ref[...] = grads[...].astype(jnp.bfloat16)


def attention_back(spans, query, memory, segments, key_segments, out, logs, d_out, table):
    vmem = pl.BlockSpec(memory_space=pltpu.VMEM)
    return pl.pallas_call(
        attention_back_kernel,
        out_shape=[
            jax.ShapeDtypeStruct(query.shape, jnp.bfloat16),
            jax.ShapeDtypeStruct(memory.shape, jnp.bfloat16),
        ],
        in_specs=[pl.BlockSpec(memory_space=pltpu.SMEM)] * 3 + [vmem] * 8,
        out_specs=[vmem] * 2,
        scratch_shapes=[pltpu.VMEM(memory.shape, jnp.float32)],
        compiler_params=pltpu.CompilerParams(vmem_limit_bytes=56 << 20),
        name="attention_back",
    )(*spans, query, memory, segments, key_segments, out, logs, d_out, table)


MERGED_INPUTS = 30


def mixer_back_kernel(merged, chunks, *refs):
    refs = list(refs)

    def take(count):
        nonlocal refs
        now, refs = refs[:count], refs[count:]
        return now

    if merged:
        given = take(MERGED_INPUTS)
        early, came = take(4), take(2)
        d_tokens_ref, *outs, small_out = take(7)
        copies = take(MERGED_INPUTS)
        (sem_load,) = take(1)
        loads = [
            pltpu.make_async_copy(source, target, sem_load.at[k])
            for k, (source, target) in enumerate(zip(given, copies))
        ]
        for load in loads:
            load.start()
        refs = copies + refs
    (
        tokens_ref,
        gain_ref,
        seg_ref,
        table_ref,
        gate_weight,
        input_weight,
        maps_weight,
        step_weight,
        query_weight,
        memory_weight,
        taps_ref,
        rate_ref,
        skip_ref,
        pre_ref,
        conv_ref,
        raw_ref,
        cum_ref,
        y_ref,
        states_ref,
        d_second_ref,
        d_y_ref,
        d_gate_z_ref,
    ) = take(22)
    if merged:
        (
            query_ref,
            memory_ref,
            key_seg_ref,
            attention_ref,
            logs_ref,
            d_attention_ref,
            feed_gain_ref,
            mamba_gain_ref,
        ) = take(8)
    else:
        d_query_ref, d_memory_ref = take(2)
        d_tokens_ref, g_side_ref, g_taps_ref, g_gain_ref, g_heads_ref = take(5)
    (
        normed,
        spread_ref,
        act,
        d_conv,
        d_scaled,
        d_maps,
        row_term,
        added,
        local,
        total,
        state,
        skip_sum,
        side,
        chain_out,
        chain_in,
        maps_send,
        maps_recv,
        memory_recv,
        norm_send,
        norm_recv,
        sem_memory,
        sem_halo,
        sem_chain,
        sem_maps,
        sem_norm,
    ) = take(25)
    if merged:
        g_side_ref, grads, d_memory_ref, small_in, small_buf, sem_small = take(6)
        g_taps_ref = g_gain_ref = g_heads_ref = small_in
    seq, head, batch = lax.axis_index("seq"), lax.axis_index("head"), lax.axis_index("batch")
    count = lax.axis_size("seq")
    rows = tokens_ref.shape[0]
    tiles = rows // CHUNK
    inner = y_ref.shape[1]
    width = pre_ref.shape[1]
    state_width = (width - inner) // 2
    model = tokens_ref.shape[1]
    peer = peer_device()
    previous = (lax.rem(seq - 1 + count, count), head, batch)
    pieces = inner // PIECE
    step_at = width
    query_at = step_at + LANES
    memory_at = query_at + query_weight.shape[1]
    if merged:
        greet_all(pltpu.get_barrier_semaphore(), True)
        reduction = Reduction(chunks, list(early) + [g_side_ref], outs, refs, came)
        reduction.allow(sum(1 for c in chunks if c[0] < len(early)))
        advance = reduction.advance
        for load in loads:
            load.wait()
    else:
        greet_seq(pltpu.get_barrier_semaphore(), 1)

        def advance():
            return None

    spread_ref[...] = spread_matrix(inner, HD)

    def chain_copy(p):
        columns = pl.ds(p * PIECE, PIECE)
        return exchange(
            chain_out.at[:, columns],
            chain_in.at[:, columns],
            sem_chain.at[0, p],
            sem_chain.at[1, p],
            previous,
        )

    def memory_copy(step):
        place = lax.rem(seq - step + count, count)
        return exchange(
            d_memory_ref.at[place],
            memory_recv.at[step - 1],
            sem_memory.at[0, step],
            sem_memory.at[1, step],
            (place, head, batch),
        )

    halo_copy = exchange(
        d_conv.at[pl.ds(0, HALO)],
        d_conv.at[pl.ds(rows, HALO)],
        sem_halo.at[0],
        sem_halo.at[1],
        previous,
    )
    maps_copy = exchange(maps_send, maps_recv, sem_maps.at[0], sem_maps.at[1], peer)

    def norm_copy(i):
        at = tile_rows(i)
        return exchange(
            norm_send.at[at], norm_recv.at[at], sem_norm.at[0, i], sem_norm.at[1, i], peer
        )

    def input_map(at):
        return act[at, inner : inner + state_width].astype(jnp.bfloat16)

    def output_map(at):
        return act[at, inner + state_width :].astype(jnp.bfloat16)

    def keep_of(c, start):
        last = cum_ref[tile_rows(c), :][CHUNK - 1 :]
        keep = jnp.broadcast_to(jnp.exp(last) * start[CHUNK - 1 :], (HALO, LANES))
        return spread_heads(keep, spread_ref[...])

    def carried_of(c, start):
        return spread_heads(jnp.exp(cum_ref[tile_rows(c), :]) * start, spread_ref[...])

    def activate(i):
        at = tile_rows(i)
        value = conv_ref[at, :]
        act[at, :] = value * sigmoid(value)

    each(tiles, activate)
    local[...] = jnp.zeros_like(local)
    total[...] = jnp.ones_like(total)

    def local_chunk(step):
        c = tiles - 1 - step
        at = tile_rows(c)
        _, start, _ = chunk_flags(seg_ref, c)
        keep = keep_of(c, start)
        value = (d_y_ref[at, :] * carried_of(c, start)).astype(jnp.bfloat16)
        fresh = matmul_first(output_map(at), value)
        added[c] = fresh
        local[...] = local[...] * keep[:1] + fresh
        total[...] = total[...] * keep

    each(tiles, local_chunk)

    @pl.when(seq == count - 1)
    def _():
        state[...] = jnp.zeros_like(state)
        chain_out[...] = local[...].astype(jnp.bfloat16)
        if count > 1:
            for p in range(pieces):
                chain_copy(p).start()

    if merged:
        first = seq * rows
        grads[...] = jnp.zeros_like(grads)

        def attention_block(i):
            at = tile_rows(i)
            d_turned = attend_back_block(
                first,
                0,
                (first + i * TILE + TILE - 1) // KEY_TILE,
                i,
                query_ref[at, :],
                d_attention_ref[at, :],
                attention_ref[at, :],
                logs_ref[i][:1],
                lambda k: memory_ref[pl.ds(pl.multiple_of(k * KEY_TILE, KEY_TILE), KEY_TILE), :],
                seg_ref,
                key_seg_ref,
                grads,
            )
            for pair, tile in enumerate(unstacked_heads(d_turned, True)):
                turned = tile * table_ref[at, :LANES] - turn_half(tile) * table_ref[at, LANES:]
                columns = pl.ds(query_at + pair * LANES, LANES)
                side[at, columns] = turned.astype(jnp.bfloat16)

        span(0, 1, attention_block)
        advance()

    def chain_wait(p):
        columns = pl.ds(p * PIECE, PIECE)
        chain_copy(p).wait_recv()
        came = chain_in[:, columns].astype(jnp.float32)
        state[:, columns] = came
        return came

    @pl.when((seq > 0) & (seq < count - 1))
    def _():
        for p in range(pieces):
            columns = pl.ds(p * PIECE, PIECE)
            came = chain_wait(p)
            chain_out[:, columns] = (came * total[:1, columns] + local[:, columns]).astype(
                jnp.bfloat16
            )
            chain_copy(p).start()

    if merged:
        for i in range(1, tiles):
            span(i, i + 1, attention_block)
            advance()

        def low_block(place):
            at = pl.ds(pl.multiple_of(place * rows, rows), rows)
            d_memory_ref[place] = grads[at, :].astype(jnp.bfloat16)

        each(count, low_block)

    def memory_start(step, carry):
        @pl.when(seq - step >= 0)
        def _():
            memory_copy(step).start()

        return carry

    lax.fori_loop(1, count, memory_start, 0)
    skip_sum[...] = jnp.zeros_like(skip_sum)

    def inside_chunk(c):
        at = tile_rows(c)
        own, start, _ = chunk_flags(seg_ref, c)
        cum = cum_ref[at, :]
        turned = cum.T
        spread = spread_ref[...]
        low_in, low_out = input_map(at), output_map(at)
        allowed = ordered(CHUNK).astype(jnp.float32).T * jnp.where(own == own.T, 1.0, 0.0)
        meet = matmul_last(low_in, low_out) * allowed
        value = act[at, :inner]
        scaled = value * spread_heads(soft_plus(raw_ref[at, :]), spread)
        d_y = d_y_ref[at, :]
        d_meet = jnp.zeros((CHUNK, CHUNK), jnp.float32)
        for i in range(inner // LANES):
            columns = slice(i * LANES, (i + 1) * LANES)
            d_tile = d_y[:, columns]
            d_mixing = matmul_last(halves(scaled[:, columns], HD), d_tile.astype(jnp.bfloat16))
            mixing = []
            for k, h in enumerate((2 * i, 2 * i + 1)):
                gap = turned[h : h + 1, :] - cum[:, h : h + 1]
                fade = jnp.exp(jnp.minimum(gap, 0.0))
                mixing.append(meet * fade)
                d_meet = d_meet + d_mixing[k * CHUNK : (k + 1) * CHUNK] * fade
            d_scaled[at, columns] = matmul(
                jnp.concatenate(mixing, axis=1).astype(jnp.bfloat16), halves(d_tile, HD)
            )
        d_meet = (d_meet * allowed).astype(jnp.bfloat16)
        d_maps[at, :state_width] = matmul(d_meet, low_out)
        carried = (d_y * carried_of(c, start)).astype(jnp.bfloat16)
        d_maps[at, state_width:] = matmul_first(d_meet, low_in) + matmul_last(
            carried, states_ref[c]
        )
        product = d_y * value
        skip_sum[...] += jnp.sum(product, axis=0, keepdims=True)
        low = d_y.astype(jnp.bfloat16).astype(jnp.float32)
        row_term[at, :] = sum_heads(low * (y_ref[at, :] - skip_ref[...] * value), spread)

    span(0, tiles // 2, inside_chunk)
    advance()
    span(tiles // 2, tiles, inside_chunk)
    advance()

    @pl.when((seq == 0) & (seq < count - 1))
    def _():
        for p in range(pieces):
            chain_wait(p)

    if merged:
        small_in[...] = jnp.zeros_like(small_in)
        small_in[4:5, :inner] = mamba_gain_ref[...]
        small_in[6:7, :] = feed_gain_ref[...]
    else:
        g_heads_ref[...] = jnp.zeros_like(g_heads_ref)

    gain_row = 5 if merged else 0

    def add_heads(k, values):
        row, lane = (7, k * LANES) if merged else (k, 0)
        g_heads_ref[row : row + 1, lane : lane + LANES] += values

    upper = jnp.where(ordered(CHUNK), 1.0, 0.0).T

    def across_chunk(step):
        c = tiles - 1 - step
        at = tile_rows(c)
        _, start, end = chunk_flags(seg_ref, c)
        spread = spread_ref[...]
        cum = cum_ref[at, :]
        last = cum[CHUNK - 1 :]
        now = state[...]
        low = now.astype(jnp.bfloat16)
        raw = raw_ref[at, :]
        steps = soft_plus(raw)
        steps_wide = spread_heads(steps, spread)
        value = act[at, :inner]
        scaled = value * steps_wide
        weight = spread_heads(jnp.exp(last - cum) * end, spread)
        d_value = d_scaled[at, :] + matmul(input_map(at), low) * weight
        d_maps[at, :state_width] += matmul_last((scaled * weight).astype(jnp.bfloat16), low)
        final = jnp.sum(
            states_ref[c + 1].astype(jnp.float32) * low.astype(jnp.float32), axis=0, keepdims=True
        )
        final = sum_heads(jnp.broadcast_to(final, (HALO, inner)), spread)[:1]
        low_scaled = scaled.astype(jnp.bfloat16).astype(jnp.float32)
        d_cum = row_term[at, :] - sum_heads(low_scaled * d_value, spread)
        d_rate = jnp.dot(upper, d_cum, precision=highest) + final
        rate = rate_ref[...]
        d_steps = sum_heads(value * d_value, spread) + rate * d_rate
        d_raw = d_steps * sigmoid(raw)
        add_heads(0, rate * jnp.sum(steps * d_rate, axis=0, keepdims=True))
        add_heads(1, jnp.sum(d_raw, axis=0, keepdims=True))
        side[at, step_at:query_at] = d_raw.astype(jnp.bfloat16)
        d_conv[at, :inner] = steps_wide * d_value + skip_ref[...] * d_y_ref[at, :]
        state[...] = now * keep_of(c, start)[:1] + added[c]

    span(0, tiles // 2, across_chunk)
    advance()
    span(tiles // 2, tiles, across_chunk)
    advance()
    add_heads(2, sum_heads(jnp.broadcast_to(skip_sum[:1], (HALO, inner)), spread_ref[...])[:1])
    maps_send[...] = d_maps[...].astype(jnp.bfloat16)
    maps_copy.start()

    def copy_tile(i):
        at = tile_rows(i)
        hidden = tokens_ref[at, :].astype(jnp.float32)
        inverse = lax.rsqrt(jnp.mean(hidden * hidden, axis=1, keepdims=True) + eps_norm)
        normed[at, :] = (hidden * inverse * gain_ref[...]).astype(jnp.bfloat16)

    each(tiles, copy_tile)
    maps_copy.wait()

    def conv_back_tile(i):
        at = tile_rows(i)
        d_conv[at, inner:] = maps_send[at, :].astype(jnp.float32) + maps_recv[at, :].astype(
            jnp.float32
        )
        value = conv_ref[at, :]
        sig = sigmoid(value)
        d_conv[at, :] = d_conv[at, :] * (sig * (1.0 + value * (1.0 - sig)))

    each(tiles, conv_back_tile)

    @pl.when(seq > 0)
    def _():
        halo_copy.start()

    @pl.when(seq == count - 1)
    def _():
        d_conv[pl.ds(rows, HALO), :] = jnp.zeros((HALO, width), jnp.float32)

    @pl.when(seq < count - 1)
    def _():
        halo_copy.wait_recv()

    if not merged:
        g_taps_ref[...] = jnp.zeros_like(g_taps_ref)

    def taps_tile(i):
        at = tile_rows(i)
        window_at = pl.ds(pl.multiple_of(i * TILE, TILE), TILE + HALO)
        seg = seg_ref[pl.ds(pl.multiple_of(i * TILE, TILE), TILE + 2 * HALO), :]
        own = seg[HALO : HALO + TILE]
        before = [
            jnp.where(seg[HALO - 3 + k : HALO - 3 + k + TILE] == own, 1.0, 0.0) for k in range(3)
        ]
        after = [
            jnp.where(seg[HALO + 3 - k : HALO + 3 - k + TILE] == own, 1.0, 0.0) for k in range(3)
        ]
        for j in range(width // LANES):
            columns = slice(j * LANES, (j + 1) * LANES)
            window = pre_ref[window_at, columns]
            grads = d_conv[window_at, columns]
            own_grad = grads[:TILE]
            summed = taps_ref[3:4, columns] * own_grad
            g_taps_ref[3:4, columns] += jnp.sum(own_grad * window[HALO:], axis=0, keepdims=True)
            for k in range(3):
                summed = summed + taps_ref[k : k + 1, columns] * (
                    grads[3 - k : 3 - k + TILE] * after[k]
                )
                g_taps_ref[k : k + 1, columns] += jnp.sum(
                    own_grad * (window[HALO - 3 + k : HALO - 3 + k + TILE] * before[k]),
                    axis=0,
                    keepdims=True,
                )
            side[at, j * LANES : (j + 1) * LANES] = summed.astype(jnp.bfloat16)

    each(tiles, taps_tile)
    advance()

    def memory_wait(step, carry):
        @pl.when(seq - step >= 0)
        def _():
            memory_copy(step).wait_send()

        @pl.when(seq + step < count)
        def _():
            memory_copy(step).wait_recv()

        return carry

    lax.fori_loop(1, count, memory_wait, 0)

    def memory_tile(i):
        at = tile_rows(i)

        def one(step, carry):
            came = memory_recv[step - 1, at, :].astype(jnp.float32)
            return carry + jnp.where(seq + step < count, came, 0.0)

        grad = lax.fori_loop(1, count, one, d_memory_ref[seq, at, :].astype(jnp.float32))
        lane = lax.broadcasted_iota(jnp.int32, grad.shape, 1)
        turned = grad * table_ref[at, :LANES] - turn_half(grad) * table_ref[at, LANES:]
        side[at, memory_at : memory_at + LANES] = jnp.where(lane < HD, turned, grad).astype(
            jnp.bfloat16
        )
        if not merged:
            side[at, query_at:memory_at] = d_query_ref[at, :]

    each(tiles, memory_tile)

    def weight_block(k):
        size = model // count
        block = pl.ds(pl.multiple_of(k * size, LANES), size)
        grad = matmul_first(normed[:, block], side[...])
        if merged:
            bits = seq_bits()
            g_side_ref[place_bits(k, bits)] = grad.reshape(g_side_ref.shape[bits:]).astype(
                jnp.bfloat16
            )
        else:
            g_side_ref[block, :] = grad.astype(jnp.bfloat16)

    each(count, weight_block)
    if merged:
        reduction.allow(len(chunks))
    advance()

    def norm_tile(i):
        at = tile_rows(i)
        part = (
            matmul_last(d_gate_z_ref[at, :], gate_weight[...])
            + matmul_last(side[at, :inner], input_weight[...])
            + matmul_last(side[at, inner:step_at], maps_weight[...]) / lax.axis_size("head")
            + matmul(side[at, step_at:query_at], step_weight[...])
            + matmul_last(side[at, query_at:memory_at], query_weight[...])
            + matmul_last(side[at, memory_at:], memory_weight[...])
        )
        norm_send[at, :] = part.astype(jnp.bfloat16)
        norm_copy(i).start()

    each(tiles, norm_tile)

    advance()
    if not merged:
        g_gain_ref[...] = jnp.zeros_like(g_gain_ref)

    def last_tile(i):
        at = tile_rows(i)
        norm_copy(i).wait()
        d_norm = norm_send[at, :].astype(jnp.float32) + norm_recv[at, :].astype(jnp.float32)
        hidden = tokens_ref[at, :].astype(jnp.float32)
        inverse = lax.rsqrt(jnp.mean(hidden * hidden, axis=1, keepdims=True) + eps_norm)
        e_one = d_norm * gain_ref[...]
        cross = jnp.sum(e_one * hidden, axis=1, keepdims=True) / model
        d_tokens_ref[at, :] = (
            d_second_ref[at, :] + inverse * e_one - hidden * (inverse * inverse * inverse * cross)
        )
        g_gain_ref[gain_row : gain_row + 1, :] += jnp.sum(
            d_norm * hidden * inverse, axis=0, keepdims=True
        )

    each(tiles, last_tile)
    if merged:
        small_sum = SmallSum(small_in, small_buf, sem_small)
        small_sum.start()
        reduction.finish()
        small_out[...] = small_sum.finish()

    @pl.when(seq > 0)
    def _():
        halo_copy.wait_send()
        for p in range(pieces):
            chain_copy(p).wait_send()


def mixer_back(common, saved, attention, grads=None, came=()):
    tokens = common[0]
    rows, model = tokens.shape
    gate_weight, query_weight, memory_weight, taps = common[4], common[8], common[9], common[10]
    merged = grads is not None
    count = lax.axis_size("seq")
    inner = gate_weight.shape[1]
    width = taps.shape[1]
    state_width = (width - inner) // 2
    tiles = rows // CHUNK
    pieces = inner // PIECE
    memory_width = memory_weight.shape[1]
    side = width + LANES + query_weight.shape[1] + memory_width
    vmem = pl.BlockSpec(memory_space=pltpu.VMEM)
    hbm = pl.BlockSpec(memory_space=pl.ANY)
    low, full = jnp.bfloat16, jnp.float32
    shape = jax.ShapeDtypeStruct
    operands = [*common, *saved]
    in_specs = [vmem] * (len(operands) + len(attention))
    operands += attention
    chunks = None
    scratch = [
        pltpu.VMEM((rows, model), low),
        pltpu.VMEM((LANES, inner), low),
        pltpu.VMEM((rows, width), full),
        pltpu.VMEM((rows + HALO, width), full),
        pltpu.VMEM((rows, inner), full),
        pltpu.VMEM((rows, 2 * state_width), full),
        pltpu.VMEM((rows, LANES), full),
        pltpu.VMEM((tiles, state_width, inner), full),
        pltpu.VMEM((state_width, inner), full),
        pltpu.VMEM((HALO, inner), full),
        pltpu.VMEM((state_width, inner), full),
        pltpu.VMEM((1, inner), full),
        pltpu.VMEM((rows, side), low),
        pltpu.VMEM((state_width, inner), low),
        pltpu.VMEM((state_width, inner), low),
        pltpu.VMEM((rows, 2 * state_width), low),
        pltpu.VMEM((rows, 2 * state_width), low),
        pltpu.VMEM((max(count - 1, 1), rows, memory_width), low),
        pltpu.VMEM((rows, model), low),
        pltpu.VMEM((rows, model), low),
        pltpu.SemaphoreType.DMA((2, count)),
        pltpu.SemaphoreType.DMA((2,)),
        pltpu.SemaphoreType.DMA((2, pieces)),
        pltpu.SemaphoreType.DMA((2,)),
        pltpu.SemaphoreType.DMA((2, tiles)),
    ]
    if merged:
        blocks = list(grads)
        widths = [g.shape[-1] for g in grads] + [side]
        chunks = column_chunks(widths)
        loaded = [pltpu.VMEM(x.shape, x.dtype) for x in operands]
        scratch = loaded + [pltpu.SemaphoreType.DMA((len(loaded),))] + scratch
        operands += blocks + list(came)
        in_specs = [hbm] * len(operands)
        own = blocks[0].shape[-2]
        small = (HALO, model)
        out_shape = (
            [shape((rows, model), full)]
            + [shape((2, 2, own, w), low) for w in widths]
            + [shape(small, full)]
        )
        scratch += [
            pltpu.VMEM(blocks[0].shape[:-1] + (side,), low),
            pltpu.VMEM((count * rows, memory_width), full),
            pltpu.VMEM((count, rows, memory_width), low),
        ]
        scratch += small_scratch(small) + reduction_scratch(chunks, widths, own)
    else:
        out_shape = [
            shape((rows, model), full),
            shape((model, side), low),
            shape((HALO, width), full),
            shape((1, model), full),
            shape((HALO, LANES), full),
        ]
    return pl.pallas_call(
        functools.partial(mixer_back_kernel, merged, chunks),
        out_shape=out_shape,
        in_specs=in_specs,
        out_specs=[vmem] * len(out_shape),
        scratch_shapes=scratch,
        compiler_params=pltpu.CompilerParams(
            collective_id=3, has_side_effects=True, vmem_limit_bytes=62 << 20
        ),
        name="mixer_back",
    )(*operands)


def finish_kernel(sizes, count, *refs):
    inner, maps, heads, query, own = sizes
    full = jnp.float32
    refs = list(refs)

    def take(number):
        nonlocal refs
        now, refs = refs[:number], refs[number:]
        return now

    sums, (small,), passed = take(5), take(1), take(2)
    outs, small_outs, passed_outs = take(count), take(9), take(2)
    loaded, held, wide = take(5), take(2), take(count)
    sem_in, sem_out = refs
    loads = [
        pltpu.make_async_copy(a, b, sem_in.at[k])
        for k, (a, b) in enumerate(zip([*sums, *passed], loaded + held))
    ]
    for copy in loads:
        copy.start()
    down, feed, mixed, gate, side = loaded
    half = feed.shape[1] // 2
    step_at = inner + maps
    query_at = step_at + LANES
    memory_at = query_at + query
    parts = (
        (0, lambda: down[...]),
        (1, lambda: feed[:, :half]),
        (1, lambda: feed[:, half:]),
        (2, lambda: mixed[:, :inner]),
        (2, lambda: mixed[:, inner:]),
        (3, lambda: gate[...]),
        (4, lambda: side[:, :inner]),
        (4, lambda: side[:, inner:step_at]),
        (4, lambda: side[:, query_at:memory_at]),
        (4, lambda: side[:, memory_at:]),
    )
    stores = []
    for k, (group, value) in enumerate(parts):
        if k == 0 or parts[k - 1][0] != group:
            loads[group].wait()
        wide[k][...] = value().astype(full)
        stores.append(pltpu.make_async_copy(wide[k], outs[k], sem_out.at[k]))
        stores[-1].start()
    o_step, o_conv_inner, o_conv_maps, o_mixer_gain, o_rate, o_bias, o_skip, o_mamba, o_feed = (
        small_outs
    )
    o_step[...] = side[:, step_at:query_at].astype(full).T[:heads]
    seq = lax.axis_index("seq")
    value = small[...]
    width = value.shape[1]
    o_conv_inner[...] = value[:4, :inner]
    o_conv_maps[...] = value[:4, inner:]
    turned = pltpu.roll(value, lax.rem(width - seq * own, width), 1)
    o_mixer_gain[...] = turned[5:6, :own]
    o_feed[...] = turned[6:7, :own]
    for k, out in enumerate((o_rate, o_bias, o_skip)):
        out[...] = value[7:8, k * LANES : (k + 1) * LANES][:, :heads]
    for k in range(inner // LANES):
        o_mamba[k : k + 1, :] = value[4:5, k * LANES : (k + 1) * LANES]
    for k, (a, b) in enumerate(zip(held, passed_outs)):
        loads[5 + k].wait()
        stores.append(pltpu.make_async_copy(a, b, sem_out.at[count + k]))
        stores[-1].start()
    for copy in stores:
        copy.wait()


def finish_outputs(sums, small, passed, sizes):
    inner, maps, heads, query, own = sizes
    sums = [s.reshape(own, s.shape[-1]) for s in sums]
    half = sums[1].shape[1] // 2
    attention = sums[2].shape[1] - inner
    memory = sums[4].shape[1] - inner - maps - LANES - query
    full = jnp.float32
    widths = (sums[0].shape[1], half, half, inner, attention, inner, inner, maps, query, memory)
    big = [jax.ShapeDtypeStruct((own, w), full) for w in widths]
    little = [
        jax.ShapeDtypeStruct(s, full)
        for s in (
            (heads, own),
            (4, inner),
            (4, maps),
            (1, own),
            (1, heads),
            (1, heads),
            (1, heads),
            (inner // LANES, LANES),
            (1, own),
        )
    ]
    vmem = pl.BlockSpec(memory_space=pltpu.VMEM)
    hbm = pl.BlockSpec(memory_space=pl.ANY)
    return pl.pallas_call(
        functools.partial(finish_kernel, sizes, len(big)),
        out_shape=big + little + [jax.ShapeDtypeStruct(p.shape, p.dtype) for p in passed],
        in_specs=[hbm] * 5 + [vmem] + [hbm] * 2,
        out_specs=[hbm] * len(big) + [vmem] * len(little) + [hbm] * 2,
        scratch_shapes=[pltpu.VMEM(s.shape, s.dtype) for s in [*sums, *passed]]
        + [pltpu.VMEM(s.shape, full) for s in big]
        + [
            pltpu.SemaphoreType.DMA((7,)),
            pltpu.SemaphoreType.DMA((len(big) + 2,)),
        ],
        compiler_params=pltpu.CompilerParams(vmem_limit_bytes=60 << 20),
        name="finish_outputs",
    )(*sums, small, *passed)


def rotation_table(position):
    half = HD // 2
    lane = jnp.arange(LANES)
    inverse_freq = rope_base ** (-(lane % half).astype(jnp.float32) / half)
    angles = position.astype(jnp.float32)[:, None] * inverse_freq[None, :]
    sign = jnp.where(lane % HD < half, -1.0, 1.0)
    return jnp.concatenate([jnp.cos(angles), sign[None, :] * jnp.sin(angles)], axis=1)


def body(
    tokens,
    seg_ids,
    mixer_gain,
    mamba_gate,
    mamba_input,
    mamba_maps,
    mamba_step,
    conv_inner,
    conv_maps,
    log_rate,
    step_bias,
    skip_gain,
    mamba_gain,
    mamba_output,
    query_weight,
    memory_weight,
    attention_out,
    feed_gain,
    gate_weight,
    lift_weight,
    down_weight,
    cotangent,
):
    tokens, cotangent = tokens[0], cotangent[0]
    rows, wide = tokens.shape
    tap_count, inner = conv_inner.shape
    head_count = log_rate.shape[0]
    offset = lax.axis_index("seq") * rows
    table = rotation_table(offset + jnp.arange(rows, dtype=jnp.int32))
    (
        gate_z,
        pre,
        conv,
        raw,
        cum,
        y,
        states,
        query,
        memory,
        attention,
        attention_low,
        logs,
        window,
        key_segments,
        step_weight,
        taps,
        rate,
        skip,
    ) = mixer_forward(
        tokens,
        mixer_gain[None],
        seg_ids,
        table,
        mamba_gate,
        mamba_input,
        mamba_maps,
        mamba_step.T,
        query_weight,
        memory_weight,
        conv_inner,
        conv_maps,
        step_bias,
        log_rate,
        skip_gain,
    )
    all_memory = memory.reshape(memory.shape[0] * rows, memory.shape[2])
    (
        layer_out,
        d_second,
        d_y,
        d_gate_z,
        d_attention,
        g_feed,
        g_mixed,
        g_down,
        g_gate,
        g_feed_gain,
        g_mamba_gain,
        *came,
    ) = feed_layer(
        y,
        gate_z,
        attention_low,
        tokens,
        cotangent,
        mixer_gain,
        mamba_gain,
        feed_gain,
        mamba_output,
        attention_out,
        gate_weight,
        lift_weight,
        down_weight,
    )
    common = [
        tokens,
        mixer_gain[None],
        window,
        table,
        mamba_gate,
        mamba_input,
        mamba_maps,
        step_weight,
        query_weight,
        memory_weight,
        taps,
        rate,
        skip,
    ]
    saved = [pre, conv, raw, cum, y, states, d_second, d_y, d_gate_z]
    early = [g_down, g_feed, g_mixed, g_gate]
    if lax.axis_size("seq") == 4:
        grad_tokens, *sums, small = mixer_back(
            common,
            saved,
            [
                query,
                all_memory,
                key_segments,
                attention,
                logs,
                d_attention,
                g_feed_gain,
                g_mamba_gain,
            ],
            early,
            came,
        )
    else:
        starts = offset + jnp.arange(rows // TILE, dtype=jnp.int32) * TILE
        reach = seg_ids[0, KEY_TILE - 1 :: KEY_TILE]
        own = lax.dynamic_slice_in_dim(seg_ids[0], offset, rows)[::TILE]
        low = jnp.sum((reach[None, :] < own[:, None]).astype(jnp.int32), axis=1)
        spans = (offset[None], low, (starts + TILE - 1) // KEY_TILE)
        d_query, d_memory = attention_back(
            spans, query, all_memory, window, key_segments, attention, logs, d_attention, table
        )
        grad_tokens, g_side, g_taps, g_mixer_gain, g_heads = mixer_back(
            common, saved, [d_query, d_memory.reshape(memory.shape)]
        )
        *sums, small = reduce_gradients(
            early + [g_side],
            jnp.concatenate(
                [
                    g_taps[:tap_count],
                    jnp.pad(g_mamba_gain, ((0, 0), (0, wide - inner))),
                    g_mixer_gain,
                    g_feed_gain,
                    jnp.pad(g_heads[:3].reshape(1, 3 * LANES), ((0, 0), (0, wide - 3 * LANES))),
                ],
                axis=0,
            ),
        )
    sizes = (
        inner,
        conv_maps.shape[1],
        head_count,
        query_weight.shape[1],
        wide // lax.axis_size("seq"),
    )
    (
        o_down,
        o_gate,
        o_lift,
        o_output,
        o_attention,
        o_gate_z,
        o_inner,
        o_maps,
        o_query,
        o_memory,
        o_step,
        o_conv_inner,
        o_conv_maps,
        o_mixer_gain,
        o_rate,
        o_bias,
        o_skip,
        o_mamba_gain,
        o_feed_gain,
        layer_out,
        grad_tokens,
    ) = finish_outputs(sums, small, (layer_out, grad_tokens), sizes)
    return (
        layer_out[None],
        grad_tokens[None],
        o_mixer_gain[0],
        o_gate_z,
        o_inner,
        o_maps,
        o_step.T,
        o_conv_inner,
        o_conv_maps,
        o_rate[0],
        o_bias[0],
        o_skip[0],
        o_mamba_gain.reshape(inner),
        o_output,
        o_query,
        o_memory,
        o_attention,
        o_feed_gain[0],
        o_gate,
        o_lift,
        o_down,
    )


def solution(mesh):
    return jax.shard_map(
        body,
        mesh=mesh,
        in_specs=(
            P("batch", "seq", None),
            P("batch", None),
            P(),
            P(None, "head"),
            P(None, "head"),
            P(),
            P(None, "head"),
            P(None, "head"),
            P(),
            P("head"),
            P("head"),
            P("head"),
            P("head"),
            P(None, "head"),
            P(None, "head"),
            P(None, "head"),
            P(None, "head"),
            P(),
            P(None, "head"),
            P(None, "head"),
            P(None, "head"),
            P("batch", "seq", None),
        ),
        out_specs=(
            P("batch", "seq", None),
            P("batch", "seq", None),
            P("seq"),
            P("seq", "head"),
            P("seq", "head"),
            P("seq", None),
            P("seq", "head"),
            P(None, "head"),
            P(),
            P("head"),
            P("head"),
            P("head"),
            P("head"),
            P("seq", "head"),
            P("seq", "head"),
            P("seq", "head"),
            P("seq", "head"),
            P("seq"),
            P("seq", "head"),
            P("seq", "head"),
            P("seq", "head"),
        ),
        check_vma=False,
    )
```

```python
import functools

import jax
import jax.numpy as jnp
from jax import lax
from jax.experimental import pallas as pl
from jax.experimental.pallas import tpu as pltpu
from jax.sharding import PartitionSpec as P

HD = 64
eps_norm = 1e-05
rope_base = 10000.0
neg_large = -1e30
highest = lax.Precision.HIGHEST


LANES = 128
MOST = 512
TAIL = (512, 384, 256, 128, 128, 128)
AHEAD = 7
EARLIER = 3
LAG = 3
PATTERN = (0, 1, 2, 0, 1, 3, 0, 1, 0, 1, 2, 0, 1, 3, 0, 1)
MESH = pl.DeviceIdType.MESH


def exchange(source, target, send_sem, recv_sem, device):
    return pltpu.make_async_remote_copy(
        src_ref=source,
        dst_ref=target,
        send_sem=send_sem,
        recv_sem=recv_sem,
        device_id=device,
        device_id_type=MESH,
    )


def moving(kernel, inputs, loaded, outputs, *refs):
    given, refs = refs[:inputs], refs[inputs:]
    targets, refs = refs[:outputs], refs[outputs:]
    taken, refs = refs[:loaded], refs[loaded:]
    held, refs = refs[:outputs], refs[outputs:]
    sem_in, sem_out, refs = refs[0], refs[1], refs[2:]
    loads = [
        pltpu.make_async_copy(source, target, sem_in.at[k])
        for k, (source, target) in enumerate(zip(given[:loaded], taken))
    ]
    for load in loads:
        load.start()
    stores = [
        pltpu.make_async_copy(source, target, sem_out.at[k])
        for k, (source, target) in enumerate(zip(held, targets))
    ]
    kernel(loads, stores, *taken, *given[loaded:], *held, *refs)
    for store in stores:
        store.wait()


def moving_scratch(operands, results):
    return [pltpu.VMEM(x.shape, x.dtype) for x in [*operands, *results]] + [
        pltpu.SemaphoreType.DMA((len(operands),)),
        pltpu.SemaphoreType.DMA((len(results),)),
    ]


def start_all(stores, *which):
    for k in which:
        stores[k].start()


def each(count, action):
    span(0, count, action)


def span(first, last, action):
    lax.fori_loop(first, last, lambda i, carry: (action(i), carry)[1], 0)


def column_chunks(widths):
    chunks = []
    for group, width in enumerate(widths):
        count = -(-width // MOST)
        tiles = width // LANES
        sizes = [(tiles // count + (1 if k < tiles % count else 0)) * LANES for k in range(count)]
        if group == len(widths) - 1 and width == sum(TAIL):
            sizes = TAIL
        start = 0
        for size in sizes:
            chunks.append((group, start, size))
            start += size
    return chunks


def seq_bits():
    return (lax.axis_size("seq") - 1).bit_length()


def place_bits(place, bits):
    return tuple(lax.rem(place // 2 ** (bits - 1 - b), 2) for b in range(bits))


def seq_blocks(grad):
    bits = seq_bits() + 2
    return grad.reshape((2,) * bits + (grad.shape[0] >> bits, grad.shape[1]))


def peer_device():
    return (lax.axis_index("seq"), 1 - lax.axis_index("head"), lax.axis_index("batch"))


def other_device(step):
    seq, batch = lax.axis_index("seq"), lax.axis_index("batch")
    batches = lax.axis_size("batch")
    place = lax.rem(seq * batches + batch + step, lax.axis_size("seq") * batches)
    return (place // batches, lax.axis_index("head"), lax.rem(place, batches))


def greet_all(barrier, with_peer):
    world = lax.axis_size("seq") * lax.axis_size("batch")
    span(
        1,
        world,
        lambda step: pl.semaphore_signal(
            barrier, inc=1, device_id=other_device(step), device_id_type=MESH
        ),
    )
    if with_peer:
        pl.semaphore_signal(barrier, inc=1, device_id=peer_device(), device_id_type=MESH)
    pl.semaphore_wait(barrier, world - 1 + (1 if with_peer else 0))


class SmallSum:
    def __init__(self, source, slots, sems):
        self.source, self.slots, self.sems = source, slots, sems
        self.world = slots.shape[0]
        self.mine = lax.axis_index("seq") * lax.axis_size("batch") + lax.axis_index("batch")

    def copy(self, step):
        return exchange(
            self.source,
            self.slots.at[self.mine],
            self.sems.at[0, step],
            self.sems.at[1, step],
            other_device(step),
        )

    def start(self):
        span(1, self.world, lambda step: self.copy(step).start())

    def finish(self):
        span(1, self.world, lambda step: self.copy(step).wait())
        self.slots[self.mine] = self.source[...]
        return lax.fori_loop(
            1, self.world, lambda k, total: total + self.slots[k], self.slots[0]
        )


def small_scratch(shape):
    world = lax.axis_size("seq") * lax.axis_size("batch")
    return [
        pltpu.VMEM(shape, jnp.float32),
        pltpu.VMEM((world,) + shape, jnp.float32),
        pltpu.SemaphoreType.DMA((2, world)),
    ]


class Reduction:
    def __init__(self, chunks, sources, outs, scratch, given=()):
        self.chunks, self.sources, self.outs, self.given = chunks, sources, outs, given
        groups = len(sources)
        self.bits = seq_bits() + 2
        scratch = list(scratch)
        self.parts = [scratch[k * groups : (k + 1) * groups] for k in range(self.bits)]
        self.own, self.sem_own, self.sem_halve, self.sem_back = scratch[self.bits * groups :]
        self.setup()

    def setup(self):
        self.seq, self.head = lax.axis_index("seq"), lax.axis_index("head")
        self.batch = lax.axis_index("batch")
        place = self.seq * 4 + self.batch
        self.mine = [lax.rem(place // 2 ** (self.bits - 1 - k), 2) for k in range(self.bits)]
        self.done = [0] * (self.bits + 2)
        self.sent = self.held = self.limit = 0

    def peer(self, bit):
        step = (1 - 2 * self.mine[bit]) * 2 ** (self.bits - 1 - bit)
        if bit < self.bits - 2:
            return (self.seq + step // 4, self.head, self.batch)
        return (self.seq, self.head, self.batch + step)

    def order(self, k):
        low, high, last = self.bits - 1, self.bits - 2, self.bits - 3
        rest = [b for b in range(self.bits - 3, -1, -1)]
        if last < 0:
            return [low, high] if k % 2 == 0 else [high, low]
        kind = PATTERN[k % len(PATTERN)]
        if kind == 0:
            return [low, high] + rest
        if kind == 1:
            return [high, low] + rest
        if kind == 2:
            return [last, low, high] + rest[1:]
        return [last, high, low] + rest[1:]

    def place(self, k):
        group, start, size = self.chunks[k]
        return group, pl.ds(start, size)

    def cut(self, k, step, kept):
        order = self.order(k)
        left = [b for b in range(self.bits) if b not in order[:step]]
        bit = order[step]
        value = self.mine[bit] if kept else 1 - self.mine[bit]
        return tuple(value if b == bit else slice(None) for b in left)

    def halve_copy(self, k, step):
        group, columns = self.place(k)
        source = self.sources[group] if step == 0 else self.parts[step - 1][group]
        target = self.parts[step][group]
        away = self.cut(k, step, False)
        return exchange(
            source.at[away + (slice(None), columns)],
            target.at[(slice(None),) * (len(away) - 1) + (slice(None), columns)],
            self.sem_halve.at[0, k, step],
            self.sem_halve.at[1, k, step],
            self.peer(self.order(k)[step]),
        )

    def first_copy(self, k):
        group, columns = self.place(k)
        if group >= len(self.given) or k >= EARLIER:
            return self.halve_copy(k, 0)
        where = (slice(None),) * self.bits + (columns,)
        return pltpu.make_async_copy(
            self.given[group].at[where], self.parts[0][group].at[where], self.sem_halve.at[0, k, 0]
        )

    def own_copy(self, k):
        group, columns = self.place(k)
        size = self.chunks[k][2]
        kept = self.cut(k, 0, True)
        return pltpu.make_async_copy(
            self.sources[group].at[kept + (slice(None), columns)],
            self.own.at[(k % 2,) + (slice(None),) * self.bits + (pl.ds(0, size),)],
            self.sem_own.at[k],
        )

    def add(self, k, step):
        group, columns = self.place(k)
        size = self.chunks[k][2]
        target = self.parts[step][group]
        left = self.bits - 1 - step

        def one(index):
            every = index + (slice(None), columns)
            if step == 0:
                own = self.own[(k % 2,) + index + (slice(None), slice(0, size))]
            else:
                kept = self.cut(k, step, True)
                spot = [v for v in kept]
                rest = iter(index)
                spot = tuple(v if not isinstance(v, slice) else next(rest) for v in spot)
                own = self.parts[step - 1][group][spot + (slice(None), columns)]
            value = own + target[every]
            if step == self.bits - 1:
                self.outs[group][self.mine[-2], self.mine[-1], :, columns] = value
            else:
                target[every] = value

        span(
            0,
            2**left,
            lambda n: one(place_bits(n, left)),
        )

    def back_copy(self, k, turn):
        group, columns = self.place(k)
        out = self.outs[group]
        high, low = self.mine[-2], self.mine[-1]
        first_low = self.order(k).index(self.bits - 1) < self.order(k).index(self.bits - 2)
        bit = self.bits - 2 if first_low == (turn == 0) else self.bits - 1
        if turn == 0:
            part = out.at[high, low, :, columns]
        elif first_low:
            part = out.at[:, low, :, columns]
        else:
            part = out.at[high, :, :, columns]
        return exchange(
            part, part, self.sem_back.at[0, k, turn], self.sem_back.at[1, k, turn], self.peer(bit)
        )

    def refill(self):
        while self.sent < min(self.limit, self.done[0] + AHEAD):
            self.first_copy(self.sent).start()
            self.sent += 1
        while self.held < min(self.limit, self.done[0] + 2):
            self.own_copy(self.held).start()
            self.held += 1

    def allow(self, limit):
        self.limit = limit
        self.refill()

    def advance(self):
        stages = self.bits + 2
        for step in range(stages - 1, -1, -1):
            k = self.done[step]
            before = self.done[step - 1] if step else self.limit
            if k >= before or (step and before - k < LAG and before < self.limit):
                continue
            if step < self.bits:
                if step == 0:
                    self.first_copy(k).wait()
                    self.own_copy(k).wait()
                else:
                    self.halve_copy(k, step).wait()
                self.add(k, step)
                if step + 1 < self.bits:
                    self.halve_copy(k, step + 1).start()
                else:
                    self.back_copy(k, 0).start()
            elif step == self.bits:
                self.back_copy(k, 0).wait()
                self.back_copy(k, 1).start()
            else:
                self.back_copy(k, 1).wait()
            self.done[step] += 1
            if step == 0:
                self.refill()

    def finish(self):
        while self.done[-1] < len(self.chunks):
            self.advance()


class FirstHalving(Reduction):
    def __init__(self, chunks, sources, targets, sems):
        self.chunks, self.sources = chunks, sources
        self.bits = seq_bits() + 2
        self.parts, self.sem_halve = [targets], sems
        self.setup()


def reduction_scratch(chunks, widths, rows):
    bits = seq_bits() + 2
    parts = len(chunks)
    most = max(size for _, _, size in chunks)
    low = jnp.bfloat16
    return [
        pltpu.VMEM((2,) * (bits - 1 - step) + (rows, w), low)
        for step in range(bits)
        for w in widths
    ] + [
        pltpu.VMEM((2,) * bits + (rows, most), low),
        pltpu.SemaphoreType.DMA((parts,)),
        pltpu.SemaphoreType.DMA((2, parts, bits)),
        pltpu.SemaphoreType.DMA((2, parts, 2)),
    ]


def reduce_kernel(chunks, *refs):
    count = 1 + max(c[0] for c in chunks)
    sources, refs = refs[:count], refs[count:]
    small_given, refs = refs[0], refs[1:]
    outs, refs = refs[:count], refs[count:]
    small_out, small_in, small_buf, sem_small, *refs = refs
    greet_all(pltpu.get_barrier_semaphore(), False)
    reduction = Reduction(chunks, sources, outs, refs)
    reduction.allow(len(chunks))
    small_in[...] = small_given[...]
    small_sum = SmallSum(small_in, small_buf, sem_small)
    small_sum.start()
    reduction.finish()
    small_out[...] = small_sum.finish()


def reduce_gradients(grads, small):
    widths = [g.shape[1] for g in grads]
    chunks = column_chunks(widths)
    blocks = [seq_blocks(g) for g in grads]
    rows = blocks[0].shape[-2]
    vmem = pl.BlockSpec(memory_space=pltpu.VMEM)
    return pl.pallas_call(
        functools.partial(reduce_kernel, chunks),
        out_shape=[jax.ShapeDtypeStruct((2, 2, rows, w), jnp.bfloat16) for w in widths]
        + [jax.ShapeDtypeStruct(small.shape, jnp.float32)],
        in_specs=[pl.BlockSpec(memory_space=pl.ANY)] * len(grads) + [vmem],
        out_specs=[vmem] * (len(grads) + 1),
        scratch_shapes=small_scratch(small.shape) + reduction_scratch(chunks, widths, rows),
        compiler_params=pltpu.CompilerParams(
            collective_id=0, has_side_effects=True, vmem_limit_bytes=56 << 20
        ),
        name="reduce_gradients",
    )(*blocks, small)


def matmul(former, latter):
    return jnp.dot(former, latter, preferred_element_type=jnp.float32)


def matmul_last(former, latter):
    return lax.dot_general(
        former, latter, (((1,), (1,)), ((), ())), preferred_element_type=jnp.float32
    )


def matmul_first(former, latter):
    return lax.dot_general(
        former, latter, (((0,), (0,)), ((), ())), preferred_element_type=jnp.float32
    )


TILE = 128


def sigmoid(v):
    return 1.0 / (1.0 + jnp.exp(-v))


def greet(barrier, devices):
    for device in devices:
        pl.semaphore_signal(barrier, inc=1, device_id=device, device_id_type=MESH)
    pl.semaphore_wait(barrier, len(devices))


def tile_rows(i):
    return pl.ds(pl.multiple_of(i * TILE, TILE), TILE)


FEED_TILE = 256


def feed_rows(i):
    return pl.ds(pl.multiple_of(i * FEED_TILE, FEED_TILE), FEED_TILE)


def feed_kernel(merged, loads, stores, *refs):
    (
        y_ref,
        gate_z_ref,
        attention_ref,
        tokens_ref,
        cotangent_ref,
        mixer_gain_ref,
        mamba_gain_ref,
        feed_gain_ref,
        mamba_output_ref,
        attention_out_ref,
        gate_weight_hbm,
        lift_weight_hbm,
        down_weight_hbm,
        out_ref,
        d_second_ref,
        d_y_ref,
        d_gate_z_ref,
        d_attention_ref,
        g_feed_ref,
        g_mixed_ref,
        g_down_ref,
        g_gate_ref,
        g_feed_gain_ref,
        g_mamba_gain_ref,
    ) = refs[: 24]
    refs = refs[24:]
    if merged:
        came_refs, refs = refs[:2], refs[2:]
    (
        gate_weight,
        lift_weight,
        down_weight,
        normed,
        gated,
        g_six,
        inverse_six,
        second,
        inverse_two,
        normed2,
        active,
        d_feed,
        d_mix,
        d_gated,
        square_send,
        square_recv,
        cross_send,
        cross_recv,
        mixed_send,
        mixed_recv,
        lift_send,
        lift_recv,
        norm_send,
        norm_recv,
        weight_sem,
        sem_square,
        sem_cross,
        sem_mixed,
        sem_lift,
        sem_norm,
        *sem_first,
    ) = refs
    rows = y_ref.shape[0]
    tiles = rows // FEED_TILE
    inner = y_ref.shape[1]
    width = feed_gain_ref.shape[1]
    feed = down_weight.shape[1]
    all_inner = inner * lax.axis_size("head")
    peer = peer_device()
    weight_loads = [
        pltpu.make_async_copy(source, target, weight_sem.at[k])
        for k, (source, target) in enumerate(
            (
                (gate_weight_hbm, gate_weight),
                (lift_weight_hbm, lift_weight),
                (down_weight_hbm, down_weight),
            )
        )
    ]
    for load in weight_loads:
        load.start()
    devices = [peer]
    if merged:
        first = FirstHalving(
            column_chunks((g_down_ref.shape[-1], g_feed_ref.shape[-1]))[:EARLIER],
            [g_down_ref, g_feed_ref],
            came_refs,
            sem_first[0],
        )
        devices += [first.peer(bit) for bit in range(first.bits - 3, first.bits)]
    greet(pltpu.get_barrier_semaphore(), devices)
    for load in loads:
        load.wait()
    mamba_gain = jnp.concatenate(
        [mamba_gain_ref[k : k + 1, :] for k in range(mamba_gain_ref.shape[0])], axis=1
    )

    def swap(send, recv, sems, i):
        rows_now = feed_rows(i)
        return exchange(send.at[rows_now], recv.at[rows_now], sems.at[0, i], sems.at[1, i], peer)

    def gate_tile(i):
        at = feed_rows(i)
        hidden = tokens_ref[at, :].astype(jnp.float32)
        inverse = lax.rsqrt(jnp.mean(hidden * hidden, axis=1, keepdims=True) + eps_norm)
        normed[at, :] = (hidden * inverse * mixer_gain_ref[...]).astype(jnp.bfloat16)
        gate_now = gate_z_ref[at, :]
        value = y_ref[at, :] * gate_now * sigmoid(gate_now)
        g_six[at, :] = value
        square_send[at, :] = jnp.broadcast_to(
            jnp.sum(value * value, axis=1, keepdims=True), (FEED_TILE, LANES)
        )
        swap(square_send, square_recv, sem_square, i).start()

    each(tiles, gate_tile)

    def mixed_tile(i):
        at = feed_rows(i)
        swap(square_send, square_recv, sem_square, i).wait()
        total = square_send[at, :] + square_recv[at, :]
        inverse = lax.rsqrt(total[:, :1] / all_inner + eps_norm)
        inverse_six[at, :] = jnp.broadcast_to(inverse, (FEED_TILE, LANES))
        low = (g_six[at, :] * inverse * mamba_gain).astype(jnp.bfloat16)
        gated[at, :] = low
        part = matmul_last(low, mamba_output_ref[...]) + matmul_last(
            attention_ref[at, :], attention_out_ref[...]
        )
        mixed_send[at, :] = part.astype(jnp.bfloat16)
        swap(mixed_send, mixed_recv, sem_mixed, i).start()

    each(tiles, mixed_tile)
    for load in weight_loads:
        load.wait()

    def feed_tile(i):
        at = feed_rows(i)
        swap(mixed_send, mixed_recv, sem_mixed, i).wait()
        total = mixed_send[at, :].astype(jnp.float32) + mixed_recv[at, :].astype(jnp.float32)
        hidden = tokens_ref[at, :].astype(jnp.float32) + total
        second[at, :] = hidden
        inverse = lax.rsqrt(jnp.mean(hidden * hidden, axis=1, keepdims=True) + eps_norm)
        inverse_two[at, :] = jnp.broadcast_to(inverse, (FEED_TILE, LANES))
        low = (hidden * inverse * feed_gain_ref[...]).astype(jnp.bfloat16)
        normed2[at, :] = low
        gate_now = matmul(low, gate_weight[...])
        lift_now = matmul(low, lift_weight[...])
        sig = sigmoid(gate_now)
        silu = gate_now * sig
        act = (silu * lift_now).astype(jnp.bfloat16)
        active[at, :] = act
        lift_send[at, :] = matmul_last(act, down_weight[...]).astype(jnp.bfloat16)
        swap(lift_send, lift_recv, sem_lift, i).start()
        d_act = matmul(cotangent_ref[at, :], down_weight[...])
        d_gate = (d_act * lift_now * (sig * (1.0 + gate_now * (1.0 - sig)))).astype(jnp.bfloat16)
        d_lift = (d_act * silu).astype(jnp.bfloat16)
        d_feed[at, :feed] = d_gate
        d_feed[at, feed:] = d_lift
        part = matmul_last(d_gate, gate_weight[...]) + matmul_last(d_lift, lift_weight[...])
        norm_send[at, :] = part.astype(jnp.bfloat16)
        swap(norm_send, norm_recv, sem_norm, i).start()

    each(tiles, feed_tile)
    blocks = lax.axis_size("seq") if merged else width // 256

    def store(target, k, grad):
        if merged:
            index = place_bits(k, seq_bits())
            target[index] = grad.reshape(target.shape[len(index) :]).astype(jnp.bfloat16)
        else:
            target[pl.ds(pl.multiple_of(k * 256, 256), 256), :] = grad.astype(jnp.bfloat16)

    def block_columns(k):
        size = width // blocks
        return pl.ds(pl.multiple_of(k * size, LANES), size)

    def feed_weights(k):
        block = block_columns(k)
        store(g_down_ref, k, matmul_first(cotangent_ref[:, block], active[...]))
        store(g_feed_ref, k, matmul_first(normed2[:, block], d_feed[...]))

    each(blocks, feed_weights)
    if merged:
        for k in range(EARLIER):
            first.halve_copy(k, 0).start()
    start_all(stores, 5, 7)
    g_feed_gain_ref[...] = jnp.zeros_like(g_feed_gain_ref)
    g_mamba_gain_ref[...] = jnp.zeros_like(g_mamba_gain_ref)

    def norm_tile(i):
        at = feed_rows(i)
        swap(norm_send, norm_recv, sem_norm, i).wait()
        d_norm = norm_send[at, :].astype(jnp.float32) + norm_recv[at, :].astype(jnp.float32)
        hidden = second[at, :]
        inverse = inverse_two[at, :][:, :1]
        e_two = d_norm * feed_gain_ref[...]
        g_feed_gain_ref[...] += jnp.sum(d_norm * hidden * inverse, axis=0, keepdims=True)
        cross = jnp.sum(e_two * hidden, axis=1, keepdims=True) / width
        d_hidden = (
            cotangent_ref[at, :].astype(jnp.float32)
            + inverse * e_two
            - hidden * (inverse * inverse * inverse * cross)
        )
        d_second_ref[at, :] = d_hidden
        low = d_hidden.astype(jnp.bfloat16)
        d_mix[at, :] = low
        d_attention_ref[at, :] = matmul(low, attention_out_ref[...])
        d_gated_now = matmul(low, mamba_output_ref[...])
        d_gated[at, :] = d_gated_now
        six = g_six[at, :]
        g_mamba_gain_ref[...] += jnp.sum(
            d_gated_now * six * inverse_six[at, :][:, :1], axis=0, keepdims=True
        )
        cross_send[at, :] = jnp.broadcast_to(
            jnp.sum(d_gated_now * mamba_gain * six, axis=1, keepdims=True), (FEED_TILE, LANES)
        )
        swap(cross_send, cross_recv, sem_cross, i).start()

    each(tiles, norm_tile)

    def gate_back(i):
        at = feed_rows(i)
        swap(cross_send, cross_recv, sem_cross, i).wait()
        cross = (cross_send[at, :] + cross_recv[at, :])[:, :1] / all_inner
        inverse = inverse_six[at, :][:, :1]
        d_six = inverse * (d_gated[at, :] * mamba_gain) - g_six[at, :] * (
            inverse * inverse * inverse * cross
        )
        gate_now = gate_z_ref[at, :]
        sig = sigmoid(gate_now)
        d_y_ref[at, :] = d_six * gate_now * sig
        d_gate_z_ref[at, :] = (
            d_six * y_ref[at, :] * (sig * (1.0 + gate_now * (1.0 - sig)))
        ).astype(jnp.bfloat16)

    each(tiles, gate_back)
    start_all(stores, 1, 2, 3, 4)

    def out_tile(i):
        at = feed_rows(i)
        swap(lift_send, lift_recv, sem_lift, i).wait()
        total = lift_send[at, :].astype(jnp.float32) + lift_recv[at, :].astype(jnp.float32)
        out_ref[at, :] = (second[at, :] + total).astype(jnp.bfloat16)

    each(tiles, out_tile)
    start_all(stores, 0)

    def mixed_weights(k):
        block = block_columns(k)
        store(g_gate_ref, k, matmul_first(normed[:, block], d_gate_z_ref[...]))
        d_mix_now = d_mix[:, block]
        grad = jnp.concatenate(
            [matmul_first(d_mix_now, gated[...]), matmul_first(d_mix_now, attention_ref[...])],
            axis=1,
        )
        store(g_mixed_ref, k, grad)

    each(blocks, mixed_weights)
    start_all(stores, 6, 8, 9, 10)
    if merged:
        for k in range(EARLIER):
            first.halve_copy(k, 0).wait()
        start_all(stores, 11, 12)


def feed_layer(
    y,
    gate_z,
    attention_low,
    tokens,
    cotangent,
    mixer_gain,
    mamba_gain,
    feed_gain,
    mamba_output,
    attention_out,
    gate_weight,
    lift_weight,
    down_weight,
):
    rows, inner = y.shape
    width = tokens.shape[1]
    feed = gate_weight.shape[1]
    att = attention_low.shape[1]
    tiles = rows // FEED_TILE
    vmem = pl.BlockSpec(memory_space=pltpu.VMEM)
    hbm = pl.BlockSpec(memory_space=pl.ANY)
    low, full = jnp.bfloat16, jnp.float32
    shape = jax.ShapeDtypeStruct
    merged = lax.axis_size("seq") == 4

    def grad_shape(columns):
        if merged:
            return shape((2,) * (seq_bits() + 2) + (width // 16, columns), low)
        return shape((width, columns), low)

    out_shape = [
            shape((rows, width), low),
            shape((rows, width), full),
            shape((rows, inner), full),
            shape((rows, inner), low),
            shape((rows, att), full),
            grad_shape(2 * feed),
            grad_shape(inner + att),
            grad_shape(feed),
            grad_shape(inner),
            shape((1, width), full),
            shape((1, inner), full),
        ]
    scratch = []
    if merged:
        out_shape += [shape((2,) * 3 + (width // 16, n), low) for n in (feed, MOST)]
        scratch = [pltpu.SemaphoreType.DMA((2, EARLIER, 1))]
    operands = [
        y,
        gate_z,
        attention_low,
        tokens,
        cotangent,
        mixer_gain[None],
        mamba_gain.reshape(inner // LANES, LANES),
        feed_gain[None],
        mamba_output,
        attention_out,
        gate_weight,
        lift_weight,
        down_weight,
    ]
    return pl.pallas_call(
        functools.partial(moving, functools.partial(feed_kernel, merged), 13, 10, len(out_shape)),
        out_shape=out_shape,
        in_specs=[hbm] * 13,
        out_specs=[hbm] * len(out_shape),
        scratch_shapes=moving_scratch(operands[:10], out_shape)
        + [
            pltpu.VMEM((width, feed), low),
            pltpu.VMEM((width, feed), low),
            pltpu.VMEM((width, feed), low),
            pltpu.VMEM((rows, width), low),
            pltpu.VMEM((rows, inner), low),
            pltpu.VMEM((rows, inner), full),
            pltpu.VMEM((rows, LANES), full),
            pltpu.VMEM((rows, width), full),
            pltpu.VMEM((rows, LANES), full),
            pltpu.VMEM((rows, width), low),
            pltpu.VMEM((rows, feed), low),
            pltpu.VMEM((rows, 2 * feed), low),
            pltpu.VMEM((rows, width), low),
            pltpu.VMEM((rows, inner), full),
            pltpu.VMEM((rows, LANES), full),
            pltpu.VMEM((rows, LANES), full),
            pltpu.VMEM((rows, LANES), full),
            pltpu.VMEM((rows, LANES), full),
        ]
        + [pltpu.VMEM((rows, width), low)] * 6
        + [pltpu.SemaphoreType.DMA((3,))]
        + [pltpu.SemaphoreType.DMA((2, tiles))] * 5
        + scratch,
        compiler_params=pltpu.CompilerParams(
            collective_id=1, has_side_effects=True, vmem_limit_bytes=60 << 20
        ),
        name="feed_layer",
    )(*operands)


CHUNK = 128
HALO = 8
PIECE = 256


def turn_half(values):
    lane = lax.broadcasted_iota(jnp.int32, values.shape, 1)
    return jnp.where(
        lax.rem(lane, HD) < HD // 2,
        pltpu.roll(values, LANES - HD // 2, 1),
        pltpu.roll(values, HD // 2, 1),
    )


def two_parts(values):
    high = values.astype(jnp.bfloat16)
    return high, (values - high.astype(jnp.float32)).astype(jnp.bfloat16)


def spread_heads(values, spread):
    high, rest = two_parts(values)
    return matmul(high, spread) + matmul(rest, spread)


def sum_heads(values, spread):
    high, rest = two_parts(values)
    return matmul_last(high, spread) + matmul_last(rest, spread)


def spread_matrix(inner, size):
    row = lax.broadcasted_iota(jnp.int32, (LANES, inner), 0)
    lane = lax.broadcasted_iota(jnp.int32, (LANES, inner), 1)
    return jnp.where(lane // size == row, 1.0, 0.0).astype(jnp.bfloat16)


def ordered(count):
    row = lax.broadcasted_iota(jnp.int32, (count, count), 0)
    lane = lax.broadcasted_iota(jnp.int32, (count, count), 1)
    return row >= lane


def halves(values, size):
    lane = lax.broadcasted_iota(jnp.int32, values.shape, 1)
    return jnp.concatenate(
        [jnp.where(lane < size, values, 0.0), jnp.where(lane < size, 0.0, values)], axis=0
    ).astype(jnp.bfloat16)


def soft_plus(v):
    return jnp.maximum(v, 0.0) + jnp.log1p(jnp.exp(-jnp.abs(v)))


def chunk_flags(seg_ref, c):
    window = seg_ref[pl.ds(pl.multiple_of(c * CHUNK, CHUNK), CHUNK + HALO), :]
    own = window[HALO:]
    start = jnp.where(own == window[HALO - 1 : HALO], 1.0, 0.0)
    end = jnp.where(own == own[CHUNK - 1 :], 1.0, 0.0)
    return own, start, end


def greet_seq(barrier, with_peer):
    seq, head, batch = lax.axis_index("seq"), lax.axis_index("head"), lax.axis_index("batch")
    count = lax.axis_size("seq")

    def one(step, carry):
        pl.semaphore_signal(
            barrier,
            inc=1,
            device_id=(lax.rem(seq + step, count), head, batch),
            device_id_type=MESH,
        )
        return carry

    lax.fori_loop(1, count, one, 0)
    if with_peer:
        pl.semaphore_signal(barrier, inc=1, device_id=peer_device(), device_id_type=MESH)
    pl.semaphore_wait(barrier, count - 1 + with_peer)


def mixer_kernel(
    loads,
    stores,
    tokens_ref,
    gain_ref,
    seg_row_ref,
    table_ref,
    gate_weight,
    input_weight,
    maps_weight,
    step_given,
    query_weight,
    memory_weight,
    conv_inner_ref,
    conv_maps_ref,
    step_bias_ref,
    log_rate_ref,
    skip_gain_ref,
    gate_z_ref,
    pre_ref,
    conv_ref,
    raw_ref,
    cum_ref,
    y_ref,
    states_ref,
    query_ref,
    memory_ref,
    attention_ref,
    attention_low_ref,
    logs_ref,
    seg_ref,
    key_seg_ref,
    step_weight,
    taps_ref,
    rate_ref,
    skip_ref,
    step_wide,
    bias_ref,
    normed,
    spread_ref,
    act,
    scaled,
    added,
    decay,
    total,
    local,
    state,
    chain_out,
    chain_in,
    memory_turned,
    sem_memory,
    sem_halo,
    sem_chain,
):
    seq, head, batch = lax.axis_index("seq"), lax.axis_index("head"), lax.axis_index("batch")
    count = lax.axis_size("seq")
    rows = tokens_ref.shape[0]
    tiles = rows // CHUNK
    inner = y_ref.shape[1]
    width = pre_ref.shape[1]
    state_width = (width - inner) // 2
    following = (lax.rem(seq + 1, count), head, batch)
    greet_seq(pltpu.get_barrier_semaphore(), 0)
    for load in loads:
        load.wait()
    first = seq * rows

    def memory_copy(hop, owner):
        return exchange(
            memory_ref.at[owner],
            memory_ref.at[owner],
            sem_memory.at[0, hop],
            sem_memory.at[1, hop],
            following,
        )

    def memory_send(hop):
        @pl.when((seq - hop + 1 >= 0) & (seq < count - 1))
        def _():
            memory_copy(hop, lax.rem(seq - hop + 1 + count, count)).start()

    def memory_receive(hop):
        @pl.when(seq - hop >= 0)
        def _():
            memory_copy(hop, lax.rem(seq - hop + count, count)).wait_recv()

    def memory_hop(hop):
        memory_receive(hop - 1)
        memory_send(hop)

    halo_copy = exchange(
        pre_ref.at[pl.ds(rows, HALO)],
        pre_ref.at[pl.ds(0, HALO)],
        sem_halo.at[0],
        sem_halo.at[1],
        following,
    )

    def memory_tile(i):
        at = feed_rows(i)
        hidden = tokens_ref[at, :].astype(jnp.float32)
        inverse = lax.rsqrt(jnp.mean(hidden * hidden, axis=1, keepdims=True) + eps_norm)
        low = (hidden * inverse * gain_ref[...]).astype(jnp.bfloat16)
        normed[at, :] = low
        value = matmul(low, memory_weight[...])
        lane = lax.broadcasted_iota(jnp.int32, value.shape, 1)
        turned = value * table_ref[at, :LANES] + turn_half(value) * table_ref[at, LANES:]
        memory_ref[seq, at, :] = jnp.where(lane < HD, turned, value).astype(jnp.bfloat16)

    wide_tiles = rows // FEED_TILE
    each(wide_tiles, memory_tile)

    memory_send(1)

    def pre_tile(i):
        at = feed_rows(i)
        to = pl.ds(pl.multiple_of(i * FEED_TILE + HALO, HALO), FEED_TILE)
        low = normed[at, :]
        pre_ref[to, :inner] = matmul(low, input_weight[...])
        pre_ref[to, inner:] = matmul(low, maps_weight[...])

    each(wide_tiles, lambda i: pre_tile(wide_tiles - 1 - i))

    @pl.when(seq < count - 1)
    def _():
        halo_copy.start()

    if count > 2:
        memory_hop(2)

    def key_block(k):
        at = pl.ds(pl.multiple_of(k * LANES, LANES), LANES)
        row = seg_row_ref[:, at].astype(jnp.float32)
        key_seg_ref[at, :] = jnp.broadcast_to(row, (LANES, LANES)).T

    each(seg_row_ref.shape[1] // LANES, key_block)
    seg_ref[HALO : HALO + rows, :] = key_seg_ref[pl.ds(pl.multiple_of(first, TILE), rows), :]
    seg_ref[:HALO, :] = jnp.full((HALO, LANES), -1.0, jnp.float32)
    seg_ref[HALO + rows :, :] = jnp.full((HALO, LANES), -2.0, jnp.float32)

    @pl.when(seq > 0)
    def _():
        seg_ref[:HALO, :] = key_seg_ref[pl.ds(pl.multiple_of(first - HALO, HALO), HALO), :]

    @pl.when(seq < count - 1)
    def _():
        seg_ref[HALO + rows :, :] = key_seg_ref[pl.ds(pl.multiple_of(first + rows, TILE), HALO), :]

    heads = step_given.shape[0]
    lane = lax.broadcasted_iota(jnp.int32, (1, LANES), 1)
    wide_lane = lax.broadcasted_iota(jnp.int32, (1, inner), 1)
    bias_row = log_row = jnp.zeros((1, LANES), jnp.float32)
    skip_row = jnp.zeros((1, inner), jnp.float32)
    for h in range(heads):
        bias_row = jnp.where(lane == h, step_bias_ref[h], bias_row)
        log_row = jnp.where(lane == h, log_rate_ref[h], log_row)
        skip_row = jnp.where(wide_lane // HD == h, skip_gain_ref[h], skip_row)
    bias_ref[...] = bias_row
    rate_ref[...] = jnp.where(lane < heads, -jnp.exp(log_row), 0.0)
    skip_ref[...] = skip_row
    step_wide[...] = jnp.zeros_like(step_wide)
    step_wide[:heads, :] = step_given[...].astype(jnp.float32)
    step_weight[...] = step_wide[...].astype(jnp.bfloat16)
    taps_ref[...] = jnp.zeros_like(taps_ref)
    taps_ref[: conv_inner_ref.shape[0], :inner] = conv_inner_ref[...]
    taps_ref[: conv_inner_ref.shape[0], inner:] = conv_maps_ref[...]
    spread_ref[...] = spread_matrix(inner, HD)
    lower = jnp.where(ordered(CHUNK), 1.0, 0.0)

    def step_tile(i):
        at = tile_rows(i)
        raw = matmul_last(normed[at, :], step_weight[...]) + bias_ref[...]
        raw_ref[at, :] = raw
        cum_ref[at, :] = jnp.dot(lower, rate_ref[...] * soft_plus(raw), precision=highest)

    each(tiles, step_tile)

    @pl.when(seq == 0)
    def _():
        pre_ref[:HALO, :] = jnp.zeros((HALO, width), jnp.float32)

    @pl.when(seq > 0)
    def _():
        halo_copy.wait_recv()

    def conv_tile(i):
        at = tile_rows(i)
        window_at = pl.ds(pl.multiple_of(i * TILE, TILE), TILE + HALO)
        seg = seg_ref[window_at, :]
        own = seg[HALO:]
        masks = [
            jnp.where(seg[HALO - 3 + k : HALO - 3 + k + TILE] == own, 1.0, 0.0) for k in range(3)
        ]
        for j in range(width // LANES):
            columns = slice(j * LANES, (j + 1) * LANES)
            window = pre_ref[window_at, columns]
            summed = taps_ref[3:4, columns] * window[HALO:]
            for k in range(3):
                summed = summed + taps_ref[k : k + 1, columns] * (
                    window[HALO - 3 + k : HALO - 3 + k + TILE] * masks[k]
                )
            conv_ref[at, columns] = summed
            act[at, columns] = summed * sigmoid(summed)

    each(tiles, conv_tile)
    start_all(stores, 1, 2, 3, 4, 12, 13, 14, 15, 16, 17)
    local[...] = jnp.zeros_like(local)
    total[...] = jnp.ones_like(total)

    def input_map(at):
        return act[at, inner : inner + state_width].astype(jnp.bfloat16)

    def output_map(at):
        return act[at, inner + state_width :].astype(jnp.bfloat16)

    def local_chunk(c):
        at = tile_rows(c)
        _, start, end = chunk_flags(seg_ref, c)
        cum = cum_ref[at, :]
        last = cum[CHUNK - 1 :]
        spread = spread_ref[...]
        value = act[at, :inner] * spread_heads(soft_plus(raw_ref[at, :]), spread)
        scaled[at, :] = value.astype(jnp.bfloat16)
        weight = spread_heads(jnp.exp(last - cum) * end, spread)
        fresh = matmul_first(input_map(at), (value * weight).astype(jnp.bfloat16))
        keep = jnp.broadcast_to(jnp.exp(last) * start[CHUNK - 1 :], (HALO, LANES))
        keep = spread_heads(keep, spread)
        added[c] = fresh
        decay[c] = keep
        local[...] = local[...] * keep[:1] + fresh
        total[...] = total[...] * keep

    each(tiles, local_chunk)
    pieces = inner // PIECE

    def chain_copy(p):
        columns = pl.ds(p * PIECE, PIECE)
        return exchange(
            chain_out.at[:, columns],
            chain_in.at[:, columns],
            sem_chain.at[0, p],
            sem_chain.at[1, p],
            following,
        )

    @pl.when(seq == 0)
    def _():
        state[...] = jnp.zeros_like(state)
        chain_out[...] = local[...].astype(jnp.bfloat16)
        if count > 1:
            for p in range(pieces):
                chain_copy(p).start()

    if count > 3:
        memory_hop(3)

    def inside_chunk(c):
        at = tile_rows(c)
        own, _, _ = chunk_flags(seg_ref, c)
        cum = cum_ref[at, :]
        turned = cum.T
        meet = matmul_last(output_map(at), input_map(at))
        meet = jnp.where(ordered(CHUNK) & (own == own.T), meet, 0.0)
        for i in range(inner // LANES):
            columns = slice(i * LANES, (i + 1) * LANES)
            mixing = []
            for h in (2 * i, 2 * i + 1):
                gap = cum[:, h : h + 1] - turned[h : h + 1, :]
                mixing.append(meet * jnp.exp(jnp.minimum(gap, 0.0)))
            y_ref[at, columns] = matmul(
                jnp.concatenate(mixing, axis=1).astype(jnp.bfloat16),
                halves(scaled[at, columns].astype(jnp.float32), HD),
            )

    each(tiles, inside_chunk)

    def project_tile(i):
        at = feed_rows(i)
        low = normed[at, :]
        gate_z_ref[at, :] = matmul(low, gate_weight[...])
        value = matmul(low, query_weight[...])
        for k in range(value.shape[1] // LANES):
            part = value[:, k * LANES : (k + 1) * LANES]
            turned = part * table_ref[at, :LANES] + turn_half(part) * table_ref[at, LANES:]
            query_ref[at, k * LANES : (k + 1) * LANES] = turned.astype(jnp.bfloat16)

    def chain_wait(p):
        columns = pl.ds(p * PIECE, PIECE)
        chain_copy(p).wait_recv()
        came = chain_in[:, columns].astype(jnp.float32)
        state[:, columns] = came
        return came

    @pl.when(seq >= 2)
    def _():
        each(wide_tiles, project_tile)

    @pl.when((seq > 0) & (seq < count - 1))
    def _():
        for p in range(pieces):
            columns = pl.ds(p * PIECE, PIECE)
            chain_out[:, columns] = (
                chain_wait(p) * total[:1, columns] + local[:, columns]
            ).astype(jnp.bfloat16)
            chain_copy(p).start()

    @pl.when(seq < 2)
    def _():
        each(wide_tiles, project_tile)

    span(4, count, memory_hop)
    if count > 1:
        memory_receive(count - 1)

    def memory_rest(hop):
        @pl.when((seq - hop + 1 >= 0) & (seq < count - 1))
        def _():
            memory_copy(hop, lax.rem(seq - hop + 1 + count, count)).wait_send()

        @pl.when(seq + hop < count)
        def _():
            memory_ref[lax.rem(seq + hop, count)] = jnp.zeros(memory_ref.shape[1:], jnp.bfloat16)

    span(1, count, memory_rest)
    def turn_block(k):
        memory_turned[k] = memory_ref[k].astype(jnp.float32).T.astype(jnp.bfloat16)

    each(seq + 1, turn_block)

    def attention_block(i):
        at = tile_rows(i)
        turned, log = attend_block(
            first,
            0,
            (first + i * TILE + TILE - 1) // KEY_TILE,
            i,
            query_ref[at, :],
            lambda k: (memory_ref[k], memory_turned[k]),
            seg_ref,
            key_seg_ref,
        )
        for pair, tile in enumerate(unstacked_heads(turned, False)):
            columns = slice(pair * LANES, (pair + 1) * LANES)
            attention_ref[at, columns] = tile
            attention_low_ref[at, columns] = tile.astype(jnp.bfloat16)
        logs_ref[i] = jnp.broadcast_to(log, logs_ref.shape[1:])

    start_all(stores, 0, 7, 8)
    each(tiles, attention_block)
    start_all(stores, 9, 10, 11)

    @pl.when((seq > 0) & (seq == count - 1))
    def _():
        for p in range(pieces):
            chain_wait(p)

    def across_chunk(c):
        at = tile_rows(c)
        _, start, _ = chunk_flags(seg_ref, c)
        now = state[...]
        low = now.astype(jnp.bfloat16)
        states_ref[c] = low
        carried = spread_heads(jnp.exp(cum_ref[at, :]) * start, spread_ref[...])
        y_ref[at, :] += matmul(output_map(at), low) * carried + skip_ref[...] * act[at, :inner]
        state[...] = now * decay[c][:1] + added[c]

    each(tiles, across_chunk)
    states_ref[tiles] = state[...].astype(jnp.bfloat16)
    start_all(stores, 5, 6)

    @pl.when(seq < count - 1)
    def _():
        halo_copy.wait_send()
        for p in range(pieces):
            chain_copy(p).wait_send()


def mixer_forward(*operands):
    tokens, seg_row, table = operands[0], operands[2], operands[3]
    mamba_gate, step_given, query_weight, memory_weight = (
        operands[4],
        operands[7],
        operands[8],
        operands[9],
    )
    rows, width = tokens.shape
    total = seg_row.shape[1]
    count = lax.axis_size("seq")
    inner = mamba_gate.shape[1]
    conv_width = inner + operands[6].shape[1]
    state_width = (conv_width - inner) // 2
    query = query_weight.shape[1]
    chunks = rows // CHUNK
    pieces = inner // PIECE
    smem = pl.BlockSpec(memory_space=pltpu.SMEM)
    vmem = pl.BlockSpec(memory_space=pltpu.VMEM)
    low, full = jnp.bfloat16, jnp.float32
    shape = jax.ShapeDtypeStruct
    hbm = pl.BlockSpec(memory_space=pl.ANY)
    out_shape = [
            shape((rows, inner), full),
            shape((rows + HALO, conv_width), full),
            shape((rows, conv_width), full),
            shape((rows, LANES), full),
            shape((rows, LANES), full),
            shape((rows, inner), full),
            shape((chunks + 1, state_width, inner), low),
            shape((rows, query), low),
            shape((count, rows, memory_weight.shape[1]), low),
            shape((rows, query), full),
            shape((rows, query), low),
            shape((chunks, HALO, query // HD * TILE), full),
            shape((rows + 2 * HALO, LANES), full),
            shape((total, LANES), full),
            shape((LANES, width), low),
            shape((HALO, conv_width), full),
            shape((1, LANES), full),
            shape((1, inner), full),
        ]
    return pl.pallas_call(
        functools.partial(moving, mixer_kernel, 15, 12, len(out_shape)),
        out_shape=out_shape,
        in_specs=[hbm] * 12 + [smem] * 3,
        out_specs=[hbm] * len(out_shape),
        scratch_shapes=moving_scratch(operands[:12], out_shape)
        + [
            pltpu.VMEM((LANES, width), full),
            pltpu.VMEM((1, LANES), full),
            pltpu.VMEM((rows, width), low),
            pltpu.VMEM((LANES, inner), low),
            pltpu.VMEM((rows, conv_width), full),
            pltpu.VMEM((rows, inner), low),
            pltpu.VMEM((chunks, state_width, inner), full),
            pltpu.VMEM((chunks, HALO, inner), full),
            pltpu.VMEM((HALO, inner), full),
            pltpu.VMEM((state_width, inner), full),
            pltpu.VMEM((state_width, inner), full),
            pltpu.VMEM((state_width, inner), low),
            pltpu.VMEM((state_width, inner), low),
            pltpu.VMEM((count, memory_weight.shape[1], rows), low),
            pltpu.SemaphoreType.DMA((2, count)),
            pltpu.SemaphoreType.DMA((2,)),
            pltpu.SemaphoreType.DMA((2, pieces)),
        ],
        compiler_params=pltpu.CompilerParams(
            collective_id=2, has_side_effects=True, vmem_limit_bytes=60 << 20
        ),
        name="mixer_forward",
    )(*operands)


KEY_TILE = 512


def stacked_heads(values, first, factor):
    lane = lax.broadcasted_iota(jnp.int32, (values.shape[0], LANES), 1)
    keep = (lane < HD) if first else (lane >= HD)
    parts = []
    for h in range(values.shape[1] // HD):
        tile = values[:, (h // 2) * LANES : (h // 2 + 1) * LANES].astype(jnp.float32)
        if (h % 2 == 0) != first:
            tile = pltpu.roll(tile, HD, 1)
        parts.append(jnp.where(keep, tile * factor, 0.0))
    return jnp.concatenate(parts, axis=0)


def unstacked_heads(turned, first):
    heads = turned.shape[1] // TILE
    blocks = [turned[:, h * TILE : (h + 1) * TILE].T for h in range(heads)]
    lane = lax.broadcasted_iota(jnp.int32, (TILE, LANES), 1)
    tiles = []
    for even, odd in zip(blocks[::2], blocks[1::2]):
        if first:
            odd = pltpu.roll(odd, HD, 1)
        else:
            even = pltpu.roll(even, HD, 1)
        tiles.append(jnp.where(lane < HD, even, odd))
    return tiles


def key_tile(seg_turned, key_seg_ref, first, i, k):
    at = pl.ds(pl.multiple_of(k * KEY_TILE, KEY_TILE), KEY_TILE)
    place = k * KEY_TILE + lax.broadcasted_iota(jnp.int32, (KEY_TILE, TILE), 0)
    row = first + i * TILE + lax.broadcasted_iota(jnp.int32, (KEY_TILE, TILE), 1)
    return at, (place <= row) & (key_seg_ref[at, :] == seg_turned)


def query_segments(seg_ref, i):
    own = seg_ref[pl.ds(pl.multiple_of(i * TILE, TILE) + HALO, TILE), :].T
    return jnp.concatenate([own] * (KEY_TILE // TILE), axis=0)


def attend_block(first, low, high, i, queries_in, memory_of, seg_ref, key_seg_ref):
    heads = queries_in.shape[1] // HD
    turned = stacked_heads(queries_in, True, HD ** (-0.5)).T.astype(jnp.bfloat16)
    segs = query_segments(seg_ref, i)
    parts = [turned[:, h * TILE : (h + 1) * TILE] for h in range(heads)]

    def one(step, carry):
        at, allowed = key_tile(segs, key_seg_ref, first, i, high - step)
        keys, keys_turned = memory_of(high - step)
        after = []
        for part, (most, total, acc) in zip(parts, carry):
            scores = jnp.where(allowed, matmul(keys, part), neg_large)
            new = jnp.maximum(most, jnp.max(scores, axis=0, keepdims=True))
            weights = jnp.exp(scores - new)
            factor = jnp.exp(most - new)
            total = total * factor + jnp.sum(weights, axis=0, keepdims=True)
            acc = acc * factor + matmul(keys_turned, weights.astype(jnp.bfloat16))
            after.append((new, total, acc))
        return tuple(after)

    zero = (
        jnp.full((1, TILE), neg_large, jnp.float32),
        jnp.zeros((1, TILE), jnp.float32),
        jnp.zeros((LANES, TILE), jnp.float32),
    )
    result = lax.fori_loop(0, high - low + 1, one, (zero,) * heads)
    return (
        jnp.concatenate([acc / total for _, total, acc in result], axis=1),
        jnp.concatenate([most + jnp.log(total) for most, total, _ in result], axis=1),
    )


def attend_back_block(
    first, low, high, i, queries_in, d_out, out, log, memory_of, seg_ref, key_seg_ref, grads
):
    heads = queries_in.shape[1] // HD
    queries = stacked_heads(queries_in, True, HD ** (-0.5))
    outer = stacked_heads(d_out, False, 1.0)
    queries_turned, outer_turned = queries.T.astype(jnp.bfloat16), outer.T.astype(jnp.bfloat16)
    queries, outer = queries.astype(jnp.bfloat16), outer.astype(jnp.bfloat16)
    segs = query_segments(seg_ref, i)
    row = lax.broadcasted_iota(jnp.int32, (HALO, heads * HD), 0)
    lane = lax.broadcasted_iota(jnp.int32, (HALO, heads * HD), 1)
    pick = jnp.where(lane // HD == row, 1.0, 0.0).astype(jnp.bfloat16)
    high_part, low_part = two_parts(d_out * out)
    deltas = matmul_last(pick, high_part) + matmul_last(pick, low_part)
    spans = [slice(h * TILE, (h + 1) * TILE) for h in range(heads)]

    def one(step, totals):
        at, allowed = key_tile(segs, key_seg_ref, first, i, high - step)
        keys = memory_of(high - step)
        slopes, lows, after = [], [], []
        for h, (part, total) in enumerate(zip(spans, totals)):
            weights = jnp.exp(matmul(keys, queries_turned[:, part]) - log[:, part])
            weights = jnp.where(allowed, weights, 0.0)
            slope = weights * (matmul(keys, outer_turned[:, part]) - deltas[h : h + 1])
            slopes.append(slope.astype(jnp.bfloat16))
            lows.append(weights.astype(jnp.bfloat16))
            after.append(total + matmul_first(keys, slopes[-1]))
        grads[at, :] += matmul(jnp.concatenate(slopes, axis=1), queries) + matmul(
            jnp.concatenate(lows, axis=1), outer
        )
        return tuple(after)

    totals = lax.fori_loop(
        0, high - low + 1, one, (jnp.zeros((LANES, TILE), jnp.float32),) * heads
    )
    return jnp.concatenate(totals, axis=1) * HD ** (-0.5)


def attention_back_kernel(
    first_ref,
    low_ref,
    high_ref,
    query_ref,
    memory_ref,
    seg_ref,
    key_seg_ref,
    out_ref,
    log_ref,
    d_out_ref,
    table_ref,
    d_query_ref,
    d_memory_ref,
    grads,
):
    grads[...] = jnp.zeros_like(grads)

    def block(i):
        at = tile_rows(i)
        d_turned = attend_back_block(
            first_ref[0],
            low_ref[i],
            high_ref[i],
            i,
            query_ref[at, :],
            d_out_ref[at, :],
            out_ref[at, :],
            log_ref[i][:1],
            lambda k: memory_ref[pl.ds(pl.multiple_of(k * KEY_TILE, KEY_TILE), KEY_TILE), :],
            seg_ref,
            key_seg_ref,
            grads,
        )
        for pair, tile in enumerate(unstacked_heads(d_turned, True)):
            turned = tile * table_ref[at, :LANES] - turn_half(tile) * table_ref[at, LANES:]
            d_query_ref[at, pair * LANES : (pair + 1) * LANES] = turned.astype(jnp.bfloat16)

    each(query_ref.shape[0] // TILE, block)
    d_memory_ref[...] = grads[...].astype(jnp.bfloat16)


def attention_back(spans, query, memory, segments, key_segments, out, logs, d_out, table):
    vmem = pl.BlockSpec(memory_space=pltpu.VMEM)
    return pl.pallas_call(
        attention_back_kernel,
        out_shape=[
            jax.ShapeDtypeStruct(query.shape, jnp.bfloat16),
            jax.ShapeDtypeStruct(memory.shape, jnp.bfloat16),
        ],
        in_specs=[pl.BlockSpec(memory_space=pltpu.SMEM)] * 3 + [vmem] * 8,
        out_specs=[vmem] * 2,
        scratch_shapes=[pltpu.VMEM(memory.shape, jnp.float32)],
        compiler_params=pltpu.CompilerParams(vmem_limit_bytes=56 << 20),
        name="attention_back",
    )(*spans, query, memory, segments, key_segments, out, logs, d_out, table)


MERGED_INPUTS = 30


def mixer_back_kernel(merged, chunks, *refs):
    refs = list(refs)

    def take(count):
        nonlocal refs
        now, refs = refs[:count], refs[count:]
        return now

    if merged:
        given = take(MERGED_INPUTS)
        early, came = take(4), take(2)
        d_tokens_ref, *outs, small_out = take(7)
        copies = take(MERGED_INPUTS)
        (sem_load,) = take(1)
        loads = [
            pltpu.make_async_copy(source, target, sem_load.at[k])
            for k, (source, target) in enumerate(zip(given, copies))
        ]
        for load in loads:
            load.start()
        refs = copies + refs
    (
        tokens_ref,
        gain_ref,
        seg_ref,
        table_ref,
        gate_weight,
        input_weight,
        maps_weight,
        step_weight,
        query_weight,
        memory_weight,
        taps_ref,
        rate_ref,
        skip_ref,
        pre_ref,
        conv_ref,
        raw_ref,
        cum_ref,
        y_ref,
        states_ref,
        d_second_ref,
        d_y_ref,
        d_gate_z_ref,
    ) = take(22)
    if merged:
        (
            query_ref,
            memory_ref,
            key_seg_ref,
            attention_ref,
            logs_ref,
            d_attention_ref,
            feed_gain_ref,
            mamba_gain_ref,
        ) = take(8)
    else:
        d_query_ref, d_memory_ref = take(2)
        d_tokens_ref, g_side_ref, g_taps_ref, g_gain_ref, g_heads_ref = take(5)
    (
        normed,
        spread_ref,
        act,
        d_conv,
        d_scaled,
        d_maps,
        row_term,
        added,
        local,
        total,
        state,
        skip_sum,
        side,
        chain_out,
        chain_in,
        maps_send,
        maps_recv,
        memory_recv,
        norm_send,
        norm_recv,
        sem_memory,
        sem_halo,
        sem_chain,
        sem_maps,
        sem_norm,
    ) = take(25)
    if merged:
        g_side_ref, grads, d_memory_ref, small_in, small_buf, sem_small = take(6)
        g_taps_ref = g_gain_ref = g_heads_ref = small_in
    seq, head, batch = lax.axis_index("seq"), lax.axis_index("head"), lax.axis_index("batch")
    count = lax.axis_size("seq")
    rows = tokens_ref.shape[0]
    tiles = rows // CHUNK
    inner = y_ref.shape[1]
    width = pre_ref.shape[1]
    state_width = (width - inner) // 2
    model = tokens_ref.shape[1]
    peer = peer_device()
    previous = (lax.rem(seq - 1 + count, count), head, batch)
    pieces = inner // PIECE
    step_at = width
    query_at = step_at + LANES
    memory_at = query_at + query_weight.shape[1]
    if merged:
        greet_all(pltpu.get_barrier_semaphore(), True)
        reduction = Reduction(chunks, list(early) + [g_side_ref], outs, refs, came)
        reduction.allow(sum(1 for c in chunks if c[0] < len(early)))
        advance = reduction.advance
        for load in loads:
            load.wait()
    else:
        greet_seq(pltpu.get_barrier_semaphore(), 1)

        def advance():
            return None

    spread_ref[...] = spread_matrix(inner, HD)

    def chain_copy(p):
        columns = pl.ds(p * PIECE, PIECE)
        return exchange(
            chain_out.at[:, columns],
            chain_in.at[:, columns],
            sem_chain.at[0, p],
            sem_chain.at[1, p],
            previous,
        )

    def memory_copy(step):
        place = lax.rem(seq - step + count, count)
        return exchange(
            d_memory_ref.at[place],
            memory_recv.at[step - 1],
            sem_memory.at[0, step],
            sem_memory.at[1, step],
            (place, head, batch),
        )

    halo_copy = exchange(
        d_conv.at[pl.ds(0, HALO)],
        d_conv.at[pl.ds(rows, HALO)],
        sem_halo.at[0],
        sem_halo.at[1],
        previous,
    )
    maps_copy = exchange(maps_send, maps_recv, sem_maps.at[0], sem_maps.at[1], peer)

    def norm_copy(i):
        at = tile_rows(i)
        return exchange(
            norm_send.at[at], norm_recv.at[at], sem_norm.at[0, i], sem_norm.at[1, i], peer
        )

    def input_map(at):
        return act[at, inner : inner + state_width].astype(jnp.bfloat16)

    def output_map(at):
        return act[at, inner + state_width :].astype(jnp.bfloat16)

    def keep_of(c, start):
        last = cum_ref[tile_rows(c), :][CHUNK - 1 :]
        keep = jnp.broadcast_to(jnp.exp(last) * start[CHUNK - 1 :], (HALO, LANES))
        return spread_heads(keep, spread_ref[...])

    def carried_of(c, start):
        return spread_heads(jnp.exp(cum_ref[tile_rows(c), :]) * start, spread_ref[...])

    def activate(i):
        at = tile_rows(i)
        value = conv_ref[at, :]
        act[at, :] = value * sigmoid(value)

    each(tiles, activate)
    local[...] = jnp.zeros_like(local)
    total[...] = jnp.ones_like(total)

    def local_chunk(step):
        c = tiles - 1 - step
        at = tile_rows(c)
        _, start, _ = chunk_flags(seg_ref, c)
        keep = keep_of(c, start)
        value = (d_y_ref[at, :] * carried_of(c, start)).astype(jnp.bfloat16)
        fresh = matmul_first(output_map(at), value)
        added[c] = fresh
        local[...] = local[...] * keep[:1] + fresh
        total[...] = total[...] * keep

    each(tiles, local_chunk)

    @pl.when(seq == count - 1)
    def _():
        state[...] = jnp.zeros_like(state)
        chain_out[...] = local[...].astype(jnp.bfloat16)
        if count > 1:
            for p in range(pieces):
                chain_copy(p).start()

    if merged:
        first = seq * rows
        grads[...] = jnp.zeros_like(grads)

        def attention_block(i):
            at = tile_rows(i)
            d_turned = attend_back_block(
                first,
                0,
                (first + i * TILE + TILE - 1) // KEY_TILE,
                i,
                query_ref[at, :],
                d_attention_ref[at, :],
                attention_ref[at, :],
                logs_ref[i][:1],
                lambda k: memory_ref[pl.ds(pl.multiple_of(k * KEY_TILE, KEY_TILE), KEY_TILE), :],
                seg_ref,
                key_seg_ref,
                grads,
            )
            for pair, tile in enumerate(unstacked_heads(d_turned, True)):
                turned = tile * table_ref[at, :LANES] - turn_half(tile) * table_ref[at, LANES:]
                columns = pl.ds(query_at + pair * LANES, LANES)
                side[at, columns] = turned.astype(jnp.bfloat16)

        span(0, 1, attention_block)
        advance()

    def chain_wait(p):
        columns = pl.ds(p * PIECE, PIECE)
        chain_copy(p).wait_recv()
        came = chain_in[:, columns].astype(jnp.float32)
        state[:, columns] = came
        return came

    @pl.when((seq > 0) & (seq < count - 1))
    def _():
        for p in range(pieces):
            columns = pl.ds(p * PIECE, PIECE)
            came = chain_wait(p)
            chain_out[:, columns] = (came * total[:1, columns] + local[:, columns]).astype(
                jnp.bfloat16
            )
            chain_copy(p).start()

    if merged:
        for i in range(1, tiles):
            span(i, i + 1, attention_block)
            advance()

        def low_block(place):
            at = pl.ds(pl.multiple_of(place * rows, rows), rows)
            d_memory_ref[place] = grads[at, :].astype(jnp.bfloat16)

        each(count, low_block)

    def memory_start(step, carry):
        @pl.when(seq - step >= 0)
        def _():
            memory_copy(step).start()

        return carry

    lax.fori_loop(1, count, memory_start, 0)
    skip_sum[...] = jnp.zeros_like(skip_sum)

    def inside_chunk(c):
        at = tile_rows(c)
        own, start, _ = chunk_flags(seg_ref, c)
        cum = cum_ref[at, :]
        turned = cum.T
        spread = spread_ref[...]
        low_in, low_out = input_map(at), output_map(at)
        allowed = ordered(CHUNK).astype(jnp.float32).T * jnp.where(own == own.T, 1.0, 0.0)
        meet = matmul_last(low_in, low_out) * allowed
        value = act[at, :inner]
        scaled = value * spread_heads(soft_plus(raw_ref[at, :]), spread)
        d_y = d_y_ref[at, :]
        d_meet = jnp.zeros((CHUNK, CHUNK), jnp.float32)
        for i in range(inner // LANES):
            columns = slice(i * LANES, (i + 1) * LANES)
            d_tile = d_y[:, columns]
            d_mixing = matmul_last(halves(scaled[:, columns], HD), d_tile.astype(jnp.bfloat16))
            mixing = []
            for k, h in enumerate((2 * i, 2 * i + 1)):
                gap = turned[h : h + 1, :] - cum[:, h : h + 1]
                fade = jnp.exp(jnp.minimum(gap, 0.0))
                mixing.append(meet * fade)
                d_meet = d_meet + d_mixing[k * CHUNK : (k + 1) * CHUNK] * fade
            d_scaled[at, columns] = matmul(
                jnp.concatenate(mixing, axis=1).astype(jnp.bfloat16), halves(d_tile, HD)
            )
        d_meet = (d_meet * allowed).astype(jnp.bfloat16)
        d_maps[at, :state_width] = matmul(d_meet, low_out)
        carried = (d_y * carried_of(c, start)).astype(jnp.bfloat16)
        d_maps[at, state_width:] = matmul_first(d_meet, low_in) + matmul_last(
            carried, states_ref[c]
        )
        product = d_y * value
        skip_sum[...] += jnp.sum(product, axis=0, keepdims=True)
        low = d_y.astype(jnp.bfloat16).astype(jnp.float32)
        row_term[at, :] = sum_heads(low * (y_ref[at, :] - skip_ref[...] * value), spread)

    span(0, tiles // 2, inside_chunk)
    advance()
    span(tiles // 2, tiles, inside_chunk)
    advance()

    @pl.when((seq == 0) & (seq < count - 1))
    def _():
        for p in range(pieces):
            chain_wait(p)

    if merged:
        small_in[...] = jnp.zeros_like(small_in)
        small_in[4:5, :inner] = mamba_gain_ref[...]
        small_in[6:7, :] = feed_gain_ref[...]
    else:
        g_heads_ref[...] = jnp.zeros_like(g_heads_ref)

    gain_row = 5 if merged else 0

    def add_heads(k, values):
        row, lane = (7, k * LANES) if merged else (k, 0)
        g_heads_ref[row : row + 1, lane : lane + LANES] += values

    upper = jnp.where(ordered(CHUNK), 1.0, 0.0).T

    def across_chunk(step):
        c = tiles - 1 - step
        at = tile_rows(c)
        _, start, end = chunk_flags(seg_ref, c)
        spread = spread_ref[...]
        cum = cum_ref[at, :]
        last = cum[CHUNK - 1 :]
        now = state[...]
        low = now.astype(jnp.bfloat16)
        raw = raw_ref[at, :]
        steps = soft_plus(raw)
        steps_wide = spread_heads(steps, spread)
        value = act[at, :inner]
        scaled = value * steps_wide
        weight = spread_heads(jnp.exp(last - cum) * end, spread)
        d_value = d_scaled[at, :] + matmul(input_map(at), low) * weight
        d_maps[at, :state_width] += matmul_last((scaled * weight).astype(jnp.bfloat16), low)
        final = jnp.sum(
            states_ref[c + 1].astype(jnp.float32) * low.astype(jnp.float32), axis=0, keepdims=True
        )
        final = sum_heads(jnp.broadcast_to(final, (HALO, inner)), spread)[:1]
        low_scaled = scaled.astype(jnp.bfloat16).astype(jnp.float32)
        d_cum = row_term[at, :] - sum_heads(low_scaled * d_value, spread)
        d_rate = jnp.dot(upper, d_cum, precision=highest) + final
        rate = rate_ref[...]
        d_steps = sum_heads(value * d_value, spread) + rate * d_rate
        d_raw = d_steps * sigmoid(raw)
        add_heads(0, rate * jnp.sum(steps * d_rate, axis=0, keepdims=True))
        add_heads(1, jnp.sum(d_raw, axis=0, keepdims=True))
        side[at, step_at:query_at] = d_raw.astype(jnp.bfloat16)
        d_conv[at, :inner] = steps_wide * d_value + skip_ref[...] * d_y_ref[at, :]
        state[...] = now * keep_of(c, start)[:1] + added[c]

    span(0, tiles // 2, across_chunk)
    advance()
    span(tiles // 2, tiles, across_chunk)
    advance()
    add_heads(2, sum_heads(jnp.broadcast_to(skip_sum[:1], (HALO, inner)), spread_ref[...])[:1])
    maps_send[...] = d_maps[...].astype(jnp.bfloat16)
    maps_copy.start()

    def copy_tile(i):
        at = tile_rows(i)
        hidden = tokens_ref[at, :].astype(jnp.float32)
        inverse = lax.rsqrt(jnp.mean(hidden * hidden, axis=1, keepdims=True) + eps_norm)
        normed[at, :] = (hidden * inverse * gain_ref[...]).astype(jnp.bfloat16)

    each(tiles, copy_tile)
    maps_copy.wait()

    def conv_back_tile(i):
        at = tile_rows(i)
        d_conv[at, inner:] = maps_send[at, :].astype(jnp.float32) + maps_recv[at, :].astype(
            jnp.float32
        )
        value = conv_ref[at, :]
        sig = sigmoid(value)
        d_conv[at, :] = d_conv[at, :] * (sig * (1.0 + value * (1.0 - sig)))

    each(tiles, conv_back_tile)

    @pl.when(seq > 0)
    def _():
        halo_copy.start()

    @pl.when(seq == count - 1)
    def _():
        d_conv[pl.ds(rows, HALO), :] = jnp.zeros((HALO, width), jnp.float32)

    @pl.when(seq < count - 1)
    def _():
        halo_copy.wait_recv()

    if not merged:
        g_taps_ref[...] = jnp.zeros_like(g_taps_ref)

    def taps_tile(i):
        at = tile_rows(i)
        window_at = pl.ds(pl.multiple_of(i * TILE, TILE), TILE + HALO)
        seg = seg_ref[pl.ds(pl.multiple_of(i * TILE, TILE), TILE + 2 * HALO), :]
        own = seg[HALO : HALO + TILE]
        before = [
            jnp.where(seg[HALO - 3 + k : HALO - 3 + k + TILE] == own, 1.0, 0.0) for k in range(3)
        ]
        after = [
            jnp.where(seg[HALO + 3 - k : HALO + 3 - k + TILE] == own, 1.0, 0.0) for k in range(3)
        ]
        for j in range(width // LANES):
            columns = slice(j * LANES, (j + 1) * LANES)
            window = pre_ref[window_at, columns]
            grads = d_conv[window_at, columns]
            own_grad = grads[:TILE]
            summed = taps_ref[3:4, columns] * own_grad
            g_taps_ref[3:4, columns] += jnp.sum(own_grad * window[HALO:], axis=0, keepdims=True)
            for k in range(3):
                summed = summed + taps_ref[k : k + 1, columns] * (
                    grads[3 - k : 3 - k + TILE] * after[k]
                )
                g_taps_ref[k : k + 1, columns] += jnp.sum(
                    own_grad * (window[HALO - 3 + k : HALO - 3 + k + TILE] * before[k]),
                    axis=0,
                    keepdims=True,
                )
            side[at, j * LANES : (j + 1) * LANES] = summed.astype(jnp.bfloat16)

    each(tiles, taps_tile)
    advance()

    def memory_wait(step, carry):
        @pl.when(seq - step >= 0)
        def _():
            memory_copy(step).wait_send()

        @pl.when(seq + step < count)
        def _():
            memory_copy(step).wait_recv()

        return carry

    lax.fori_loop(1, count, memory_wait, 0)

    def memory_tile(i):
        at = tile_rows(i)

        def one(step, carry):
            came = memory_recv[step - 1, at, :].astype(jnp.float32)
            return carry + jnp.where(seq + step < count, came, 0.0)

        grad = lax.fori_loop(1, count, one, d_memory_ref[seq, at, :].astype(jnp.float32))
        lane = lax.broadcasted_iota(jnp.int32, grad.shape, 1)
        turned = grad * table_ref[at, :LANES] - turn_half(grad) * table_ref[at, LANES:]
        side[at, memory_at : memory_at + LANES] = jnp.where(lane < HD, turned, grad).astype(
            jnp.bfloat16
        )
        if not merged:
            side[at, query_at:memory_at] = d_query_ref[at, :]

    each(tiles, memory_tile)

    def weight_block(k):
        size = model // count
        block = pl.ds(pl.multiple_of(k * size, LANES), size)
        grad = matmul_first(normed[:, block], side[...])
        if merged:
            bits = seq_bits()
            g_side_ref[place_bits(k, bits)] = grad.reshape(g_side_ref.shape[bits:]).astype(
                jnp.bfloat16
            )
        else:
            g_side_ref[block, :] = grad.astype(jnp.bfloat16)

    each(count, weight_block)
    if merged:
        reduction.allow(len(chunks))
    advance()

    def norm_tile(i):
        at = tile_rows(i)
        part = (
            matmul_last(d_gate_z_ref[at, :], gate_weight[...])
            + matmul_last(side[at, :inner], input_weight[...])
            + matmul_last(side[at, inner:step_at], maps_weight[...]) / lax.axis_size("head")
            + matmul(side[at, step_at:query_at], step_weight[...])
            + matmul_last(side[at, query_at:memory_at], query_weight[...])
            + matmul_last(side[at, memory_at:], memory_weight[...])
        )
        norm_send[at, :] = part.astype(jnp.bfloat16)
        norm_copy(i).start()

    each(tiles, norm_tile)

    advance()
    if not merged:
        g_gain_ref[...] = jnp.zeros_like(g_gain_ref)

    def last_tile(i):
        at = tile_rows(i)
        norm_copy(i).wait()
        d_norm = norm_send[at, :].astype(jnp.float32) + norm_recv[at, :].astype(jnp.float32)
        hidden = tokens_ref[at, :].astype(jnp.float32)
        inverse = lax.rsqrt(jnp.mean(hidden * hidden, axis=1, keepdims=True) + eps_norm)
        e_one = d_norm * gain_ref[...]
        cross = jnp.sum(e_one * hidden, axis=1, keepdims=True) / model
        d_tokens_ref[at, :] = (
            d_second_ref[at, :] + inverse * e_one - hidden * (inverse * inverse * inverse * cross)
        )
        g_gain_ref[gain_row : gain_row + 1, :] += jnp.sum(
            d_norm * hidden * inverse, axis=0, keepdims=True
        )

    each(tiles, last_tile)
    if merged:
        small_sum = SmallSum(small_in, small_buf, sem_small)
        small_sum.start()
        reduction.finish()
        small_out[...] = small_sum.finish()

    @pl.when(seq > 0)
    def _():
        halo_copy.wait_send()
        for p in range(pieces):
            chain_copy(p).wait_send()


def mixer_back(common, saved, attention, grads=None, came=()):
    tokens = common[0]
    rows, model = tokens.shape
    gate_weight, query_weight, memory_weight, taps = common[4], common[8], common[9], common[10]
    merged = grads is not None
    count = lax.axis_size("seq")
    inner = gate_weight.shape[1]
    width = taps.shape[1]
    state_width = (width - inner) // 2
    tiles = rows // CHUNK
    pieces = inner // PIECE
    memory_width = memory_weight.shape[1]
    side = width + LANES + query_weight.shape[1] + memory_width
    vmem = pl.BlockSpec(memory_space=pltpu.VMEM)
    hbm = pl.BlockSpec(memory_space=pl.ANY)
    low, full = jnp.bfloat16, jnp.float32
    shape = jax.ShapeDtypeStruct
    operands = [*common, *saved]
    in_specs = [vmem] * (len(operands) + len(attention))
    operands += attention
    chunks = None
    scratch = [
        pltpu.VMEM((rows, model), low),
        pltpu.VMEM((LANES, inner), low),
        pltpu.VMEM((rows, width), full),
        pltpu.VMEM((rows + HALO, width), full),
        pltpu.VMEM((rows, inner), full),
        pltpu.VMEM((rows, 2 * state_width), full),
        pltpu.VMEM((rows, LANES), full),
        pltpu.VMEM((tiles, state_width, inner), full),
        pltpu.VMEM((state_width, inner), full),
        pltpu.VMEM((HALO, inner), full),
        pltpu.VMEM((state_width, inner), full),
        pltpu.VMEM((1, inner), full),
        pltpu.VMEM((rows, side), low),
        pltpu.VMEM((state_width, inner), low),
        pltpu.VMEM((state_width, inner), low),
        pltpu.VMEM((rows, 2 * state_width), low),
        pltpu.VMEM((rows, 2 * state_width), low),
        pltpu.VMEM((max(count - 1, 1), rows, memory_width), low),
        pltpu.VMEM((rows, model), low),
        pltpu.VMEM((rows, model), low),
        pltpu.SemaphoreType.DMA((2, count)),
        pltpu.SemaphoreType.DMA((2,)),
        pltpu.SemaphoreType.DMA((2, pieces)),
        pltpu.SemaphoreType.DMA((2,)),
        pltpu.SemaphoreType.DMA((2, tiles)),
    ]
    if merged:
        blocks = list(grads)
        widths = [g.shape[-1] for g in grads] + [side]
        chunks = column_chunks(widths)
        loaded = [pltpu.VMEM(x.shape, x.dtype) for x in operands]
        scratch = loaded + [pltpu.SemaphoreType.DMA((len(loaded),))] + scratch
        operands += blocks + list(came)
        in_specs = [hbm] * len(operands)
        own = blocks[0].shape[-2]
        small = (HALO, model)
        out_shape = (
            [shape((rows, model), full)]
            + [shape((2, 2, own, w), low) for w in widths]
            + [shape(small, full)]
        )
        scratch += [
            pltpu.VMEM(blocks[0].shape[:-1] + (side,), low),
            pltpu.VMEM((count * rows, memory_width), full),
            pltpu.VMEM((count, rows, memory_width), low),
        ]
        scratch += small_scratch(small) + reduction_scratch(chunks, widths, own)
    else:
        out_shape = [
            shape((rows, model), full),
            shape((model, side), low),
            shape((HALO, width), full),
            shape((1, model), full),
            shape((HALO, LANES), full),
        ]
    return pl.pallas_call(
        functools.partial(mixer_back_kernel, merged, chunks),
        out_shape=out_shape,
        in_specs=in_specs,
        out_specs=[vmem] * len(out_shape),
        scratch_shapes=scratch,
        compiler_params=pltpu.CompilerParams(
            collective_id=3, has_side_effects=True, vmem_limit_bytes=62 << 20
        ),
        name="mixer_back",
    )(*operands)


def finish_kernel(sizes, count, *refs):
    inner, maps, heads, query, own = sizes
    full = jnp.float32
    refs = list(refs)

    def take(number):
        nonlocal refs
        now, refs = refs[:number], refs[number:]
        return now

    sums, (small,), passed = take(5), take(1), take(2)
    outs, small_outs, passed_outs = take(count), take(9), take(2)
    loaded, held, wide = take(5), take(2), take(count)
    sem_in, sem_out = refs
    loads = [
        pltpu.make_async_copy(a, b, sem_in.at[k])
        for k, (a, b) in enumerate(zip([*sums, *passed], loaded + held))
    ]
    for copy in loads:
        copy.start()
    down, feed, mixed, gate, side = loaded
    half = feed.shape[1] // 2
    step_at = inner + maps
    query_at = step_at + LANES
    memory_at = query_at + query
    parts = (
        (0, lambda: down[...]),
        (1, lambda: feed[:, :half]),
        (1, lambda: feed[:, half:]),
        (2, lambda: mixed[:, :inner]),
        (2, lambda: mixed[:, inner:]),
        (3, lambda: gate[...]),
        (4, lambda: side[:, :inner]),
        (4, lambda: side[:, inner:step_at]),
        (4, lambda: side[:, query_at:memory_at]),
        (4, lambda: side[:, memory_at:]),
    )
    stores = []
    for k, (group, value) in enumerate(parts):
        if k == 0 or parts[k - 1][0] != group:
            loads[group].wait()
        wide[k][...] = value().astype(full)
        stores.append(pltpu.make_async_copy(wide[k], outs[k], sem_out.at[k]))
        stores[-1].start()
    o_step, o_conv_inner, o_conv_maps, o_mixer_gain, o_rate, o_bias, o_skip, o_mamba, o_feed = (
        small_outs
    )
    o_step[...] = side[:, step_at:query_at].astype(full).T[:heads]
    seq = lax.axis_index("seq")
    value = small[...]
    width = value.shape[1]
    o_conv_inner[...] = value[:4, :inner]
    o_conv_maps[...] = value[:4, inner:]
    turned = pltpu.roll(value, lax.rem(width - seq * own, width), 1)
    o_mixer_gain[...] = turned[5:6, :own]
    o_feed[...] = turned[6:7, :own]
    for k, out in enumerate((o_rate, o_bias, o_skip)):
        out[...] = value[7:8, k * LANES : (k + 1) * LANES][:, :heads]
    for k in range(inner // LANES):
        o_mamba[k : k + 1, :] = value[4:5, k * LANES : (k + 1) * LANES]
    for k, (a, b) in enumerate(zip(held, passed_outs)):
        loads[5 + k].wait()
        stores.append(pltpu.make_async_copy(a, b, sem_out.at[count + k]))
        stores[-1].start()
    for copy in stores:
        copy.wait()


def finish_outputs(sums, small, passed, sizes):
    inner, maps, heads, query, own = sizes
    sums = [s.reshape(own, s.shape[-1]) for s in sums]
    half = sums[1].shape[1] // 2
    attention = sums[2].shape[1] - inner
    memory = sums[4].shape[1] - inner - maps - LANES - query
    full = jnp.float32
    widths = (sums[0].shape[1], half, half, inner, attention, inner, inner, maps, query, memory)
    big = [jax.ShapeDtypeStruct((own, w), full) for w in widths]
    little = [
        jax.ShapeDtypeStruct(s, full)
        for s in (
            (heads, own),
            (4, inner),
            (4, maps),
            (1, own),
            (1, heads),
            (1, heads),
            (1, heads),
            (inner // LANES, LANES),
            (1, own),
        )
    ]
    vmem = pl.BlockSpec(memory_space=pltpu.VMEM)
    hbm = pl.BlockSpec(memory_space=pl.ANY)
    return pl.pallas_call(
        functools.partial(finish_kernel, sizes, len(big)),
        out_shape=big + little + [jax.ShapeDtypeStruct(p.shape, p.dtype) for p in passed],
        in_specs=[hbm] * 5 + [vmem] + [hbm] * 2,
        out_specs=[hbm] * len(big) + [vmem] * len(little) + [hbm] * 2,
        scratch_shapes=[pltpu.VMEM(s.shape, s.dtype) for s in [*sums, *passed]]
        + [pltpu.VMEM(s.shape, full) for s in big]
        + [
            pltpu.SemaphoreType.DMA((7,)),
            pltpu.SemaphoreType.DMA((len(big) + 2,)),
        ],
        compiler_params=pltpu.CompilerParams(vmem_limit_bytes=60 << 20),
        name="finish_outputs",
    )(*sums, small, *passed)


def rotation_table(position):
    half = HD // 2
    lane = jnp.arange(LANES)
    inverse_freq = rope_base ** (-(lane % half).astype(jnp.float32) / half)
    angles = position.astype(jnp.float32)[:, None] * inverse_freq[None, :]
    sign = jnp.where(lane % HD < half, -1.0, 1.0)
    return jnp.concatenate([jnp.cos(angles), sign[None, :] * jnp.sin(angles)], axis=1)


def body(
    tokens,
    seg_ids,
    mixer_gain,
    mamba_gate,
    mamba_input,
    mamba_maps,
    mamba_step,
    conv_inner,
    conv_maps,
    log_rate,
    step_bias,
    skip_gain,
    mamba_gain,
    mamba_output,
    query_weight,
    memory_weight,
    attention_out,
    feed_gain,
    gate_weight,
    lift_weight,
    down_weight,
    cotangent,
):
    tokens, cotangent = tokens[0], cotangent[0]
    rows, wide = tokens.shape
    tap_count, inner = conv_inner.shape
    head_count = log_rate.shape[0]
    offset = lax.axis_index("seq") * rows
    table = rotation_table(offset + jnp.arange(rows, dtype=jnp.int32))
    (
        gate_z,
        pre,
        conv,
        raw,
        cum,
        y,
        states,
        query,
        memory,
        attention,
        attention_low,
        logs,
        window,
        key_segments,
        step_weight,
        taps,
        rate,
        skip,
    ) = mixer_forward(
        tokens,
        mixer_gain[None],
        seg_ids,
        table,
        mamba_gate,
        mamba_input,
        mamba_maps,
        mamba_step.T,
        query_weight,
        memory_weight,
        conv_inner,
        conv_maps,
        step_bias,
        log_rate,
        skip_gain,
    )
    all_memory = memory.reshape(memory.shape[0] * rows, memory.shape[2])
    (
        layer_out,
        d_second,
        d_y,
        d_gate_z,
        d_attention,
        g_feed,
        g_mixed,
        g_down,
        g_gate,
        g_feed_gain,
        g_mamba_gain,
        *came,
    ) = feed_layer(
        y,
        gate_z,
        attention_low,
        tokens,
        cotangent,
        mixer_gain,
        mamba_gain,
        feed_gain,
        mamba_output,
        attention_out,
        gate_weight,
        lift_weight,
        down_weight,
    )
    common = [
        tokens,
        mixer_gain[None],
        window,
        table,
        mamba_gate,
        mamba_input,
        mamba_maps,
        step_weight,
        query_weight,
        memory_weight,
        taps,
        rate,
        skip,
    ]
    saved = [pre, conv, raw, cum, y, states, d_second, d_y, d_gate_z]
    early = [g_down, g_feed, g_mixed, g_gate]
    if lax.axis_size("seq") == 4:
        grad_tokens, *sums, small = mixer_back(
            common,
            saved,
            [
                query,
                all_memory,
                key_segments,
                attention,
                logs,
                d_attention,
                g_feed_gain,
                g_mamba_gain,
            ],
            early,
            came,
        )
    else:
        starts = offset + jnp.arange(rows // TILE, dtype=jnp.int32) * TILE
        reach = seg_ids[0, KEY_TILE - 1 :: KEY_TILE]
        own = lax.dynamic_slice_in_dim(seg_ids[0], offset, rows)[::TILE]
        low = jnp.sum((reach[None, :] < own[:, None]).astype(jnp.int32), axis=1)
        spans = (offset[None], low, (starts + TILE - 1) // KEY_TILE)
        d_query, d_memory = attention_back(
            spans, query, all_memory, window, key_segments, attention, logs, d_attention, table
        )
        grad_tokens, g_side, g_taps, g_mixer_gain, g_heads = mixer_back(
            common, saved, [d_query, d_memory.reshape(memory.shape)]
        )
        *sums, small = reduce_gradients(
            early + [g_side],
            jnp.concatenate(
                [
                    g_taps[:tap_count],
                    jnp.pad(g_mamba_gain, ((0, 0), (0, wide - inner))),
                    g_mixer_gain,
                    g_feed_gain,
                    jnp.pad(g_heads[:3].reshape(1, 3 * LANES), ((0, 0), (0, wide - 3 * LANES))),
                ],
                axis=0,
            ),
        )
    sizes = (
        inner,
        conv_maps.shape[1],
        head_count,
        query_weight.shape[1],
        wide // lax.axis_size("seq"),
    )
    (
        o_down,
        o_gate,
        o_lift,
        o_output,
        o_attention,
        o_gate_z,
        o_inner,
        o_maps,
        o_query,
        o_memory,
        o_step,
        o_conv_inner,
        o_conv_maps,
        o_mixer_gain,
        o_rate,
        o_bias,
        o_skip,
        o_mamba_gain,
        o_feed_gain,
        layer_out,
        grad_tokens,
    ) = finish_outputs(sums, small, (layer_out, grad_tokens), sizes)
    return (
        layer_out[None],
        grad_tokens[None],
        o_mixer_gain[0],
        o_gate_z,
        o_inner,
        o_maps,
        o_step.T,
        o_conv_inner,
        o_conv_maps,
        o_rate[0],
        o_bias[0],
        o_skip[0],
        o_mamba_gain.reshape(inner),
        o_output,
        o_query,
        o_memory,
        o_attention,
        o_feed_gain[0],
        o_gate,
        o_lift,
        o_down,
    )


def solution(mesh):
    return jax.shard_map(
        body,
        mesh=mesh,
        in_specs=(
            P("batch", "seq", None),
            P("batch", None),
            P(),
            P(None, "head"),
            P(None, "head"),
            P(),
            P(None, "head"),
            P(None, "head"),
            P(),
            P("head"),
            P("head"),
            P("head"),
            P("head"),
            P(None, "head"),
            P(None, "head"),
            P(None, "head"),
            P(None, "head"),
            P(),
            P(None, "head"),
            P(None, "head"),
            P(None, "head"),
            P("batch", "seq", None),
        ),
        out_specs=(
            P("batch", "seq", None),
            P("batch", "seq", None),
            P("seq"),
            P("seq", "head"),
            P("seq", "head"),
            P("seq", None),
            P("seq", "head"),
            P(None, "head"),
            P(),
            P("head"),
            P("head"),
            P("head"),
            P("head"),
            P("seq", "head"),
            P("seq", "head"),
            P("seq", "head"),
            P("seq", "head"),
            P("seq"),
            P("seq", "head"),
            P("seq", "head"),
            P("seq", "head"),
        ),
        check_vma=False,
    )
```

```python
import functools

import jax
import jax.numpy as jnp
from jax import lax
from jax.experimental import pallas as pl
from jax.experimental.pallas import tpu as pltpu
from jax.sharding import PartitionSpec as P

HD = 64
eps_norm = 1e-05
rope_base = 10000.0
neg_large = -1e30
highest = lax.Precision.HIGHEST


LANES = 128
MOST = 512
TAIL = (512, 512, 384, 128)
AHEAD = 8
EARLIER = 3
LAG = 3
PATTERN = (0, 1, 2, 0, 1, 3, 0, 1, 0, 1, 2, 0, 1, 3, 0, 1)
MESH = pl.DeviceIdType.MESH


def exchange(source, target, send_sem, recv_sem, device):
    return pltpu.make_async_remote_copy(
        src_ref=source,
        dst_ref=target,
        send_sem=send_sem,
        recv_sem=recv_sem,
        device_id=device,
        device_id_type=MESH,
    )


def moving(kernel, inputs, loaded, outputs, *refs):
    given, refs = refs[:inputs], refs[inputs:]
    targets, refs = refs[:outputs], refs[outputs:]
    taken, refs = refs[:loaded], refs[loaded:]
    held, refs = refs[:outputs], refs[outputs:]
    sem_in, sem_out, refs = refs[0], refs[1], refs[2:]
    loads = [
        pltpu.make_async_copy(source, target, sem_in.at[k])
        for k, (source, target) in enumerate(zip(given[:loaded], taken))
    ]
    for load in loads:
        load.start()
    stores = [
        pltpu.make_async_copy(source, target, sem_out.at[k])
        for k, (source, target) in enumerate(zip(held, targets))
    ]
    kernel(loads, stores, *taken, *given[loaded:], *held, *refs)
    for store in stores:
        store.wait()


def moving_scratch(operands, results):
    return [pltpu.VMEM(x.shape, x.dtype) for x in [*operands, *results]] + [
        pltpu.SemaphoreType.DMA((len(operands),)),
        pltpu.SemaphoreType.DMA((len(results),)),
    ]


def start_all(stores, *which):
    for k in which:
        stores[k].start()


def each(count, action):
    span(0, count, action)


def span(first, last, action):
    lax.fori_loop(first, last, lambda i, carry: (action(i), carry)[1], 0)


def column_chunks(widths):
    chunks = []
    for group, width in enumerate(widths):
        count = -(-width // MOST)
        tiles = width // LANES
        sizes = [(tiles // count + (1 if k < tiles % count else 0)) * LANES for k in range(count)]
        if group == len(widths) - 1 and width == sum(TAIL):
            sizes = TAIL
        start = 0
        for size in sizes:
            chunks.append((group, start, size))
            start += size
    return chunks


def seq_bits():
    return (lax.axis_size("seq") - 1).bit_length()


def place_bits(place, bits):
    return tuple(lax.rem(place // 2 ** (bits - 1 - b), 2) for b in range(bits))


def seq_blocks(grad):
    bits = seq_bits() + 2
    return grad.reshape((2,) * bits + (grad.shape[0] >> bits, grad.shape[1]))


def peer_device():
    return (lax.axis_index("seq"), 1 - lax.axis_index("head"), lax.axis_index("batch"))


def other_device(step):
    seq, batch = lax.axis_index("seq"), lax.axis_index("batch")
    batches = lax.axis_size("batch")
    place = lax.rem(seq * batches + batch + step, lax.axis_size("seq") * batches)
    return (place // batches, lax.axis_index("head"), lax.rem(place, batches))


def greet_all(barrier, with_peer):
    world = lax.axis_size("seq") * lax.axis_size("batch")
    span(
        1,
        world,
        lambda step: pl.semaphore_signal(
            barrier, inc=1, device_id=other_device(step), device_id_type=MESH
        ),
    )
    if with_peer:
        pl.semaphore_signal(barrier, inc=1, device_id=peer_device(), device_id_type=MESH)
    pl.semaphore_wait(barrier, world - 1 + (1 if with_peer else 0))


class SmallSum:
    def __init__(self, source, slots, sems):
        self.source, self.slots, self.sems = source, slots, sems
        self.world = slots.shape[0]
        self.mine = lax.axis_index("seq") * lax.axis_size("batch") + lax.axis_index("batch")

    def copy(self, step):
        return exchange(
            self.source,
            self.slots.at[self.mine],
            self.sems.at[0, step],
            self.sems.at[1, step],
            other_device(step),
        )

    def start(self):
        span(1, self.world, lambda step: self.copy(step).start())

    def finish(self):
        span(1, self.world, lambda step: self.copy(step).wait())
        self.slots[self.mine] = self.source[...]
        return lax.fori_loop(
            1, self.world, lambda k, total: total + self.slots[k], self.slots[0]
        )


def small_scratch(shape):
    world = lax.axis_size("seq") * lax.axis_size("batch")
    return [
        pltpu.VMEM(shape, jnp.float32),
        pltpu.VMEM((world,) + shape, jnp.float32),
        pltpu.SemaphoreType.DMA((2, world)),
    ]


class Reduction:
    def __init__(self, chunks, sources, outs, scratch, given=()):
        self.chunks, self.sources, self.outs, self.given = chunks, sources, outs, given
        groups = len(sources)
        self.bits = seq_bits() + 2
        scratch = list(scratch)
        self.parts = [scratch[k * groups : (k + 1) * groups] for k in range(self.bits)]
        self.own, self.sem_own, self.sem_halve, self.sem_back = scratch[self.bits * groups :]
        self.setup()

    def setup(self):
        self.seq, self.head = lax.axis_index("seq"), lax.axis_index("head")
        self.batch = lax.axis_index("batch")
        place = self.seq * 4 + self.batch
        self.mine = [lax.rem(place // 2 ** (self.bits - 1 - k), 2) for k in range(self.bits)]
        self.done = [0] * (self.bits + 2)
        self.sent = self.held = self.limit = 0

    def peer(self, bit):
        step = (1 - 2 * self.mine[bit]) * 2 ** (self.bits - 1 - bit)
        if bit < self.bits - 2:
            return (self.seq + step // 4, self.head, self.batch)
        return (self.seq, self.head, self.batch + step)

    def order(self, k):
        low, high, last = self.bits - 1, self.bits - 2, self.bits - 3
        rest = [b for b in range(self.bits - 3, -1, -1)]
        if last < 0:
            return [low, high] if k % 2 == 0 else [high, low]
        kind = PATTERN[k % len(PATTERN)]
        if kind == 0:
            return [low, high] + rest
        if kind == 1:
            return [high, low] + rest
        if kind == 2:
            return [last, low, high] + rest[1:]
        return [last, high, low] + rest[1:]

    def place(self, k):
        group, start, size = self.chunks[k]
        return group, pl.ds(start, size)

    def cut(self, k, step, kept):
        order = self.order(k)
        left = [b for b in range(self.bits) if b not in order[:step]]
        bit = order[step]
        value = self.mine[bit] if kept else 1 - self.mine[bit]
        return tuple(value if b == bit else slice(None) for b in left)

    def halve_copy(self, k, step):
        group, columns = self.place(k)
        source = self.sources[group] if step == 0 else self.parts[step - 1][group]
        target = self.parts[step][group]
        away = self.cut(k, step, False)
        return exchange(
            source.at[away + (slice(None), columns)],
            target.at[(slice(None),) * (len(away) - 1) + (slice(None), columns)],
            self.sem_halve.at[0, k, step],
            self.sem_halve.at[1, k, step],
            self.peer(self.order(k)[step]),
        )

    def first_copy(self, k):
        group, columns = self.place(k)
        if group >= len(self.given) or k >= EARLIER:
            return self.halve_copy(k, 0)
        where = (slice(None),) * self.bits + (columns,)
        return pltpu.make_async_copy(
            self.given[group].at[where], self.parts[0][group].at[where], self.sem_halve.at[0, k, 0]
        )

    def own_copy(self, k):
        group, columns = self.place(k)
        size = self.chunks[k][2]
        kept = self.cut(k, 0, True)
        return pltpu.make_async_copy(
            self.sources[group].at[kept + (slice(None), columns)],
            self.own.at[(k % 2,) + (slice(None),) * self.bits + (pl.ds(0, size),)],
            self.sem_own.at[k],
        )

    def add(self, k, step):
        group, columns = self.place(k)
        size = self.chunks[k][2]
        target = self.parts[step][group]
        left = self.bits - 1 - step

        def one(index):
            every = index + (slice(None), columns)
            if step == 0:
                own = self.own[(k % 2,) + index + (slice(None), slice(0, size))]
            else:
                kept = self.cut(k, step, True)
                spot = [v for v in kept]
                rest = iter(index)
                spot = tuple(v if not isinstance(v, slice) else next(rest) for v in spot)
                own = self.parts[step - 1][group][spot + (slice(None), columns)]
            value = own + target[every]
            if step == self.bits - 1:
                self.outs[group][self.mine[-2], self.mine[-1], :, columns] = value
            else:
                target[every] = value

        span(
            0,
            2**left,
            lambda n: one(place_bits(n, left)),
        )

    def back_copy(self, k, turn):
        group, columns = self.place(k)
        out = self.outs[group]
        high, low = self.mine[-2], self.mine[-1]
        first_low = self.order(k).index(self.bits - 1) < self.order(k).index(self.bits - 2)
        bit = self.bits - 2 if first_low == (turn == 0) else self.bits - 1
        if turn == 0:
            part = out.at[high, low, :, columns]
        elif first_low:
            part = out.at[:, low, :, columns]
        else:
            part = out.at[high, :, :, columns]
        return exchange(
            part, part, self.sem_back.at[0, k, turn], self.sem_back.at[1, k, turn], self.peer(bit)
        )

    def refill(self):
        while self.sent < min(self.limit, self.done[0] + AHEAD):
            self.first_copy(self.sent).start()
            self.sent += 1
        while self.held < min(self.limit, self.done[0] + 2):
            self.own_copy(self.held).start()
            self.held += 1

    def allow(self, limit):
        self.limit = limit
        self.refill()

    def advance(self):
        stages = self.bits + 2
        for step in range(stages - 1, -1, -1):
            k = self.done[step]
            before = self.done[step - 1] if step else self.limit
            if k >= before or (step and before - k < LAG and before < self.limit):
                continue
            if step < self.bits:
                if step == 0:
                    self.first_copy(k).wait()
                    self.own_copy(k).wait()
                else:
                    self.halve_copy(k, step).wait()
                self.add(k, step)
                if step + 1 < self.bits:
                    self.halve_copy(k, step + 1).start()
                else:
                    self.back_copy(k, 0).start()
            elif step == self.bits:
                self.back_copy(k, 0).wait()
                self.back_copy(k, 1).start()
            else:
                self.back_copy(k, 1).wait()
            self.done[step] += 1
            if step == 0:
                self.refill()

    def finish(self):
        while self.done[-1] < len(self.chunks):
            self.advance()


class FirstHalving(Reduction):
    def __init__(self, chunks, sources, targets, sems):
        self.chunks, self.sources = chunks, sources
        self.bits = seq_bits() + 2
        self.parts, self.sem_halve = [targets], sems
        self.setup()


def reduction_scratch(chunks, widths, rows):
    bits = seq_bits() + 2
    parts = len(chunks)
    most = max(size for _, _, size in chunks)
    low = jnp.bfloat16
    return [
        pltpu.VMEM((2,) * (bits - 1 - step) + (rows, w), low)
        for step in range(bits)
        for w in widths
    ] + [
        pltpu.VMEM((2,) * bits + (rows, most), low),
        pltpu.SemaphoreType.DMA((parts,)),
        pltpu.SemaphoreType.DMA((2, parts, bits)),
        pltpu.SemaphoreType.DMA((2, parts, 2)),
    ]


def reduce_kernel(chunks, *refs):
    count = 1 + max(c[0] for c in chunks)
    sources, refs = refs[:count], refs[count:]
    small_given, refs = refs[0], refs[1:]
    outs, refs = refs[:count], refs[count:]
    small_out, small_in, small_buf, sem_small, *refs = refs
    greet_all(pltpu.get_barrier_semaphore(), False)
    reduction = Reduction(chunks, sources, outs, refs)
    reduction.allow(len(chunks))
    small_in[...] = small_given[...]
    small_sum = SmallSum(small_in, small_buf, sem_small)
    small_sum.start()
    reduction.finish()
    small_out[...] = small_sum.finish()


def reduce_gradients(grads, small):
    widths = [g.shape[1] for g in grads]
    chunks = column_chunks(widths)
    blocks = [seq_blocks(g) for g in grads]
    rows = blocks[0].shape[-2]
    vmem = pl.BlockSpec(memory_space=pltpu.VMEM)
    return pl.pallas_call(
        functools.partial(reduce_kernel, chunks),
        out_shape=[jax.ShapeDtypeStruct((2, 2, rows, w), jnp.bfloat16) for w in widths]
        + [jax.ShapeDtypeStruct(small.shape, jnp.float32)],
        in_specs=[pl.BlockSpec(memory_space=pl.ANY)] * len(grads) + [vmem],
        out_specs=[vmem] * (len(grads) + 1),
        scratch_shapes=small_scratch(small.shape) + reduction_scratch(chunks, widths, rows),
        compiler_params=pltpu.CompilerParams(
            collective_id=0, has_side_effects=True, vmem_limit_bytes=56 << 20
        ),
        name="reduce_gradients",
    )(*blocks, small)


def matmul(former, latter):
    return jnp.dot(former, latter, preferred_element_type=jnp.float32)


def matmul_last(former, latter):
    return lax.dot_general(
        former, latter, (((1,), (1,)), ((), ())), preferred_element_type=jnp.float32
    )


def matmul_first(former, latter):
    return lax.dot_general(
        former, latter, (((0,), (0,)), ((), ())), preferred_element_type=jnp.float32
    )


TILE = 128


def sigmoid(v):
    return 1.0 / (1.0 + jnp.exp(-v))


def greet(barrier, devices):
    for device in devices:
        pl.semaphore_signal(barrier, inc=1, device_id=device, device_id_type=MESH)
    pl.semaphore_wait(barrier, len(devices))


def tile_rows(i):
    return pl.ds(pl.multiple_of(i * TILE, TILE), TILE)


FEED_TILE = 256


def feed_rows(i):
    return pl.ds(pl.multiple_of(i * FEED_TILE, FEED_TILE), FEED_TILE)


def feed_kernel(merged, loads, stores, *refs):
    (
        y_ref,
        gate_z_ref,
        attention_ref,
        tokens_ref,
        cotangent_ref,
        mixer_gain_ref,
        mamba_gain_ref,
        feed_gain_ref,
        mamba_output_ref,
        attention_out_ref,
        gate_weight_hbm,
        lift_weight_hbm,
        down_weight_hbm,
        out_ref,
        d_second_ref,
        d_y_ref,
        d_gate_z_ref,
        d_attention_ref,
        g_feed_ref,
        g_mixed_ref,
        g_down_ref,
        g_gate_ref,
        g_feed_gain_ref,
        g_mamba_gain_ref,
    ) = refs[: 24]
    refs = refs[24:]
    if merged:
        came_refs, refs = refs[:2], refs[2:]
    (
        gate_weight,
        lift_weight,
        down_weight,
        normed,
        gated,
        g_six,
        inverse_six,
        second,
        inverse_two,
        normed2,
        active,
        d_feed,
        d_mix,
        d_gated,
        square_send,
        square_recv,
        cross_send,
        cross_recv,
        mixed_send,
        mixed_recv,
        lift_send,
        lift_recv,
        norm_send,
        norm_recv,
        weight_sem,
        sem_square,
        sem_cross,
        sem_mixed,
        sem_lift,
        sem_norm,
        *sem_first,
    ) = refs
    rows = y_ref.shape[0]
    tiles = rows // FEED_TILE
    inner = y_ref.shape[1]
    width = feed_gain_ref.shape[1]
    feed = down_weight.shape[1]
    all_inner = inner * lax.axis_size("head")
    peer = peer_device()
    weight_loads = [
        pltpu.make_async_copy(source, target, weight_sem.at[k])
        for k, (source, target) in enumerate(
            (
                (gate_weight_hbm, gate_weight),
                (lift_weight_hbm, lift_weight),
                (down_weight_hbm, down_weight),
            )
        )
    ]
    for load in weight_loads:
        load.start()
    devices = [peer]
    if merged:
        first = FirstHalving(
            column_chunks((g_down_ref.shape[-1], g_feed_ref.shape[-1]))[:EARLIER],
            [g_down_ref, g_feed_ref],
            came_refs,
            sem_first[0],
        )
        devices += [first.peer(bit) for bit in range(first.bits - 3, first.bits)]
    greet(pltpu.get_barrier_semaphore(), devices)
    for load in loads:
        load.wait()
    mamba_gain = jnp.concatenate(
        [mamba_gain_ref[k : k + 1, :] for k in range(mamba_gain_ref.shape[0])], axis=1
    )

    def swap(send, recv, sems, i):
        rows_now = feed_rows(i)
        return exchange(send.at[rows_now], recv.at[rows_now], sems.at[0, i], sems.at[1, i], peer)

    def gate_tile(i):
        at = feed_rows(i)
        hidden = tokens_ref[at, :].astype(jnp.float32)
        inverse = lax.rsqrt(jnp.mean(hidden * hidden, axis=1, keepdims=True) + eps_norm)
        normed[at, :] = (hidden * inverse * mixer_gain_ref[...]).astype(jnp.bfloat16)
        gate_now = gate_z_ref[at, :]
        value = y_ref[at, :] * gate_now * sigmoid(gate_now)
        g_six[at, :] = value
        square_send[at, :] = jnp.broadcast_to(
            jnp.sum(value * value, axis=1, keepdims=True), (FEED_TILE, LANES)
        )
        swap(square_send, square_recv, sem_square, i).start()

    each(tiles, gate_tile)

    def mixed_tile(i):
        at = feed_rows(i)
        swap(square_send, square_recv, sem_square, i).wait()
        total = square_send[at, :] + square_recv[at, :]
        inverse = lax.rsqrt(total[:, :1] / all_inner + eps_norm)
        inverse_six[at, :] = jnp.broadcast_to(inverse, (FEED_TILE, LANES))
        low = (g_six[at, :] * inverse * mamba_gain).astype(jnp.bfloat16)
        gated[at, :] = low
        part = matmul_last(low, mamba_output_ref[...]) + matmul_last(
            attention_ref[at, :], attention_out_ref[...]
        )
        mixed_send[at, :] = part.astype(jnp.bfloat16)
        swap(mixed_send, mixed_recv, sem_mixed, i).start()

    each(tiles, mixed_tile)
    for load in weight_loads:
        load.wait()

    def feed_tile(i):
        at = feed_rows(i)
        swap(mixed_send, mixed_recv, sem_mixed, i).wait()
        total = mixed_send[at, :].astype(jnp.float32) + mixed_recv[at, :].astype(jnp.float32)
        hidden = tokens_ref[at, :].astype(jnp.float32) + total
        second[at, :] = hidden
        inverse = lax.rsqrt(jnp.mean(hidden * hidden, axis=1, keepdims=True) + eps_norm)
        inverse_two[at, :] = jnp.broadcast_to(inverse, (FEED_TILE, LANES))
        low = (hidden * inverse * feed_gain_ref[...]).astype(jnp.bfloat16)
        normed2[at, :] = low
        gate_now = matmul(low, gate_weight[...])
        lift_now = matmul(low, lift_weight[...])
        sig = sigmoid(gate_now)
        silu = gate_now * sig
        act = (silu * lift_now).astype(jnp.bfloat16)
        active[at, :] = act
        lift_send[at, :] = matmul_last(act, down_weight[...]).astype(jnp.bfloat16)
        swap(lift_send, lift_recv, sem_lift, i).start()
        d_act = matmul(cotangent_ref[at, :], down_weight[...])
        d_gate = (d_act * lift_now * (sig * (1.0 + gate_now * (1.0 - sig)))).astype(jnp.bfloat16)
        d_lift = (d_act * silu).astype(jnp.bfloat16)
        d_feed[at, :feed] = d_gate
        d_feed[at, feed:] = d_lift
        part = matmul_last(d_gate, gate_weight[...]) + matmul_last(d_lift, lift_weight[...])
        norm_send[at, :] = part.astype(jnp.bfloat16)
        swap(norm_send, norm_recv, sem_norm, i).start()

    each(tiles, feed_tile)
    blocks = lax.axis_size("seq") if merged else width // 256

    def store(target, k, grad):
        if merged:
            index = place_bits(k, seq_bits())
            target[index] = grad.reshape(target.shape[len(index) :]).astype(jnp.bfloat16)
        else:
            target[pl.ds(pl.multiple_of(k * 256, 256), 256), :] = grad.astype(jnp.bfloat16)

    def block_columns(k):
        size = width // blocks
        return pl.ds(pl.multiple_of(k * size, LANES), size)

    def feed_weights(k):
        block = block_columns(k)
        store(g_down_ref, k, matmul_first(cotangent_ref[:, block], active[...]))
        store(g_feed_ref, k, matmul_first(normed2[:, block], d_feed[...]))

    each(blocks, feed_weights)
    if merged:
        for k in range(EARLIER):
            first.halve_copy(k, 0).start()
    start_all(stores, 5, 7)
    g_feed_gain_ref[...] = jnp.zeros_like(g_feed_gain_ref)
    g_mamba_gain_ref[...] = jnp.zeros_like(g_mamba_gain_ref)

    def norm_tile(i):
        at = feed_rows(i)
        swap(norm_send, norm_recv, sem_norm, i).wait()
        d_norm = norm_send[at, :].astype(jnp.float32) + norm_recv[at, :].astype(jnp.float32)
        hidden = second[at, :]
        inverse = inverse_two[at, :][:, :1]
        e_two = d_norm * feed_gain_ref[...]
        g_feed_gain_ref[...] += jnp.sum(d_norm * hidden * inverse, axis=0, keepdims=True)
        cross = jnp.sum(e_two * hidden, axis=1, keepdims=True) / width
        d_hidden = (
            cotangent_ref[at, :].astype(jnp.float32)
            + inverse * e_two
            - hidden * (inverse * inverse * inverse * cross)
        )
        d_second_ref[at, :] = d_hidden
        low = d_hidden.astype(jnp.bfloat16)
        d_mix[at, :] = low
        d_attention_ref[at, :] = matmul(low, attention_out_ref[...])
        d_gated_now = matmul(low, mamba_output_ref[...])
        d_gated[at, :] = d_gated_now
        six = g_six[at, :]
        g_mamba_gain_ref[...] += jnp.sum(
            d_gated_now * six * inverse_six[at, :][:, :1], axis=0, keepdims=True
        )
        cross_send[at, :] = jnp.broadcast_to(
            jnp.sum(d_gated_now * mamba_gain * six, axis=1, keepdims=True), (FEED_TILE, LANES)
        )
        swap(cross_send, cross_recv, sem_cross, i).start()

    each(tiles, norm_tile)

    def gate_back(i):
        at = feed_rows(i)
        swap(cross_send, cross_recv, sem_cross, i).wait()
        cross = (cross_send[at, :] + cross_recv[at, :])[:, :1] / all_inner
        inverse = inverse_six[at, :][:, :1]
        d_six = inverse * (d_gated[at, :] * mamba_gain) - g_six[at, :] * (
            inverse * inverse * inverse * cross
        )
        gate_now = gate_z_ref[at, :]
        sig = sigmoid(gate_now)
        d_y_ref[at, :] = d_six * gate_now * sig
        d_gate_z_ref[at, :] = (
            d_six * y_ref[at, :] * (sig * (1.0 + gate_now * (1.0 - sig)))
        ).astype(jnp.bfloat16)

    each(tiles, gate_back)
    start_all(stores, 1, 2, 3, 4)

    def out_tile(i):
        at = feed_rows(i)
        swap(lift_send, lift_recv, sem_lift, i).wait()
        total = lift_send[at, :].astype(jnp.float32) + lift_recv[at, :].astype(jnp.float32)
        out_ref[at, :] = (second[at, :] + total).astype(jnp.bfloat16)

    each(tiles, out_tile)
    start_all(stores, 0)

    def mixed_weights(k):
        block = block_columns(k)
        store(g_gate_ref, k, matmul_first(normed[:, block], d_gate_z_ref[...]))
        d_mix_now = d_mix[:, block]
        grad = jnp.concatenate(
            [matmul_first(d_mix_now, gated[...]), matmul_first(d_mix_now, attention_ref[...])],
            axis=1,
        )
        store(g_mixed_ref, k, grad)

    each(blocks, mixed_weights)
    start_all(stores, 6, 8, 9, 10)
    if merged:
        for k in range(EARLIER):
            first.halve_copy(k, 0).wait()
        start_all(stores, 11, 12)


def feed_layer(
    y,
    gate_z,
    attention_low,
    tokens,
    cotangent,
    mixer_gain,
    mamba_gain,
    feed_gain,
    mamba_output,
    attention_out,
    gate_weight,
    lift_weight,
    down_weight,
):
    rows, inner = y.shape
    width = tokens.shape[1]
    feed = gate_weight.shape[1]
    att = attention_low.shape[1]
    tiles = rows // FEED_TILE
    vmem = pl.BlockSpec(memory_space=pltpu.VMEM)
    hbm = pl.BlockSpec(memory_space=pl.ANY)
    low, full = jnp.bfloat16, jnp.float32
    shape = jax.ShapeDtypeStruct
    merged = lax.axis_size("seq") == 4

    def grad_shape(columns):
        if merged:
            return shape((2,) * (seq_bits() + 2) + (width // 16, columns), low)
        return shape((width, columns), low)

    out_shape = [
            shape((rows, width), low),
            shape((rows, width), full),
            shape((rows, inner), full),
            shape((rows, inner), low),
            shape((rows, att), full),
            grad_shape(2 * feed),
            grad_shape(inner + att),
            grad_shape(feed),
            grad_shape(inner),
            shape((1, width), full),
            shape((1, inner), full),
        ]
    scratch = []
    if merged:
        out_shape += [shape((2,) * 3 + (width // 16, n), low) for n in (feed, MOST)]
        scratch = [pltpu.SemaphoreType.DMA((2, EARLIER, 1))]
    operands = [
        y,
        gate_z,
        attention_low,
        tokens,
        cotangent,
        mixer_gain[None],
        mamba_gain.reshape(inner // LANES, LANES),
        feed_gain[None],
        mamba_output,
        attention_out,
        gate_weight,
        lift_weight,
        down_weight,
    ]
    return pl.pallas_call(
        functools.partial(moving, functools.partial(feed_kernel, merged), 13, 10, len(out_shape)),
        out_shape=out_shape,
        in_specs=[hbm] * 13,
        out_specs=[hbm] * len(out_shape),
        scratch_shapes=moving_scratch(operands[:10], out_shape)
        + [
            pltpu.VMEM((width, feed), low),
            pltpu.VMEM((width, feed), low),
            pltpu.VMEM((width, feed), low),
            pltpu.VMEM((rows, width), low),
            pltpu.VMEM((rows, inner), low),
            pltpu.VMEM((rows, inner), full),
            pltpu.VMEM((rows, LANES), full),
            pltpu.VMEM((rows, width), full),
            pltpu.VMEM((rows, LANES), full),
            pltpu.VMEM((rows, width), low),
            pltpu.VMEM((rows, feed), low),
            pltpu.VMEM((rows, 2 * feed), low),
            pltpu.VMEM((rows, width), low),
            pltpu.VMEM((rows, inner), full),
            pltpu.VMEM((rows, LANES), full),
            pltpu.VMEM((rows, LANES), full),
            pltpu.VMEM((rows, LANES), full),
            pltpu.VMEM((rows, LANES), full),
        ]
        + [pltpu.VMEM((rows, width), low)] * 6
        + [pltpu.SemaphoreType.DMA((3,))]
        + [pltpu.SemaphoreType.DMA((2, tiles))] * 5
        + scratch,
        compiler_params=pltpu.CompilerParams(
            collective_id=1, has_side_effects=True, vmem_limit_bytes=60 << 20
        ),
        name="feed_layer",
    )(*operands)


CHUNK = 128
HALO = 8
PIECE = 256


def turn_half(values):
    lane = lax.broadcasted_iota(jnp.int32, values.shape, 1)
    return jnp.where(
        lax.rem(lane, HD) < HD // 2,
        pltpu.roll(values, LANES - HD // 2, 1),
        pltpu.roll(values, HD // 2, 1),
    )


def two_parts(values):
    high = values.astype(jnp.bfloat16)
    return high, (values - high.astype(jnp.float32)).astype(jnp.bfloat16)


def spread_heads(values, spread):
    high, rest = two_parts(values)
    return matmul(high, spread) + matmul(rest, spread)


def sum_heads(values, spread):
    high, rest = two_parts(values)
    return matmul_last(high, spread) + matmul_last(rest, spread)


def spread_matrix(inner, size):
    row = lax.broadcasted_iota(jnp.int32, (LANES, inner), 0)
    lane = lax.broadcasted_iota(jnp.int32, (LANES, inner), 1)
    return jnp.where(lane // size == row, 1.0, 0.0).astype(jnp.bfloat16)


def ordered(count):
    row = lax.broadcasted_iota(jnp.int32, (count, count), 0)
    lane = lax.broadcasted_iota(jnp.int32, (count, count), 1)
    return row >= lane


def halves(values, size):
    lane = lax.broadcasted_iota(jnp.int32, values.shape, 1)
    return jnp.concatenate(
        [jnp.where(lane < size, values, 0.0), jnp.where(lane < size, 0.0, values)], axis=0
    ).astype(jnp.bfloat16)


def soft_plus(v):
    return jnp.maximum(v, 0.0) + jnp.log1p(jnp.exp(-jnp.abs(v)))


def chunk_flags(seg_ref, c):
    window = seg_ref[pl.ds(pl.multiple_of(c * CHUNK, CHUNK), CHUNK + HALO), :]
    own = window[HALO:]
    start = jnp.where(own == window[HALO - 1 : HALO], 1.0, 0.0)
    end = jnp.where(own == own[CHUNK - 1 :], 1.0, 0.0)
    return own, start, end


def greet_seq(barrier, with_peer):
    seq, head, batch = lax.axis_index("seq"), lax.axis_index("head"), lax.axis_index("batch")
    count = lax.axis_size("seq")

    def one(step, carry):
        pl.semaphore_signal(
            barrier,
            inc=1,
            device_id=(lax.rem(seq + step, count), head, batch),
            device_id_type=MESH,
        )
        return carry

    lax.fori_loop(1, count, one, 0)
    if with_peer:
        pl.semaphore_signal(barrier, inc=1, device_id=peer_device(), device_id_type=MESH)
    pl.semaphore_wait(barrier, count - 1 + with_peer)


def mixer_kernel(
    loads,
    stores,
    tokens_ref,
    gain_ref,
    seg_row_ref,
    table_ref,
    gate_weight,
    input_weight,
    maps_weight,
    step_given,
    query_weight,
    memory_weight,
    conv_inner_ref,
    conv_maps_ref,
    step_bias_ref,
    log_rate_ref,
    skip_gain_ref,
    gate_z_ref,
    pre_ref,
    conv_ref,
    raw_ref,
    cum_ref,
    y_ref,
    states_ref,
    query_ref,
    memory_ref,
    attention_ref,
    attention_low_ref,
    logs_ref,
    seg_ref,
    key_seg_ref,
    step_weight,
    taps_ref,
    rate_ref,
    skip_ref,
    step_wide,
    bias_ref,
    normed,
    spread_ref,
    act,
    scaled,
    added,
    decay,
    total,
    local,
    state,
    chain_out,
    chain_in,
    memory_turned,
    sem_memory,
    sem_halo,
    sem_chain,
):
    seq, head, batch = lax.axis_index("seq"), lax.axis_index("head"), lax.axis_index("batch")
    count = lax.axis_size("seq")
    rows = tokens_ref.shape[0]
    tiles = rows // CHUNK
    inner = y_ref.shape[1]
    width = pre_ref.shape[1]
    state_width = (width - inner) // 2
    following = (lax.rem(seq + 1, count), head, batch)
    greet_seq(pltpu.get_barrier_semaphore(), 0)
    for load in loads:
        load.wait()
    first = seq * rows

    def memory_copy(hop, owner):
        return exchange(
            memory_ref.at[owner],
            memory_ref.at[owner],
            sem_memory.at[0, hop],
            sem_memory.at[1, hop],
            following,
        )

    def memory_send(hop):
        @pl.when((seq - hop + 1 >= 0) & (seq < count - 1))
        def _():
            memory_copy(hop, lax.rem(seq - hop + 1 + count, count)).start()

    def memory_receive(hop):
        @pl.when(seq - hop >= 0)
        def _():
            memory_copy(hop, lax.rem(seq - hop + count, count)).wait_recv()

    def memory_hop(hop):
        memory_receive(hop - 1)
        memory_send(hop)

    halo_copy = exchange(
        pre_ref.at[pl.ds(rows, HALO)],
        pre_ref.at[pl.ds(0, HALO)],
        sem_halo.at[0],
        sem_halo.at[1],
        following,
    )

    def memory_tile(i):
        at = feed_rows(i)
        hidden = tokens_ref[at, :].astype(jnp.float32)
        inverse = lax.rsqrt(jnp.mean(hidden * hidden, axis=1, keepdims=True) + eps_norm)
        low = (hidden * inverse * gain_ref[...]).astype(jnp.bfloat16)
        normed[at, :] = low
        value = matmul(low, memory_weight[...])
        lane = lax.broadcasted_iota(jnp.int32, value.shape, 1)
        turned = value * table_ref[at, :LANES] + turn_half(value) * table_ref[at, LANES:]
        memory_ref[seq, at, :] = jnp.where(lane < HD, turned, value).astype(jnp.bfloat16)

    wide_tiles = rows // FEED_TILE
    each(wide_tiles, memory_tile)

    memory_send(1)

    def pre_tile(i):
        at = feed_rows(i)
        to = pl.ds(pl.multiple_of(i * FEED_TILE + HALO, HALO), FEED_TILE)
        low = normed[at, :]
        pre_ref[to, :inner] = matmul(low, input_weight[...])
        pre_ref[to, inner:] = matmul(low, maps_weight[...])

    each(wide_tiles, lambda i: pre_tile(wide_tiles - 1 - i))

    @pl.when(seq < count - 1)
    def _():
        halo_copy.start()

    if count > 2:
        memory_hop(2)

    def key_block(k):
        at = pl.ds(pl.multiple_of(k * LANES, LANES), LANES)
        row = seg_row_ref[:, at].astype(jnp.float32)
        key_seg_ref[at, :] = jnp.broadcast_to(row, (LANES, LANES)).T

    each(seg_row_ref.shape[1] // LANES, key_block)
    seg_ref[HALO : HALO + rows, :] = key_seg_ref[pl.ds(pl.multiple_of(first, TILE), rows), :]
    seg_ref[:HALO, :] = jnp.full((HALO, LANES), -1.0, jnp.float32)
    seg_ref[HALO + rows :, :] = jnp.full((HALO, LANES), -2.0, jnp.float32)

    @pl.when(seq > 0)
    def _():
        seg_ref[:HALO, :] = key_seg_ref[pl.ds(pl.multiple_of(first - HALO, HALO), HALO), :]

    @pl.when(seq < count - 1)
    def _():
        seg_ref[HALO + rows :, :] = key_seg_ref[pl.ds(pl.multiple_of(first + rows, TILE), HALO), :]

    heads = step_given.shape[0]
    lane = lax.broadcasted_iota(jnp.int32, (1, LANES), 1)
    wide_lane = lax.broadcasted_iota(jnp.int32, (1, inner), 1)
    bias_row = log_row = jnp.zeros((1, LANES), jnp.float32)
    skip_row = jnp.zeros((1, inner), jnp.float32)
    for h in range(heads):
        bias_row = jnp.where(lane == h, step_bias_ref[h], bias_row)
        log_row = jnp.where(lane == h, log_rate_ref[h], log_row)
        skip_row = jnp.where(wide_lane // HD == h, skip_gain_ref[h], skip_row)
    bias_ref[...] = bias_row
    rate_ref[...] = jnp.where(lane < heads, -jnp.exp(log_row), 0.0)
    skip_ref[...] = skip_row
    step_wide[...] = jnp.zeros_like(step_wide)
    step_wide[:heads, :] = step_given[...].astype(jnp.float32)
    step_weight[...] = step_wide[...].astype(jnp.bfloat16)
    taps_ref[...] = jnp.zeros_like(taps_ref)
    taps_ref[: conv_inner_ref.shape[0], :inner] = conv_inner_ref[...]
    taps_ref[: conv_inner_ref.shape[0], inner:] = conv_maps_ref[...]
    spread_ref[...] = spread_matrix(inner, HD)
    lower = jnp.where(ordered(CHUNK), 1.0, 0.0)

    def step_tile(i):
        at = tile_rows(i)
        raw = matmul_last(normed[at, :], step_weight[...]) + bias_ref[...]
        raw_ref[at, :] = raw
        cum_ref[at, :] = jnp.dot(lower, rate_ref[...] * soft_plus(raw), precision=highest)

    each(tiles, step_tile)

    @pl.when(seq == 0)
    def _():
        pre_ref[:HALO, :] = jnp.zeros((HALO, width), jnp.float32)

    @pl.when(seq > 0)
    def _():
        halo_copy.wait_recv()

    def conv_tile(i):
        at = tile_rows(i)
        window_at = pl.ds(pl.multiple_of(i * TILE, TILE), TILE + HALO)
        seg = seg_ref[window_at, :]
        own = seg[HALO:]
        masks = [
            jnp.where(seg[HALO - 3 + k : HALO - 3 + k + TILE] == own, 1.0, 0.0) for k in range(3)
        ]
        for j in range(width // LANES):
            columns = slice(j * LANES, (j + 1) * LANES)
            window = pre_ref[window_at, columns]
            summed = taps_ref[3:4, columns] * window[HALO:]
            for k in range(3):
                summed = summed + taps_ref[k : k + 1, columns] * (
                    window[HALO - 3 + k : HALO - 3 + k + TILE] * masks[k]
                )
            conv_ref[at, columns] = summed
            act[at, columns] = summed * sigmoid(summed)

    each(tiles, conv_tile)
    start_all(stores, 1, 2, 3, 4, 12, 13, 14, 15, 16, 17)
    local[...] = jnp.zeros_like(local)
    total[...] = jnp.ones_like(total)

    def input_map(at):
        return act[at, inner : inner + state_width].astype(jnp.bfloat16)

    def output_map(at):
        return act[at, inner + state_width :].astype(jnp.bfloat16)

    def local_chunk(c):
        at = tile_rows(c)
        _, start, end = chunk_flags(seg_ref, c)
        cum = cum_ref[at, :]
        last = cum[CHUNK - 1 :]
        spread = spread_ref[...]
        value = act[at, :inner] * spread_heads(soft_plus(raw_ref[at, :]), spread)
        scaled[at, :] = value.astype(jnp.bfloat16)
        weight = spread_heads(jnp.exp(last - cum) * end, spread)
        fresh = matmul_first(input_map(at), (value * weight).astype(jnp.bfloat16))
        keep = jnp.broadcast_to(jnp.exp(last) * start[CHUNK - 1 :], (HALO, LANES))
        keep = spread_heads(keep, spread)
        added[c] = fresh
        decay[c] = keep
        local[...] = local[...] * keep[:1] + fresh
        total[...] = total[...] * keep

    each(tiles, local_chunk)
    pieces = inner // PIECE

    def chain_copy(p):
        columns = pl.ds(p * PIECE, PIECE)
        return exchange(
            chain_out.at[:, columns],
            chain_in.at[:, columns],
            sem_chain.at[0, p],
            sem_chain.at[1, p],
            following,
        )

    @pl.when(seq == 0)
    def _():
        state[...] = jnp.zeros_like(state)
        chain_out[...] = local[...].astype(jnp.bfloat16)
        if count > 1:
            for p in range(pieces):
                chain_copy(p).start()

    if count > 3:
        memory_hop(3)

    def inside_chunk(c):
        at = tile_rows(c)
        own, _, _ = chunk_flags(seg_ref, c)
        cum = cum_ref[at, :]
        turned = cum.T
        meet = matmul_last(output_map(at), input_map(at))
        meet = jnp.where(ordered(CHUNK) & (own == own.T), meet, 0.0)
        for i in range(inner // LANES):
            columns = slice(i * LANES, (i + 1) * LANES)
            mixing = []
            for h in (2 * i, 2 * i + 1):
                gap = cum[:, h : h + 1] - turned[h : h + 1, :]
                mixing.append(meet * jnp.exp(jnp.minimum(gap, 0.0)))
            y_ref[at, columns] = matmul(
                jnp.concatenate(mixing, axis=1).astype(jnp.bfloat16),
                halves(scaled[at, columns].astype(jnp.float32), HD),
            )

    each(tiles, inside_chunk)

    def project_tile(i):
        at = feed_rows(i)
        low = normed[at, :]
        gate_z_ref[at, :] = matmul(low, gate_weight[...])
        value = matmul(low, query_weight[...])
        for k in range(value.shape[1] // LANES):
            part = value[:, k * LANES : (k + 1) * LANES]
            turned = part * table_ref[at, :LANES] + turn_half(part) * table_ref[at, LANES:]
            query_ref[at, k * LANES : (k + 1) * LANES] = turned.astype(jnp.bfloat16)

    def chain_wait(p):
        columns = pl.ds(p * PIECE, PIECE)
        chain_copy(p).wait_recv()
        came = chain_in[:, columns].astype(jnp.float32)
        state[:, columns] = came
        return came

    @pl.when(seq >= 2)
    def _():
        each(wide_tiles, project_tile)

    @pl.when((seq > 0) & (seq < count - 1))
    def _():
        for p in range(pieces):
            columns = pl.ds(p * PIECE, PIECE)
            chain_out[:, columns] = (
                chain_wait(p) * total[:1, columns] + local[:, columns]
            ).astype(jnp.bfloat16)
            chain_copy(p).start()

    @pl.when(seq < 2)
    def _():
        each(wide_tiles, project_tile)

    span(4, count, memory_hop)
    if count > 1:
        memory_receive(count - 1)

    def memory_rest(hop):
        @pl.when((seq - hop + 1 >= 0) & (seq < count - 1))
        def _():
            memory_copy(hop, lax.rem(seq - hop + 1 + count, count)).wait_send()

        @pl.when(seq + hop < count)
        def _():
            memory_ref[lax.rem(seq + hop, count)] = jnp.zeros(memory_ref.shape[1:], jnp.bfloat16)

    span(1, count, memory_rest)
    def turn_block(k):
        memory_turned[k] = memory_ref[k].astype(jnp.float32).T.astype(jnp.bfloat16)

    each(seq + 1, turn_block)

    def attention_block(i):
        at = tile_rows(i)
        turned, log = attend_block(
            first,
            0,
            (first + i * TILE + TILE - 1) // KEY_TILE,
            i,
            query_ref[at, :],
            lambda k: (memory_ref[k], memory_turned[k]),
            seg_ref,
            key_seg_ref,
        )
        for pair, tile in enumerate(unstacked_heads(turned, False)):
            columns = slice(pair * LANES, (pair + 1) * LANES)
            attention_ref[at, columns] = tile
            attention_low_ref[at, columns] = tile.astype(jnp.bfloat16)
        logs_ref[i] = jnp.broadcast_to(log, logs_ref.shape[1:])

    start_all(stores, 0, 7, 8)
    each(tiles, attention_block)
    start_all(stores, 9, 10, 11)

    @pl.when((seq > 0) & (seq == count - 1))
    def _():
        for p in range(pieces):
            chain_wait(p)

    def across_chunk(c):
        at = tile_rows(c)
        _, start, _ = chunk_flags(seg_ref, c)
        now = state[...]
        low = now.astype(jnp.bfloat16)
        states_ref[c] = low
        carried = spread_heads(jnp.exp(cum_ref[at, :]) * start, spread_ref[...])
        y_ref[at, :] += matmul(output_map(at), low) * carried + skip_ref[...] * act[at, :inner]
        state[...] = now * decay[c][:1] + added[c]

    each(tiles, across_chunk)
    states_ref[tiles] = state[...].astype(jnp.bfloat16)
    start_all(stores, 5, 6)

    @pl.when(seq < count - 1)
    def _():
        halo_copy.wait_send()
        for p in range(pieces):
            chain_copy(p).wait_send()


def mixer_forward(*operands):
    tokens, seg_row, table = operands[0], operands[2], operands[3]
    mamba_gate, step_given, query_weight, memory_weight = (
        operands[4],
        operands[7],
        operands[8],
        operands[9],
    )
    rows, width = tokens.shape
    total = seg_row.shape[1]
    count = lax.axis_size("seq")
    inner = mamba_gate.shape[1]
    conv_width = inner + operands[6].shape[1]
    state_width = (conv_width - inner) // 2
    query = query_weight.shape[1]
    chunks = rows // CHUNK
    pieces = inner // PIECE
    smem = pl.BlockSpec(memory_space=pltpu.SMEM)
    vmem = pl.BlockSpec(memory_space=pltpu.VMEM)
    low, full = jnp.bfloat16, jnp.float32
    shape = jax.ShapeDtypeStruct
    hbm = pl.BlockSpec(memory_space=pl.ANY)
    out_shape = [
            shape((rows, inner), full),
            shape((rows + HALO, conv_width), full),
            shape((rows, conv_width), full),
            shape((rows, LANES), full),
            shape((rows, LANES), full),
            shape((rows, inner), full),
            shape((chunks + 1, state_width, inner), low),
            shape((rows, query), low),
            shape((count, rows, memory_weight.shape[1]), low),
            shape((rows, query), full),
            shape((rows, query), low),
            shape((chunks, HALO, query // HD * TILE), full),
            shape((rows + 2 * HALO, LANES), full),
            shape((total, LANES), full),
            shape((LANES, width), low),
            shape((HALO, conv_width), full),
            shape((1, LANES), full),
            shape((1, inner), full),
        ]
    return pl.pallas_call(
        functools.partial(moving, mixer_kernel, 15, 12, len(out_shape)),
        out_shape=out_shape,
        in_specs=[hbm] * 12 + [smem] * 3,
        out_specs=[hbm] * len(out_shape),
        scratch_shapes=moving_scratch(operands[:12], out_shape)
        + [
            pltpu.VMEM((LANES, width), full),
            pltpu.VMEM((1, LANES), full),
            pltpu.VMEM((rows, width), low),
            pltpu.VMEM((LANES, inner), low),
            pltpu.VMEM((rows, conv_width), full),
            pltpu.VMEM((rows, inner), low),
            pltpu.VMEM((chunks, state_width, inner), full),
            pltpu.VMEM((chunks, HALO, inner), full),
            pltpu.VMEM((HALO, inner), full),
            pltpu.VMEM((state_width, inner), full),
            pltpu.VMEM((state_width, inner), full),
            pltpu.VMEM((state_width, inner), low),
            pltpu.VMEM((state_width, inner), low),
            pltpu.VMEM((count, memory_weight.shape[1], rows), low),
            pltpu.SemaphoreType.DMA((2, count)),
            pltpu.SemaphoreType.DMA((2,)),
            pltpu.SemaphoreType.DMA((2, pieces)),
        ],
        compiler_params=pltpu.CompilerParams(
            collective_id=2, has_side_effects=True, vmem_limit_bytes=60 << 20
        ),
        name="mixer_forward",
    )(*operands)


KEY_TILE = 512


def stacked_heads(values, first, factor):
    lane = lax.broadcasted_iota(jnp.int32, (values.shape[0], LANES), 1)
    keep = (lane < HD) if first else (lane >= HD)
    parts = []
    for h in range(values.shape[1] // HD):
        tile = values[:, (h // 2) * LANES : (h // 2 + 1) * LANES].astype(jnp.float32)
        if (h % 2 == 0) != first:
            tile = pltpu.roll(tile, HD, 1)
        parts.append(jnp.where(keep, tile * factor, 0.0))
    return jnp.concatenate(parts, axis=0)


def unstacked_heads(turned, first):
    heads = turned.shape[1] // TILE
    blocks = [turned[:, h * TILE : (h + 1) * TILE].T for h in range(heads)]
    lane = lax.broadcasted_iota(jnp.int32, (TILE, LANES), 1)
    tiles = []
    for even, odd in zip(blocks[::2], blocks[1::2]):
        if first:
            odd = pltpu.roll(odd, HD, 1)
        else:
            even = pltpu.roll(even, HD, 1)
        tiles.append(jnp.where(lane < HD, even, odd))
    return tiles


def key_tile(seg_turned, key_seg_ref, first, i, k):
    at = pl.ds(pl.multiple_of(k * KEY_TILE, KEY_TILE), KEY_TILE)
    place = k * KEY_TILE + lax.broadcasted_iota(jnp.int32, (KEY_TILE, TILE), 0)
    row = first + i * TILE + lax.broadcasted_iota(jnp.int32, (KEY_TILE, TILE), 1)
    return at, (place <= row) & (key_seg_ref[at, :] == seg_turned)


def query_segments(seg_ref, i):
    own = seg_ref[pl.ds(pl.multiple_of(i * TILE, TILE) + HALO, TILE), :].T
    return jnp.concatenate([own] * (KEY_TILE // TILE), axis=0)


def attend_block(first, low, high, i, queries_in, memory_of, seg_ref, key_seg_ref):
    heads = queries_in.shape[1] // HD
    turned = stacked_heads(queries_in, True, HD ** (-0.5)).T.astype(jnp.bfloat16)
    segs = query_segments(seg_ref, i)
    parts = [turned[:, h * TILE : (h + 1) * TILE] for h in range(heads)]

    def one(step, carry):
        at, allowed = key_tile(segs, key_seg_ref, first, i, high - step)
        keys, keys_turned = memory_of(high - step)
        after = []
        for part, (most, total, acc) in zip(parts, carry):
            scores = jnp.where(allowed, matmul(keys, part), neg_large)
            new = jnp.maximum(most, jnp.max(scores, axis=0, keepdims=True))
            weights = jnp.exp(scores - new)
            factor = jnp.exp(most - new)
            total = total * factor + jnp.sum(weights, axis=0, keepdims=True)
            acc = acc * factor + matmul(keys_turned, weights.astype(jnp.bfloat16))
            after.append((new, total, acc))
        return tuple(after)

    zero = (
        jnp.full((1, TILE), neg_large, jnp.float32),
        jnp.zeros((1, TILE), jnp.float32),
        jnp.zeros((LANES, TILE), jnp.float32),
    )
    result = lax.fori_loop(0, high - low + 1, one, (zero,) * heads)
    return (
        jnp.concatenate([acc / total for _, total, acc in result], axis=1),
        jnp.concatenate([most + jnp.log(total) for most, total, _ in result], axis=1),
    )


def attend_back_block(
    first, low, high, i, queries_in, d_out, out, log, memory_of, seg_ref, key_seg_ref, grads
):
    heads = queries_in.shape[1] // HD
    queries = stacked_heads(queries_in, True, HD ** (-0.5))
    outer = stacked_heads(d_out, False, 1.0)
    queries_turned, outer_turned = queries.T.astype(jnp.bfloat16), outer.T.astype(jnp.bfloat16)
    queries, outer = queries.astype(jnp.bfloat16), outer.astype(jnp.bfloat16)
    segs = query_segments(seg_ref, i)
    row = lax.broadcasted_iota(jnp.int32, (HALO, heads * HD), 0)
    lane = lax.broadcasted_iota(jnp.int32, (HALO, heads * HD), 1)
    pick = jnp.where(lane // HD == row, 1.0, 0.0).astype(jnp.bfloat16)
    high_part, low_part = two_parts(d_out * out)
    deltas = matmul_last(pick, high_part) + matmul_last(pick, low_part)
    spans = [slice(h * TILE, (h + 1) * TILE) for h in range(heads)]

    def one(step, totals):
        at, allowed = key_tile(segs, key_seg_ref, first, i, high - step)
        keys = memory_of(high - step)
        slopes, lows, after = [], [], []
        for h, (part, total) in enumerate(zip(spans, totals)):
            weights = jnp.exp(matmul(keys, queries_turned[:, part]) - log[:, part])
            weights = jnp.where(allowed, weights, 0.0)
            slope = weights * (matmul(keys, outer_turned[:, part]) - deltas[h : h + 1])
            slopes.append(slope.astype(jnp.bfloat16))
            lows.append(weights.astype(jnp.bfloat16))
            after.append(total + matmul_first(keys, slopes[-1]))
        grads[at, :] += matmul(jnp.concatenate(slopes, axis=1), queries) + matmul(
            jnp.concatenate(lows, axis=1), outer
        )
        return tuple(after)

    totals = lax.fori_loop(
        0, high - low + 1, one, (jnp.zeros((LANES, TILE), jnp.float32),) * heads
    )
    return jnp.concatenate(totals, axis=1) * HD ** (-0.5)


def attention_back_kernel(
    first_ref,
    low_ref,
    high_ref,
    query_ref,
    memory_ref,
    seg_ref,
    key_seg_ref,
    out_ref,
    log_ref,
    d_out_ref,
    table_ref,
    d_query_ref,
    d_memory_ref,
    grads,
):
    grads[...] = jnp.zeros_like(grads)

    def block(i):
        at = tile_rows(i)
        d_turned = attend_back_block(
            first_ref[0],
            low_ref[i],
            high_ref[i],
            i,
            query_ref[at, :],
            d_out_ref[at, :],
            out_ref[at, :],
            log_ref[i][:1],
            lambda k: memory_ref[pl.ds(pl.multiple_of(k * KEY_TILE, KEY_TILE), KEY_TILE), :],
            seg_ref,
            key_seg_ref,
            grads,
        )
        for pair, tile in enumerate(unstacked_heads(d_turned, True)):
            turned = tile * table_ref[at, :LANES] - turn_half(tile) * table_ref[at, LANES:]
            d_query_ref[at, pair * LANES : (pair + 1) * LANES] = turned.astype(jnp.bfloat16)

    each(query_ref.shape[0] // TILE, block)
    d_memory_ref[...] = grads[...].astype(jnp.bfloat16)


def attention_back(spans, query, memory, segments, key_segments, out, logs, d_out, table):
    vmem = pl.BlockSpec(memory_space=pltpu.VMEM)
    return pl.pallas_call(
        attention_back_kernel,
        out_shape=[
            jax.ShapeDtypeStruct(query.shape, jnp.bfloat16),
            jax.ShapeDtypeStruct(memory.shape, jnp.bfloat16),
        ],
        in_specs=[pl.BlockSpec(memory_space=pltpu.SMEM)] * 3 + [vmem] * 8,
        out_specs=[vmem] * 2,
        scratch_shapes=[pltpu.VMEM(memory.shape, jnp.float32)],
        compiler_params=pltpu.CompilerParams(vmem_limit_bytes=56 << 20),
        name="attention_back",
    )(*spans, query, memory, segments, key_segments, out, logs, d_out, table)


MERGED_INPUTS = 30


def mixer_back_kernel(merged, chunks, *refs):
    refs = list(refs)

    def take(count):
        nonlocal refs
        now, refs = refs[:count], refs[count:]
        return now

    if merged:
        given = take(MERGED_INPUTS)
        early, came = take(4), take(2)
        d_tokens_ref, *outs, small_out = take(7)
        copies = take(MERGED_INPUTS)
        (sem_load,) = take(1)
        loads = [
            pltpu.make_async_copy(source, target, sem_load.at[k])
            for k, (source, target) in enumerate(zip(given, copies))
        ]
        for load in loads:
            load.start()
        refs = copies + refs
    (
        tokens_ref,
        gain_ref,
        seg_ref,
        table_ref,
        gate_weight,
        input_weight,
        maps_weight,
        step_weight,
        query_weight,
        memory_weight,
        taps_ref,
        rate_ref,
        skip_ref,
        pre_ref,
        conv_ref,
        raw_ref,
        cum_ref,
        y_ref,
        states_ref,
        d_second_ref,
        d_y_ref,
        d_gate_z_ref,
    ) = take(22)
    if merged:
        (
            query_ref,
            memory_ref,
            key_seg_ref,
            attention_ref,
            logs_ref,
            d_attention_ref,
            feed_gain_ref,
            mamba_gain_ref,
        ) = take(8)
    else:
        d_query_ref, d_memory_ref = take(2)
        d_tokens_ref, g_side_ref, g_taps_ref, g_gain_ref, g_heads_ref = take(5)
    (
        normed,
        spread_ref,
        act,
        d_conv,
        d_scaled,
        d_maps,
        row_term,
        added,
        local,
        total,
        state,
        skip_sum,
        side,
        chain_out,
        chain_in,
        maps_send,
        maps_recv,
        memory_recv,
        norm_send,
        norm_recv,
        sem_memory,
        sem_halo,
        sem_chain,
        sem_maps,
        sem_norm,
    ) = take(25)
    if merged:
        g_side_ref, grads, d_memory_ref, small_in, small_buf, sem_small = take(6)
        g_taps_ref = g_gain_ref = g_heads_ref = small_in
    seq, head, batch = lax.axis_index("seq"), lax.axis_index("head"), lax.axis_index("batch")
    count = lax.axis_size("seq")
    rows = tokens_ref.shape[0]
    tiles = rows // CHUNK
    inner = y_ref.shape[1]
    width = pre_ref.shape[1]
    state_width = (width - inner) // 2
    model = tokens_ref.shape[1]
    peer = peer_device()
    previous = (lax.rem(seq - 1 + count, count), head, batch)
    pieces = inner // PIECE
    step_at = width
    query_at = step_at + LANES
    memory_at = query_at + query_weight.shape[1]
    if merged:
        greet_all(pltpu.get_barrier_semaphore(), True)
        reduction = Reduction(chunks, list(early) + [g_side_ref], outs, refs, came)
        reduction.allow(sum(1 for c in chunks if c[0] < len(early)))
        advance = reduction.advance
        for load in loads:
            load.wait()
    else:
        greet_seq(pltpu.get_barrier_semaphore(), 1)

        def advance():
            return None

    spread_ref[...] = spread_matrix(inner, HD)

    def chain_copy(p):
        columns = pl.ds(p * PIECE, PIECE)
        return exchange(
            chain_out.at[:, columns],
            chain_in.at[:, columns],
            sem_chain.at[0, p],
            sem_chain.at[1, p],
            previous,
        )

    def memory_copy(step):
        place = lax.rem(seq - step + count, count)
        return exchange(
            d_memory_ref.at[place],
            memory_recv.at[step - 1],
            sem_memory.at[0, step],
            sem_memory.at[1, step],
            (place, head, batch),
        )

    halo_copy = exchange(
        d_conv.at[pl.ds(0, HALO)],
        d_conv.at[pl.ds(rows, HALO)],
        sem_halo.at[0],
        sem_halo.at[1],
        previous,
    )
    maps_copy = exchange(maps_send, maps_recv, sem_maps.at[0], sem_maps.at[1], peer)

    def norm_copy(i):
        at = tile_rows(i)
        return exchange(
            norm_send.at[at], norm_recv.at[at], sem_norm.at[0, i], sem_norm.at[1, i], peer
        )

    def input_map(at):
        return act[at, inner : inner + state_width].astype(jnp.bfloat16)

    def output_map(at):
        return act[at, inner + state_width :].astype(jnp.bfloat16)

    def keep_of(c, start):
        last = cum_ref[tile_rows(c), :][CHUNK - 1 :]
        keep = jnp.broadcast_to(jnp.exp(last) * start[CHUNK - 1 :], (HALO, LANES))
        return spread_heads(keep, spread_ref[...])

    def carried_of(c, start):
        return spread_heads(jnp.exp(cum_ref[tile_rows(c), :]) * start, spread_ref[...])

    def activate(i):
        at = tile_rows(i)
        value = conv_ref[at, :]
        act[at, :] = value * sigmoid(value)

    each(tiles, activate)
    local[...] = jnp.zeros_like(local)
    total[...] = jnp.ones_like(total)

    def local_chunk(step):
        c = tiles - 1 - step
        at = tile_rows(c)
        _, start, _ = chunk_flags(seg_ref, c)
        keep = keep_of(c, start)
        value = (d_y_ref[at, :] * carried_of(c, start)).astype(jnp.bfloat16)
        fresh = matmul_first(output_map(at), value)
        added[c] = fresh
        local[...] = local[...] * keep[:1] + fresh
        total[...] = total[...] * keep

    each(tiles, local_chunk)

    @pl.when(seq == count - 1)
    def _():
        state[...] = jnp.zeros_like(state)
        chain_out[...] = local[...].astype(jnp.bfloat16)
        if count > 1:
            for p in range(pieces):
                chain_copy(p).start()

    if merged:
        first = seq * rows
        grads[...] = jnp.zeros_like(grads)

        def attention_block(i):
            at = tile_rows(i)
            d_turned = attend_back_block(
                first,
                0,
                (first + i * TILE + TILE - 1) // KEY_TILE,
                i,
                query_ref[at, :],
                d_attention_ref[at, :],
                attention_ref[at, :],
                logs_ref[i][:1],
                lambda k: memory_ref[pl.ds(pl.multiple_of(k * KEY_TILE, KEY_TILE), KEY_TILE), :],
                seg_ref,
                key_seg_ref,
                grads,
            )
            for pair, tile in enumerate(unstacked_heads(d_turned, True)):
                turned = tile * table_ref[at, :LANES] - turn_half(tile) * table_ref[at, LANES:]
                columns = pl.ds(query_at + pair * LANES, LANES)
                side[at, columns] = turned.astype(jnp.bfloat16)

        span(0, 1, attention_block)
        advance()

    def chain_wait(p):
        columns = pl.ds(p * PIECE, PIECE)
        chain_copy(p).wait_recv()
        came = chain_in[:, columns].astype(jnp.float32)
        state[:, columns] = came
        return came

    @pl.when((seq > 0) & (seq < count - 1))
    def _():
        for p in range(pieces):
            columns = pl.ds(p * PIECE, PIECE)
            came = chain_wait(p)
            chain_out[:, columns] = (came * total[:1, columns] + local[:, columns]).astype(
                jnp.bfloat16
            )
            chain_copy(p).start()

    if merged:
        for i in range(1, tiles):
            span(i, i + 1, attention_block)
            advance()

        def low_block(place):
            at = pl.ds(pl.multiple_of(place * rows, rows), rows)
            d_memory_ref[place] = grads[at, :].astype(jnp.bfloat16)

        each(count, low_block)

    def memory_start(step, carry):
        @pl.when(seq - step >= 0)
        def _():
            memory_copy(step).start()

        return carry

    lax.fori_loop(1, count, memory_start, 0)
    skip_sum[...] = jnp.zeros_like(skip_sum)

    def inside_chunk(c):
        at = tile_rows(c)
        own, start, _ = chunk_flags(seg_ref, c)
        cum = cum_ref[at, :]
        turned = cum.T
        spread = spread_ref[...]
        low_in, low_out = input_map(at), output_map(at)
        allowed = ordered(CHUNK).astype(jnp.float32).T * jnp.where(own == own.T, 1.0, 0.0)
        meet = matmul_last(low_in, low_out) * allowed
        value = act[at, :inner]
        scaled = value * spread_heads(soft_plus(raw_ref[at, :]), spread)
        d_y = d_y_ref[at, :]
        d_meet = jnp.zeros((CHUNK, CHUNK), jnp.float32)
        for i in range(inner // LANES):
            columns = slice(i * LANES, (i + 1) * LANES)
            d_tile = d_y[:, columns]
            d_mixing = matmul_last(halves(scaled[:, columns], HD), d_tile.astype(jnp.bfloat16))
            mixing = []
            for k, h in enumerate((2 * i, 2 * i + 1)):
                gap = turned[h : h + 1, :] - cum[:, h : h + 1]
                fade = jnp.exp(jnp.minimum(gap, 0.0))
                mixing.append(meet * fade)
                d_meet = d_meet + d_mixing[k * CHUNK : (k + 1) * CHUNK] * fade
            d_scaled[at, columns] = matmul(
                jnp.concatenate(mixing, axis=1).astype(jnp.bfloat16), halves(d_tile, HD)
            )
        d_meet = (d_meet * allowed).astype(jnp.bfloat16)
        d_maps[at, :state_width] = matmul(d_meet, low_out)
        carried = (d_y * carried_of(c, start)).astype(jnp.bfloat16)
        d_maps[at, state_width:] = matmul_first(d_meet, low_in) + matmul_last(
            carried, states_ref[c]
        )
        product = d_y * value
        skip_sum[...] += jnp.sum(product, axis=0, keepdims=True)
        low = d_y.astype(jnp.bfloat16).astype(jnp.float32)
        row_term[at, :] = sum_heads(low * (y_ref[at, :] - skip_ref[...] * value), spread)

    span(0, tiles // 2, inside_chunk)
    advance()
    span(tiles // 2, tiles, inside_chunk)
    advance()

    @pl.when((seq == 0) & (seq < count - 1))
    def _():
        for p in range(pieces):
            chain_wait(p)

    if merged:
        small_in[...] = jnp.zeros_like(small_in)
        small_in[4:5, :inner] = mamba_gain_ref[...]
        small_in[6:7, :] = feed_gain_ref[...]
    else:
        g_heads_ref[...] = jnp.zeros_like(g_heads_ref)

    gain_row = 5 if merged else 0

    def add_heads(k, values):
        row, lane = (7, k * LANES) if merged else (k, 0)
        g_heads_ref[row : row + 1, lane : lane + LANES] += values

    upper = jnp.where(ordered(CHUNK), 1.0, 0.0).T

    def across_chunk(step):
        c = tiles - 1 - step
        at = tile_rows(c)
        _, start, end = chunk_flags(seg_ref, c)
        spread = spread_ref[...]
        cum = cum_ref[at, :]
        last = cum[CHUNK - 1 :]
        now = state[...]
        low = now.astype(jnp.bfloat16)
        raw = raw_ref[at, :]
        steps = soft_plus(raw)
        steps_wide = spread_heads(steps, spread)
        value = act[at, :inner]
        scaled = value * steps_wide
        weight = spread_heads(jnp.exp(last - cum) * end, spread)
        d_value = d_scaled[at, :] + matmul(input_map(at), low) * weight
        d_maps[at, :state_width] += matmul_last((scaled * weight).astype(jnp.bfloat16), low)
        final = jnp.sum(
            states_ref[c + 1].astype(jnp.float32) * low.astype(jnp.float32), axis=0, keepdims=True
        )
        final = sum_heads(jnp.broadcast_to(final, (HALO, inner)), spread)[:1]
        low_scaled = scaled.astype(jnp.bfloat16).astype(jnp.float32)
        d_cum = row_term[at, :] - sum_heads(low_scaled * d_value, spread)
        d_rate = jnp.dot(upper, d_cum, precision=highest) + final
        rate = rate_ref[...]
        d_steps = sum_heads(value * d_value, spread) + rate * d_rate
        d_raw = d_steps * sigmoid(raw)
        add_heads(0, rate * jnp.sum(steps * d_rate, axis=0, keepdims=True))
        add_heads(1, jnp.sum(d_raw, axis=0, keepdims=True))
        side[at, step_at:query_at] = d_raw.astype(jnp.bfloat16)
        d_conv[at, :inner] = steps_wide * d_value + skip_ref[...] * d_y_ref[at, :]
        state[...] = now * keep_of(c, start)[:1] + added[c]

    span(0, tiles // 2, across_chunk)
    advance()
    span(tiles // 2, tiles, across_chunk)
    advance()
    add_heads(2, sum_heads(jnp.broadcast_to(skip_sum[:1], (HALO, inner)), spread_ref[...])[:1])
    maps_send[...] = d_maps[...].astype(jnp.bfloat16)
    maps_copy.start()

    def copy_tile(i):
        at = tile_rows(i)
        hidden = tokens_ref[at, :].astype(jnp.float32)
        inverse = lax.rsqrt(jnp.mean(hidden * hidden, axis=1, keepdims=True) + eps_norm)
        normed[at, :] = (hidden * inverse * gain_ref[...]).astype(jnp.bfloat16)

    each(tiles, copy_tile)
    maps_copy.wait()

    def conv_back_tile(i):
        at = tile_rows(i)
        d_conv[at, inner:] = maps_send[at, :].astype(jnp.float32) + maps_recv[at, :].astype(
            jnp.float32
        )
        value = conv_ref[at, :]
        sig = sigmoid(value)
        d_conv[at, :] = d_conv[at, :] * (sig * (1.0 + value * (1.0 - sig)))

    each(tiles, conv_back_tile)

    @pl.when(seq > 0)
    def _():
        halo_copy.start()

    @pl.when(seq == count - 1)
    def _():
        d_conv[pl.ds(rows, HALO), :] = jnp.zeros((HALO, width), jnp.float32)

    @pl.when(seq < count - 1)
    def _():
        halo_copy.wait_recv()

    if not merged:
        g_taps_ref[...] = jnp.zeros_like(g_taps_ref)

    def taps_tile(i):
        at = tile_rows(i)
        window_at = pl.ds(pl.multiple_of(i * TILE, TILE), TILE + HALO)
        seg = seg_ref[pl.ds(pl.multiple_of(i * TILE, TILE), TILE + 2 * HALO), :]
        own = seg[HALO : HALO + TILE]
        before = [
            jnp.where(seg[HALO - 3 + k : HALO - 3 + k + TILE] == own, 1.0, 0.0) for k in range(3)
        ]
        after = [
            jnp.where(seg[HALO + 3 - k : HALO + 3 - k + TILE] == own, 1.0, 0.0) for k in range(3)
        ]
        for j in range(width // LANES):
            columns = slice(j * LANES, (j + 1) * LANES)
            window = pre_ref[window_at, columns]
            grads = d_conv[window_at, columns]
            own_grad = grads[:TILE]
            summed = taps_ref[3:4, columns] * own_grad
            g_taps_ref[3:4, columns] += jnp.sum(own_grad * window[HALO:], axis=0, keepdims=True)
            for k in range(3):
                summed = summed + taps_ref[k : k + 1, columns] * (
                    grads[3 - k : 3 - k + TILE] * after[k]
                )
                g_taps_ref[k : k + 1, columns] += jnp.sum(
                    own_grad * (window[HALO - 3 + k : HALO - 3 + k + TILE] * before[k]),
                    axis=0,
                    keepdims=True,
                )
            side[at, j * LANES : (j + 1) * LANES] = summed.astype(jnp.bfloat16)

    each(tiles, taps_tile)
    advance()

    def memory_wait(step, carry):
        @pl.when(seq - step >= 0)
        def _():
            memory_copy(step).wait_send()

        @pl.when(seq + step < count)
        def _():
            memory_copy(step).wait_recv()

        return carry

    lax.fori_loop(1, count, memory_wait, 0)

    def memory_tile(i):
        at = tile_rows(i)

        def one(step, carry):
            came = memory_recv[step - 1, at, :].astype(jnp.float32)
            return carry + jnp.where(seq + step < count, came, 0.0)

        grad = lax.fori_loop(1, count, one, d_memory_ref[seq, at, :].astype(jnp.float32))
        lane = lax.broadcasted_iota(jnp.int32, grad.shape, 1)
        turned = grad * table_ref[at, :LANES] - turn_half(grad) * table_ref[at, LANES:]
        side[at, memory_at : memory_at + LANES] = jnp.where(lane < HD, turned, grad).astype(
            jnp.bfloat16
        )
        if not merged:
            side[at, query_at:memory_at] = d_query_ref[at, :]

    each(tiles, memory_tile)

    def weight_block(k):
        size = model // count
        block = pl.ds(pl.multiple_of(k * size, LANES), size)
        grad = matmul_first(normed[:, block], side[...])
        if merged:
            bits = seq_bits()
            g_side_ref[place_bits(k, bits)] = grad.reshape(g_side_ref.shape[bits:]).astype(
                jnp.bfloat16
            )
        else:
            g_side_ref[block, :] = grad.astype(jnp.bfloat16)

    each(count, weight_block)
    if merged:
        reduction.allow(len(chunks))
    advance()

    def norm_tile(i):
        at = tile_rows(i)
        part = (
            matmul_last(d_gate_z_ref[at, :], gate_weight[...])
            + matmul_last(side[at, :inner], input_weight[...])
            + matmul_last(side[at, inner:step_at], maps_weight[...]) / lax.axis_size("head")
            + matmul(side[at, step_at:query_at], step_weight[...])
            + matmul_last(side[at, query_at:memory_at], query_weight[...])
            + matmul_last(side[at, memory_at:], memory_weight[...])
        )
        norm_send[at, :] = part.astype(jnp.bfloat16)
        norm_copy(i).start()

    each(tiles, norm_tile)

    advance()
    if not merged:
        g_gain_ref[...] = jnp.zeros_like(g_gain_ref)

    def last_tile(i):
        at = tile_rows(i)
        norm_copy(i).wait()
        d_norm = norm_send[at, :].astype(jnp.float32) + norm_recv[at, :].astype(jnp.float32)
        hidden = tokens_ref[at, :].astype(jnp.float32)
        inverse = lax.rsqrt(jnp.mean(hidden * hidden, axis=1, keepdims=True) + eps_norm)
        e_one = d_norm * gain_ref[...]
        cross = jnp.sum(e_one * hidden, axis=1, keepdims=True) / model
        d_tokens_ref[at, :] = (
            d_second_ref[at, :] + inverse * e_one - hidden * (inverse * inverse * inverse * cross)
        )
        g_gain_ref[gain_row : gain_row + 1, :] += jnp.sum(
            d_norm * hidden * inverse, axis=0, keepdims=True
        )

    each(tiles, last_tile)
    if merged:
        small_sum = SmallSum(small_in, small_buf, sem_small)
        small_sum.start()
        reduction.finish()
        small_out[...] = small_sum.finish()

    @pl.when(seq > 0)
    def _():
        halo_copy.wait_send()
        for p in range(pieces):
            chain_copy(p).wait_send()


def mixer_back(common, saved, attention, grads=None, came=()):
    tokens = common[0]
    rows, model = tokens.shape
    gate_weight, query_weight, memory_weight, taps = common[4], common[8], common[9], common[10]
    merged = grads is not None
    count = lax.axis_size("seq")
    inner = gate_weight.shape[1]
    width = taps.shape[1]
    state_width = (width - inner) // 2
    tiles = rows // CHUNK
    pieces = inner // PIECE
    memory_width = memory_weight.shape[1]
    side = width + LANES + query_weight.shape[1] + memory_width
    vmem = pl.BlockSpec(memory_space=pltpu.VMEM)
    hbm = pl.BlockSpec(memory_space=pl.ANY)
    low, full = jnp.bfloat16, jnp.float32
    shape = jax.ShapeDtypeStruct
    operands = [*common, *saved]
    in_specs = [vmem] * (len(operands) + len(attention))
    operands += attention
    chunks = None
    scratch = [
        pltpu.VMEM((rows, model), low),
        pltpu.VMEM((LANES, inner), low),
        pltpu.VMEM((rows, width), full),
        pltpu.VMEM((rows + HALO, width), full),
        pltpu.VMEM((rows, inner), full),
        pltpu.VMEM((rows, 2 * state_width), full),
        pltpu.VMEM((rows, LANES), full),
        pltpu.VMEM((tiles, state_width, inner), full),
        pltpu.VMEM((state_width, inner), full),
        pltpu.VMEM((HALO, inner), full),
        pltpu.VMEM((state_width, inner), full),
        pltpu.VMEM((1, inner), full),
        pltpu.VMEM((rows, side), low),
        pltpu.VMEM((state_width, inner), low),
        pltpu.VMEM((state_width, inner), low),
        pltpu.VMEM((rows, 2 * state_width), low),
        pltpu.VMEM((rows, 2 * state_width), low),
        pltpu.VMEM((max(count - 1, 1), rows, memory_width), low),
        pltpu.VMEM((rows, model), low),
        pltpu.VMEM((rows, model), low),
        pltpu.SemaphoreType.DMA((2, count)),
        pltpu.SemaphoreType.DMA((2,)),
        pltpu.SemaphoreType.DMA((2, pieces)),
        pltpu.SemaphoreType.DMA((2,)),
        pltpu.SemaphoreType.DMA((2, tiles)),
    ]
    if merged:
        blocks = list(grads)
        widths = [g.shape[-1] for g in grads] + [side]
        chunks = column_chunks(widths)
        loaded = [pltpu.VMEM(x.shape, x.dtype) for x in operands]
        scratch = loaded + [pltpu.SemaphoreType.DMA((len(loaded),))] + scratch
        operands += blocks + list(came)
        in_specs = [hbm] * len(operands)
        own = blocks[0].shape[-2]
        small = (HALO, model)
        out_shape = (
            [shape((rows, model), full)]
            + [shape((2, 2, own, w), low) for w in widths]
            + [shape(small, full)]
        )
        scratch += [
            pltpu.VMEM(blocks[0].shape[:-1] + (side,), low),
            pltpu.VMEM((count * rows, memory_width), full),
            pltpu.VMEM((count, rows, memory_width), low),
        ]
        scratch += small_scratch(small) + reduction_scratch(chunks, widths, own)
    else:
        out_shape = [
            shape((rows, model), full),
            shape((model, side), low),
            shape((HALO, width), full),
            shape((1, model), full),
            shape((HALO, LANES), full),
        ]
    return pl.pallas_call(
        functools.partial(mixer_back_kernel, merged, chunks),
        out_shape=out_shape,
        in_specs=in_specs,
        out_specs=[vmem] * len(out_shape),
        scratch_shapes=scratch,
        compiler_params=pltpu.CompilerParams(
            collective_id=3, has_side_effects=True, vmem_limit_bytes=62 << 20
        ),
        name="mixer_back",
    )(*operands)


def finish_kernel(sizes, count, *refs):
    inner, maps, heads, query, own = sizes
    full = jnp.float32
    refs = list(refs)

    def take(number):
        nonlocal refs
        now, refs = refs[:number], refs[number:]
        return now

    sums, (small,), passed = take(5), take(1), take(2)
    outs, small_outs, passed_outs = take(count), take(9), take(2)
    loaded, held, wide = take(5), take(2), take(count)
    sem_in, sem_out = refs
    loads = [
        pltpu.make_async_copy(a, b, sem_in.at[k])
        for k, (a, b) in enumerate(zip([*sums, *passed], loaded + held))
    ]
    for copy in loads[5:] + loads[:5]:
        copy.start()
    down, feed, mixed, gate, side = loaded
    half = feed.shape[1] // 2
    step_at = inner + maps
    query_at = step_at + LANES
    memory_at = query_at + query
    parts = (
        (0, lambda: down[...]),
        (1, lambda: feed[:, :half]),
        (1, lambda: feed[:, half:]),
        (2, lambda: mixed[:, :inner]),
        (2, lambda: mixed[:, inner:]),
        (3, lambda: gate[...]),
        (4, lambda: side[:, :inner]),
        (4, lambda: side[:, inner:step_at]),
        (4, lambda: side[:, query_at:memory_at]),
        (4, lambda: side[:, memory_at:]),
    )
    stores = []
    for k, (a, b) in enumerate(zip(held, passed_outs)):
        loads[5 + k].wait()
        stores.append(pltpu.make_async_copy(a, b, sem_out.at[count + k]))
        stores[-1].start()
    for k, (group, value) in enumerate(parts):
        if k == 0 or parts[k - 1][0] != group:
            loads[group].wait()
        wide[k][...] = value().astype(full)
        stores.append(pltpu.make_async_copy(wide[k], outs[k], sem_out.at[k]))
        stores[-1].start()
    o_step, o_conv_inner, o_conv_maps, o_mixer_gain, o_rate, o_bias, o_skip, o_mamba, o_feed = (
        small_outs
    )
    o_step[...] = side[:, step_at:query_at].astype(full).T[:heads]
    seq = lax.axis_index("seq")
    value = small[...]
    width = value.shape[1]
    o_conv_inner[...] = value[:4, :inner]
    o_conv_maps[...] = value[:4, inner:]
    turned = pltpu.roll(value, lax.rem(width - seq * own, width), 1)
    o_mixer_gain[...] = turned[5:6, :own]
    o_feed[...] = turned[6:7, :own]
    for k, out in enumerate((o_rate, o_bias, o_skip)):
        out[...] = value[7:8, k * LANES : (k + 1) * LANES][:, :heads]
    for k in range(inner // LANES):
        o_mamba[k : k + 1, :] = value[4:5, k * LANES : (k + 1) * LANES]
    for copy in stores:
        copy.wait()


def finish_outputs(sums, small, passed, sizes):
    inner, maps, heads, query, own = sizes
    sums = [s.reshape(own, s.shape[-1]) for s in sums]
    half = sums[1].shape[1] // 2
    attention = sums[2].shape[1] - inner
    memory = sums[4].shape[1] - inner - maps - LANES - query
    full = jnp.float32
    widths = (sums[0].shape[1], half, half, inner, attention, inner, inner, maps, query, memory)
    big = [jax.ShapeDtypeStruct((own, w), full) for w in widths]
    little = [
        jax.ShapeDtypeStruct(s, full)
        for s in (
            (heads, own),
            (4, inner),
            (4, maps),
            (1, own),
            (1, heads),
            (1, heads),
            (1, heads),
            (inner // LANES, LANES),
            (1, own),
        )
    ]
    vmem = pl.BlockSpec(memory_space=pltpu.VMEM)
    hbm = pl.BlockSpec(memory_space=pl.ANY)
    return pl.pallas_call(
        functools.partial(finish_kernel, sizes, len(big)),
        out_shape=big + little + [jax.ShapeDtypeStruct(p.shape, p.dtype) for p in passed],
        in_specs=[hbm] * 5 + [vmem] + [hbm] * 2,
        out_specs=[hbm] * len(big) + [vmem] * len(little) + [hbm] * 2,
        scratch_shapes=[pltpu.VMEM(s.shape, s.dtype) for s in [*sums, *passed]]
        + [pltpu.VMEM(s.shape, full) for s in big]
        + [
            pltpu.SemaphoreType.DMA((7,)),
            pltpu.SemaphoreType.DMA((len(big) + 2,)),
        ],
        compiler_params=pltpu.CompilerParams(vmem_limit_bytes=60 << 20),
        name="finish_outputs",
    )(*sums, small, *passed)


def rotation_table(position):
    half = HD // 2
    lane = jnp.arange(LANES)
    inverse_freq = rope_base ** (-(lane % half).astype(jnp.float32) / half)
    angles = position.astype(jnp.float32)[:, None] * inverse_freq[None, :]
    sign = jnp.where(lane % HD < half, -1.0, 1.0)
    return jnp.concatenate([jnp.cos(angles), sign[None, :] * jnp.sin(angles)], axis=1)


def body(
    tokens,
    seg_ids,
    mixer_gain,
    mamba_gate,
    mamba_input,
    mamba_maps,
    mamba_step,
    conv_inner,
    conv_maps,
    log_rate,
    step_bias,
    skip_gain,
    mamba_gain,
    mamba_output,
    query_weight,
    memory_weight,
    attention_out,
    feed_gain,
    gate_weight,
    lift_weight,
    down_weight,
    cotangent,
):
    tokens, cotangent = tokens[0], cotangent[0]
    rows, wide = tokens.shape
    tap_count, inner = conv_inner.shape
    head_count = log_rate.shape[0]
    offset = lax.axis_index("seq") * rows
    table = rotation_table(offset + jnp.arange(rows, dtype=jnp.int32))
    (
        gate_z,
        pre,
        conv,
        raw,
        cum,
        y,
        states,
        query,
        memory,
        attention,
        attention_low,
        logs,
        window,
        key_segments,
        step_weight,
        taps,
        rate,
        skip,
    ) = mixer_forward(
        tokens,
        mixer_gain[None],
        seg_ids,
        table,
        mamba_gate,
        mamba_input,
        mamba_maps,
        mamba_step.T,
        query_weight,
        memory_weight,
        conv_inner,
        conv_maps,
        step_bias,
        log_rate,
        skip_gain,
    )
    all_memory = memory.reshape(memory.shape[0] * rows, memory.shape[2])
    (
        layer_out,
        d_second,
        d_y,
        d_gate_z,
        d_attention,
        g_feed,
        g_mixed,
        g_down,
        g_gate,
        g_feed_gain,
        g_mamba_gain,
        *came,
    ) = feed_layer(
        y,
        gate_z,
        attention_low,
        tokens,
        cotangent,
        mixer_gain,
        mamba_gain,
        feed_gain,
        mamba_output,
        attention_out,
        gate_weight,
        lift_weight,
        down_weight,
    )
    common = [
        tokens,
        mixer_gain[None],
        window,
        table,
        mamba_gate,
        mamba_input,
        mamba_maps,
        step_weight,
        query_weight,
        memory_weight,
        taps,
        rate,
        skip,
    ]
    saved = [pre, conv, raw, cum, y, states, d_second, d_y, d_gate_z]
    early = [g_down, g_feed, g_mixed, g_gate]
    if lax.axis_size("seq") == 4:
        grad_tokens, *sums, small = mixer_back(
            common,
            saved,
            [
                query,
                all_memory,
                key_segments,
                attention,
                logs,
                d_attention,
                g_feed_gain,
                g_mamba_gain,
            ],
            early,
            came,
        )
    else:
        starts = offset + jnp.arange(rows // TILE, dtype=jnp.int32) * TILE
        reach = seg_ids[0, KEY_TILE - 1 :: KEY_TILE]
        own = lax.dynamic_slice_in_dim(seg_ids[0], offset, rows)[::TILE]
        low = jnp.sum((reach[None, :] < own[:, None]).astype(jnp.int32), axis=1)
        spans = (offset[None], low, (starts + TILE - 1) // KEY_TILE)
        d_query, d_memory = attention_back(
            spans, query, all_memory, window, key_segments, attention, logs, d_attention, table
        )
        grad_tokens, g_side, g_taps, g_mixer_gain, g_heads = mixer_back(
            common, saved, [d_query, d_memory.reshape(memory.shape)]
        )
        *sums, small = reduce_gradients(
            early + [g_side],
            jnp.concatenate(
                [
                    g_taps[:tap_count],
                    jnp.pad(g_mamba_gain, ((0, 0), (0, wide - inner))),
                    g_mixer_gain,
                    g_feed_gain,
                    jnp.pad(g_heads[:3].reshape(1, 3 * LANES), ((0, 0), (0, wide - 3 * LANES))),
                ],
                axis=0,
            ),
        )
    sizes = (
        inner,
        conv_maps.shape[1],
        head_count,
        query_weight.shape[1],
        wide // lax.axis_size("seq"),
    )
    (
        o_down,
        o_gate,
        o_lift,
        o_output,
        o_attention,
        o_gate_z,
        o_inner,
        o_maps,
        o_query,
        o_memory,
        o_step,
        o_conv_inner,
        o_conv_maps,
        o_mixer_gain,
        o_rate,
        o_bias,
        o_skip,
        o_mamba_gain,
        o_feed_gain,
        layer_out,
        grad_tokens,
    ) = finish_outputs(sums, small, (layer_out, grad_tokens), sizes)
    return (
        layer_out[None],
        grad_tokens[None],
        o_mixer_gain[0],
        o_gate_z,
        o_inner,
        o_maps,
        o_step.T,
        o_conv_inner,
        o_conv_maps,
        o_rate[0],
        o_bias[0],
        o_skip[0],
        o_mamba_gain.reshape(inner),
        o_output,
        o_query,
        o_memory,
        o_attention,
        o_feed_gain[0],
        o_gate,
        o_lift,
        o_down,
    )


def solution(mesh):
    return jax.shard_map(
        body,
        mesh=mesh,
        in_specs=(
            P("batch", "seq", None),
            P("batch", None),
            P(),
            P(None, "head"),
            P(None, "head"),
            P(),
            P(None, "head"),
            P(None, "head"),
            P(),
            P("head"),
            P("head"),
            P("head"),
            P("head"),
            P(None, "head"),
            P(None, "head"),
            P(None, "head"),
            P(None, "head"),
            P(),
            P(None, "head"),
            P(None, "head"),
            P(None, "head"),
            P("batch", "seq", None),
        ),
        out_specs=(
            P("batch", "seq", None),
            P("batch", "seq", None),
            P("seq"),
            P("seq", "head"),
            P("seq", "head"),
            P("seq", None),
            P("seq", "head"),
            P(None, "head"),
            P(),
            P("head"),
            P("head"),
            P("head"),
            P("head"),
            P("seq", "head"),
            P("seq", "head"),
            P("seq", "head"),
            P("seq", "head"),
            P("seq"),
            P("seq", "head"),
            P("seq", "head"),
            P("seq", "head"),
        ),
        check_vma=False,
    )
```
